32 devices in a mesh: dp: 8 (over y, x, core), ctx: 4 (over z).
Axes of the slice: x: 2, y: 2, z: 4, core: 2. Of those that a mesh axis runs over, the one named last changes fastest.
Arguments:
- tokens: bfloat16 [4096, 1152], P(('dp', 'ctx')), may hold values from -6 to 6
- cotangent: bfloat16 [4096, 1152], P(('dp', 'ctx')), may hold values from -6 to 6
- lengths: int32 [8, 2], P('dp'), may hold values from 32 to 256, as said below
- w_query: bfloat16 [1152, 1024], P(('dp', 'ctx')), may hold values from -0.1875 to 0.1875
- w_key: bfloat16 [1152, 256], P(('dp', 'ctx')), may hold values from -0.1875 to 0.1875
- w_value: bfloat16 [1152, 256], P(('dp', 'ctx')), may hold values from -0.1875 to 0.1875
- w_out: bfloat16 [1024, 1152], P(('dp', 'ctx')), may hold values from -0.1875 to 0.1875
- w_gate: bfloat16 [1152, 6912], P(('dp', 'ctx')), may hold values from -0.1875 to 0.1875
- w_up: bfloat16 [1152, 6912], P(('dp', 'ctx')), may hold values from -0.1875 to 0.1875
- w_down: bfloat16 [6912, 1152], P(('dp', 'ctx')), may hold values from -0.078125 to 0.078125
- gain_in: bfloat16 [1152], P(('dp', 'ctx')), may hold values from -0.75 to 0.75
- gain_query: bfloat16 [256], P(('dp', 'ctx')), may hold values from -0.75 to 0.75
- gain_key: bfloat16 [256], P(('dp', 'ctx')), may hold values from -0.75 to 0.75
- gain_attn: bfloat16 [1152], P(('dp', 'ctx')), may hold values from -0.75 to 0.75
- gain_pre: bfloat16 [1152], P(('dp', 'ctx')), may hold values from -0.75 to 0.75
- gain_post: bfloat16 [1152], P(('dp', 'ctx')), may hold values from -0.75 to 0.75
Outputs:
- output: bfloat16 [4096, 1152], P(('dp', 'ctx'))
- input_grad: bfloat16 [4096, 1152], P(('dp', 'ctx'))
- grad_query: float32 [1152, 1024], P('dp', 'ctx')
- grad_key: float32 [1152, 256], P('dp', 'ctx')
- grad_value: float32 [1152, 256], P('dp', 'ctx')
- grad_out: float32 [1024, 1152], P('ctx', 'dp')
- grad_gate: float32 [1152, 6912], P('dp', 'ctx')
- grad_up: float32 [1152, 6912], P('dp', 'ctx')
- grad_down: float32 [6912, 1152], P('ctx', 'dp')
- grad_gain_in: float32 [1152], P(('dp', 'ctx'))
- grad_gain_query: float32 [256], P(('dp', 'ctx'))
- grad_gain_key: float32 [256], P(('dp', 'ctx'))
- grad_gain_attn: float32 [1152], P(('dp', 'ctx'))
- grad_gain_pre: float32 [1152], P(('dp', 'ctx'))
- grad_gain_post: float32 [1152], P(('dp', 'ctx'))
The draws below stay inside these ranges and needn't reach their ends.
Inputs may be any that keep to these rules, and one draw needn't show every extreme that they name: In every row of lengths one sequence, which one drawn from the seed, has length 256.
All inputs are finite; a program needn't handle non-finite values.
Results may differ from the reference program's by a relative error of at most 0.024.
Values may be sent and summed in bfloat16 or wider, within the bound.
No kernel may reach another device: no remote copies, remote signals or barrier semaphores. Data moves between devices by JAX's collectives and lax.ppermute only.
A program may use at most 192 MiB of HBM per device.

```python
from functools import partial
import jax
import jax.numpy as jnp
from jax import lax

D = 1152
HEADS = 4
HEAD_DIM = 256
FF = 6912
STRETCH = 32
SEQS = 2
BUCKET = 256
TOKENS = 4096
N_DP = 8
N_CTX = 4


def draw_lengths(key, part):
    key = jax.random.fold_in(key, 11)
    first_key, second_key, third_key = jax.random.split(key, 3)
    left = jax.random.randint(first_key, (N_DP, SEQS), 1, BUCKET + 1)
    right = jax.random.randint(second_key, (N_DP, SEQS), 1, BUCKET + 1)
    base = jnp.maximum(STRETCH, left * right // BUCKET)
    chosen = jax.random.randint(third_key, (N_DP, 1), 0, SEQS)
    slots = jnp.arange(SEQS, dtype=jnp.int32)[None, :]
    return jnp.where(slots == chosen, BUCKET, base).astype(jnp.int32)


def strengthened(values, stream_key, source, target, blocks, factor):
    def block_of(position):
        return (jnp.arange(values.shape[position]) // (values.shape[position] // blocks)).reshape((-1,) + (1,) * (values.ndim - 1 - position))

    first = jax.random.permutation(stream_key, blocks)[block_of(target)]
    far = (block_of(target) + blocks // 2) % blocks
    return jnp.where((block_of(source) == first) | (block_of(source) == far), factor * values, values)


def block_levels(key, shape, pieces, low, high):
    gain = 1.0
    for dim, shards_of in pieces:
        steps = jax.random.uniform(jax.random.fold_in(jax.random.fold_in(key, 6), dim), (shards_of,), jnp.float32, low / len(pieces), high / len(pieces))
        gain = gain * jnp.repeat(jnp.exp(steps), shape[dim] // shards_of).reshape((-1,) + (1,) * (len(shape) - 1 - dim))
    return gain


def scatter_about(rng, extent, scale, bound, shards=(), held_as=jnp.bfloat16):
    values = scale * jax.random.normal(rng, extent, jnp.float32)
    if shards:
        values = values * block_levels(rng, extent, shards, -0.22, 0.18)
    return jnp.clip(values, -bound, bound).astype(held_as)


def heavy_noise(key, extent, deviation, most, shards, heavy, held_as=jnp.bfloat16):
    array = deviation * jax.random.normal(key, extent, jnp.float32)
    if shards:
        array = array * block_levels(key, extent, shards, -0.22, 0.18)
    return jnp.clip(strengthened(array, jax.random.fold_in(key, 3), *heavy), -most, most).astype(held_as)


def setup_inputs(seed: int = 0) -> dict:
    arg_keys = jax.random.split(jax.random.key(seed), 17)
    tokens = heavy_noise(arg_keys[0], (TOKENS, D), 1.0, 6.0, ((0, 32),), (0, 1, 32, 2.75))
    cotangent = scatter_about(arg_keys[1], (TOKENS, D), 1.0, 6.0, ((0, 32),))
    lengths = draw_lengths(jax.random.fold_in(arg_keys[16], 71), 0)
    w_query = scatter_about(arg_keys[3], (D, HEADS * HEAD_DIM), D ** -0.5, 0.1875, ((0, 32),))
    w_key = scatter_about(arg_keys[4], (D, HEAD_DIM), D ** -0.5, 0.1875, ((0, 32),))
    w_value = scatter_about(arg_keys[5], (D, HEAD_DIM), D ** -0.5, 0.1875, ((0, 32),))
    w_out = scatter_about(arg_keys[6], (HEADS * HEAD_DIM, D), (HEADS * HEAD_DIM) ** -0.5, 0.1875, ((0, 32),))
    w_gate = scatter_about(arg_keys[7], (D, FF), D ** -0.5, 0.1875, ((0, 32),))
    w_up = scatter_about(arg_keys[8], (D, FF), D ** -0.5, 0.1875, ((0, 32),))
    w_down = scatter_about(arg_keys[9], (FF, D), FF ** -0.5, 0.078125, ((0, 32),))
    gain_in = scatter_about(arg_keys[10], (D,), 0.3, 0.75, ((0, 32),))
    gain_query = scatter_about(arg_keys[11], (HEAD_DIM,), 0.3, 0.75, ((0, 32),))
    gain_key = scatter_about(arg_keys[12], (HEAD_DIM,), 0.3, 0.75, ((0, 32),))
    gain_attn = scatter_about(arg_keys[13], (D,), 0.3, 0.75, ((0, 32),))
    gain_pre = scatter_about(arg_keys[14], (D,), 0.3, 0.75, ((0, 32),))
    gain_post = scatter_about(arg_keys[15], (D,), 0.3, 0.75, ((0, 32),))
    return {"tokens": tokens, "cotangent": cotangent, "lengths": lengths, "w_query": w_query, "w_key": w_key, "w_value": w_value, "w_out": w_out, "w_gate": w_gate, "w_up": w_up, "w_down": w_down, "gain_in": gain_in, "gain_query": gain_query, "gain_key": gain_key, "gain_attn": gain_attn, "gain_pre": gain_pre, "gain_post": gain_post}


@jax.custom_vjp
def low(v):
    return lax.optimization_barrier(v.astype(jnp.bfloat16)).astype(jnp.float32)

@jax.custom_vjp
def low_back(v):
    return v

def low_keep(v):
    return (low(v), None)

def low_pass(kept, grad):
    return (grad,)

def back_keep(v):
    return (v, None)

def back_low(kept, grad):
    return (low(grad),)
low.defvjp(low_keep, low_pass)
low_back.defvjp(back_keep, back_low)
epsilon = 1e-06
rope_base = 1000000.0
highest = lax.Precision.HIGHEST

def rms_norm(value, weight):
    scale = lax.rsqrt(lax.optimization_barrier(jnp.mean(value * value, axis=-1, keepdims=True)) + epsilon)
    return value * scale * (1.0 + weight)

def rope_tables(positions, width):
    half = width // 2
    freqs = jnp.power(rope_base, -2.0 * jnp.arange(half, dtype=jnp.float32) / width)
    angles = positions[:, None] * freqs[None, :]
    cosine = jnp.concatenate([jnp.cos(angles), jnp.cos(angles)], axis=-1)
    sine = jnp.concatenate([jnp.sin(angles), jnp.sin(angles)], axis=-1)
    return (cosine, sine)

def rotate(value, cosine, sine):
    half = value.shape[-1] // 2
    turned = jnp.concatenate([-value[..., half:], value[..., :half]], axis=-1)
    return value * cosine + turned * sine

def matmul(left, right):
    return jnp.dot(left, right, precision=highest)

def attend(item):
    query, keys, values, length = item
    span = keys.shape[0]
    rows = query.reshape(span * HEADS, HEAD_DIM)
    positions = jnp.arange(span, dtype=jnp.int32)
    query_pos = jnp.repeat(positions, HEADS)
    allowed = (positions[None, :] <= query_pos[:, None]) & (positions[None, :] < length)
    scores = low_back(matmul(rows, keys.T) * HEAD_DIM ** (-0.5))
    probs = jax.nn.softmax(jnp.where(allowed, scores, -1e+30), axis=-1)
    mixed = low(low_back(matmul(low(probs), values)))
    return mixed.reshape(span, HEADS * HEAD_DIM)

def group_layer(params, item):
    w_query, w_key, w_value, w_out, w_gate, w_up, w_down, gain_in, gain_query, gain_key, gain_attn, gain_pre, gain_post = params
    hidden, lens = item
    seq_count, span, width = hidden.shape
    valid = (jnp.arange(span, dtype=jnp.int32)[None, :] < lens[:, None]).astype(jnp.float32)[..., None]
    cosine, sine = rope_tables(jnp.arange(span, dtype=jnp.float32), HEAD_DIM)
    normed = low(rms_norm(hidden, gain_in))
    query_raw = low_back(matmul(normed, w_query))
    key_raw = low_back(matmul(normed, w_key))
    values = low(low_back(matmul(normed, w_value)))
    query_heads = rms_norm(query_raw.reshape(seq_count, span, HEADS, HEAD_DIM), gain_query)
    query = low(rotate(query_heads, cosine[:, None, :], sine[:, None, :]))
    keys = low(rotate(rms_norm(key_raw, gain_key), cosine, sine))
    mixed = lax.map(jax.checkpoint(attend), (query, keys, values, lens))
    attn_raw = low_back(matmul(mixed, w_out))
    after_attn = hidden + valid * rms_norm(attn_raw, gain_attn)
    normed_two = low(rms_norm(after_attn, gain_pre))
    gate = low_back(matmul(normed_two, w_gate))
    upper = low_back(matmul(normed_two, w_up))
    inner = low(jax.nn.gelu(gate, approximate=True) * upper)
    ffn_raw = low_back(matmul(inner, w_down))
    return after_attn + valid * rms_norm(ffn_raw, gain_post)

def to_sequences(flat):
    arr = flat.reshape(N_DP, N_CTX, SEQS, 2, STRETCH, flat.shape[-1])
    first = arr[:, :, :, 0].transpose(0, 2, 1, 3, 4).reshape(N_DP, SEQS, N_CTX * STRETCH, flat.shape[-1])
    second = arr[:, ::-1, :, 1].transpose(0, 2, 1, 3, 4).reshape(N_DP, SEQS, N_CTX * STRETCH, flat.shape[-1])
    return jnp.concatenate([first, second], axis=2)

def from_sequences(seqs):
    width = seqs.shape[-1]
    arr = seqs.reshape(N_DP, SEQS, 2, N_CTX, STRETCH, width)
    first = arr[:, :, 0].transpose(0, 2, 1, 3, 4)
    second = arr[:, :, 1].transpose(0, 2, 1, 3, 4)[:, ::-1]
    return jnp.stack([first, second], axis=3).reshape(N_DP * N_CTX * SEQS * 2 * STRETCH, width)

def reference(tokens, cotangent, lengths, w_query, w_key, w_value, w_out, w_gate, w_up, w_down, gain_in, gain_query, gain_key, gain_attn, gain_pre, gain_post):
    params = tuple((a.astype(jnp.float32) for a in (w_query, w_key, w_value, w_out, w_gate, w_up, w_down, gain_in, gain_query, gain_key, gain_attn, gain_pre, gain_post)))
    hidden = to_sequences(tokens.astype(jnp.float32))
    grad_seq = to_sequences(cotangent.astype(jnp.float32))

    def forward(weights, inputs):
        return lax.map(jax.checkpoint(partial(group_layer, weights)), (inputs, lengths))
    result, pull = jax.vjp(forward, params, hidden)
    grads, input_grad = pull(grad_seq)
    return (from_sequences(result).astype(jnp.bfloat16), from_sequences(input_grad).astype(jnp.bfloat16), grads[0], grads[1], grads[2], grads[3], grads[4], grads[5], grads[6], grads[7], grads[8], grads[9], grads[10], grads[11], grads[12])
```

```python
import jax
import jax.numpy as jnp
from jax import lax
from jax.sharding import PartitionSpec as P

epsilon = 1e-06
rope_base = 1000000.0


def rms_norm(value, weight):
    scale = lax.rsqrt(jnp.mean(value * value, axis=-1, keepdims=True) + epsilon)
    return value * scale * (1.0 + weight)


def rms_back(value, weight, grad):
    scale = lax.rsqrt(jnp.mean(value * value, axis=-1, keepdims=True) + epsilon)
    normed = value * scale
    weighted = grad * (1.0 + weight)
    value_grad = scale * (weighted - normed * jnp.mean(weighted * normed, axis=-1, keepdims=True))
    weight_grad = jnp.sum(grad * normed, axis=tuple(range(value.ndim - 1)))
    return (value_grad, weight_grad)


def rope_tables(positions, width):
    half = width // 2
    freqs = jnp.power(rope_base, -2.0 * jnp.arange(half, dtype=jnp.float32) / width)
    angles = positions[:, None] * freqs[None, :]
    cosine = jnp.concatenate([jnp.cos(angles), jnp.cos(angles)], axis=-1)
    sine = jnp.concatenate([jnp.sin(angles), jnp.sin(angles)], axis=-1)
    return (cosine, sine)


def rotate(value, cosine, sine):
    half = value.shape[-1] // 2
    turned = jnp.concatenate([-value[..., half:], value[..., :half]], axis=-1)
    return value * cosine + turned * sine


def rotate_back(grad, cosine, sine):
    half = grad.shape[-1] // 2
    scaled = grad * sine
    return grad * cosine + jnp.concatenate([scaled[..., half:], -scaled[..., :half]], axis=-1)


def geglu(gate, upper):
    return jax.nn.gelu(gate, approximate=True) * upper


def dot(left, right, left_dim, right_dim):
    return lax.dot_general(
        left, right, (((left_dim,), (right_dim,)), ((), ())), preferred_element_type=jnp.float32
    )


def swap(value, bit):
    size = lax.axis_size("dp")
    return lax.ppermute(value, "dp", [(i, i ^ (1 << bit)) for i in range(size)])


def shift(value, step):
    size = lax.axis_size("ctx")
    return lax.ppermute(value, "ctx", [(i, (i + step) % size) for i in range(size)])


def pick(value, index, axis=0):
    return lax.dynamic_index_in_dim(value, index, axis, keepdims=False)


def plane_bits():
    return list(range(1, lax.axis_size("dp").bit_length() - 1))


def ctx_gather(value):
    return [value] + [shift(value, k) for k in range(1, lax.axis_size("ctx"))]


def ctx_ordered(pieces):
    size = lax.axis_size("ctx")
    stacked = jnp.stack(pieces)
    mine = lax.axis_index("ctx")
    return jnp.stack([pick(stacked, (mine - a + size) % size) for a in range(size)])


def ctx_reduce(pieces):
    total = pieces[0].astype(jnp.float32)
    for k in range(1, len(pieces)):
        total = total + shift(pieces[k].astype(jnp.bfloat16), -k).astype(jnp.float32)
    return total


def ctx_exchange(blocks):
    size = lax.axis_size("ctx")
    mine = lax.axis_index("ctx")
    return [pick(blocks, mine)] + [
        shift(pick(blocks, (mine + k) % size), k) for k in range(1, size)
    ]


def row_parts(rows, count):
    unit = 8 if rows % 8 == 0 else 1
    edges = [unit * (rows // unit * p // count) for p in range(count + 1)]
    return [(edges[p], edges[p + 1]) for p in range(count)]


def dp_gather(value):
    bits = plane_bits()
    plane = lax.axis_index("dp") // 2
    core = lax.axis_index("dp") % 2
    count = 1 << len(bits)
    parts = []
    for p, (low, high) in enumerate(row_parts(value.shape[0], len(bits))):
        current = value[None, low:high]
        masks = [0]
        for bit in bits[p:] + bits[:p]:
            current = jnp.concatenate([current, swap(current, bit)])
            masks = masks + [m ^ (1 << (bit - 1)) for m in masks]
        other = swap(current, 0)
        place = jnp.asarray([masks.index(m) for m in range(count)], jnp.int32)
        rows_of = []
        for a in range(count):
            at = pick(place, plane ^ a)
            first, second = pick(current, at), pick(other, at)
            rows_of.append(
                jnp.stack([lax.select(core == 0, first, second), lax.select(core == 0, second, first)])
            )
        parts.append(jnp.stack(rows_of))
    whole = jnp.concatenate(parts, axis=2)
    return whole.reshape((2 * count,) + value.shape)


def dp_reduce(kept, sent):
    bits = plane_bits()
    plane = lax.axis_index("dp") // 2
    total = (kept + swap(sent.astype(jnp.bfloat16), 0).astype(jnp.float32)).astype(jnp.bfloat16)
    parts = []
    for p, (low, high) in enumerate(row_parts(total.shape[1], len(bits))):
        current = total[:, low:high]
        current = current.reshape((2,) * len(bits) + current.shape[1:])
        left = sorted(bits, reverse=True)
        for bit in bits[p:] + bits[:p]:
            axis = left.index(bit)
            mine = (plane >> (bit - 1)) & 1
            got = swap(pick(current, 1 - mine, axis), bit)
            current = pick(current, mine, axis).astype(jnp.float32) + got.astype(jnp.float32)
            left.remove(bit)
            if left:
                current = current.astype(jnp.bfloat16)
        parts.append(current)
    return jnp.concatenate(parts, axis=0)


def columns_of(value, core):
    dp = lax.axis_size("dp")
    wide = value.reshape(value.shape[0], dp // 2, 2, value.shape[1] // dp)
    return pick(wide, core, 2).reshape(value.shape[0], -1)


def weight_grad(left, right, extra=None):
    core = lax.axis_index("dp") % 2
    dp = lax.axis_size("dp")
    blocks = []
    for side in (core, 1 - core):
        block = dot(columns_of(left, side), right, 0, 0)
        block = block.reshape(dp // 2, left.shape[1] // dp, right.shape[1])
        if extra is not None:
            block = jnp.concatenate([block, pick(extra, side, 1)], axis=1)
        blocks.append(block)
    return dp_reduce(blocks[0], blocks[1])


def on_device(
    tokens,
    cotangent,
    lengths,
    w_query,
    w_key,
    w_value,
    w_out,
    w_gate,
    w_up,
    w_down,
    gain_in,
    gain_query,
    gain_key,
    gain_attn,
    gain_pre,
    gain_post,
):
    count, width = tokens.shape
    seq_count = lengths.shape[1]
    stretch = count // (2 * seq_count)
    dp = lax.axis_size("dp")
    ctx = lax.axis_size("ctx")
    mine = lax.axis_index("ctx")
    head_dim = w_key.shape[1]
    heads = w_query.shape[1] // head_dim
    inner = w_gate.shape[1] // ctx
    span = 2 * ctx * stretch
    offsets = jnp.arange(stretch, dtype=jnp.int32)

    def positions_of(index):
        return jnp.concatenate(
            [index * stretch + offsets, (2 * ctx - 1 - index) * stretch + offsets]
        )

    local_pos = positions_of(mine)
    valid = (local_pos[None, :] < lengths[0][:, None]).astype(jnp.float32).reshape(count, 1)
    cosine, sine = rope_tables(jnp.tile(local_pos, seq_count).astype(jnp.float32), head_dim)
    key_pos = jnp.concatenate([positions_of((mine - k + ctx) % ctx) for k in range(ctx)])
    query_pos = jnp.repeat(local_pos, heads)
    allowed = (key_pos[None, None, :] <= query_pos[None, :, None]) & (
        key_pos[None, None, :] < lengths[0][:, None, None]
    )
    inv_root = head_dim ** (-0.5)

    gains = [gain_in, gain_query, gain_key, gain_attn, gain_pre, gain_post]
    sizes = [g.shape[0] for g in gains]
    small = jnp.concatenate(gains)
    qkv_shard = jnp.concatenate([w_query, w_key, w_value], axis=1)
    in_rows, in_cols = qkv_shard.shape
    out_rows = w_out.shape[0]
    top = max(in_rows, out_rows)
    packed_rows = -(-(top + 1) // 8) * 8
    packed = jnp.concatenate(
        [
            jnp.pad(qkv_shard, ((0, top - in_rows), (0, 0))),
            jnp.pad(w_out, ((0, top - out_rows), (0, 0))),
        ],
        axis=1,
    )
    last = jnp.pad(small[None], ((0, packed_rows - top - 1), (0, packed.shape[1] - small.shape[0])))
    packed = jnp.concatenate([packed, last], axis=0)
    near = ctx_ordered(ctx_gather(packed)).reshape(ctx * packed_rows, -1)
    everything = dp_gather(near).reshape(dp * ctx, packed_rows, -1)
    full_qkv = everything[:, :in_rows, :in_cols].reshape(width, in_cols)
    full_out = everything[:, :out_rows, in_cols:].reshape(heads * head_dim, width)
    smalls = everything[:, top, : small.shape[0]]
    norms, start = [], 0
    for size in sizes:
        norms.append(smalls[:, start : start + size].reshape(-1).astype(jnp.float32))
        start += size
    norm_in, norm_query, norm_key, norm_attn, norm_pre, norm_post = norms

    def column_blocks(weight):
        return weight.reshape(weight.shape[0], ctx, inner).transpose(1, 0, 2)

    gate_up = jnp.stack([column_blocks(w_gate), column_blocks(w_up)], axis=1)
    gate_up = ctx_ordered(ctx_exchange(gate_up)).transpose(1, 0, 2, 3)
    gate_up = gate_up.reshape(2, width // dp, inner)
    per = dp // ctx
    down = w_down.T.reshape(dp, width // dp, w_down.shape[0])
    down = lax.all_to_all(down, "dp", split_axis=0, concat_axis=0, tiled=True)
    down = down.reshape(ctx, per, width // dp, w_down.shape[0])
    down = ctx_ordered(ctx_exchange(down))
    down = down.transpose(2, 1, 0, 3).reshape(width // dp, inner)
    full_gate = dp_gather(gate_up[0]).reshape(width, inner)
    full_up = dp_gather(gate_up[1]).reshape(width, inner)
    full_down = dp_gather(down).reshape(width, inner)

    hidden = tokens.astype(jnp.float32)
    normed = rms_norm(hidden, norm_in).astype(jnp.bfloat16)
    qkv_raw = dot(normed, full_qkv, 1, 0)
    query_raw = qkv_raw[:, : heads * head_dim]
    key_raw = qkv_raw[:, heads * head_dim : (heads + 1) * head_dim]
    value_raw = qkv_raw[:, (heads + 1) * head_dim :]
    query_heads = query_raw.reshape(count, heads, head_dim)
    query_bf = rotate(
        rms_norm(query_heads, norm_query), cosine[:, None, :], sine[:, None, :]
    ).astype(jnp.bfloat16)
    query_bf = query_bf.reshape(seq_count, 2 * stretch * heads, head_dim)
    key_bf = rotate(rms_norm(key_raw, norm_key), cosine, sine).astype(jnp.bfloat16)
    both = jnp.concatenate([key_bf, value_raw.astype(jnp.bfloat16)], axis=1)
    both = jnp.stack(
        [p.reshape(seq_count, 2 * stretch, 2 * head_dim) for p in ctx_gather(both)], axis=1
    ).reshape(seq_count, span, 2 * head_dim)
    keys, values = both[..., :head_dim], both[..., head_dim:]
    scores = (
        jnp.einsum("sqd,skd->sqk", query_bf, keys, preferred_element_type=jnp.float32) * inv_root
    )
    masked = jnp.where(allowed, scores, -1e30)
    peak = jnp.max(masked, axis=-1, keepdims=True)
    expo = jnp.exp(masked - peak)
    total = jnp.sum(expo, axis=-1, keepdims=True)
    probs = expo / total
    probs_bf = probs.astype(jnp.bfloat16)
    mixed = jnp.einsum("sqk,skd->sqd", probs_bf, values, preferred_element_type=jnp.float32)
    mixed_bf = mixed.astype(jnp.bfloat16).reshape(count, heads * head_dim)
    attn_raw = dot(mixed_bf, full_out, 1, 0)
    after_attn = hidden + valid * rms_norm(attn_raw, norm_attn)
    normed_two = rms_norm(after_attn, norm_pre).astype(jnp.bfloat16)

    group_two = jnp.concatenate(ctx_gather(normed_two))
    gate = dot(group_two, full_gate, 1, 0)
    upper = dot(group_two, full_up, 1, 0)
    inner_bf = geglu(gate, upper).astype(jnp.bfloat16)
    ffn_part = dot(inner_bf, full_down, 1, 1)
    ffn_raw = ctx_reduce(list(ffn_part.reshape(ctx, count, width)))
    output = (after_attn + valid * rms_norm(ffn_raw, norm_post)).astype(jnp.bfloat16)

    grad_top = cotangent.astype(jnp.float32)
    ffn_grad, grad_gain_post = rms_back(ffn_raw, norm_post, valid * grad_top)
    group_ffn = jnp.concatenate(ctx_gather(ffn_grad.astype(jnp.bfloat16)))
    inner_grad = dot(group_ffn, full_down, 1, 0)
    _, geglu_pull = jax.vjp(geglu, gate, upper)
    gate_grad, upper_grad = geglu_pull(inner_grad)
    gate_grad_bf = gate_grad.astype(jnp.bfloat16)
    upper_grad_bf = upper_grad.astype(jnp.bfloat16)
    two_part = dot(gate_grad_bf, full_gate, 1, 1) + dot(upper_grad_bf, full_up, 1, 1)
    normed_two_grad = ctx_reduce(list(two_part.reshape(ctx, count, width)))
    grad_down = weight_grad(group_ffn, inner_bf).T
    grad_gate = weight_grad(group_two, gate_grad_bf)
    grad_up = weight_grad(group_two, upper_grad_bf)

    through_pre, grad_gain_pre = rms_back(after_attn, norm_pre, normed_two_grad)
    after_grad = grad_top + through_pre
    attn_grad, grad_gain_attn = rms_back(attn_raw, norm_attn, valid * after_grad)
    attn_grad_bf = attn_grad.astype(jnp.bfloat16)
    grad_out = weight_grad(attn_grad_bf, mixed_bf)
    grad_out = sum_of_ctx(grad_out.reshape(grad_out.shape[0], ctx, -1).transpose(1, 0, 2)).T
    mixed_grad_bf = dot(attn_grad_bf, full_out, 1, 1).astype(jnp.bfloat16)
    mixed_grad_bf = mixed_grad_bf.reshape(seq_count, 2 * stretch * heads, head_dim)
    prob_grad = jnp.einsum(
        "sqd,skd->sqk", mixed_grad_bf, values, preferred_element_type=jnp.float32
    )
    row_dot = jnp.sum(probs * prob_grad, axis=-1, keepdims=True)
    score_grad_bf = (probs * (prob_grad - row_dot)).astype(jnp.bfloat16)
    query_grad = (
        jnp.einsum("sqk,skd->sqd", score_grad_bf, keys, preferred_element_type=jnp.float32)
        * inv_root
    )
    keys_grad = (
        jnp.einsum("sqk,sqd->skd", score_grad_bf, query_bf, preferred_element_type=jnp.float32)
        * inv_root
    )
    values_grad = jnp.einsum(
        "sqk,sqd->skd", probs_bf, mixed_grad_bf, preferred_element_type=jnp.float32
    )
    both_grad = jnp.concatenate([keys_grad, values_grad], axis=-1)
    both_grad = both_grad.reshape(seq_count, ctx, 2 * stretch, 2 * head_dim).transpose(1, 0, 2, 3)
    own_grad = ctx_reduce(list(both_grad.reshape(ctx, count, 2 * head_dim)))
    own_keys_grad, own_values_grad = own_grad[:, :head_dim], own_grad[:, head_dim:]
    query_grad = rotate_back(
        query_grad.reshape(count, heads, head_dim), cosine[:, None, :], sine[:, None, :]
    )
    query_raw_grad, grad_gain_query = rms_back(query_heads, norm_query, query_grad)
    query_raw_bf = query_raw_grad.reshape(count, heads * head_dim).astype(jnp.bfloat16)
    key_raw_grad, grad_gain_key = rms_back(
        key_raw, norm_key, rotate_back(own_keys_grad, cosine, sine)
    )
    key_raw_bf = key_raw_grad.astype(jnp.bfloat16)
    value_raw_bf = own_values_grad.astype(jnp.bfloat16)
    raw_bf = jnp.concatenate([query_raw_bf, key_raw_bf, value_raw_bf], axis=1)
    normed_grad = dot(raw_bf, full_qkv, 1, 1)
    through_in, grad_gain_in = rms_back(hidden, norm_in, normed_grad)
    input_grad = (after_grad + through_in).astype(jnp.bfloat16)

    by_ctx = jnp.concatenate(
        [r.reshape(count, ctx, -1) for r in (query_raw_bf, key_raw_bf, value_raw_bf)], axis=2
    )
    each = by_ctx.shape[2]
    gain_grads = jnp.concatenate(
        [
            g.reshape(dp * ctx, -1)
            for g in (
                grad_gain_in,
                grad_gain_query,
                grad_gain_key,
                grad_gain_attn,
                grad_gain_pre,
                grad_gain_post,
            )
        ],
        axis=1,
    )
    small_size = gain_grads.shape[1]
    extra = jnp.pad(gain_grads, ((0, 0), (0, each - small_size))).reshape(
        dp // 2, 2, 1, ctx * each
    )
    extra = jnp.pad(extra, ((0, 0), (0, 0), (0, 7), (0, 0)))
    grad_qkv = weight_grad(normed, by_ctx.reshape(count, ctx * each), extra)
    grad_qkv = sum_of_ctx(grad_qkv.reshape(grad_qkv.shape[0], ctx, each).transpose(1, 0, 2))
    rows = width // dp
    gain_out = grad_qkv[rows, :small_size]
    grad_qkv = grad_qkv[:rows]
    q_cols, k_cols = heads * head_dim // ctx, head_dim // ctx
    outs, start = [], 0
    for size in sizes:
        outs.append(gain_out[start : start + size])
        start += size
    return (
        output,
        input_grad,
        grad_qkv[:, :q_cols],
        grad_qkv[:, q_cols : q_cols + k_cols],
        grad_qkv[:, q_cols + k_cols :],
        grad_out,
        grad_gate,
        grad_up,
        grad_down,
        *outs,
    )


def sum_of_ctx(blocks):
    size = lax.axis_size("ctx")
    mine = lax.axis_index("ctx")
    total = pick(blocks, mine).astype(jnp.float32)
    for k in range(1, size):
        got = shift(pick(blocks, (mine + k) % size).astype(jnp.bfloat16), k)
        total = total + got.astype(jnp.float32)
    return total


def solution(mesh):
    in_specs = (
        P(("dp", "ctx"), None),
        P(("dp", "ctx"), None),
        P("dp", None),
        P(("dp", "ctx"), None),
        P(("dp", "ctx"), None),
        P(("dp", "ctx"), None),
        P(("dp", "ctx"), None),
        P(("dp", "ctx"), None),
        P(("dp", "ctx"), None),
        P(("dp", "ctx"), None),
        P(("dp", "ctx")),
        P(("dp", "ctx")),
        P(("dp", "ctx")),
        P(("dp", "ctx")),
        P(("dp", "ctx")),
        P(("dp", "ctx")),
    )
    out_specs = (
        P(("dp", "ctx"), None),
        P(("dp", "ctx"), None),
        P("dp", "ctx"),
        P("dp", "ctx"),
        P("dp", "ctx"),
        P("ctx", "dp"),
        P("dp", "ctx"),
        P("dp", "ctx"),
        P("ctx", "dp"),
        P(("dp", "ctx")),
        P(("dp", "ctx")),
        P(("dp", "ctx")),
        P(("dp", "ctx")),
        P(("dp", "ctx")),
        P(("dp", "ctx")),
    )
    return jax.shard_map(
        on_device, mesh=mesh, in_specs=in_specs, out_specs=out_specs, check_vma=False
    )
```

```python
import jax
import jax.numpy as jnp
import numpy as np
from jax import lax
from jax.experimental import pallas as pl
from jax.experimental.pallas import tpu as pltpu
from jax.sharding import PartitionSpec as P

epsilon = 1e-06
rope_base = 1000000.0


def rms_norm(value, weight):
    scale = lax.rsqrt(jnp.mean(value * value, axis=-1, keepdims=True) + epsilon)
    return value * scale * (1.0 + weight)


def rms_back(value, weight, grad):
    scale = lax.rsqrt(jnp.mean(value * value, axis=-1, keepdims=True) + epsilon)
    normed = value * scale
    weighted = grad * (1.0 + weight)
    value_grad = scale * (weighted - normed * jnp.mean(weighted * normed, axis=-1, keepdims=True))
    weight_grad = jnp.sum(grad * normed, axis=tuple(range(value.ndim - 1)))
    return (value_grad, weight_grad)


def rope_tables(positions, width):
    half = width // 2
    freqs = jnp.power(rope_base, -2.0 * jnp.arange(half, dtype=jnp.float32) / width)
    angles = positions[:, None] * freqs[None, :]
    cosine = jnp.concatenate([jnp.cos(angles), jnp.cos(angles)], axis=-1)
    sine = jnp.concatenate([jnp.sin(angles), jnp.sin(angles)], axis=-1)
    return (cosine, sine)


def rotate(value, cosine, sine):
    half = value.shape[-1] // 2
    turned = jnp.concatenate([-value[..., half:], value[..., :half]], axis=-1)
    return value * cosine + turned * sine


def rotate_back(grad, cosine, sine):
    half = grad.shape[-1] // 2
    scaled = grad * sine
    return grad * cosine + jnp.concatenate([scaled[..., half:], -scaled[..., :half]], axis=-1)


def geglu(gate, upper):
    return jax.nn.gelu(gate, approximate=True) * upper


def dot(left, right, left_dim, right_dim):
    return lax.dot_general(
        left, right, (((left_dim,), (right_dim,)), ((), ())), preferred_element_type=jnp.float32
    )


def swap(value, bit):
    size = lax.axis_size("dp")
    return lax.ppermute(value, "dp", [(i, i ^ (1 << bit)) for i in range(size)])


def shift(value, step):
    size = lax.axis_size("ctx")
    return lax.ppermute(value, "ctx", [(i, (i + step) % size) for i in range(size)])


def pick(value, index, axis=0):
    return lax.dynamic_index_in_dim(value, index, axis, keepdims=False)


def plane_bits():
    return list(range(1, lax.axis_size("dp").bit_length() - 1))


def ctx_gather(value):
    return [value] + [shift(value, k) for k in range(1, lax.axis_size("ctx"))]


def ctx_ordered(pieces):
    size = lax.axis_size("ctx")
    stacked = jnp.stack(pieces)
    mine = lax.axis_index("ctx")
    return jnp.stack([pick(stacked, (mine - a + size) % size) for a in range(size)])


def ctx_reduce(pieces):
    total = pieces[0].astype(jnp.float32)
    for k in range(1, len(pieces)):
        total = total + shift(pieces[k].astype(jnp.bfloat16), -k).astype(jnp.float32)
    return total


def ctx_exchange(blocks):
    size = lax.axis_size("ctx")
    mine = lax.axis_index("ctx")
    return [pick(blocks, mine)] + [
        shift(pick(blocks, (mine + k) % size), k) for k in range(1, size)
    ]


def row_parts(rows, count):
    unit = 8 if rows % 8 == 0 else 1
    edges = [unit * (rows // unit * p // count) for p in range(count + 1)]
    return [(edges[p], edges[p + 1]) for p in range(count)]


def dp_gather(value):
    bits = plane_bits()
    plane = lax.axis_index("dp") // 2
    core = lax.axis_index("dp") % 2
    count = 1 << len(bits)
    parts = []
    for p, (low, high) in enumerate(row_parts(value.shape[0], len(bits))):
        current = value[None, low:high]
        masks = [0]
        for bit in bits[p:] + bits[:p]:
            current = jnp.concatenate([current, swap(current, bit)])
            masks = masks + [m ^ (1 << (bit - 1)) for m in masks]
        other = swap(current, 0)
        place = jnp.asarray([masks.index(m) for m in range(count)], jnp.int32)
        rows_of = []
        for a in range(count):
            at = pick(place, plane ^ a)
            first, second = pick(current, at), pick(other, at)
            rows_of.append(
                jnp.stack([lax.select(core == 0, first, second), lax.select(core == 0, second, first)])
            )
        parts.append(jnp.stack(rows_of))
    whole = jnp.concatenate(parts, axis=2)
    return whole.reshape((2 * count,) + value.shape)


def dp_reduce(kept, sent):
    bits = plane_bits()
    plane = lax.axis_index("dp") // 2
    total = (kept + swap(sent.astype(jnp.bfloat16), 0).astype(jnp.float32)).astype(jnp.bfloat16)
    parts = []
    for p, (low, high) in enumerate(row_parts(total.shape[1], len(bits))):
        current = total[:, low:high]
        current = current.reshape((2,) * len(bits) + current.shape[1:])
        left = sorted(bits, reverse=True)
        for bit in bits[p:] + bits[:p]:
            axis = left.index(bit)
            mine = (plane >> (bit - 1)) & 1
            got = swap(pick(current, 1 - mine, axis), bit)
            current = pick(current, mine, axis).astype(jnp.float32) + got.astype(jnp.float32)
            left.remove(bit)
            if left:
                current = current.astype(jnp.bfloat16)
        parts.append(current)
    return jnp.concatenate(parts, axis=0)


def columns_of(value, core):
    dp = lax.axis_size("dp")
    wide = value.reshape(value.shape[0], dp // 2, 2, value.shape[1] // dp)
    return pick(wide, core, 2).reshape(value.shape[0], -1)


def weight_grad(left, right, extra=None):
    core = lax.axis_index("dp") % 2
    dp = lax.axis_size("dp")
    blocks = []
    for side in (core, 1 - core):
        block = dot(columns_of(left, side), right, 0, 0)
        block = block.reshape(dp // 2, left.shape[1] // dp, right.shape[1])
        if extra is not None:
            block = jnp.concatenate([block, pick(extra, side, 1)], axis=1)
        blocks.append(block)
    return dp_reduce(blocks[0], blocks[1])


def plain(
    tokens,
    cotangent,
    lengths,
    w_query,
    w_key,
    w_value,
    w_out,
    w_gate,
    w_up,
    w_down,
    gain_in,
    gain_query,
    gain_key,
    gain_attn,
    gain_pre,
    gain_post,
):
    count, width = tokens.shape
    seq_count = lengths.shape[1]
    stretch = count // (2 * seq_count)
    dp = lax.axis_size("dp")
    ctx = lax.axis_size("ctx")
    mine = lax.axis_index("ctx")
    head_dim = w_key.shape[1]
    heads = w_query.shape[1] // head_dim
    inner = w_gate.shape[1] // ctx
    span = 2 * ctx * stretch
    offsets = jnp.arange(stretch, dtype=jnp.int32)

    def positions_of(index):
        return jnp.concatenate(
            [index * stretch + offsets, (2 * ctx - 1 - index) * stretch + offsets]
        )

    local_pos = positions_of(mine)
    valid = (local_pos[None, :] < lengths[0][:, None]).astype(jnp.float32).reshape(count, 1)
    cosine, sine = rope_tables(jnp.tile(local_pos, seq_count).astype(jnp.float32), head_dim)
    key_pos = jnp.concatenate([positions_of((mine - k + ctx) % ctx) for k in range(ctx)])
    query_pos = jnp.repeat(local_pos, heads)
    allowed = (key_pos[None, None, :] <= query_pos[None, :, None]) & (
        key_pos[None, None, :] < lengths[0][:, None, None]
    )
    inv_root = head_dim ** (-0.5)

    gains = [gain_in, gain_query, gain_key, gain_attn, gain_pre, gain_post]
    sizes = [g.shape[0] for g in gains]
    small = jnp.concatenate(gains)
    qkv_shard = jnp.concatenate([w_query, w_key, w_value], axis=1)
    in_rows, in_cols = qkv_shard.shape
    out_rows = w_out.shape[0]
    top = max(in_rows, out_rows)
    packed_rows = -(-(top + 1) // 8) * 8
    packed = jnp.concatenate(
        [
            jnp.pad(qkv_shard, ((0, top - in_rows), (0, 0))),
            jnp.pad(w_out, ((0, top - out_rows), (0, 0))),
        ],
        axis=1,
    )
    last = jnp.pad(small[None], ((0, packed_rows - top - 1), (0, packed.shape[1] - small.shape[0])))
    packed = jnp.concatenate([packed, last], axis=0)
    near = ctx_ordered(ctx_gather(packed)).reshape(ctx * packed_rows, -1)
    everything = dp_gather(near).reshape(dp * ctx, packed_rows, -1)
    full_qkv = everything[:, :in_rows, :in_cols].reshape(width, in_cols)
    full_out = everything[:, :out_rows, in_cols:].reshape(heads * head_dim, width)
    smalls = everything[:, top, : small.shape[0]]
    norms, start = [], 0
    for size in sizes:
        norms.append(smalls[:, start : start + size].reshape(-1).astype(jnp.float32))
        start += size
    norm_in, norm_query, norm_key, norm_attn, norm_pre, norm_post = norms

    def column_blocks(weight):
        return weight.reshape(weight.shape[0], ctx, inner).transpose(1, 0, 2)

    gate_up = jnp.stack([column_blocks(w_gate), column_blocks(w_up)], axis=1)
    gate_up = ctx_ordered(ctx_exchange(gate_up)).transpose(1, 0, 2, 3)
    gate_up = gate_up.reshape(2, width // dp, inner)
    per = dp // ctx
    down = w_down.T.reshape(dp, width // dp, w_down.shape[0])
    down = lax.all_to_all(down, "dp", split_axis=0, concat_axis=0, tiled=True)
    down = down.reshape(ctx, per, width // dp, w_down.shape[0])
    down = ctx_ordered(ctx_exchange(down))
    down = down.transpose(2, 1, 0, 3).reshape(width // dp, inner)
    full_gate = dp_gather(gate_up[0]).reshape(width, inner)
    full_up = dp_gather(gate_up[1]).reshape(width, inner)
    full_down = dp_gather(down).reshape(width, inner)

    hidden = tokens.astype(jnp.float32)
    normed = rms_norm(hidden, norm_in).astype(jnp.bfloat16)
    qkv_raw = dot(normed, full_qkv, 1, 0)
    query_raw = qkv_raw[:, : heads * head_dim]
    key_raw = qkv_raw[:, heads * head_dim : (heads + 1) * head_dim]
    value_raw = qkv_raw[:, (heads + 1) * head_dim :]
    query_heads = query_raw.reshape(count, heads, head_dim)
    query_bf = rotate(
        rms_norm(query_heads, norm_query), cosine[:, None, :], sine[:, None, :]
    ).astype(jnp.bfloat16)
    query_bf = query_bf.reshape(seq_count, 2 * stretch * heads, head_dim)
    key_bf = rotate(rms_norm(key_raw, norm_key), cosine, sine).astype(jnp.bfloat16)
    both = jnp.concatenate([key_bf, value_raw.astype(jnp.bfloat16)], axis=1)
    both = jnp.stack(
        [p.reshape(seq_count, 2 * stretch, 2 * head_dim) for p in ctx_gather(both)], axis=1
    ).reshape(seq_count, span, 2 * head_dim)
    keys, values = both[..., :head_dim], both[..., head_dim:]
    scores = (
        jnp.einsum("sqd,skd->sqk", query_bf, keys, preferred_element_type=jnp.float32) * inv_root
    )
    masked = jnp.where(allowed, scores, -1e30)
    peak = jnp.max(masked, axis=-1, keepdims=True)
    expo = jnp.exp(masked - peak)
    total = jnp.sum(expo, axis=-1, keepdims=True)
    probs = expo / total
    probs_bf = probs.astype(jnp.bfloat16)
    mixed = jnp.einsum("sqk,skd->sqd", probs_bf, values, preferred_element_type=jnp.float32)
    mixed_bf = mixed.astype(jnp.bfloat16).reshape(count, heads * head_dim)
    attn_raw = dot(mixed_bf, full_out, 1, 0)
    after_attn = hidden + valid * rms_norm(attn_raw, norm_attn)
    normed_two = rms_norm(after_attn, norm_pre).astype(jnp.bfloat16)

    group_two = jnp.concatenate(ctx_gather(normed_two))
    gate = dot(group_two, full_gate, 1, 0)
    upper = dot(group_two, full_up, 1, 0)
    inner_bf = geglu(gate, upper).astype(jnp.bfloat16)
    ffn_part = dot(inner_bf, full_down, 1, 1)
    ffn_raw = ctx_reduce(list(ffn_part.reshape(ctx, count, width)))
    output = (after_attn + valid * rms_norm(ffn_raw, norm_post)).astype(jnp.bfloat16)

    grad_top = cotangent.astype(jnp.float32)
    ffn_grad, grad_gain_post = rms_back(ffn_raw, norm_post, valid * grad_top)
    group_ffn = jnp.concatenate(ctx_gather(ffn_grad.astype(jnp.bfloat16)))
    inner_grad = dot(group_ffn, full_down, 1, 0)
    _, geglu_pull = jax.vjp(geglu, gate, upper)
    gate_grad, upper_grad = geglu_pull(inner_grad)
    gate_grad_bf = gate_grad.astype(jnp.bfloat16)
    upper_grad_bf = upper_grad.astype(jnp.bfloat16)
    two_part = dot(gate_grad_bf, full_gate, 1, 1) + dot(upper_grad_bf, full_up, 1, 1)
    normed_two_grad = ctx_reduce(list(two_part.reshape(ctx, count, width)))
    grad_down = weight_grad(group_ffn, inner_bf).T
    grad_gate = weight_grad(group_two, gate_grad_bf)
    grad_up = weight_grad(group_two, upper_grad_bf)

    through_pre, grad_gain_pre = rms_back(after_attn, norm_pre, normed_two_grad)
    after_grad = grad_top + through_pre
    attn_grad, grad_gain_attn = rms_back(attn_raw, norm_attn, valid * after_grad)
    attn_grad_bf = attn_grad.astype(jnp.bfloat16)
    grad_out = weight_grad(attn_grad_bf, mixed_bf)
    grad_out = sum_of_ctx(grad_out.reshape(grad_out.shape[0], ctx, -1).transpose(1, 0, 2)).T
    mixed_grad_bf = dot(attn_grad_bf, full_out, 1, 1).astype(jnp.bfloat16)
    mixed_grad_bf = mixed_grad_bf.reshape(seq_count, 2 * stretch * heads, head_dim)
    prob_grad = jnp.einsum(
        "sqd,skd->sqk", mixed_grad_bf, values, preferred_element_type=jnp.float32
    )
    row_dot = jnp.sum(probs * prob_grad, axis=-1, keepdims=True)
    score_grad_bf = (probs * (prob_grad - row_dot)).astype(jnp.bfloat16)
    query_grad = (
        jnp.einsum("sqk,skd->sqd", score_grad_bf, keys, preferred_element_type=jnp.float32)
        * inv_root
    )
    keys_grad = (
        jnp.einsum("sqk,sqd->skd", score_grad_bf, query_bf, preferred_element_type=jnp.float32)
        * inv_root
    )
    values_grad = jnp.einsum(
        "sqk,sqd->skd", probs_bf, mixed_grad_bf, preferred_element_type=jnp.float32
    )
    both_grad = jnp.concatenate([keys_grad, values_grad], axis=-1)
    both_grad = both_grad.reshape(seq_count, ctx, 2 * stretch, 2 * head_dim).transpose(1, 0, 2, 3)
    own_grad = ctx_reduce(list(both_grad.reshape(ctx, count, 2 * head_dim)))
    own_keys_grad, own_values_grad = own_grad[:, :head_dim], own_grad[:, head_dim:]
    query_grad = rotate_back(
        query_grad.reshape(count, heads, head_dim), cosine[:, None, :], sine[:, None, :]
    )
    query_raw_grad, grad_gain_query = rms_back(query_heads, norm_query, query_grad)
    query_raw_bf = query_raw_grad.reshape(count, heads * head_dim).astype(jnp.bfloat16)
    key_raw_grad, grad_gain_key = rms_back(
        key_raw, norm_key, rotate_back(own_keys_grad, cosine, sine)
    )
    key_raw_bf = key_raw_grad.astype(jnp.bfloat16)
    value_raw_bf = own_values_grad.astype(jnp.bfloat16)
    raw_bf = jnp.concatenate([query_raw_bf, key_raw_bf, value_raw_bf], axis=1)
    normed_grad = dot(raw_bf, full_qkv, 1, 1)
    through_in, grad_gain_in = rms_back(hidden, norm_in, normed_grad)
    input_grad = (after_grad + through_in).astype(jnp.bfloat16)

    by_ctx = jnp.concatenate(
        [r.reshape(count, ctx, -1) for r in (query_raw_bf, key_raw_bf, value_raw_bf)], axis=2
    )
    each = by_ctx.shape[2]
    gain_grads = jnp.concatenate(
        [
            g.reshape(dp * ctx, -1)
            for g in (
                grad_gain_in,
                grad_gain_query,
                grad_gain_key,
                grad_gain_attn,
                grad_gain_pre,
                grad_gain_post,
            )
        ],
        axis=1,
    )
    small_size = gain_grads.shape[1]
    extra = jnp.pad(gain_grads, ((0, 0), (0, each - small_size))).reshape(
        dp // 2, 2, 1, ctx * each
    )
    extra = jnp.pad(extra, ((0, 0), (0, 0), (0, 7), (0, 0)))
    grad_qkv = weight_grad(normed, by_ctx.reshape(count, ctx * each), extra)
    grad_qkv = sum_of_ctx(grad_qkv.reshape(grad_qkv.shape[0], ctx, each).transpose(1, 0, 2))
    rows = width // dp
    gain_out = grad_qkv[rows, :small_size]
    grad_qkv = grad_qkv[:rows]
    q_cols, k_cols = heads * head_dim // ctx, head_dim // ctx
    outs, start = [], 0
    for size in sizes:
        outs.append(gain_out[start : start + size])
        start += size
    return (
        output,
        input_grad,
        grad_qkv[:, :q_cols],
        grad_qkv[:, q_cols : q_cols + k_cols],
        grad_qkv[:, q_cols + k_cols :],
        grad_out,
        grad_gate,
        grad_up,
        grad_down,
        *outs,
    )


def sum_of_ctx(blocks):
    size = lax.axis_size("ctx")
    mine = lax.axis_index("ctx")
    total = pick(blocks, mine).astype(jnp.float32)
    for k in range(1, size):
        got = shift(pick(blocks, (mine + k) % size).astype(jnp.bfloat16), k)
        total = total + got.astype(jnp.float32)
    return total


mega = 2**20


def place(name):
    return {"vmem": pl.BlockSpec(memory_space=pltpu.VMEM), "smem": pl.BlockSpec(memory_space=pltpu.SMEM), "any": pl.BlockSpec(memory_space=pl.ANY)}[name]


def kernel_call(body, outs, args, where=None, scratch=(), flops=0):
    where = where or {}
    size = sum(a.size * a.dtype.itemsize for a in args)
    size += sum(int(np.prod(s)) * jnp.dtype(t).itemsize for s, t in outs)
    return pl.pallas_call(
        body,
        out_shape=[jax.ShapeDtypeStruct(s, t) for s, t in outs],
        in_specs=[place(where.get(i, "vmem")) for i in range(len(args))],
        out_specs=[place("vmem") for _ in outs],
        scratch_shapes=list(scratch),
        compiler_params=pltpu.CompilerParams(vmem_limit_bytes=58 * mega),
        cost_estimate=pl.CostEstimate(flops=flops, bytes_accessed=size, transcendentals=0),
    )(*args)


def norm_back(value, weight, grad):
    scale = lax.rsqrt(jnp.mean(value * value, axis=-1, keepdims=True) + epsilon)
    normed = value * scale
    weighted = grad * (1.0 + weight)
    value_grad = scale * (weighted - normed * jnp.mean(weighted * normed, axis=-1, keepdims=True))
    return value_grad, jnp.sum(grad * normed, axis=0, keepdims=True)


def put_rows(target, at, pieces, masks, rows):
    for piece, mask in zip(pieces, masks):
        start = pl.multiple_of((at ^ mask) * rows, 16)
        target[pl.ds(start, rows), :] = piece[:rows, :]


def spread(where_ref, parts, masks, rows, lane, size, ctx):
    dp = len(parts)
    shards = jnp.concatenate([p[rows:, lane : lane + 128] for p in parts], axis=0)
    tail = shards.shape[0] // dp
    whole = dp * ctx * size
    column = lax.broadcasted_iota(jnp.int32, (128, whole), 1)
    line = lax.broadcasted_iota(jnp.int32, (128, whole), 0)
    spots = jnp.where(column % size == line, 1.0, 0.0).astype(jnp.bfloat16)
    values = dot(shards, spots, 1, 0)
    column = lax.broadcasted_iota(jnp.int32, (tail, whole), 1) // size
    line = lax.broadcasted_iota(jnp.int32, (tail, whole), 0)
    total = jnp.zeros((tail, whole), jnp.float32)
    for k, mask in enumerate(masks):
        owner = jnp.where(line < ctx, (where_ref[0] ^ mask) * ctx + line, -1)
        total = total + jnp.where(column == owner, values[k * tail : (k + 1) * tail], 0.0)
    return jnp.sum(total, axis=0, keepdims=True)


def pack(w_query, w_key, w_value, gains):
    rows = w_query.shape[0]
    ends = np.cumsum([w_query.shape[1], w_key.shape[1], w_value.shape[1]])
    tall = -(-(rows + 1) // 8) * 8

    def body(query_ref, key_ref, value_ref, *rest):
        shards, out, wide = rest[: len(gains)], rest[-2], rest[-1]
        wide[rows:, :] = jnp.zeros((tall - rows, wide.shape[1]), jnp.float32)
        wide[:rows, : ends[0]] = query_ref[...].astype(jnp.float32)
        wide[:rows, ends[0] : ends[1]] = key_ref[...].astype(jnp.float32)
        wide[:rows, ends[1] :] = value_ref[...].astype(jnp.float32)
        for i, shard in enumerate(shards):
            wide[rows : rows + 1, i * 128 : i * 128 + shard.shape[1]] = shard[...].astype(
                jnp.float32
            )
        out[...] = wide[...].astype(jnp.bfloat16)

    return kernel_call(
        body,
        [((tall, int(ends[2])), jnp.bfloat16)],
        [w_query, w_key, w_value, *[g.reshape(1, -1) for g in gains]],
        scratch=[pltpu.VMEM((tall, int(ends[2])), jnp.float32)],
    )[0]


def tables(where, lengths, count, stretch, ctx, head_dim):
    seqs = lengths.shape[1]
    each, half = count // seqs, head_dim // 2
    span = 2 * ctx * stretch
    freqs = rope_base ** (-2.0 * np.arange(half, dtype=np.float64) / head_dim)
    freqs = jnp.asarray(freqs[None].astype(np.float32))

    def positions(index, owner):
        block, step = index // stretch % 2, index % stretch
        return jnp.where(block == 0, owner, 2 * ctx - 1 - owner) * stretch + step

    def body(where_ref, lengths_ref, freqs_ref, cos_out, sin_out, valid_out, allowed_out):
        mine = where_ref[4]
        rows = lax.broadcasted_iota(jnp.int32, (each, 1), 0)
        local = positions(rows, mine)
        angles = local.astype(jnp.float32) * freqs_ref[...]
        cos, sin = jnp.cos(angles), jnp.sin(angles)
        cols = lax.broadcasted_iota(jnp.int32, (1, span), 1)
        owner = (mine - cols // each + ctx) % ctx
        keys = positions(cols % each, owner)
        for s in range(seqs):
            part = slice(s * each, (s + 1) * each)
            for low, high in ((0, half), (half, head_dim)):
                cos_out[part, low:high] = cos
                sin_out[part, low:high] = sin
            length = lengths_ref[0, s]
            valid_out[part, :] = jnp.where(local < length, 1.0, 0.0)
            allowed_out[s] = jnp.where((keys <= local) & (keys < length), 1.0, 0.0)

    return kernel_call(
        body,
        [
            ((count, head_dim), jnp.float32),
            ((count, head_dim), jnp.float32),
            ((count, 1), jnp.float32),
            ((seqs, each, span), jnp.float32),
        ],
        [where, lengths, freqs],
        {0: "smem", 1: "smem"},
    )


def late_gains(where, pieces, masks, rows, lanes, sizes, ctx, after):
    def body(where_ref, after_ref, *rest):
        parts, outs = rest[: len(pieces)], rest[len(pieces) :]
        for out, lane, size in zip(outs, lanes, sizes):
            out[...] = spread(where_ref, parts, masks, rows, lane, size, ctx)

    return kernel_call(
        body,
        [((1, len(pieces) * ctx * size), jnp.float32) for size in sizes],
        [where, after, *pieces],
        {0: "smem", 1: "any"},
    )


def project(where, tokens, pieces, sizes, cosine, sine, masks, heads, ctx):
    count, width = tokens.shape
    wide = pieces[0].shape[1]
    head_dim = cosine.shape[1]
    total = len(pieces)
    rows = width // total

    def body(where_ref, x_ref, cos_ref, sin_ref, *rest):
        parts = rest[:total]
        normed_ref, query_out, both_out, raw_out, in_ref, query_ref, key_ref, weight = rest[total:]
        for i, ref in enumerate((in_ref, query_ref, key_ref)):
            ref[...] = spread(where_ref, parts, masks, rows, i * 128, sizes[i], ctx)
        put_rows(weight, where_ref[0], parts, masks, rows)
        normed = rms_norm(x_ref[...].astype(jnp.float32), in_ref[...]).astype(jnp.bfloat16)
        normed_ref[...] = normed
        cos, sin = cos_ref[...], sin_ref[...]
        for h in range(heads + 1):
            cols = slice(h * head_dim, (h + 1) * head_dim)
            raw = dot(normed, weight[:, cols], 1, 0)
            raw_out[:, cols] = raw
            gain = query_ref[...] if h < heads else key_ref[...]
            turned = rotate(rms_norm(raw, gain), cos, sin).astype(jnp.bfloat16)
            if h < heads:
                query_out[:, cols] = turned
            else:
                both_out[:, :head_dim] = turned
        both_out[:, head_dim:] = dot(normed, weight[:, (heads + 1) * head_dim :], 1, 0).astype(
            jnp.bfloat16
        )

    return kernel_call(
        body,
        [
            ((count, width), jnp.bfloat16),
            ((count, heads * head_dim), jnp.bfloat16),
            ((count, 2 * head_dim), jnp.bfloat16),
            ((count, (heads + 1) * head_dim), jnp.float32),
            ((1, width), jnp.float32),
            ((1, head_dim), jnp.float32),
            ((1, head_dim), jnp.float32),
        ],
        [where, tokens, cosine, sine, *pieces],
        {0: "smem"},
        [pltpu.VMEM((width, wide), jnp.bfloat16)],
        2 * count * width * wide,
    )


def attend(where, tokens, query, both, allowed, valid, norm_attn, norm_pre, pieces, masks, heads):
    count, width = tokens.shape
    seqs, each, span = allowed.shape
    head_dim = query.shape[1] // heads
    inv_root = head_dim ** (-0.5)
    near, total = len(both), len(pieces)

    def body(where_ref, x_ref, query_ref, allowed_ref, valid_ref, attn_ref, pre_ref, *rest):
        got, parts = rest[:near], rest[near : near + total]
        probs_out, mixed_out, raw_out, after_out, two_out, weight = rest[near + total :]
        put_rows(weight, where_ref[0], parts, masks, parts[0].shape[0])
        for s in range(seqs):
            rows = slice(s * each, (s + 1) * each)
            queries = jnp.concatenate(
                [query_ref[rows, h * head_dim : (h + 1) * head_dim] for h in range(heads)], axis=0
            )
            keys = jnp.concatenate([g[rows, :head_dim] for g in got], axis=0)
            values = jnp.concatenate([g[rows, head_dim:] for g in got], axis=0)
            scores = dot(queries, keys, 1, 1) * inv_root
            keep = jnp.concatenate([allowed_ref[s]] * heads, axis=0)
            scores = jnp.where(keep > 0.0, scores, -1e30)
            expo = jnp.exp(scores - jnp.max(scores, axis=-1, keepdims=True))
            probs = expo / jnp.sum(expo, axis=-1, keepdims=True)
            probs_out[s] = probs
            mixed = dot(probs.astype(jnp.bfloat16), values, 1, 0).astype(jnp.bfloat16)
            for h in range(heads):
                mixed_out[rows, h * head_dim : (h + 1) * head_dim] = mixed[
                    h * each : (h + 1) * each
                ]
        raw = dot(mixed_out[...], weight[...], 1, 0)
        raw_out[...] = raw
        after = x_ref[...].astype(jnp.float32) + valid_ref[...] * rms_norm(raw, attn_ref[...])
        after_out[...] = after
        two_out[...] = rms_norm(after, pre_ref[...]).astype(jnp.bfloat16)

    return kernel_call(
        body,
        [
            ((seqs, heads * each, span), jnp.float32),
            ((count, heads * head_dim), jnp.bfloat16),
            ((count, width), jnp.float32),
            ((count, width), jnp.float32),
            ((count, width), jnp.bfloat16),
        ],
        [where, tokens, query, allowed, valid, norm_attn, norm_pre, *both, *pieces],
        {0: "smem"},
        [pltpu.VMEM((heads * head_dim, width), jnp.bfloat16)],
        2 * count * heads * head_dim * (width + 2 * span),
    )


def column_steps(size, step):
    return [(s, min(size, s + step)) for s in range(0, size, step)]


def halves_of(rows):
    first = -(-rows // 32) * 16
    return first, rows - first


def wide_pieces(parts, far, chunk):
    first, second = halves_of(chunk)
    shapes = [(0, 0, chunk), (2, 0, chunk), (4, 0, chunk), (6, 0, first), (6, first, second)]
    return [(ref, mask, at, rows) for ref, (mask, at, rows) in zip(parts, shapes)] + [
        (ref, mask ^ 1, at, rows) for ref, (mask, at, rows) in zip(far, shapes)
    ]


def load_weights(index, pieces, chunk, target, sems):
    def copies(m):
        result = []
        for i, (ref, mask, at, rows) in enumerate(pieces):
            start = pl.multiple_of((index ^ mask) * chunk + at, 16)
            result.append(
                pltpu.make_async_copy(ref.at[m], target.at[m, pl.ds(start, rows)], sems.at[m, i])
            )
        return result

    return [copies(m) for m in range(target.shape[0])]


def feed_forward(where, pieces, weights):
    count, width = pieces[0].shape
    kinds, chunk, inner = weights[0].shape
    lanes = -(-inner // 128) * 128
    near, spots = len(pieces), len(weights)
    total = near * count
    slope = (2.0 / np.pi) ** 0.5

    def body(where_ref, *rest):
        shards, rest = rest[:spots], rest[spots:]
        parts = rest[:near]
        group_out, act_out, one_out, two_out = rest[near : near + 4]
        sums = rest[near + 4 : near + 4 + near]
        weight, sems = rest[near + 4 + near :]
        shards = wide_pieces(shards[: spots // 2], shards[spots // 2 :], chunk)
        copies = load_weights(where_ref[0], shards, chunk, weight, sems)
        for kind in copies:
            for copy in kind:
                copy.start()
        for k in range(near):
            group_out[k * count : (k + 1) * count, :] = parts[k][...]
        for kind in copies[:2]:
            for copy in kind:
                copy.wait()
        for low, high in column_steps(inner, 256):
            gate = dot(group_out[...], weight[0, :, low:high], 1, 0)
            upper = dot(group_out[...], weight[1, :, low:high], 1, 0)
            bent = jnp.tanh(slope * (gate + 0.044715 * (gate * gate * gate)))
            half = 0.5 * (1.0 + bent)
            gelu = gate * half
            steep = half + 0.5 * gate * (1.0 - bent * bent) * (
                slope * (1.0 + 3.0 * 0.044715 * gate * gate)
            )
            act_out[:, low:high] = (gelu * upper).astype(jnp.bfloat16)
            one_out[:, low:high] = (steep * upper).astype(jnp.bfloat16)
            two_out[:, low:high] = gelu.astype(jnp.bfloat16)
        if lanes > inner:
            act_out[:, inner:] = jnp.zeros((total, lanes - inner), jnp.bfloat16)
        for copy in copies[2]:
            copy.wait()
        for low, high in column_steps(width, 384):
            part = dot(act_out[:, :inner], weight[2, low:high, :], 1, 1)
            for k in range(near):
                sums[k][:, low:high] = part[k * count : (k + 1) * count].astype(sums[k].dtype)

    return kernel_call(
        body,
        [((total, width), jnp.bfloat16)]
        + [((total, lanes), jnp.bfloat16)]
        + [((total, inner), jnp.bfloat16)] * 2
        + [((count, width), jnp.float32)]
        + [((count, width), jnp.bfloat16)] * (near - 1),
        [where, *weights, *pieces],
        {0: "smem", **{1 + i: "any" for i in range(spots)}},
        [
            pltpu.VMEM((kinds, width, inner), jnp.bfloat16),
            pltpu.SemaphoreType.DMA((kinds, spots)),
        ],
        6 * total * width * inner,
    )


def finish(parts, after, cotangent, valid, norm_post):
    count, width = after.shape
    near = len(parts)

    def body(after_ref, cot_ref, valid_ref, post_ref, *rest):
        got = rest[:near]
        output_out, grad_out, gain_out = rest[near:]
        raw = got[0][...]
        for g in got[1:]:
            raw = raw + g[...].astype(jnp.float32)
        ok = valid_ref[...]
        output_out[...] = (after_ref[...] + ok * rms_norm(raw, post_ref[...])).astype(jnp.bfloat16)
        grad, gain = norm_back(raw, post_ref[...], ok * cot_ref[...].astype(jnp.float32))
        grad_out[...] = grad.astype(jnp.bfloat16)
        gain_out[...] = gain

    return kernel_call(
        body,
        [
            ((count, width), jnp.bfloat16),
            ((count, width), jnp.bfloat16),
            ((1, width), jnp.float32),
        ],
        [after, cotangent, valid, norm_post, *parts],
    )


def feed_back(where, pieces, weights, one, two):
    count, width = pieces[0].shape
    kinds, chunk, inner = weights[0].shape
    lanes = -(-inner // 128) * 128
    near, spots = len(pieces), len(weights)
    total = near * count

    def body(where_ref, one_ref, two_ref, *rest):
        shards, rest = rest[:spots], rest[spots:]
        parts = rest[:near]
        group_out, gate_out, upper_out = rest[near : near + 3]
        sums = rest[near + 3 : near + 3 + near]
        weight, sems = rest[near + 3 + near :]
        shards = wide_pieces(shards[: spots // 2], shards[spots // 2 :], chunk)
        copies = load_weights(where_ref[0], shards, chunk, weight, sems)
        for kind in (copies[2], copies[0], copies[1]):
            for copy in kind:
                copy.start()
        for k in range(near):
            group_out[k * count : (k + 1) * count, :] = parts[k][...]
        for copy in copies[2]:
            copy.wait()
        for low, high in column_steps(inner, 256):
            grad = dot(group_out[...], weight[2, :, low:high], 1, 0)
            gate_out[:, low:high] = (grad * one_ref[:, low:high].astype(jnp.float32)).astype(
                jnp.bfloat16
            )
            upper_out[:, low:high] = (grad * two_ref[:, low:high].astype(jnp.float32)).astype(
                jnp.bfloat16
            )
        if lanes > inner:
            gate_out[:, inner:] = jnp.zeros((total, lanes - inner), jnp.bfloat16)
            upper_out[:, inner:] = jnp.zeros((total, lanes - inner), jnp.bfloat16)
        for kind in copies[:2]:
            for copy in kind:
                copy.wait()
        for low, high in column_steps(width, 384):
            part = dot(gate_out[:, :inner], weight[0, low:high, :], 1, 1)
            part = part + dot(upper_out[:, :inner], weight[1, low:high, :], 1, 1)
            for k in range(near):
                sums[k][:, low:high] = part[k * count : (k + 1) * count].astype(sums[k].dtype)

    return kernel_call(
        body,
        [((total, width), jnp.bfloat16)]
        + [((total, lanes), jnp.bfloat16)] * 2
        + [((count, width), jnp.float32)]
        + [((count, width), jnp.bfloat16)] * (near - 1),
        [where, one, two, *weights, *pieces],
        {0: "smem", **{3 + i: "any" for i in range(spots)}},
        [
            pltpu.VMEM((kinds, width, inner), jnp.bfloat16),
            pltpu.SemaphoreType.DMA((kinds, spots)),
        ],
        6 * total * width * inner,
    )


def wide_grads(where, two, two_far, back, back_far, act, act_far, gate, gate_far, upper, upper_far):
    total, width = two.shape
    inner = act.shape[1]
    chunk = width // 8
    first, second = halves_of(chunk)

    def body(where_ref, *rest):
        lefts = [rest[0:2], rest[2:4]]
        rights = [rest[6:8], rest[8:10], rest[4:6]]
        outs = rest[10:14]
        turned, left = rest[14:]
        core, x, y = where_ref[1], where_ref[2], where_ref[3]
        order = []
        for flip in (1, 0):
            order.append([(j * 2 + jnp.bitwise_xor(x, flip), 0, first) for j in range(2)])
        for flip in (1, 0):
            order.append([(jnp.bitwise_xor(y, flip) * 2 + j, first, second) for j in range(2)])
        for index, kinds in ((0, (0, 1)), (1, (2,))):
            for side in range(2):
                turned[:, side * total : (side + 1) * total] = lefts[index][side][...].T
            at = 0
            for block in order:
                for plane, offset, size in block:
                    start = pl.multiple_of((plane * 2 + core) * chunk + offset, 16)
                    left[at : at + size, :] = turned[pl.ds(start, size), :]
                    at += size
            for m in kinds:
                own, far = rights[m]
                for low, high in column_steps(inner, 256):
                    part = dot(left[:, :total], own[:, low:high], 1, 0)
                    part = part + dot(left[:, total:], far[:, low:high], 1, 0)
                    part = part.astype(jnp.bfloat16)
                    at = 0
                    for out, block in zip(outs, order):
                        size = 2 * block[0][2]
                        out[m, :, low:high] = part[at : at + size]
                        at += size

    return kernel_call(
        body,
        [
            ((3, 2 * first, inner), jnp.bfloat16),
            ((3, 2 * first, inner), jnp.bfloat16),
            ((3, 2 * second, inner), jnp.bfloat16),
            ((3, 2 * second, inner), jnp.bfloat16),
        ],
        [where, two, two_far, back, back_far, act, act_far, gate, gate_far, upper, upper_far],
        {0: "smem"},
        [
            pltpu.VMEM((width, 2 * total), jnp.bfloat16),
            pltpu.VMEM((width // 2, 2 * total), jnp.bfloat16),
        ],
        6 * total * width * inner,
    )


def wide_middle(where, kept_a, got_a, kept_b, got_b):
    kinds, twice_a, inner = kept_a.shape
    first, second = twice_a // 2, kept_b.shape[1] // 2

    def body(where_ref, kept_a_ref, got_a_ref, kept_b_ref, got_b_ref, *outs):
        x, y = where_ref[2], where_ref[3]
        for m in range(kinds):
            for flip, out in ((1, outs[0]), (0, outs[1])):
                rows = pl.ds(pl.multiple_of(jnp.bitwise_xor(y, flip) * first, 16), first)
                total = kept_a_ref[m, rows, :].astype(jnp.float32) + got_a_ref[m, rows, :].astype(
                    jnp.float32
                )
                out[m] = total.astype(jnp.bfloat16)
            for flip, out in ((1, outs[2]), (0, outs[3])):
                rows = pl.ds(pl.multiple_of(jnp.bitwise_xor(x, flip) * second, 16), second)
                total = kept_b_ref[m, rows, :].astype(jnp.float32) + got_b_ref[m, rows, :].astype(
                    jnp.float32
                )
                out[m] = total.astype(jnp.bfloat16)

    return kernel_call(
        body,
        [
            ((kinds, first, inner), jnp.bfloat16),
            ((kinds, first, inner), jnp.bfloat16),
            ((kinds, second, inner), jnp.bfloat16),
            ((kinds, second, inner), jnp.bfloat16),
        ],
        [where, kept_a, got_a, kept_b, got_b],
        {0: "smem"},
    )


def wide_last(kept_a, got_a, kept_b, got_b, inner):
    kinds, first, _ = kept_a.shape
    second = kept_b.shape[1]

    def body(kept_a_ref, got_a_ref, kept_b_ref, got_b_ref, *outs):
        for m in range(kinds):
            total = kept_a_ref[m].astype(jnp.float32) + got_a_ref[m].astype(jnp.float32)
            outs[m][:first, :] = total[:, :inner]
            total = kept_b_ref[m].astype(jnp.float32) + got_b_ref[m].astype(jnp.float32)
            outs[m][first:, :] = total[:, :inner]

    return kernel_call(
        body,
        [((first + second, inner), jnp.float32)] * kinds,
        [kept_a, got_a, kept_b, got_b],
    )


def attend_back(
    where,
    parts,
    after,
    cotangent,
    valid,
    attn_raw,
    norm_pre,
    norm_attn,
    norm_query,
    probs,
    query,
    raw,
    both,
    pieces,
    cosine,
    sine,
    masks,
    heads,
):
    count, width = after.shape
    seqs, _, span = probs.shape
    each = count // seqs
    head_dim = norm_query.shape[1]
    inv_root = head_dim ** (-0.5)
    near, total = len(both), len(pieces)

    def body(
        where_ref,
        after_ref,
        cot_ref,
        valid_ref,
        attn_ref,
        pre_ref,
        norm_ref,
        query_gain_ref,
        probs_ref,
        query_ref,
        raw_ref,
        cos_ref,
        sin_ref,
        *rest,
    ):
        sums = rest[:near]
        got = rest[near : 2 * near]
        shards = rest[2 * near : 2 * near + total]
        rest = rest[2 * near + total :]
        dx_out, attn_grad_out, raw_grad_out, pre_out, attn_gain_out, query_gain_out = rest[:6]
        both_outs = rest[6 : 6 + near]
        weight, mixed_grad, query_grad = rest[6 + near :]
        put_rows(weight, where_ref[0], shards, masks, shards[0].shape[0])
        grad = sums[0][...]
        for s in sums[1:]:
            grad = grad + s[...].astype(jnp.float32)
        through, gain = norm_back(after_ref[...], pre_ref[...], grad)
        pre_out[...] = gain
        dx = cot_ref[...].astype(jnp.float32) + through
        dx_out[...] = dx
        attn_grad, gain = norm_back(attn_ref[...], norm_ref[...], valid_ref[...] * dx)
        attn_gain_out[...] = gain
        attn_grad = attn_grad.astype(jnp.bfloat16)
        attn_grad_out[...] = attn_grad
        mixed_grad[...] = dot(attn_grad, weight[...], 1, 1).astype(jnp.bfloat16)
        for s in range(seqs):
            rows = slice(s * each, (s + 1) * each)
            queries = jnp.concatenate(
                [query_ref[rows, h * head_dim : (h + 1) * head_dim] for h in range(heads)], axis=0
            )
            grads = jnp.concatenate(
                [mixed_grad[rows, h * head_dim : (h + 1) * head_dim] for h in range(heads)], axis=0
            )
            keys = jnp.concatenate([g[rows, :head_dim] for g in got], axis=0)
            values = jnp.concatenate([g[rows, head_dim:] for g in got], axis=0)
            probs = probs_ref[s]
            prob_grad = dot(grads, values, 1, 1)
            row = jnp.sum(probs * prob_grad, axis=-1, keepdims=True)
            score_grad = (probs * (prob_grad - row)).astype(jnp.bfloat16)
            back = dot(score_grad, keys, 1, 0) * inv_root
            for h in range(heads):
                query_grad[rows, h * head_dim : (h + 1) * head_dim] = back[
                    h * each : (h + 1) * each
                ]
            keys_grad = dot(score_grad, queries, 0, 0) * inv_root
            values_grad = dot(probs.astype(jnp.bfloat16), grads, 0, 0)
            for k in range(near):
                part = slice(k * each, (k + 1) * each)
                both_outs[k][rows, :head_dim] = keys_grad[part].astype(both_outs[k].dtype)
                both_outs[k][rows, head_dim:] = values_grad[part].astype(both_outs[k].dtype)
        cos, sin = cos_ref[...], sin_ref[...]
        gain_sum = jnp.zeros((1, head_dim), jnp.float32)
        for h in range(heads):
            cols = slice(h * head_dim, (h + 1) * head_dim)
            turned = rotate_back(query_grad[:, cols], cos, sin)
            value_grad, gain = norm_back(raw_ref[:, cols], query_gain_ref[...], turned)
            raw_grad_out[:, cols] = value_grad.astype(jnp.bfloat16)
            gain_sum = gain_sum + gain
        query_gain_out[...] = gain_sum

    return kernel_call(
        body,
        [
            ((count, width), jnp.float32),
            ((count, width), jnp.bfloat16),
            ((count, heads * head_dim), jnp.bfloat16),
            ((1, width), jnp.float32),
            ((1, width), jnp.float32),
            ((1, head_dim), jnp.float32),
            ((count, 2 * head_dim), jnp.float32),
        ]
        + [((count, 2 * head_dim), jnp.bfloat16)] * (near - 1),
        [
            where,
            after,
            cotangent,
            valid,
            attn_raw,
            norm_pre,
            norm_attn,
            norm_query,
            probs,
            query,
            raw,
            cosine,
            sine,
            *parts,
            *both,
            *pieces,
        ],
        {0: "smem"},
        [
            pltpu.VMEM((heads * head_dim, width), jnp.bfloat16),
            pltpu.VMEM((count, heads * head_dim), jnp.bfloat16),
            pltpu.VMEM((count, heads * head_dim), jnp.float32),
        ],
        2 * count * heads * head_dim * (width + 5 * span),
    )


def project_back(
    where,
    parts,
    raw,
    query_grad,
    tokens,
    dx,
    norm_in,
    norm_key,
    cosine,
    sine,
    pieces,
    masks,
    heads,
    ctx,
    gains,
):
    count, width = tokens.shape
    wide = pieces[0].shape[1]
    head_dim = norm_key.shape[1]
    near, total = len(parts), len(pieces)
    step = heads * head_dim // ctx
    count_gains = len(gains)

    def body(
        where_ref, raw_ref, query_ref, x_ref, dx_ref, in_ref, key_ref, cos_ref, sin_ref, *rest
    ):
        sums = rest[:near]
        shards = rest[near : near + total]
        others = rest[near + total : near + total + count_gains]
        input_out, grads_out, gains_out, weight = rest[near + total + count_gains :]
        put_rows(weight, where_ref[0], shards, masks, width // total)
        grad = sums[0][...]
        for s in sums[1:]:
            grad = grad + s[...].astype(jnp.float32)
        turned = rotate_back(grad[:, :head_dim], cos_ref[...], sin_ref[...])
        key_grad, key_gain = norm_back(raw_ref[:, heads * head_dim :], key_ref[...], turned)
        grads_out[:, : heads * head_dim] = query_ref[...]
        grads_out[:, heads * head_dim : (heads + 1) * head_dim] = key_grad.astype(jnp.bfloat16)
        grads_out[:, (heads + 1) * head_dim :] = grad[:, head_dim:].astype(jnp.bfloat16)
        back = dot(grads_out[...], weight[...], 1, 1)
        through, in_gain = norm_back(x_ref[...].astype(jnp.float32), in_ref[...], back)
        input_out[...] = (dx_ref[...] + through).astype(jnp.bfloat16)
        gains_out[...] = jnp.zeros((total, wide), jnp.float32)
        lane = 0
        for gain in (in_gain, others[0][...], key_gain, *[o[...] for o in others[1:]]):
            size = gain.shape[1] // (total * ctx)
            for d in range(total):
                for c in range(ctx):
                    at = c * step + lane
                    gains_out[d : d + 1, at : at + size] = gain[
                        :, (d * ctx + c) * size : (d * ctx + c + 1) * size
                    ]
            lane += size

    return kernel_call(
        body,
        [
            ((count, width), jnp.bfloat16),
            ((count, wide), jnp.bfloat16),
            ((total, wide), jnp.float32),
        ],
        [
            where,
            raw,
            query_grad,
            tokens,
            dx,
            norm_in,
            norm_key,
            cosine,
            sine,
            *parts,
            *pieces,
            *gains,
        ],
        {0: "smem"},
        [pltpu.VMEM((width, wide), jnp.bfloat16)],
        2 * count * width * wide,
    )


def narrow_grads(where, left, left_far, right, right_far, gains=()):
    count, width = left.shape
    wide = right.shape[1]
    chunk = width // 8
    tall = chunk + 16 if gains else chunk

    def body(where_ref, left_ref, far_ref, right_ref, right_far_ref, *rest):
        rows, rest = rest[: len(gains)], rest[len(gains) :]
        outs, (turned, lefts) = rest[:4], rest[4:]
        turned[:, :count] = left_ref[...].T
        turned[:, count:] = far_ref[...].T
        plane, core = where_ref[0] // 2, where_ref[1]
        for m in range(4):
            start = pl.multiple_of((jnp.bitwise_xor(plane, m) * 2 + core) * chunk, 16)
            lefts[m * chunk : (m + 1) * chunk, :] = turned[pl.ds(start, chunk), :]
        for low, high in column_steps(wide, 256):
            part = dot(lefts[:, :count], right_ref[:, low:high], 1, 0)
            part = part + dot(lefts[:, count:], right_far_ref[:, low:high], 1, 0)
            for m in range(4):
                outs[m][:chunk, low:high] = part[m * chunk : (m + 1) * chunk].astype(outs[m].dtype)
        if gains:
            whole = rows[0][...] + rows[1][...]
            index = lax.broadcasted_iota(jnp.int32, whole.shape, 0)
            for m in range(4):
                row = jnp.bitwise_xor(plane, m) * 2 + core
                row = jnp.sum(jnp.where(index == row, whole, 0.0), axis=0, keepdims=True)
                lines = lax.broadcasted_iota(jnp.int32, (16, wide), 0)
                outs[m][chunk:, :] = jnp.where(lines == 0, row, 0.0).astype(outs[m].dtype)

    return kernel_call(
        body,
        [((tall, wide), jnp.float32)] + [((tall, wide), jnp.bfloat16)] * 3,
        [where, left, left_far, right, right_far, *gains],
        {0: "smem"},
        [
            pltpu.VMEM((width, 2 * count), jnp.bfloat16),
            pltpu.VMEM((width // 2, 2 * count), jnp.bfloat16),
        ],
        2 * count * width * wide,
    )


def narrow_middle(where, parts, sizes, ctx):
    chunk, wide = parts[0].shape
    each = wide // ctx

    def body(where_ref, *rest):
        got = rest[: len(parts)]
        outs = rest[len(parts) :]
        mine = where_ref[4]
        total = got[0][...]
        for g in got[1:]:
            total = total + g[...].astype(jnp.float32)
        for c in range(ctx):

            @pl.when(mine == c)
            def _(c=c):
                for k in range(ctx):
                    j = (c + k) % ctx
                    start, at = 0, 0
                    for size in sizes:
                        piece = size // ctx
                        outs[k][:, at : at + piece] = total[
                            :, start + j * piece : start + (j + 1) * piece
                        ].astype(outs[k].dtype)
                        start += size
                        at += piece

    return kernel_call(
        body,
        [((chunk, each), jnp.float32)] + [((chunk, each), jnp.bfloat16)] * (ctx - 1),
        [where, *parts],
        {0: "smem"},
    )


def split_columns(where, gate, up, ctx):
    rows, whole = gate.shape
    inner = whole // ctx

    def body(where_ref, gate_ref, up_ref, *outs):
        mine = where_ref[4]
        for c in range(ctx):

            @pl.when(mine == c)
            def _(c=c):
                for k in range(ctx):
                    j = (c + k) % ctx
                    outs[k][0] = gate_ref[:, j * inner : (j + 1) * inner]
                    outs[k][1] = up_ref[:, j * inner : (j + 1) * inner]

    return kernel_call(
        body, [((2, rows, inner), jnp.bfloat16)] * ctx, [where, gate, up], {0: "smem"}
    )


def join_wide(where, pairs, downs):
    ctx = len(pairs)
    _, rows, inner = pairs[0].shape
    per, chunk, part = downs[0].shape

    def body(where_ref, *rest):
        two, down, out, rows_scr = rest[:ctx], rest[ctx : 2 * ctx], rest[2 * ctx], rest[2 * ctx + 1]
        mine = where_ref[4]
        for c in range(ctx):

            @pl.when(mine == c)
            def _(c=c):
                for m in range(2):
                    for a in range(ctx):
                        rows_scr[a * rows : (a + 1) * rows, :] = two[(c - a) % ctx][m].astype(
                            jnp.float32
                        )
                    out[m] = rows_scr[...].astype(jnp.bfloat16)
                for a in range(ctx):
                    for p in range(per):
                        at = (p * ctx + a) * part
                        rows_scr[:, at : at + part] = down[(c - a) % ctx][p].astype(jnp.float32)
                out[2] = rows_scr[...].astype(jnp.bfloat16)

    return kernel_call(
        body,
        [((3, chunk, inner), jnp.bfloat16)],
        [where, *pairs, *downs],
        {0: "smem"},
        [pltpu.VMEM((chunk, inner), jnp.float32)],
    )[0]


def join_rows(where, pieces, rows):
    ctx = len(pieces)
    tall, wide = pieces[0].shape
    more = 16 if tall > rows else 0

    def body(where_ref, *rest):
        got, out, rows_scr = rest[:ctx], rest[ctx], rest[ctx + 1]
        mine = where_ref[4]
        if more:
            rows_scr[ctx * rows :, :] = jnp.zeros((more, wide), jnp.float32)
        for c in range(ctx):

            @pl.when(mine == c)
            def _(c=c):
                for a in range(ctx):
                    piece = got[(c - a) % ctx]
                    rows_scr[a * rows : (a + 1) * rows, :] = piece[:rows, :].astype(jnp.float32)
                    if more:
                        at = ctx * rows + a
                        rows_scr[at : at + 1, :] = piece[rows : rows + 1, :].astype(jnp.float32)
                out[...] = rows_scr[...].astype(jnp.bfloat16)

    return kernel_call(
        body,
        [((ctx * rows + more, wide), jnp.bfloat16)],
        [where, *pieces],
        {0: "smem"},
        [pltpu.VMEM((ctx * rows + more, wide), jnp.float32)],
    )[0]


def plane_gather(value):
    size = lax.axis_size("dp")

    def across(item, mask):
        return lax.ppermute(item, "dp", [(i, i ^ mask) for i in range(size)])

    near = [value] + [across(value, m) for m in range(2, size, 2)]
    far = [across(item, 1) for item in near]
    return near + far, list(range(0, size, 2)) + list(range(1, size, 2))


def plane_send(parts):
    size = lax.axis_size("dp")
    return [parts[0]] + [
        lax.ppermute(parts[m], "dp", [(i, i ^ (2 * m)) for i in range(size)])
        for m in range(1, len(parts))
    ]


def ctx_send(parts, sign):
    return [parts[0]] + [shift(parts[k], sign * k) for k in range(1, len(parts))]


def fused(
    tokens,
    cotangent,
    lengths,
    w_query,
    w_key,
    w_value,
    w_out,
    w_gate,
    w_up,
    w_down,
    gain_in,
    gain_query,
    gain_key,
    gain_attn,
    gain_pre,
    gain_post,
):
    count, width = tokens.shape
    seq_count = lengths.shape[1]
    stretch = count // (2 * seq_count)
    dp = lax.axis_size("dp")
    ctx = lax.axis_size("ctx")
    mine = lax.axis_index("ctx")
    group = lax.axis_index("dp")
    head_dim = w_key.shape[1]
    heads = w_query.shape[1] // head_dim
    where = jnp.stack([group, group % 2, group // 2 % 2, group // 4, mine]).astype(jnp.int32)

    gains = [gain_in, gain_query, gain_key, gain_attn, gain_pre, gain_post]
    sizes = [g.shape[0] for g in gains]
    packed = pack(w_query, w_key, w_value, gains)
    w_gate, w_up, w_down, packed = lax.optimization_barrier((w_gate, w_up, w_down, packed))
    qkv_chunk = join_rows(where, ctx_gather(packed), w_query.shape[0])
    out_chunk = join_rows(where, ctx_gather(w_out), w_out.shape[0])
    qkv_pieces, masks = plane_gather(qkv_chunk)
    out_pieces, _ = plane_gather(out_chunk)
    per = dp // ctx
    down = w_down.T.reshape(dp, width // dp, w_down.shape[0])
    down = lax.all_to_all(down, "dp", split_axis=0, concat_axis=0, tiled=True)
    down = ctx_exchange(down.reshape(ctx, per, width // dp, w_down.shape[0]))
    pairs = ctx_send(split_columns(where, w_gate, w_up, ctx), 1)
    shard = join_wide(where, pairs, down)
    cosine, sine, valid, allowed = tables(where, lengths, count, stretch, ctx, head_dim)
    shard_x, shard_y = swap(shard, 1), swap(shard, 2)

    normed, query, both, raw, norm_in, norm_query, norm_key = project(
        where, tokens, qkv_pieces, sizes[:3], cosine, sine, masks, heads, ctx
    )
    norm_attn, norm_pre, norm_post = late_gains(
        where, qkv_pieces, masks, width // dp, [384, 512, 640], sizes[3:], ctx, both
    )
    both = ctx_gather(both)
    probs, mixed, attn_raw, after, normed_two = attend(
        where, tokens, query, both, allowed, valid, norm_attn, norm_pre, out_pieces, masks, heads
    )
    shard_x, shard_y, normed_two = lax.optimization_barrier((shard_x, shard_y, normed_two))
    first = halves_of(width // dp)[0]
    weights = [shard, shard_x, shard_y, swap(shard_x[:, :first], 2), swap(shard_y[:, first:], 1)]
    weights = weights + [swap(w, 0) for w in weights]
    group_two, act, one, two, *sums = feed_forward(where, ctx_gather(normed_two), weights)
    output, ffn_grad, gain_post_grad = finish(
        ctx_send(sums, -1), after, cotangent, valid, norm_post
    )
    group_two_far = swap(group_two, 0)
    act_far = swap(act, 0)
    group_ffn, gate_grad, upper_grad, *sums = feed_back(
        where, ctx_gather(ffn_grad), weights, one, two
    )
    sums = ctx_send(sums, -1)
    group_ffn_far, gate_far, upper_far = (
        swap(group_ffn, 0),
        swap(gate_grad, 0),
        swap(upper_grad, 0),
    )
    send_a, kept_a, send_b, kept_b = wide_grads(
        where,
        group_two,
        group_two_far,
        group_ffn,
        group_ffn_far,
        act,
        act_far,
        gate_grad,
        gate_far,
        upper_grad,
        upper_far,
    )
    sums, send_a, send_b = lax.optimization_barrier((sums, send_a, send_b))
    got_a, got_b = swap(send_a, 1), swap(send_b, 2)
    dx, attn_grad, query_grad, gain_pre_grad, gain_attn_grad, gain_query_grad, *parts = attend_back(
        where,
        sums,
        after,
        cotangent,
        valid,
        attn_raw,
        norm_pre,
        norm_attn,
        norm_query,
        probs,
        query,
        raw,
        both,
        out_pieces,
        cosine,
        sine,
        masks,
        heads,
    )
    parts = ctx_send(parts, -1)
    send_a, kept_a, send_b, kept_b = wide_middle(where, kept_a, got_a, kept_b, got_b)
    out_blocks = plane_send(
        narrow_grads(where, attn_grad, swap(attn_grad, 0), mixed, swap(mixed, 0))
    )
    out_blocks = ctx_send(narrow_middle(where, out_blocks, [mixed.shape[1]], ctx), 1)
    parts, send_a, send_b, out_blocks = lax.optimization_barrier(
        (parts, send_a, send_b, out_blocks)
    )
    got_a, got_b = swap(send_a, 2), swap(send_b, 1)
    input_grad, qkv_grads, gain_rows = project_back(
        where,
        parts,
        raw,
        query_grad,
        tokens,
        dx,
        norm_in,
        norm_key,
        cosine,
        sine,
        qkv_pieces,
        masks,
        heads,
        ctx,
        [gain_query_grad, gain_attn_grad, gain_pre_grad, gain_post_grad],
    )
    blocks = plane_send(
        narrow_grads(
            where,
            normed,
            swap(normed, 0),
            qkv_grads,
            swap(qkv_grads, 0),
            [gain_rows, swap(gain_rows, 0)],
        )
    )
    blocks = ctx_send(
        narrow_middle(where, blocks, [heads * head_dim, head_dim, head_dim], ctx), 1
    )
    grad_gate, grad_up, grad_down = wide_last(
        kept_a, got_a, kept_b, got_b, w_gate.shape[1] // ctx
    )

    def total(pieces):
        result = pieces[0].astype(jnp.float32)
        for p in pieces[1:]:
            result = result + p.astype(jnp.float32)
        return result

    grad_out = total(out_blocks).T
    grad_qkv = total(blocks)

    outs, start = [], 0
    for size in sizes:
        outs.append(grad_qkv[width // dp, start : start + size])
        start += size
    grad_qkv = grad_qkv[: width // dp]
    q_cols, k_cols = heads * head_dim // ctx, head_dim // ctx
    return (
        output,
        input_grad,
        grad_qkv[:, :q_cols],
        grad_qkv[:, q_cols : q_cols + k_cols],
        grad_qkv[:, q_cols + k_cols :],
        grad_out,
        grad_gate,
        grad_up,
        grad_down.T,
        *outs,
    )


def on_device(tokens, cotangent, lengths, *params):
    dp, ctx = lax.axis_size("dp"), lax.axis_size("ctx")
    each = tokens.shape[0] // lengths.shape[1]
    fits = dp == 8 and dp % ctx == 0 and tokens.shape[1] // dp % 16 == 0 and each % 16 == 0
    run = fused if fits else plain
    return run(tokens, cotangent, lengths, *params)


def solution(mesh):
    in_specs = (
        P(("dp", "ctx"), None),
        P(("dp", "ctx"), None),
        P("dp", None),
        P(("dp", "ctx"), None),
        P(("dp", "ctx"), None),
        P(("dp", "ctx"), None),
        P(("dp", "ctx"), None),
        P(("dp", "ctx"), None),
        P(("dp", "ctx"), None),
        P(("dp", "ctx"), None),
        P(("dp", "ctx")),
        P(("dp", "ctx")),
        P(("dp", "ctx")),
        P(("dp", "ctx")),
        P(("dp", "ctx")),
        P(("dp", "ctx")),
    )
    out_specs = (
        P(("dp", "ctx"), None),
        P(("dp", "ctx"), None),
        P("dp", "ctx"),
        P("dp", "ctx"),
        P("dp", "ctx"),
        P("ctx", "dp"),
        P("dp", "ctx"),
        P("dp", "ctx"),
        P("ctx", "dp"),
        P(("dp", "ctx")),
        P(("dp", "ctx")),
        P(("dp", "ctx")),
        P(("dp", "ctx")),
        P(("dp", "ctx")),
        P(("dp", "ctx")),
    )
    return jax.shard_map(
        on_device, mesh=mesh, in_specs=in_specs, out_specs=out_specs, check_vma=False
    )
```

```python
import jax
import jax.numpy as jnp
import numpy as np
from jax import lax
from jax.experimental import pallas as pl
from jax.experimental.pallas import tpu as pltpu
from jax.sharding import PartitionSpec as P

epsilon = 1e-06
rope_base = 1000000.0


def rms_norm(value, weight):
    scale = lax.rsqrt(jnp.mean(value * value, axis=-1, keepdims=True) + epsilon)
    return value * scale * (1.0 + weight)


def rms_back(value, weight, grad):
    scale = lax.rsqrt(jnp.mean(value * value, axis=-1, keepdims=True) + epsilon)
    normed = value * scale
    weighted = grad * (1.0 + weight)
    value_grad = scale * (weighted - normed * jnp.mean(weighted * normed, axis=-1, keepdims=True))
    weight_grad = jnp.sum(grad * normed, axis=tuple(range(value.ndim - 1)))
    return (value_grad, weight_grad)


def rope_tables(positions, width):
    half = width // 2
    freqs = jnp.power(rope_base, -2.0 * jnp.arange(half, dtype=jnp.float32) / width)
    angles = positions[:, None] * freqs[None, :]
    cosine = jnp.concatenate([jnp.cos(angles), jnp.cos(angles)], axis=-1)
    sine = jnp.concatenate([jnp.sin(angles), jnp.sin(angles)], axis=-1)
    return (cosine, sine)


def rotate(value, cosine, sine):
    half = value.shape[-1] // 2
    turned = jnp.concatenate([-value[..., half:], value[..., :half]], axis=-1)
    return value * cosine + turned * sine


def rotate_back(grad, cosine, sine):
    half = grad.shape[-1] // 2
    scaled = grad * sine
    return grad * cosine + jnp.concatenate([scaled[..., half:], -scaled[..., :half]], axis=-1)


def geglu(gate, upper):
    return jax.nn.gelu(gate, approximate=True) * upper


def dot(left, right, left_dim, right_dim):
    return lax.dot_general(
        left, right, (((left_dim,), (right_dim,)), ((), ())), preferred_element_type=jnp.float32
    )


def swap(value, bit):
    size = lax.axis_size("dp")
    return lax.ppermute(value, "dp", [(i, i ^ (1 << bit)) for i in range(size)])


def shift(value, step):
    size = lax.axis_size("ctx")
    return lax.ppermute(value, "ctx", [(i, (i + step) % size) for i in range(size)])


def pick(value, index, axis=0):
    return lax.dynamic_index_in_dim(value, index, axis, keepdims=False)


def plane_bits():
    return list(range(1, lax.axis_size("dp").bit_length() - 1))


def ctx_gather(value):
    return [value] + [shift(value, k) for k in range(1, lax.axis_size("ctx"))]


def ctx_ordered(pieces):
    size = lax.axis_size("ctx")
    stacked = jnp.stack(pieces)
    mine = lax.axis_index("ctx")
    return jnp.stack([pick(stacked, (mine - a + size) % size) for a in range(size)])


def ctx_reduce(pieces):
    total = pieces[0].astype(jnp.float32)
    for k in range(1, len(pieces)):
        total = total + shift(pieces[k].astype(jnp.bfloat16), -k).astype(jnp.float32)
    return total


def ctx_exchange(blocks):
    size = lax.axis_size("ctx")
    mine = lax.axis_index("ctx")
    return [pick(blocks, mine)] + [
        shift(pick(blocks, (mine + k) % size), k) for k in range(1, size)
    ]


def row_parts(rows, count):
    unit = 8 if rows % 8 == 0 else 1
    edges = [unit * (rows // unit * p // count) for p in range(count + 1)]
    return [(edges[p], edges[p + 1]) for p in range(count)]


def dp_gather(value):
    bits = plane_bits()
    plane = lax.axis_index("dp") // 2
    core = lax.axis_index("dp") % 2
    count = 1 << len(bits)
    parts = []
    for p, (low, high) in enumerate(row_parts(value.shape[0], len(bits))):
        current = value[None, low:high]
        masks = [0]
        for bit in bits[p:] + bits[:p]:
            current = jnp.concatenate([current, swap(current, bit)])
            masks = masks + [m ^ (1 << (bit - 1)) for m in masks]
        other = swap(current, 0)
        place = jnp.asarray([masks.index(m) for m in range(count)], jnp.int32)
        rows_of = []
        for a in range(count):
            at = pick(place, plane ^ a)
            first, second = pick(current, at), pick(other, at)
            rows_of.append(
                jnp.stack([lax.select(core == 0, first, second), lax.select(core == 0, second, first)])
            )
        parts.append(jnp.stack(rows_of))
    whole = jnp.concatenate(parts, axis=2)
    return whole.reshape((2 * count,) + value.shape)


def dp_reduce(kept, sent):
    bits = plane_bits()
    plane = lax.axis_index("dp") // 2
    total = (kept + swap(sent.astype(jnp.bfloat16), 0).astype(jnp.float32)).astype(jnp.bfloat16)
    parts = []
    for p, (low, high) in enumerate(row_parts(total.shape[1], len(bits))):
        current = total[:, low:high]
        current = current.reshape((2,) * len(bits) + current.shape[1:])
        left = sorted(bits, reverse=True)
        for bit in bits[p:] + bits[:p]:
            axis = left.index(bit)
            mine = (plane >> (bit - 1)) & 1
            got = swap(pick(current, 1 - mine, axis), bit)
            current = pick(current, mine, axis).astype(jnp.float32) + got.astype(jnp.float32)
            left.remove(bit)
            if left:
                current = current.astype(jnp.bfloat16)
        parts.append(current)
    return jnp.concatenate(parts, axis=0)


def columns_of(value, core):
    dp = lax.axis_size("dp")
    wide = value.reshape(value.shape[0], dp // 2, 2, value.shape[1] // dp)
    return pick(wide, core, 2).reshape(value.shape[0], -1)


def weight_grad(left, right, extra=None):
    core = lax.axis_index("dp") % 2
    dp = lax.axis_size("dp")
    blocks = []
    for side in (core, 1 - core):
        block = dot(columns_of(left, side), right, 0, 0)
        block = block.reshape(dp // 2, left.shape[1] // dp, right.shape[1])
        if extra is not None:
            block = jnp.concatenate([block, pick(extra, side, 1)], axis=1)
        blocks.append(block)
    return dp_reduce(blocks[0], blocks[1])


def plain(
    tokens,
    cotangent,
    lengths,
    w_query,
    w_key,
    w_value,
    w_out,
    w_gate,
    w_up,
    w_down,
    gain_in,
    gain_query,
    gain_key,
    gain_attn,
    gain_pre,
    gain_post,
):
    count, width = tokens.shape
    seq_count = lengths.shape[1]
    stretch = count // (2 * seq_count)
    dp = lax.axis_size("dp")
    ctx = lax.axis_size("ctx")
    mine = lax.axis_index("ctx")
    head_dim = w_key.shape[1]
    heads = w_query.shape[1] // head_dim
    inner = w_gate.shape[1] // ctx
    span = 2 * ctx * stretch
    offsets = jnp.arange(stretch, dtype=jnp.int32)

    def positions_of(index):
        return jnp.concatenate(
            [index * stretch + offsets, (2 * ctx - 1 - index) * stretch + offsets]
        )

    local_pos = positions_of(mine)
    valid = (local_pos[None, :] < lengths[0][:, None]).astype(jnp.float32).reshape(count, 1)
    cosine, sine = rope_tables(jnp.tile(local_pos, seq_count).astype(jnp.float32), head_dim)
    key_pos = jnp.concatenate([positions_of((mine - k + ctx) % ctx) for k in range(ctx)])
    query_pos = jnp.repeat(local_pos, heads)
    allowed = (key_pos[None, None, :] <= query_pos[None, :, None]) & (
        key_pos[None, None, :] < lengths[0][:, None, None]
    )
    inv_root = head_dim ** (-0.5)

    gains = [gain_in, gain_query, gain_key, gain_attn, gain_pre, gain_post]
    sizes = [g.shape[0] for g in gains]
    small = jnp.concatenate(gains)
    qkv_shard = jnp.concatenate([w_query, w_key, w_value], axis=1)
    in_rows, in_cols = qkv_shard.shape
    out_rows = w_out.shape[0]
    top = max(in_rows, out_rows)
    packed_rows = -(-(top + 1) // 8) * 8
    packed = jnp.concatenate(
        [
            jnp.pad(qkv_shard, ((0, top - in_rows), (0, 0))),
            jnp.pad(w_out, ((0, top - out_rows), (0, 0))),
        ],
        axis=1,
    )
    last = jnp.pad(small[None], ((0, packed_rows - top - 1), (0, packed.shape[1] - small.shape[0])))
    packed = jnp.concatenate([packed, last], axis=0)
    near = ctx_ordered(ctx_gather(packed)).reshape(ctx * packed_rows, -1)
    everything = dp_gather(near).reshape(dp * ctx, packed_rows, -1)
    full_qkv = everything[:, :in_rows, :in_cols].reshape(width, in_cols)
    full_out = everything[:, :out_rows, in_cols:].reshape(heads * head_dim, width)
    smalls = everything[:, top, : small.shape[0]]
    norms, start = [], 0
    for size in sizes:
        norms.append(smalls[:, start : start + size].reshape(-1).astype(jnp.float32))
        start += size
    norm_in, norm_query, norm_key, norm_attn, norm_pre, norm_post = norms

    def column_blocks(weight):
        return weight.reshape(weight.shape[0], ctx, inner).transpose(1, 0, 2)

    gate_up = jnp.stack([column_blocks(w_gate), column_blocks(w_up)], axis=1)
    gate_up = ctx_ordered(ctx_exchange(gate_up)).transpose(1, 0, 2, 3)
    gate_up = gate_up.reshape(2, width // dp, inner)
    per = dp // ctx
    down = w_down.T.reshape(dp, width // dp, w_down.shape[0])
    down = lax.all_to_all(down, "dp", split_axis=0, concat_axis=0, tiled=True)
    down = down.reshape(ctx, per, width // dp, w_down.shape[0])
    down = ctx_ordered(ctx_exchange(down))
    down = down.transpose(2, 1, 0, 3).reshape(width // dp, inner)
    full_gate = dp_gather(gate_up[0]).reshape(width, inner)
    full_up = dp_gather(gate_up[1]).reshape(width, inner)
    full_down = dp_gather(down).reshape(width, inner)

    hidden = tokens.astype(jnp.float32)
    normed = rms_norm(hidden, norm_in).astype(jnp.bfloat16)
    qkv_raw = dot(normed, full_qkv, 1, 0)
    query_raw = qkv_raw[:, : heads * head_dim]
    key_raw = qkv_raw[:, heads * head_dim : (heads + 1) * head_dim]
    value_raw = qkv_raw[:, (heads + 1) * head_dim :]
    query_heads = query_raw.reshape(count, heads, head_dim)
    query_bf = rotate(
        rms_norm(query_heads, norm_query), cosine[:, None, :], sine[:, None, :]
    ).astype(jnp.bfloat16)
    query_bf = query_bf.reshape(seq_count, 2 * stretch * heads, head_dim)
    key_bf = rotate(rms_norm(key_raw, norm_key), cosine, sine).astype(jnp.bfloat16)
    both = jnp.concatenate([key_bf, value_raw.astype(jnp.bfloat16)], axis=1)
    both = jnp.stack(
        [p.reshape(seq_count, 2 * stretch, 2 * head_dim) for p in ctx_gather(both)], axis=1
    ).reshape(seq_count, span, 2 * head_dim)
    keys, values = both[..., :head_dim], both[..., head_dim:]
    scores = (
        jnp.einsum("sqd,skd->sqk", query_bf, keys, preferred_element_type=jnp.float32) * inv_root
    )
    masked = jnp.where(allowed, scores, -1e30)
    peak = jnp.max(masked, axis=-1, keepdims=True)
    expo = jnp.exp(masked - peak)
    total = jnp.sum(expo, axis=-1, keepdims=True)
    probs = expo / total
    probs_bf = probs.astype(jnp.bfloat16)
    mixed = jnp.einsum("sqk,skd->sqd", probs_bf, values, preferred_element_type=jnp.float32)
    mixed_bf = mixed.astype(jnp.bfloat16).reshape(count, heads * head_dim)
    attn_raw = dot(mixed_bf, full_out, 1, 0)
    after_attn = hidden + valid * rms_norm(attn_raw, norm_attn)
    normed_two = rms_norm(after_attn, norm_pre).astype(jnp.bfloat16)

    group_two = jnp.concatenate(ctx_gather(normed_two))
    gate = dot(group_two, full_gate, 1, 0)
    upper = dot(group_two, full_up, 1, 0)
    inner_bf = geglu(gate, upper).astype(jnp.bfloat16)
    ffn_part = dot(inner_bf, full_down, 1, 1)
    ffn_raw = ctx_reduce(list(ffn_part.reshape(ctx, count, width)))
    output = (after_attn + valid * rms_norm(ffn_raw, norm_post)).astype(jnp.bfloat16)

    grad_top = cotangent.astype(jnp.float32)
    ffn_grad, grad_gain_post = rms_back(ffn_raw, norm_post, valid * grad_top)
    group_ffn = jnp.concatenate(ctx_gather(ffn_grad.astype(jnp.bfloat16)))
    inner_grad = dot(group_ffn, full_down, 1, 0)
    _, geglu_pull = jax.vjp(geglu, gate, upper)
    gate_grad, upper_grad = geglu_pull(inner_grad)
    gate_grad_bf = gate_grad.astype(jnp.bfloat16)
    upper_grad_bf = upper_grad.astype(jnp.bfloat16)
    two_part = dot(gate_grad_bf, full_gate, 1, 1) + dot(upper_grad_bf, full_up, 1, 1)
    normed_two_grad = ctx_reduce(list(two_part.reshape(ctx, count, width)))
    grad_down = weight_grad(group_ffn, inner_bf).T
    grad_gate = weight_grad(group_two, gate_grad_bf)
    grad_up = weight_grad(group_two, upper_grad_bf)

    through_pre, grad_gain_pre = rms_back(after_attn, norm_pre, normed_two_grad)
    after_grad = grad_top + through_pre
    attn_grad, grad_gain_attn = rms_back(attn_raw, norm_attn, valid * after_grad)
    attn_grad_bf = attn_grad.astype(jnp.bfloat16)
    grad_out = weight_grad(attn_grad_bf, mixed_bf)
    grad_out = sum_of_ctx(grad_out.reshape(grad_out.shape[0], ctx, -1).transpose(1, 0, 2)).T
    mixed_grad_bf = dot(attn_grad_bf, full_out, 1, 1).astype(jnp.bfloat16)
    mixed_grad_bf = mixed_grad_bf.reshape(seq_count, 2 * stretch * heads, head_dim)
    prob_grad = jnp.einsum(
        "sqd,skd->sqk", mixed_grad_bf, values, preferred_element_type=jnp.float32
    )
    row_dot = jnp.sum(probs * prob_grad, axis=-1, keepdims=True)
    score_grad_bf = (probs * (prob_grad - row_dot)).astype(jnp.bfloat16)
    query_grad = (
        jnp.einsum("sqk,skd->sqd", score_grad_bf, keys, preferred_element_type=jnp.float32)
        * inv_root
    )
    keys_grad = (
        jnp.einsum("sqk,sqd->skd", score_grad_bf, query_bf, preferred_element_type=jnp.float32)
        * inv_root
    )
    values_grad = jnp.einsum(
        "sqk,sqd->skd", probs_bf, mixed_grad_bf, preferred_element_type=jnp.float32
    )
    both_grad = jnp.concatenate([keys_grad, values_grad], axis=-1)
    both_grad = both_grad.reshape(seq_count, ctx, 2 * stretch, 2 * head_dim).transpose(1, 0, 2, 3)
    own_grad = ctx_reduce(list(both_grad.reshape(ctx, count, 2 * head_dim)))
    own_keys_grad, own_values_grad = own_grad[:, :head_dim], own_grad[:, head_dim:]
    query_grad = rotate_back(
        query_grad.reshape(count, heads, head_dim), cosine[:, None, :], sine[:, None, :]
    )
    query_raw_grad, grad_gain_query = rms_back(query_heads, norm_query, query_grad)
    query_raw_bf = query_raw_grad.reshape(count, heads * head_dim).astype(jnp.bfloat16)
    key_raw_grad, grad_gain_key = rms_back(
        key_raw, norm_key, rotate_back(own_keys_grad, cosine, sine)
    )
    key_raw_bf = key_raw_grad.astype(jnp.bfloat16)
    value_raw_bf = own_values_grad.astype(jnp.bfloat16)
    raw_bf = jnp.concatenate([query_raw_bf, key_raw_bf, value_raw_bf], axis=1)
    normed_grad = dot(raw_bf, full_qkv, 1, 1)
    through_in, grad_gain_in = rms_back(hidden, norm_in, normed_grad)
    input_grad = (after_grad + through_in).astype(jnp.bfloat16)

    by_ctx = jnp.concatenate(
        [r.reshape(count, ctx, -1) for r in (query_raw_bf, key_raw_bf, value_raw_bf)], axis=2
    )
    each = by_ctx.shape[2]
    gain_grads = jnp.concatenate(
        [
            g.reshape(dp * ctx, -1)
            for g in (
                grad_gain_in,
                grad_gain_query,
                grad_gain_key,
                grad_gain_attn,
                grad_gain_pre,
                grad_gain_post,
            )
        ],
        axis=1,
    )
    small_size = gain_grads.shape[1]
    extra = jnp.pad(gain_grads, ((0, 0), (0, each - small_size))).reshape(
        dp // 2, 2, 1, ctx * each
    )
    extra = jnp.pad(extra, ((0, 0), (0, 0), (0, 7), (0, 0)))
    grad_qkv = weight_grad(normed, by_ctx.reshape(count, ctx * each), extra)
    grad_qkv = sum_of_ctx(grad_qkv.reshape(grad_qkv.shape[0], ctx, each).transpose(1, 0, 2))
    rows = width // dp
    gain_out = grad_qkv[rows, :small_size]
    grad_qkv = grad_qkv[:rows]
    q_cols, k_cols = heads * head_dim // ctx, head_dim // ctx
    outs, start = [], 0
    for size in sizes:
        outs.append(gain_out[start : start + size])
        start += size
    return (
        output,
        input_grad,
        grad_qkv[:, :q_cols],
        grad_qkv[:, q_cols : q_cols + k_cols],
        grad_qkv[:, q_cols + k_cols :],
        grad_out,
        grad_gate,
        grad_up,
        grad_down,
        *outs,
    )


def sum_of_ctx(blocks):
    size = lax.axis_size("ctx")
    mine = lax.axis_index("ctx")
    total = pick(blocks, mine).astype(jnp.float32)
    for k in range(1, size):
        got = shift(pick(blocks, (mine + k) % size).astype(jnp.bfloat16), k)
        total = total + got.astype(jnp.float32)
    return total


mega = 2**20


def place(name):
    return {"vmem": pl.BlockSpec(memory_space=pltpu.VMEM), "smem": pl.BlockSpec(memory_space=pltpu.SMEM), "any": pl.BlockSpec(memory_space=pl.ANY)}[name]


def kernel_call(body, outs, args, where=None, scratch=(), flops=0, size=0):
    where = where or {}
    return pl.pallas_call(
        body,
        out_shape=[jax.ShapeDtypeStruct(s, t) for s, t in outs],
        in_specs=[place(where.get(i, "vmem")) for i in range(len(args))],
        out_specs=[place("vmem") for _ in outs],
        scratch_shapes=list(scratch),
        compiler_params=pltpu.CompilerParams(vmem_limit_bytes=121 * mega // 2),
        cost_estimate=pl.CostEstimate(flops=flops, bytes_accessed=size, transcendentals=0),
    )(*args)


def norm_back(value, weight, grad):
    scale = lax.rsqrt(jnp.mean(value * value, axis=-1, keepdims=True) + epsilon)
    normed = value * scale
    weighted = grad * (1.0 + weight)
    value_grad = scale * (weighted - normed * jnp.mean(weighted * normed, axis=-1, keepdims=True))
    return value_grad, jnp.sum(grad * normed, axis=0, keepdims=True)


def spread(index, tails, lane, size, ctx):
    dp = len(tails)
    shards = jnp.concatenate([t[:, lane : lane + 128] for t, _ in tails], axis=0)
    tail = shards.shape[0] // dp
    whole = dp * ctx * size
    column = lax.broadcasted_iota(jnp.int32, (128, whole), 1)
    line = lax.broadcasted_iota(jnp.int32, (128, whole), 0)
    spots = jnp.where(column % size == line, 1.0, 0.0).astype(jnp.bfloat16)
    values = dot(shards, spots, 1, 0)
    column = lax.broadcasted_iota(jnp.int32, (tail, whole), 1) // size
    line = lax.broadcasted_iota(jnp.int32, (tail, whole), 0)
    total = jnp.zeros((tail, whole), jnp.float32)
    for k, (_, mask) in enumerate(tails):
        owner = jnp.where(line < ctx, (index ^ mask) * ctx + line, -1)
        total = total + jnp.where(column == owner, values[k * tail : (k + 1) * tail], 0.0)
    return jnp.sum(total, axis=0, keepdims=True)


def pack(w_query, w_key, w_value, w_out, gains):
    rows = w_query.shape[0]
    parts = [w_query, w_key, w_value, w_out]
    ends = [int(e) for e in np.cumsum([0] + [p.shape[1] for p in parts])]
    tall = -(-max(rows + 1, w_out.shape[0]) // 8) * 8

    def body(*rest):
        shards, lines = rest[: len(parts)], rest[len(parts) : len(parts) + len(gains)]
        out, wide = rest[-2], rest[-1]
        wide[...] = jnp.zeros(wide.shape, jnp.float32)
        for i, shard in enumerate(shards):
            wide[: shard.shape[0], ends[i] : ends[i + 1]] = shard[...].astype(jnp.float32)
        for i, line in enumerate(lines):
            wide[rows : rows + 1, i * 128 : i * 128 + line.shape[1]] = line[...].astype(
                jnp.float32
            )
        out[...] = wide[...].astype(jnp.bfloat16)

    return kernel_call(
        body,
        [((tall, ends[-1]), jnp.bfloat16)],
        [*parts, *[g.reshape(1, -1) for g in gains]],
        scratch=[pltpu.VMEM((tall, ends[-1]), jnp.float32)],
    )[0]


def tables(where, lengths, count, stretch, ctx, head_dim):
    seqs = lengths.shape[1]
    each, half = count // seqs, head_dim // 2
    span = 2 * ctx * stretch
    freqs = rope_base ** (-2.0 * np.arange(half, dtype=np.float64) / head_dim)
    freqs = jnp.asarray(freqs[None].astype(np.float32))

    def positions(index, owner):
        block, step = index // stretch % 2, index % stretch
        return jnp.where(block == 0, owner, 2 * ctx - 1 - owner) * stretch + step

    def body(where_ref, lengths_ref, freqs_ref, cos_out, sin_out, valid_out, allowed_out):
        mine = where_ref[4]
        rows = lax.broadcasted_iota(jnp.int32, (each, 1), 0)
        local = positions(rows, mine)
        angles = local.astype(jnp.float32) * freqs_ref[...]
        cos, sin = jnp.cos(angles), jnp.sin(angles)
        cols = lax.broadcasted_iota(jnp.int32, (1, span), 1)
        owner = (mine - cols // each + ctx) % ctx
        keys = positions(cols % each, owner)
        for s in range(seqs):
            part = slice(s * each, (s + 1) * each)
            for low, high in ((0, half), (half, head_dim)):
                cos_out[part, low:high] = cos
                sin_out[part, low:high] = sin
            length = lengths_ref[0, s]
            valid_out[part, :] = jnp.where(local < length, 1.0, 0.0)
            allowed_out[s] = jnp.where((keys <= local) & (keys < length), 1.0, 0.0)

    return kernel_call(
        body,
        [
            ((count, head_dim), jnp.float32),
            ((count, head_dim), jnp.float32),
            ((count, 1), jnp.float32),
            ((seqs, each, span), jnp.float32),
        ],
        [where, lengths, freqs],
        {0: "smem", 1: "smem"},
    )


def plane_near(value):
    return [value, swap(value, 1), swap(value, 2)]


def cut(near):
    row = near[0].ndim - 2
    first = halves_of(near[0].shape[row])[0]
    low = lax.slice_in_dim(near[1], 0, first, axis=row)
    high = lax.slice_in_dim(near[2], first, None, axis=row)
    return [low, high]


def diagonal(halves):
    return [swap(halves[0], 2), swap(halves[1], 1)]


def plane_whole(near):
    pieces = near + diagonal(cut(near))
    return pieces + [swap(p, 0) for p in pieces]


def late_gains(where, pieces, lanes, sizes, ctx, behind):
    tall = pieces[0].shape[0]

    def body(where_ref, behind_ref, *rest):
        parts, outs = rest[: len(pieces)], rest[len(pieces) :]
        tails = tails_of(parts, tall)
        for out, lane, size in zip(outs, lanes, sizes):
            out[...] = spread(where_ref[0], tails, lane, size, ctx)

    return kernel_call(
        body,
        [((1, len(tails_of([np.zeros((tall, 1))] * len(pieces), tall)) * ctx * size), jnp.float32) for size in sizes],
        [where, behind, *pieces],
        {0: "smem", 1: "any"},
    )


def project(where, tokens, pieces, sizes, cosine, sine, heads, ctx):
    count, width = tokens.shape
    tall = pieces[0].shape[0]
    head_dim = cosine.shape[1]
    wide = (heads + 2) * head_dim
    total = len(pieces)

    def body(where_ref, x_ref, cos_ref, sin_ref, *rest):
        parts = rest[:total]
        normed_ref, query_out, both_out, raw_out, in_ref, query_ref, key_ref = rest[total : total + 7]
        weight, ends, sems, end_sems = rest[total + 7 :]
        copies = load_columns(where_ref[0], parts, tall, tall - 16, 0, weight, sems)
        tails = [
            (ref, mask, rows) for ref, mask, at, rows in pieces_of(parts, tall) if at + rows == tall
        ]
        end_copies = [
            pltpu.make_async_copy(
                ref.at[pl.ds(rows - 16, 16), pl.ds(0, ends.shape[2])], ends.at[i], end_sems.at[i]
            )
            for i, (ref, _, rows) in enumerate(tails)
        ]
        for copy in end_copies:
            copy.start()
        for copy in end_copies:
            copy.wait()
        tails = [(ends[i], mask) for i, (_, mask, _) in enumerate(tails)]
        for i, ref in enumerate((in_ref, query_ref, key_ref)):
            ref[...] = spread(where_ref[0], tails, i * 128, sizes[i], ctx)
        normed = rms_norm(x_ref[...].astype(jnp.float32), in_ref[...]).astype(jnp.bfloat16)
        normed_ref[...] = normed
        cos, sin = cos_ref[...], sin_ref[...]
        for copy in copies:
            copy.wait()
        for h in range(heads + 1):
            cols = slice(h * head_dim, (h + 1) * head_dim)
            raw = dot(normed, weight[:, cols], 1, 0)
            raw_out[:, cols] = raw
            gain = query_ref[...] if h < heads else key_ref[...]
            turned = rotate(rms_norm(raw, gain), cos, sin).astype(jnp.bfloat16)
            if h < heads:
                query_out[:, cols] = turned
            else:
                both_out[:, :head_dim] = turned
        both_out[:, head_dim:] = dot(normed, weight[:, (heads + 1) * head_dim :], 1, 0).astype(
            jnp.bfloat16
        )

    return kernel_call(
        body,
        [
            ((count, width), jnp.bfloat16),
            ((count, heads * head_dim), jnp.bfloat16),
            ((count, 2 * head_dim), jnp.bfloat16),
            ((count, (heads + 1) * head_dim), jnp.float32),
            ((1, width), jnp.float32),
            ((1, head_dim), jnp.float32),
            ((1, head_dim), jnp.float32),
        ],
        [where, tokens, cosine, sine, *pieces],
        {0: "smem", **{4 + i: "any" for i in range(total)}},
        [
            pltpu.VMEM((width, wide), jnp.bfloat16),
            pltpu.VMEM((8, 16, 384), jnp.bfloat16),
            pltpu.SemaphoreType.DMA((total,)),
            pltpu.SemaphoreType.DMA((8,)),
        ],
    )


def attend(
    where, tokens, query, both, allowed, valid, norm_attn, norm_pre, pieces, out_rows, heads
):
    count, width = tokens.shape
    seqs, each, span = allowed.shape
    head_dim = query.shape[1] // heads
    inv_root = head_dim ** (-0.5)
    near, total = len(both), len(pieces)
    tall, wide = pieces[0].shape

    def body(where_ref, x_ref, query_ref, allowed_ref, valid_ref, attn_ref, pre_ref, *rest):
        got, parts = rest[:near], rest[near : near + total]
        probs_out, mixed_out, raw_out, after_out, two_out, weight, sems = rest[near + total :]
        copies = load_columns(where_ref[0], parts, tall, out_rows, wide - width, weight, sems)
        for s in range(seqs):
            rows = slice(s * each, (s + 1) * each)
            queries = jnp.concatenate(
                [query_ref[rows, h * head_dim : (h + 1) * head_dim] for h in range(heads)], axis=0
            )
            keys = jnp.concatenate([g[rows, :head_dim] for g in got], axis=0)
            values = jnp.concatenate([g[rows, head_dim:] for g in got], axis=0)
            scores = dot(queries, keys, 1, 1) * inv_root
            keep = jnp.concatenate([allowed_ref[s]] * heads, axis=0)
            scores = jnp.where(keep > 0.0, scores, -1e30)
            expo = jnp.exp(scores - jnp.max(scores, axis=-1, keepdims=True))
            probs = expo / jnp.sum(expo, axis=-1, keepdims=True)
            probs_out[s] = probs
            mixed = dot(probs.astype(jnp.bfloat16), values, 1, 0).astype(jnp.bfloat16)
            for h in range(heads):
                mixed_out[rows, h * head_dim : (h + 1) * head_dim] = mixed[
                    h * each : (h + 1) * each
                ]
        for copy in copies:
            copy.wait()
        raw = dot(mixed_out[...], weight[...], 1, 0)
        raw_out[...] = raw
        after = x_ref[...].astype(jnp.float32) + valid_ref[...] * rms_norm(raw, attn_ref[...])
        after_out[...] = after
        two_out[...] = rms_norm(after, pre_ref[...]).astype(jnp.bfloat16)

    return kernel_call(
        body,
        [
            ((seqs, heads * each, span), jnp.float32),
            ((count, heads * head_dim), jnp.bfloat16),
            ((count, width), jnp.float32),
            ((count, width), jnp.float32),
            ((count, width), jnp.bfloat16),
        ],
        [where, tokens, query, allowed, valid, norm_attn, norm_pre, *both, *pieces],
        {0: "smem", **{7 + near + i: "any" for i in range(total)}},
        [
            pltpu.VMEM((heads * head_dim, width), jnp.bfloat16),
            pltpu.SemaphoreType.DMA((total,)),
        ],
    )


def column_steps(size, step):
    return [(s, min(size, s + step)) for s in range(0, size, step)]


def halves_of(rows):
    first = -(-rows // 32) * 16
    return first, rows - first


def pieces_of(refs, chunk):
    parts, far = refs[: len(refs) // 2], refs[len(refs) // 2 :]
    first, second = halves_of(chunk)
    shapes = [(0, 0, chunk), (2, 0, chunk), (4, 0, chunk), (6, 0, first), (6, first, second)]
    return [(ref, mask, at, rows) for ref, (mask, at, rows) in zip(parts, shapes)] + [
        (ref, mask ^ 1, at, rows) for ref, (mask, at, rows) in zip(far, shapes)
    ]


def load_weights(index, refs, chunk, target, sems):
    def copies(m):
        result = []
        for i, (ref, mask, at, rows) in enumerate(pieces_of(refs, chunk)):
            start = pl.multiple_of((index ^ mask) * chunk + at, 16)
            result.append(
                pltpu.make_async_copy(ref.at[m], target.at[m, pl.ds(start, rows)], sems.at[m, i])
            )
        return result

    return [copies(m) for m in range(target.shape[0])]


def load_columns(index, refs, tall, rows, first, target, sems):
    copies = []
    for i, (ref, mask, at, size) in enumerate(pieces_of(refs, tall)):
        size = min(size, rows - at)
        if size > 0:
            start = pl.multiple_of((index ^ mask) * rows + at, 16)
            copies.append(
                pltpu.make_async_copy(
                    ref.at[pl.ds(0, size), pl.ds(first, target.shape[1])],
                    target.at[pl.ds(start, size)],
                    sems.at[i],
                )
            )
    for copy in copies:
        copy.start()
    return copies


def tails_of(refs, tall):
    return [
        (ref[rows - 16 : rows], mask) for ref, mask, at, rows in pieces_of(refs, tall) if at + rows == tall
    ]


def feed_forward(where, pieces, weights):
    count, width = pieces[0].shape
    kinds, chunk, inner = weights[0].shape
    lanes = -(-inner // 128) * 128
    near, spots = len(pieces), len(weights)
    total, early = near * count, (near - 1) * count
    slope = (2.0 / np.pi) ** 0.5

    def body(where_ref, *rest):
        shards, rest = rest[:spots], rest[spots:]
        parts = rest[:near]
        group_out, act_out, *slopes = rest[near : near + 6]
        sums = rest[near + 6 : near + 6 + near]
        weight, sems = rest[near + 6 + near :]
        copies = load_weights(where_ref[0], shards, chunk, weight, sems)
        for kind in copies:
            for copy in kind:
                copy.start()
        for k in range(near):
            group_out[k * count : (k + 1) * count, :] = parts[k][...]
        for kind in copies[:2]:
            for copy in kind:
                copy.wait()
        for low, high in column_steps(inner, 256):
            gate = dot(group_out[...], weight[0, :, low:high], 1, 0)
            upper = dot(group_out[...], weight[1, :, low:high], 1, 0)
            bent = jnp.tanh(slope * (gate + 0.044715 * (gate * gate * gate)))
            half = 0.5 * (1.0 + bent)
            gelu = gate * half
            steep = half + 0.5 * gate * (1.0 - bent * bent) * (
                slope * (1.0 + 3.0 * 0.044715 * gate * gate)
            )
            act_out[:, low:high] = (gelu * upper).astype(jnp.bfloat16)
            for value, outs in ((steep * upper, slopes[:2]), (gelu, slopes[2:])):
                outs[0][:, low:high] = value[:early].astype(jnp.bfloat16)
                outs[1][:, low:high] = value[early:].astype(jnp.bfloat16)
        if lanes > inner:
            act_out[:, inner:] = jnp.zeros((total, lanes - inner), jnp.bfloat16)
        for copy in copies[2]:
            copy.wait()
        for low, high in column_steps(width, 384):
            part = dot(act_out[:, :inner], weight[2, low:high, :], 1, 1)
            for k in range(near):
                sums[k][:, low:high] = part[k * count : (k + 1) * count].astype(sums[k].dtype)

    return kernel_call(
        body,
        [((total, width), jnp.bfloat16)]
        + [((total, lanes), jnp.bfloat16)]
        + [((early, inner), jnp.bfloat16), ((count, inner), jnp.bfloat16)] * 2
        + [((count, width), jnp.float32)]
        + [((count, width), jnp.bfloat16)] * (near - 1),
        [where, *weights, *pieces],
        {0: "smem", **{1 + i: "any" for i in range(spots)}},
        [
            pltpu.VMEM((kinds, width, inner), jnp.bfloat16),
            pltpu.SemaphoreType.DMA((kinds, spots)),
        ],
    )


def finish(parts, after, cotangent, valid, norm_post):
    count, width = after.shape
    near = len(parts)

    def body(after_ref, cot_ref, valid_ref, post_ref, *rest):
        got = rest[:near]
        output_out, grad_out, gain_out = rest[near:]
        raw = got[0][...]
        for g in got[1:]:
            raw = raw + g[...].astype(jnp.float32)
        ok = valid_ref[...]
        output_out[...] = (after_ref[...] + ok * rms_norm(raw, post_ref[...])).astype(jnp.bfloat16)
        grad, gain = norm_back(raw, post_ref[...], ok * cot_ref[...].astype(jnp.float32))
        grad_out[...] = grad.astype(jnp.bfloat16)
        gain_out[...] = gain

    return kernel_call(
        body,
        [
            ((count, width), jnp.bfloat16),
            ((count, width), jnp.bfloat16),
            ((1, width), jnp.float32),
        ],
        [after, cotangent, valid, norm_post, *parts],
    )


def feed_back(where, pieces, weights, one, two, with_own):
    count, width = pieces[0].shape
    kinds, chunk, inner = weights[0].shape
    lanes = -(-inner // 128) * 128
    near, spots = len(pieces), len(weights)
    total = near * count

    def body(where_ref, one_ref, two_ref, *rest):
        shards, rest = rest[:spots], rest[spots:]
        parts = rest[:near]
        group_out, both_out = rest[near : near + 2]
        sums = rest[near + 2 : near + 2 + near]
        weight, sems = rest[near + 2 + near :]
        copies = load_weights(where_ref[0], shards, chunk, weight, sems)
        for kind in (copies[2], copies[0], copies[1]):
            for copy in kind:
                copy.start()
        for k in range(near):
            group_out[k * count : (k + 1) * count, :] = parts[k][...]
        for copy in copies[2]:
            copy.wait()
        for low, high in column_steps(inner, 256):
            grad = dot(group_out[...], weight[2, :, low:high], 1, 0)
            for i, ref in enumerate((one_ref, two_ref)):
                both_out[i, :, low:high] = (grad * ref[:, low:high].astype(jnp.float32)).astype(
                    jnp.bfloat16
                )
        if lanes > inner:
            both_out[:, :, inner:] = jnp.zeros((2, total, lanes - inner), jnp.bfloat16)
        for kind in copies[:2]:
            for copy in kind:
                copy.wait()
        for low, high in column_steps(width, 384):
            part = dot(both_out[0, :, :inner], weight[0, low:high, :], 1, 1)
            part = part + dot(both_out[1, :, :inner], weight[1, low:high, :], 1, 1)
            for k in range(near):
                sums[k][:, low:high] = part[k * count : (k + 1) * count].astype(sums[k].dtype)

    return kernel_call(
        body,
        [((total, width), jnp.bfloat16)]
        + [((2, total, lanes), jnp.bfloat16)]
        + [((count, width), jnp.float32 if with_own and k == 0 else jnp.bfloat16) for k in range(near)],
        [where, one, two, *weights, *pieces],
        {0: "smem", **{3 + i: "any" for i in range(spots)}},
        [
            pltpu.VMEM((kinds, width, inner), jnp.bfloat16),
            pltpu.SemaphoreType.DMA((kinds, spots)),
        ],
    )


def wide_grads(where, two, two_far, back, back_far, act, act_far, both, both_far):
    total, width = two.shape
    inner = act.shape[1]
    chunk = width // 8
    first, second = halves_of(chunk)

    cuts = [(0, back[0].shape[0]), (back[0].shape[0], total)]

    def body(where_ref, *rest):
        twos, backs, acts, boths = rest[0:2], rest[2:6], rest[6:8], rest[8:12]
        outs = rest[12:16]
        turned, left = rest[16:]
        core, x, y = where_ref[1], where_ref[2], where_ref[3]
        order = []
        for flip in (1, 0):
            order.append([(j * 2 + jnp.bitwise_xor(x, flip), 0, first) for j in range(2)])
        for flip in (1, 0):
            order.append([(jnp.bitwise_xor(y, flip) * 2 + j, first, second) for j in range(2)])
        for index, kinds in ((0, (0, 1)), (1, (2,))):
            for side in range(2):
                if index == 0:
                    turned[:, side * total : (side + 1) * total] = twos[side][...].T
                else:
                    for i, (start, end) in enumerate(cuts):
                        turned[:, side * total + start : side * total + end] = backs[
                            2 * side + i
                        ][...].T
            at = 0
            for block in order:
                for plane, offset, size in block:
                    start = pl.multiple_of((plane * 2 + core) * chunk + offset, 16)
                    left[at : at + size, :] = turned[pl.ds(start, size), :]
                    at += size
            for m in kinds:
                for low, high in column_steps(inner, 256):
                    if m == 2:
                        rights = [acts[0][:, low:high], acts[1][:, low:high]]
                    else:
                        rights = [b[m, :, low:high] for b in boths]
                    right = jnp.concatenate(rights, axis=0)
                    part = dot(left[...], right, 1, 0)
                    part = part.astype(jnp.bfloat16)
                    at = 0
                    for out, block in zip(outs, order):
                        size = 2 * block[0][2]
                        out[m, :, low:high] = part[at : at + size]
                        at += size

    return kernel_call(
        body,
        [
            ((3, 2 * first, inner), jnp.bfloat16),
            ((3, 2 * first, inner), jnp.bfloat16),
            ((3, 2 * second, inner), jnp.bfloat16),
            ((3, 2 * second, inner), jnp.bfloat16),
        ],
        [where, two, two_far, *back, *back_far, act, act_far, *both, *both_far],
        {0: "smem"},
        [
            pltpu.VMEM((width, 2 * total), jnp.bfloat16),
            pltpu.VMEM((width // 2, 2 * total), jnp.bfloat16),
        ],
    )


def wide_middle(where, kept_a, got_a, kept_b, got_b):
    kinds, twice_a, inner = kept_a.shape
    first, second = twice_a // 2, kept_b.shape[1] // 2

    def body(where_ref, kept_a_ref, got_a_ref, kept_b_ref, got_b_ref, *outs):
        x, y = where_ref[2], where_ref[3]
        for m in range(kinds):
            for flip, out in ((1, outs[0]), (0, outs[1])):
                rows = pl.ds(pl.multiple_of(jnp.bitwise_xor(y, flip) * first, 16), first)
                total = kept_a_ref[m, rows, :].astype(jnp.float32) + got_a_ref[m, rows, :].astype(
                    jnp.float32
                )
                out[m] = total.astype(jnp.bfloat16)
            for flip, out in ((1, outs[2]), (0, outs[3])):
                rows = pl.ds(pl.multiple_of(jnp.bitwise_xor(x, flip) * second, 16), second)
                total = kept_b_ref[m, rows, :].astype(jnp.float32) + got_b_ref[m, rows, :].astype(
                    jnp.float32
                )
                out[m] = total.astype(jnp.bfloat16)

    return kernel_call(
        body,
        [
            ((kinds, first, inner), jnp.bfloat16),
            ((kinds, first, inner), jnp.bfloat16),
            ((kinds, second, inner), jnp.bfloat16),
            ((kinds, second, inner), jnp.bfloat16),
        ],
        [where, kept_a, got_a, kept_b, got_b],
        {0: "smem"},
    )


def wide_last(kept_a, got_a, kept_b, got_b, inner):
    kinds, first, _ = kept_a.shape
    second = kept_b.shape[1]

    def body(kept_a_ref, got_a_ref, kept_b_ref, got_b_ref, *outs):
        for m in range(kinds):
            total = kept_a_ref[m].astype(jnp.float32) + got_a_ref[m].astype(jnp.float32)
            outs[m][:first, :] = total[:, :inner]
            total = kept_b_ref[m].astype(jnp.float32) + got_b_ref[m].astype(jnp.float32)
            outs[m][first:, :] = total[:, :inner]

    return kernel_call(
        body,
        [((first + second, inner), jnp.float32)] * kinds,
        [kept_a, got_a, kept_b, got_b],
    )


def attend_back(
    where,
    parts,
    after,
    cotangent,
    valid,
    attn_raw,
    norm_pre,
    norm_attn,
    norm_query,
    probs,
    query,
    raw,
    both,
    pieces,
    out_rows,
    cosine,
    sine,
    heads,
):
    count, width = after.shape
    seqs, _, span = probs.shape
    each = count // seqs
    head_dim = norm_query.shape[1]
    inv_root = head_dim ** (-0.5)
    near, spots = len(both), len(pieces)
    tall, wide = pieces[0].shape

    def body(
        where_ref,
        after_ref,
        cot_ref,
        valid_ref,
        attn_ref,
        pre_ref,
        norm_ref,
        query_gain_ref,
        probs_ref,
        query_ref,
        raw_ref,
        cos_ref,
        sin_ref,
        *rest,
    ):
        shards, rest = rest[:spots], rest[spots:]
        sums = rest[:near]
        got = rest[near : 2 * near]
        rest = rest[2 * near :]
        dx_out, attn_grad_out, raw_grad_out, pre_out, attn_gain_out, query_gain_out = rest[:6]
        both_outs = rest[6 : 6 + near]
        mixed_grad, query_grad, weight, sems = rest[6 + near :]
        copies = load_columns(where_ref[0], shards, tall, out_rows, wide - width, weight, sems)
        grad = sums[0][...]
        for s in sums[1:]:
            grad = grad + s[...].astype(jnp.float32)
        through, gain = norm_back(after_ref[...], pre_ref[...], grad)
        pre_out[...] = gain
        dx = cot_ref[...].astype(jnp.float32) + through
        dx_out[...] = dx
        attn_grad, gain = norm_back(attn_ref[...], norm_ref[...], valid_ref[...] * dx)
        attn_gain_out[...] = gain
        attn_grad = attn_grad.astype(jnp.bfloat16)
        attn_grad_out[...] = attn_grad
        for copy in copies:
            copy.wait()
        mixed_grad[...] = dot(attn_grad, weight[...], 1, 1).astype(jnp.bfloat16)
        for s in range(seqs):
            rows = slice(s * each, (s + 1) * each)
            queries = jnp.concatenate(
                [query_ref[rows, h * head_dim : (h + 1) * head_dim] for h in range(heads)], axis=0
            )
            grads = jnp.concatenate(
                [mixed_grad[rows, h * head_dim : (h + 1) * head_dim] for h in range(heads)], axis=0
            )
            keys = jnp.concatenate([g[rows, :head_dim] for g in got], axis=0)
            values = jnp.concatenate([g[rows, head_dim:] for g in got], axis=0)
            probs = probs_ref[s]
            prob_grad = dot(grads, values, 1, 1)
            row = jnp.sum(probs * prob_grad, axis=-1, keepdims=True)
            score_grad = (probs * (prob_grad - row)).astype(jnp.bfloat16)
            back = dot(score_grad, keys, 1, 0) * inv_root
            for h in range(heads):
                query_grad[rows, h * head_dim : (h + 1) * head_dim] = back[
                    h * each : (h + 1) * each
                ]
            keys_grad = dot(score_grad, queries, 0, 0) * inv_root
            values_grad = dot(probs.astype(jnp.bfloat16), grads, 0, 0)
            for k in range(near):
                part = slice(k * each, (k + 1) * each)
                both_outs[k][rows, :head_dim] = keys_grad[part].astype(both_outs[k].dtype)
                both_outs[k][rows, head_dim:] = values_grad[part].astype(both_outs[k].dtype)
        cos, sin = cos_ref[...], sin_ref[...]
        gain_sum = jnp.zeros((1, head_dim), jnp.float32)
        for h in range(heads):
            cols = slice(h * head_dim, (h + 1) * head_dim)
            turned = rotate_back(query_grad[:, cols], cos, sin)
            value_grad, gain = norm_back(raw_ref[:, cols], query_gain_ref[...], turned)
            raw_grad_out[:, cols] = value_grad.astype(jnp.bfloat16)
            gain_sum = gain_sum + gain
        query_gain_out[...] = gain_sum

    return kernel_call(
        body,
        [
            ((count, width), jnp.float32),
            ((count, width), jnp.bfloat16),
            ((count, heads * head_dim), jnp.bfloat16),
            ((1, width), jnp.float32),
            ((1, width), jnp.float32),
            ((1, head_dim), jnp.float32),
            ((count, 2 * head_dim), jnp.float32),
        ]
        + [((count, 2 * head_dim), jnp.bfloat16)] * (near - 1),
        [
            where,
            after,
            cotangent,
            valid,
            attn_raw,
            norm_pre,
            norm_attn,
            norm_query,
            probs,
            query,
            raw,
            cosine,
            sine,
            *pieces,
            *parts,
            *both,
        ],
        {0: "smem", **{13 + i: "any" for i in range(spots)}},
        [
            pltpu.VMEM((count, heads * head_dim), jnp.bfloat16),
            pltpu.VMEM((count, heads * head_dim), jnp.float32),
            pltpu.VMEM((heads * head_dim, width), jnp.bfloat16),
            pltpu.SemaphoreType.DMA((spots,)),
        ],
    )


def project_back(
    where,
    parts,
    raw,
    query_grad,
    tokens,
    dx,
    norm_in,
    norm_key,
    cosine,
    sine,
    pieces,
    heads,
    ctx,
    gains,
):
    count, width = tokens.shape
    tall_piece = pieces[0].shape[0]
    head_dim = norm_key.shape[1]
    wide = (heads + 2) * head_dim
    near, spots, total = len(parts), len(pieces), 8
    each = wide // ctx
    count_gains = len(gains)
    tall = count + 16

    def body(
        where_ref, raw_ref, query_ref, x_ref, dx_ref, in_ref, key_ref, cos_ref, sin_ref, *rest
    ):
        sums = rest[:near]
        shards = rest[near : near + spots]
        others = rest[near + spots : near + spots + count_gains]
        input_out = rest[near + spots + count_gains]
        outs = rest[near + spots + count_gains + 1 : near + spots + count_gains + 1 + ctx]
        weight, grads_out, gains_out, sems = rest[near + spots + count_gains + 1 + ctx :]
        copies = load_columns(
            where_ref[0], shards, tall_piece, tall_piece - 16, 0, weight, sems
        )
        grad = sums[0][...]
        for s in sums[1:]:
            grad = grad + s[...].astype(jnp.float32)
        turned = rotate_back(grad[:, :head_dim], cos_ref[...], sin_ref[...])
        key_grad, key_gain = norm_back(raw_ref[:, heads * head_dim :], key_ref[...], turned)
        grads_out[:, : heads * head_dim] = query_ref[...]
        grads_out[:, heads * head_dim : (heads + 1) * head_dim] = key_grad.astype(jnp.bfloat16)
        grads_out[:, (heads + 1) * head_dim :] = grad[:, head_dim:].astype(jnp.bfloat16)
        for copy in copies:
            copy.wait()
        back = dot(grads_out[...], weight[...], 1, 1)
        through, in_gain = norm_back(x_ref[...].astype(jnp.float32), in_ref[...], back)
        input_out[...] = (dx_ref[...] + through).astype(jnp.bfloat16)
        gains_out[...] = jnp.zeros((16, wide), jnp.float32)
        lane = 0
        for gain in (in_gain, others[0][...], key_gain, *[o[...] for o in others[1:]]):
            size = gain.shape[1] // (total * ctx)
            for d in range(total):
                for c in range(ctx):
                    at = c * each + lane
                    gains_out[d : d + 1, at : at + size] = gain[
                        :, (d * ctx + c) * size : (d * ctx + c + 1) * size
                    ]
            lane += size
        spans = [(0, heads * head_dim), (heads * head_dim, head_dim), ((heads + 1) * head_dim, head_dim)]
        mine = where_ref[4]
        for c in range(ctx):

            @pl.when(mine == c)
            def _(c=c):
                for k in range(ctx):
                    j, at = (c + k) % ctx, 0
                    for first, size in spans:
                        step = size // ctx
                        outs[k][:count, at : at + step] = grads_out[
                            :, first + j * step : first + (j + 1) * step
                        ]
                        at += step
                    outs[k][count:, :] = gains_out[:, j * each : (j + 1) * each].astype(
                        jnp.bfloat16
                    )

    return kernel_call(
        body,
        [((count, width), jnp.bfloat16)] + [((tall, each), jnp.bfloat16)] * ctx,
        [
            where,
            raw,
            query_grad,
            tokens,
            dx,
            norm_in,
            norm_key,
            cosine,
            sine,
            *parts,
            *pieces,
            *gains,
        ],
        {0: "smem", **{9 + near + i: "any" for i in range(spots)}},
        [
            pltpu.VMEM((width, wide), jnp.bfloat16),
            pltpu.VMEM((count, wide), jnp.bfloat16),
            pltpu.VMEM((16, wide), jnp.float32),
            pltpu.SemaphoreType.DMA((spots,)),
        ],
    )


def narrow_grads(where, lefts, rights, with_gains):
    count, width = lefts[0].shape
    wide = rights[0].shape[1]
    chunk, near = width // 8, len(lefts)
    total = near * count
    tall = chunk + 16 if with_gains else chunk

    def body(where_ref, *rest):
        left_refs, right_refs, outs = rest[:near], rest[near : 2 * near], rest[2 * near : -3]
        turned, lines, values = rest[-3:]
        for i in range(near):
            turned[:, i * count : (i + 1) * count] = left_refs[i][...].T
            values[i * count : (i + 1) * count, :] = right_refs[i][:count, :]
        plane, core = where_ref[0] // 2, where_ref[1]
        for m in range(4):
            start = pl.multiple_of((jnp.bitwise_xor(plane, m) * 2 + core) * chunk, 16)
            lines[m * chunk : (m + 1) * chunk, :] = turned[pl.ds(start, chunk), :]
        for low, high in column_steps(wide, 256):
            part = dot(lines[...], values[:, low:high], 1, 0)
            for m in range(4):
                outs[m][:chunk, low:high] = part[m * chunk : (m + 1) * chunk].astype(outs[m].dtype)
        if with_gains:
            whole = right_refs[0][count:, :].astype(jnp.float32)
            for r in right_refs[1:]:
                whole = whole + r[count:, :].astype(jnp.float32)
            index = lax.broadcasted_iota(jnp.int32, whole.shape, 0)
            for m in range(4):
                row = jnp.bitwise_xor(plane, m) * 2 + core
                row = jnp.sum(jnp.where(index == row, whole, 0.0), axis=0, keepdims=True)
                outs[m][chunk:, :] = jnp.where(index == 0, row, 0.0).astype(outs[m].dtype)

    return kernel_call(
        body,
        [((tall, wide), jnp.float32)] + [((tall, wide), jnp.bfloat16)] * 3,
        [where, *lefts, *rights],
        {0: "smem"},
        [
            pltpu.VMEM((width, total), jnp.bfloat16),
            pltpu.VMEM((width // 2, total), jnp.bfloat16),
            pltpu.VMEM((total, wide), jnp.bfloat16),
        ],
    )


def narrow_middle(where, parts, sizes, ctx):
    chunk, wide = parts[0].shape
    each = wide // ctx

    def body(where_ref, *rest):
        got = rest[: len(parts)]
        outs = rest[len(parts) :]
        mine = where_ref[4]
        total = got[0][...]
        for g in got[1:]:
            total = total + g[...].astype(jnp.float32)
        for c in range(ctx):

            @pl.when(mine == c)
            def _(c=c):
                for k in range(ctx):
                    j = (c + k) % ctx
                    start, at = 0, 0
                    for size in sizes:
                        piece = size // ctx
                        outs[k][:, at : at + piece] = total[
                            :, start + j * piece : start + (j + 1) * piece
                        ].astype(outs[k].dtype)
                        start += size
                        at += piece

    return kernel_call(
        body,
        [((chunk, each), jnp.float32)] + [((chunk, each), jnp.bfloat16)] * (ctx - 1),
        [where, *parts],
        {0: "smem"},
    )


def split_wide(where, gate, up, down, ctx):
    rows, whole = gate.shape
    inner = whole // ctx
    groups, chunk, part = down.shape
    per, steps = groups // ctx, chunk // rows

    def body(where_ref, gate_ref, up_ref, down_ref, *rest):
        outs, wide = rest[:ctx], rest[ctx]
        mine = where_ref[4]
        for c in range(ctx):

            @pl.when(mine == c)
            def _(c=c):
                for k in range(ctx):
                    j = (c + k) % ctx
                    outs[k][0] = gate_ref[:, j * inner : (j + 1) * inner]
                    outs[k][1] = up_ref[:, j * inner : (j + 1) * inner]
                    for b in range(groups):
                        first = b % steps * rows
                        wide[:, b * part : (b + 1) * part] = down_ref[
                            j * per + b // steps, first : first + rows, :
                        ].astype(jnp.float32)
                    outs[k][2] = wide[...].astype(jnp.bfloat16)

    return kernel_call(
        body,
        [((3, rows, inner), jnp.bfloat16)] * ctx,
        [where, gate, up, down],
        {0: "smem"},
        [pltpu.VMEM((rows, inner), jnp.float32)],
    )


def join_wide(where, pieces, part):
    ctx = len(pieces)
    _, rows, inner = pieces[0].shape
    chunk, groups = ctx * rows, inner // part

    def body(where_ref, *rest):
        got, out, wide = rest[:ctx], rest[ctx], rest[ctx + 1]
        mine = where_ref[4]
        for c in range(ctx):

            @pl.when(mine == c)
            def _(c=c):
                for m in range(2):
                    for a in range(ctx):
                        wide[a * rows : (a + 1) * rows, :] = got[(c - a) % ctx][m].astype(
                            jnp.float32
                        )
                    out[m] = wide[...].astype(jnp.bfloat16)
                for a in range(ctx):
                    piece = got[(c - a) % ctx][2].astype(jnp.float32)
                    for b in range(groups):
                        first = b % ctx * rows
                        at = (b // ctx * ctx + a) * part
                        wide[first : first + rows, at : at + part] = piece[
                            :, b * part : (b + 1) * part
                        ]
                out[2] = wide[...].astype(jnp.bfloat16)

    return kernel_call(
        body,
        [((3, chunk, inner), jnp.bfloat16)],
        [where, *pieces],
        {0: "smem"},
        [pltpu.VMEM((chunk, inner), jnp.float32)],
    )[0]


def join_rows(where, pieces, rows, split, out_rows):
    ctx = len(pieces)
    _, wide = pieces[0].shape
    tall = ctx * rows + 16

    def body(where_ref, *rest):
        got, out, lines = rest[:ctx], rest[ctx], rest[ctx + 1]
        mine = where_ref[4]
        lines[ctx * rows :, :] = jnp.zeros((16, wide), jnp.float32)
        lines[ctx * out_rows :, split:] = jnp.zeros((tall - ctx * out_rows, wide - split), jnp.float32)
        for c in range(ctx):

            @pl.when(mine == c)
            def _(c=c):
                for a in range(ctx):
                    piece = got[(c - a) % ctx]
                    lines[a * rows : (a + 1) * rows, :split] = piece[:rows, :split].astype(
                        jnp.float32
                    )
                    lines[a * out_rows : (a + 1) * out_rows, split:] = piece[
                        :out_rows, split:
                    ].astype(jnp.float32)
                    at = ctx * rows + a
                    lines[at : at + 1, :split] = piece[rows : rows + 1, :split].astype(jnp.float32)
                out[...] = lines[...].astype(jnp.bfloat16)

    return kernel_call(
        body,
        [((tall, wide), jnp.bfloat16)],
        [where, *pieces],
        {0: "smem"},
        [pltpu.VMEM((tall, wide), jnp.float32)],
    )[0]


def plane_send(parts):
    size = lax.axis_size("dp")
    return [parts[0]] + [
        lax.ppermute(parts[m], "dp", [(i, i ^ (2 * m)) for i in range(size)])
        for m in range(1, len(parts))
    ]


def ctx_send(parts, sign):
    return [parts[0]] + [shift(parts[k], sign * k) for k in range(1, len(parts))]


def stage(*values):
    return lax.optimization_barrier(values)


def gate(value, *conditions):
    return lax.optimization_barrier((value, conditions))[0]


def fused(
    tokens,
    cotangent,
    lengths,
    w_query,
    w_key,
    w_value,
    w_out,
    w_gate,
    w_up,
    w_down,
    gain_in,
    gain_query,
    gain_key,
    gain_attn,
    gain_pre,
    gain_post,
):
    count, width = tokens.shape
    seq_count = lengths.shape[1]
    stretch = count // (2 * seq_count)
    dp = lax.axis_size("dp")
    ctx = lax.axis_size("ctx")
    mine = lax.axis_index("ctx")
    group = lax.axis_index("dp")
    head_dim = w_key.shape[1]
    heads = w_query.shape[1] // head_dim
    where = jnp.stack([group, group % 2, group // 2 % 2, group // 4, mine]).astype(jnp.int32)

    gains = [gain_in, gain_query, gain_key, gain_attn, gain_pre, gain_post]
    sizes = [g.shape[0] for g in gains]
    chunk, out_rows = width // dp, heads * head_dim // dp
    packed = pack(w_query, w_key, w_value, w_out, gains)
    split = packed.shape[1] - width
    downs = gate(w_down, packed).T.reshape(dp, chunk, w_down.shape[0])
    downs = lax.all_to_all(downs, "dp", split_axis=0, concat_axis=0, tiled=True)
    packed = ctx_gather(packed)
    aux = tables(where, lengths, count, stretch, ctx, head_dim)
    packed, downs, aux = stage(packed, downs, aux)
    cosine, sine, valid, allowed = aux

    blocks = list(split_wide(where, w_gate, w_up, downs.reshape(dp, chunk, -1), ctx))
    packed = gate(packed, blocks[0])
    blocks = ctx_send(blocks, 1)
    near = plane_near(join_rows(where, packed, w_query.shape[0], split, w_out.shape[0]))
    shared = plane_whole(near)
    shared, blocks = stage(shared, blocks)

    shard = join_wide(where, blocks, w_down.shape[0])
    normed, query, both, raw, norm_in, norm_query, norm_key = project(
        where, tokens, shared, sizes[:3], cosine, sine, heads, ctx
    )
    shard, normed, query, both = stage(shard, normed, query, both)

    shard = plane_near(shard)
    norm_attn, norm_pre, norm_post = late_gains(
        where, shared, [384, 512, 640], sizes[3:], ctx, both
    )
    both = ctx_gather(both)
    probs, mixed, attn_raw, residual, normed_two = attend(
        where,
        tokens,
        query,
        both,
        allowed,
        valid,
        norm_attn,
        norm_pre,
        shared,
        out_rows,
        heads,
    )
    far = [swap(gate(shard[0], both[2]), 0)]
    shard, far, halves, normed_two, mixed = stage(shard, far, cut(shard), normed_two, mixed)

    halves = diagonal(halves)
    two_pieces = ctx_gather(normed_two)
    two_pieces, halves, shard, normed = stage(two_pieces, halves, shard, normed)

    weights = shard + halves
    weights = weights + far + [swap(w, 0) for w in weights[1:]]
    two_pieces, weights, normed = stage(two_pieces, weights, normed)

    order = [0, 1, 3, 2]
    normed_group = [normed, shift(normed, 1), None, shift(normed, 3)]
    group_two, act, one, one_last, two, two_last, *sums = feed_forward(
        where, [two_pieces[k] for k in order], weights
    )
    group_two, act, one, one_last, two, two_last, sums, near_group = stage(
        group_two, act, one, one_last, two, two_last, sums, [normed_group[1], normed_group[3]]
    )
    normed_group[1], normed_group[3] = near_group

    sums = [sums[0]] + [shift(sums[i], -order[i]) for i in range(1, ctx)]
    group_two_far, act_far, mixed_far = swap(group_two, 0), swap(act, 0), swap(mixed, 0)
    sums, group_two_far, act_far, mixed_far = stage(sums, group_two_far, act_far, mixed_far)

    output, ffn_grad, gain_post_grad = finish(sums, residual, cotangent, valid, norm_post)
    ffn_pieces = ctx_gather(ffn_grad)
    ffn_early = [ffn_pieces[k] for k in order[:-1]]
    group_ffn, grads, *sums = feed_back(where, ffn_early, weights, one, two, True)
    ffn_last, group_ffn, grads, sums = stage(ffn_pieces[order[-1]], group_ffn, grads, sums)

    ffn_last, grads_last, sum_last = feed_back(
        where, [ffn_last], weights, one_last, two_last, False
    )
    sums[1] = shift(sums[1], -order[1])
    ffn_last, grads_last, sum_last, group_ffn, grads, sums = stage(
        ffn_last, grads_last, sum_last, group_ffn, grads, sums
    )

    sums[2] = shift(sums[2], -order[2])
    sums.append(shift(sum_last, -order[-1]))
    group_ffn, grads = [group_ffn, ffn_last], [grads, grads_last]
    group_ffn_far, grads_far = [swap(g, 0) for g in group_ffn], [swap(g, 0) for g in grads]
    send_a, kept_a, send_b, kept_b = wide_grads(
        where, group_two, group_two_far, group_ffn, group_ffn_far, act, act_far, grads, grads_far
    )
    sums, send_a, kept_a, send_b, kept_b = stage(sums, send_a, kept_a, send_b, kept_b)

    got_a, got_b = swap(send_a, 1), swap(send_b, 2)
    dx, attn_grad, query_grad, gain_pre_grad, gain_attn_grad, gain_query_grad, *parts = attend_back(
        where,
        sums,
        residual,
        cotangent,
        valid,
        attn_raw,
        norm_pre,
        norm_attn,
        norm_query,
        probs,
        query,
        raw,
        both,
        shared,
        out_rows,
        cosine,
        sine,
        heads,
    )
    parts = ctx_send(parts, -1)
    normed_group[2] = shift(gate(normed, parts), 2)
    out_blocks = narrow_grads(
        where, [attn_grad, swap(attn_grad, 0)], [mixed, mixed_far], False
    )
    parts = gate(parts, out_blocks)
    input_grad, *blocks = project_back(
        where,
        parts,
        raw,
        query_grad,
        tokens,
        dx,
        norm_in,
        norm_key,
        cosine,
        sine,
        shared,
        heads,
        ctx,
        [gain_query_grad, gain_attn_grad, gain_pre_grad, gain_post_grad],
    )
    out_blocks = plane_send(out_blocks)
    got_a, got_b, blocks, out_blocks, normed_group = stage(
        got_a, got_b, list(blocks), out_blocks, normed_group
    )

    blocks = ctx_send(blocks, 1)
    send_a, kept_a, send_b, kept_b = wide_middle(where, kept_a, got_a, kept_b, got_b)
    got_a, got_b = swap(send_a, 2), swap(send_b, 1)
    out_blocks = narrow_middle(where, out_blocks, [mixed.shape[1]], ctx)
    normed_far = [swap(n, 0) for n in normed_group]
    blocks = narrow_grads(
        where, normed_group + normed_far, blocks + [swap(b, 0) for b in blocks], True
    )
    got_a, got_b, out_blocks, blocks = stage(got_a, got_b, out_blocks, blocks)

    blocks, out_blocks = plane_send(blocks), ctx_send(out_blocks, 1)
    grad_gate, grad_up, grad_down = wide_last(
        kept_a, got_a, kept_b, got_b, w_gate.shape[1] // ctx
    )
    blocks, out_blocks, grad_gate = stage(blocks, out_blocks, grad_gate)

    def total(pieces):
        result = pieces[0].astype(jnp.float32)
        for p in pieces[1:]:
            result = result + p.astype(jnp.float32)
        return result

    grad_out = total(out_blocks).T
    grad_qkv = total(blocks)

    outs, start = [], 0
    for size in sizes:
        outs.append(grad_qkv[width // dp, start : start + size])
        start += size
    grad_qkv = grad_qkv[: width // dp]
    q_cols, k_cols = heads * head_dim // ctx, head_dim // ctx
    return (
        output,
        input_grad,
        grad_qkv[:, :q_cols],
        grad_qkv[:, q_cols : q_cols + k_cols],
        grad_qkv[:, q_cols + k_cols :],
        grad_out,
        grad_gate,
        grad_up,
        grad_down.T,
        *outs,
    )


def on_device(tokens, cotangent, lengths, *params):
    dp, ctx = lax.axis_size("dp"), lax.axis_size("ctx")
    each = tokens.shape[0] // lengths.shape[1]
    fits = dp == 8 and dp % ctx == 0 and tokens.shape[1] // dp % 16 == 0 and each % 16 == 0
    run = fused if fits else plain
    return run(tokens, cotangent, lengths, *params)


def solution(mesh):
    in_specs = (
        P(("dp", "ctx"), None),
        P(("dp", "ctx"), None),
        P("dp", None),
        P(("dp", "ctx"), None),
        P(("dp", "ctx"), None),
        P(("dp", "ctx"), None),
        P(("dp", "ctx"), None),
        P(("dp", "ctx"), None),
        P(("dp", "ctx"), None),
        P(("dp", "ctx"), None),
        P(("dp", "ctx")),
        P(("dp", "ctx")),
        P(("dp", "ctx")),
        P(("dp", "ctx")),
        P(("dp", "ctx")),
        P(("dp", "ctx")),
    )
    out_specs = (
        P(("dp", "ctx"), None),
        P(("dp", "ctx"), None),
        P("dp", "ctx"),
        P("dp", "ctx"),
        P("dp", "ctx"),
        P("ctx", "dp"),
        P("dp", "ctx"),
        P("dp", "ctx"),
        P("ctx", "dp"),
        P(("dp", "ctx")),
        P(("dp", "ctx")),
        P(("dp", "ctx")),
        P(("dp", "ctx")),
        P(("dp", "ctx")),
        P(("dp", "ctx")),
    )
    return jax.shard_map(
        on_device, mesh=mesh, in_specs=in_specs, out_specs=out_specs, check_vma=False
    )
```

```python
import jax
import jax.numpy as jnp
import numpy as np
from jax import lax
from jax.experimental import pallas as pl
from jax.experimental.pallas import tpu as pltpu
from jax.sharding import PartitionSpec as P

epsilon = 1e-06
rope_base = 1000000.0


def rms_norm(value, weight):
    scale = lax.rsqrt(jnp.mean(value * value, axis=-1, keepdims=True) + epsilon)
    return value * scale * (1.0 + weight)


def rms_back(value, weight, grad):
    scale = lax.rsqrt(jnp.mean(value * value, axis=-1, keepdims=True) + epsilon)
    normed = value * scale
    weighted = grad * (1.0 + weight)
    value_grad = scale * (weighted - normed * jnp.mean(weighted * normed, axis=-1, keepdims=True))
    weight_grad = jnp.sum(grad * normed, axis=tuple(range(value.ndim - 1)))
    return (value_grad, weight_grad)


def rope_tables(positions, width):
    half = width // 2
    freqs = jnp.power(rope_base, -2.0 * jnp.arange(half, dtype=jnp.float32) / width)
    angles = positions[:, None] * freqs[None, :]
    cosine = jnp.concatenate([jnp.cos(angles), jnp.cos(angles)], axis=-1)
    sine = jnp.concatenate([jnp.sin(angles), jnp.sin(angles)], axis=-1)
    return (cosine, sine)


def rotate(value, cosine, sine):
    half = value.shape[-1] // 2
    turned = jnp.concatenate([-value[..., half:], value[..., :half]], axis=-1)
    return value * cosine + turned * sine


def rotate_back(grad, cosine, sine):
    half = grad.shape[-1] // 2
    scaled = grad * sine
    return grad * cosine + jnp.concatenate([scaled[..., half:], -scaled[..., :half]], axis=-1)


def geglu(gate, upper):
    return jax.nn.gelu(gate, approximate=True) * upper


def dot(left, right, left_dim, right_dim):
    return lax.dot_general(
        left, right, (((left_dim,), (right_dim,)), ((), ())), preferred_element_type=jnp.float32
    )


def swap(value, bit):
    size = lax.axis_size("dp")
    return lax.ppermute(value, "dp", [(i, i ^ (1 << bit)) for i in range(size)])


def shift(value, step):
    size = lax.axis_size("ctx")
    return lax.ppermute(value, "ctx", [(i, (i + step) % size) for i in range(size)])


def pick(value, index, axis=0):
    return lax.dynamic_index_in_dim(value, index, axis, keepdims=False)


def plane_bits():
    return list(range(1, lax.axis_size("dp").bit_length() - 1))


def ctx_gather(value):
    return [value] + [shift(value, k) for k in range(1, lax.axis_size("ctx"))]


def ctx_ordered(pieces):
    size = lax.axis_size("ctx")
    stacked = jnp.stack(pieces)
    mine = lax.axis_index("ctx")
    return jnp.stack([pick(stacked, (mine - a + size) % size) for a in range(size)])


def ctx_reduce(pieces):
    total = pieces[0].astype(jnp.float32)
    for k in range(1, len(pieces)):
        total = total + shift(pieces[k].astype(jnp.bfloat16), -k).astype(jnp.float32)
    return total


def ctx_exchange(blocks):
    size = lax.axis_size("ctx")
    mine = lax.axis_index("ctx")
    return [pick(blocks, mine)] + [
        shift(pick(blocks, (mine + k) % size), k) for k in range(1, size)
    ]


def row_parts(rows, count):
    unit = 8 if rows % 8 == 0 else 1
    edges = [unit * (rows // unit * p // count) for p in range(count + 1)]
    return [(edges[p], edges[p + 1]) for p in range(count)]


def dp_gather(value):
    bits = plane_bits()
    plane = lax.axis_index("dp") // 2
    core = lax.axis_index("dp") % 2
    count = 1 << len(bits)
    parts = []
    for p, (low, high) in enumerate(row_parts(value.shape[0], len(bits))):
        current = value[None, low:high]
        masks = [0]
        for bit in bits[p:] + bits[:p]:
            current = jnp.concatenate([current, swap(current, bit)])
            masks = masks + [m ^ (1 << (bit - 1)) for m in masks]
        other = swap(current, 0)
        place = jnp.asarray([masks.index(m) for m in range(count)], jnp.int32)
        rows_of = []
        for a in range(count):
            at = pick(place, plane ^ a)
            first, second = pick(current, at), pick(other, at)
            rows_of.append(
                jnp.stack([lax.select(core == 0, first, second), lax.select(core == 0, second, first)])
            )
        parts.append(jnp.stack(rows_of))
    whole = jnp.concatenate(parts, axis=2)
    return whole.reshape((2 * count,) + value.shape)


def dp_reduce(kept, sent):
    bits = plane_bits()
    plane = lax.axis_index("dp") // 2
    total = (kept + swap(sent.astype(jnp.bfloat16), 0).astype(jnp.float32)).astype(jnp.bfloat16)
    parts = []
    for p, (low, high) in enumerate(row_parts(total.shape[1], len(bits))):
        current = total[:, low:high]
        current = current.reshape((2,) * len(bits) + current.shape[1:])
        left = sorted(bits, reverse=True)
        for bit in bits[p:] + bits[:p]:
            axis = left.index(bit)
            mine = (plane >> (bit - 1)) & 1
            got = swap(pick(current, 1 - mine, axis), bit)
            current = pick(current, mine, axis).astype(jnp.float32) + got.astype(jnp.float32)
            left.remove(bit)
            if left:
                current = current.astype(jnp.bfloat16)
        parts.append(current)
    return jnp.concatenate(parts, axis=0)


def columns_of(value, core):
    dp = lax.axis_size("dp")
    wide = value.reshape(value.shape[0], dp // 2, 2, value.shape[1] // dp)
    return pick(wide, core, 2).reshape(value.shape[0], -1)


def weight_grad(left, right, extra=None):
    core = lax.axis_index("dp") % 2
    dp = lax.axis_size("dp")
    blocks = []
    for side in (core, 1 - core):
        block = dot(columns_of(left, side), right, 0, 0)
        block = block.reshape(dp // 2, left.shape[1] // dp, right.shape[1])
        if extra is not None:
            block = jnp.concatenate([block, pick(extra, side, 1)], axis=1)
        blocks.append(block)
    return dp_reduce(blocks[0], blocks[1])


def plain(
    tokens,
    cotangent,
    lengths,
    w_query,
    w_key,
    w_value,
    w_out,
    w_gate,
    w_up,
    w_down,
    gain_in,
    gain_query,
    gain_key,
    gain_attn,
    gain_pre,
    gain_post,
):
    count, width = tokens.shape
    seq_count = lengths.shape[1]
    stretch = count // (2 * seq_count)
    dp = lax.axis_size("dp")
    ctx = lax.axis_size("ctx")
    mine = lax.axis_index("ctx")
    head_dim = w_key.shape[1]
    heads = w_query.shape[1] // head_dim
    inner = w_gate.shape[1] // ctx
    span = 2 * ctx * stretch
    offsets = jnp.arange(stretch, dtype=jnp.int32)

    def positions_of(index):
        return jnp.concatenate(
            [index * stretch + offsets, (2 * ctx - 1 - index) * stretch + offsets]
        )

    local_pos = positions_of(mine)
    valid = (local_pos[None, :] < lengths[0][:, None]).astype(jnp.float32).reshape(count, 1)
    cosine, sine = rope_tables(jnp.tile(local_pos, seq_count).astype(jnp.float32), head_dim)
    key_pos = jnp.concatenate([positions_of((mine - k + ctx) % ctx) for k in range(ctx)])
    query_pos = jnp.repeat(local_pos, heads)
    allowed = (key_pos[None, None, :] <= query_pos[None, :, None]) & (
        key_pos[None, None, :] < lengths[0][:, None, None]
    )
    inv_root = head_dim ** (-0.5)

    gains = [gain_in, gain_query, gain_key, gain_attn, gain_pre, gain_post]
    sizes = [g.shape[0] for g in gains]
    small = jnp.concatenate(gains)
    qkv_shard = jnp.concatenate([w_query, w_key, w_value], axis=1)
    in_rows, in_cols = qkv_shard.shape
    out_rows = w_out.shape[0]
    top = max(in_rows, out_rows)
    packed_rows = -(-(top + 1) // 8) * 8
    packed = jnp.concatenate(
        [
            jnp.pad(qkv_shard, ((0, top - in_rows), (0, 0))),
            jnp.pad(w_out, ((0, top - out_rows), (0, 0))),
        ],
        axis=1,
    )
    last = jnp.pad(small[None], ((0, packed_rows - top - 1), (0, packed.shape[1] - small.shape[0])))
    packed = jnp.concatenate([packed, last], axis=0)
    near = ctx_ordered(ctx_gather(packed)).reshape(ctx * packed_rows, -1)
    everything = dp_gather(near).reshape(dp * ctx, packed_rows, -1)
    full_qkv = everything[:, :in_rows, :in_cols].reshape(width, in_cols)
    full_out = everything[:, :out_rows, in_cols:].reshape(heads * head_dim, width)
    smalls = everything[:, top, : small.shape[0]]
    norms, start = [], 0
    for size in sizes:
        norms.append(smalls[:, start : start + size].reshape(-1).astype(jnp.float32))
        start += size
    norm_in, norm_query, norm_key, norm_attn, norm_pre, norm_post = norms

    def column_blocks(weight):
        return weight.reshape(weight.shape[0], ctx, inner).transpose(1, 0, 2)

    gate_up = jnp.stack([column_blocks(w_gate), column_blocks(w_up)], axis=1)
    gate_up = ctx_ordered(ctx_exchange(gate_up)).transpose(1, 0, 2, 3)
    gate_up = gate_up.reshape(2, width // dp, inner)
    per = dp // ctx
    down = w_down.T.reshape(dp, width // dp, w_down.shape[0])
    down = lax.all_to_all(down, "dp", split_axis=0, concat_axis=0, tiled=True)
    down = down.reshape(ctx, per, width // dp, w_down.shape[0])
    down = ctx_ordered(ctx_exchange(down))
    down = down.transpose(2, 1, 0, 3).reshape(width // dp, inner)
    full_gate = dp_gather(gate_up[0]).reshape(width, inner)
    full_up = dp_gather(gate_up[1]).reshape(width, inner)
    full_down = dp_gather(down).reshape(width, inner)

    hidden = tokens.astype(jnp.float32)
    normed = rms_norm(hidden, norm_in).astype(jnp.bfloat16)
    qkv_raw = dot(normed, full_qkv, 1, 0)
    query_raw = qkv_raw[:, : heads * head_dim]
    key_raw = qkv_raw[:, heads * head_dim : (heads + 1) * head_dim]
    value_raw = qkv_raw[:, (heads + 1) * head_dim :]
    query_heads = query_raw.reshape(count, heads, head_dim)
    query_bf = rotate(
        rms_norm(query_heads, norm_query), cosine[:, None, :], sine[:, None, :]
    ).astype(jnp.bfloat16)
    query_bf = query_bf.reshape(seq_count, 2 * stretch * heads, head_dim)
    key_bf = rotate(rms_norm(key_raw, norm_key), cosine, sine).astype(jnp.bfloat16)
    both = jnp.concatenate([key_bf, value_raw.astype(jnp.bfloat16)], axis=1)
    both = jnp.stack(
        [p.reshape(seq_count, 2 * stretch, 2 * head_dim) for p in ctx_gather(both)], axis=1
    ).reshape(seq_count, span, 2 * head_dim)
    keys, values = both[..., :head_dim], both[..., head_dim:]
    scores = (
        jnp.einsum("sqd,skd->sqk", query_bf, keys, preferred_element_type=jnp.float32) * inv_root
    )
    masked = jnp.where(allowed, scores, -1e30)
    peak = jnp.max(masked, axis=-1, keepdims=True)
    expo = jnp.exp(masked - peak)
    total = jnp.sum(expo, axis=-1, keepdims=True)
    probs = expo / total
    probs_bf = probs.astype(jnp.bfloat16)
    mixed = jnp.einsum("sqk,skd->sqd", probs_bf, values, preferred_element_type=jnp.float32)
    mixed_bf = mixed.astype(jnp.bfloat16).reshape(count, heads * head_dim)
    attn_raw = dot(mixed_bf, full_out, 1, 0)
    after_attn = hidden + valid * rms_norm(attn_raw, norm_attn)
    normed_two = rms_norm(after_attn, norm_pre).astype(jnp.bfloat16)

    group_two = jnp.concatenate(ctx_gather(normed_two))
    gate = dot(group_two, full_gate, 1, 0)
    upper = dot(group_two, full_up, 1, 0)
    inner_bf = geglu(gate, upper).astype(jnp.bfloat16)
    ffn_part = dot(inner_bf, full_down, 1, 1)
    ffn_raw = ctx_reduce(list(ffn_part.reshape(ctx, count, width)))
    output = (after_attn + valid * rms_norm(ffn_raw, norm_post)).astype(jnp.bfloat16)

    grad_top = cotangent.astype(jnp.float32)
    ffn_grad, grad_gain_post = rms_back(ffn_raw, norm_post, valid * grad_top)
    group_ffn = jnp.concatenate(ctx_gather(ffn_grad.astype(jnp.bfloat16)))
    inner_grad = dot(group_ffn, full_down, 1, 0)
    _, geglu_pull = jax.vjp(geglu, gate, upper)
    gate_grad, upper_grad = geglu_pull(inner_grad)
    gate_grad_bf = gate_grad.astype(jnp.bfloat16)
    upper_grad_bf = upper_grad.astype(jnp.bfloat16)
    two_part = dot(gate_grad_bf, full_gate, 1, 1) + dot(upper_grad_bf, full_up, 1, 1)
    normed_two_grad = ctx_reduce(list(two_part.reshape(ctx, count, width)))
    grad_down = weight_grad(group_ffn, inner_bf).T
    grad_gate = weight_grad(group_two, gate_grad_bf)
    grad_up = weight_grad(group_two, upper_grad_bf)

    through_pre, grad_gain_pre = rms_back(after_attn, norm_pre, normed_two_grad)
    after_grad = grad_top + through_pre
    attn_grad, grad_gain_attn = rms_back(attn_raw, norm_attn, valid * after_grad)
    attn_grad_bf = attn_grad.astype(jnp.bfloat16)
    grad_out = weight_grad(attn_grad_bf, mixed_bf)
    grad_out = sum_of_ctx(grad_out.reshape(grad_out.shape[0], ctx, -1).transpose(1, 0, 2)).T
    mixed_grad_bf = dot(attn_grad_bf, full_out, 1, 1).astype(jnp.bfloat16)
    mixed_grad_bf = mixed_grad_bf.reshape(seq_count, 2 * stretch * heads, head_dim)
    prob_grad = jnp.einsum(
        "sqd,skd->sqk", mixed_grad_bf, values, preferred_element_type=jnp.float32
    )
    row_dot = jnp.sum(probs * prob_grad, axis=-1, keepdims=True)
    score_grad_bf = (probs * (prob_grad - row_dot)).astype(jnp.bfloat16)
    query_grad = (
        jnp.einsum("sqk,skd->sqd", score_grad_bf, keys, preferred_element_type=jnp.float32)
        * inv_root
    )
    keys_grad = (
        jnp.einsum("sqk,sqd->skd", score_grad_bf, query_bf, preferred_element_type=jnp.float32)
        * inv_root
    )
    values_grad = jnp.einsum(
        "sqk,sqd->skd", probs_bf, mixed_grad_bf, preferred_element_type=jnp.float32
    )
    both_grad = jnp.concatenate([keys_grad, values_grad], axis=-1)
    both_grad = both_grad.reshape(seq_count, ctx, 2 * stretch, 2 * head_dim).transpose(1, 0, 2, 3)
    own_grad = ctx_reduce(list(both_grad.reshape(ctx, count, 2 * head_dim)))
    own_keys_grad, own_values_grad = own_grad[:, :head_dim], own_grad[:, head_dim:]
    query_grad = rotate_back(
        query_grad.reshape(count, heads, head_dim), cosine[:, None, :], sine[:, None, :]
    )
    query_raw_grad, grad_gain_query = rms_back(query_heads, norm_query, query_grad)
    query_raw_bf = query_raw_grad.reshape(count, heads * head_dim).astype(jnp.bfloat16)
    key_raw_grad, grad_gain_key = rms_back(
        key_raw, norm_key, rotate_back(own_keys_grad, cosine, sine)
    )
    key_raw_bf = key_raw_grad.astype(jnp.bfloat16)
    value_raw_bf = own_values_grad.astype(jnp.bfloat16)
    raw_bf = jnp.concatenate([query_raw_bf, key_raw_bf, value_raw_bf], axis=1)
    normed_grad = dot(raw_bf, full_qkv, 1, 1)
    through_in, grad_gain_in = rms_back(hidden, norm_in, normed_grad)
    input_grad = (after_grad + through_in).astype(jnp.bfloat16)

    by_ctx = jnp.concatenate(
        [r.reshape(count, ctx, -1) for r in (query_raw_bf, key_raw_bf, value_raw_bf)], axis=2
    )
    each = by_ctx.shape[2]
    gain_grads = jnp.concatenate(
        [
            g.reshape(dp * ctx, -1)
            for g in (
                grad_gain_in,
                grad_gain_query,
                grad_gain_key,
                grad_gain_attn,
                grad_gain_pre,
                grad_gain_post,
            )
        ],
        axis=1,
    )
    small_size = gain_grads.shape[1]
    extra = jnp.pad(gain_grads, ((0, 0), (0, each - small_size))).reshape(
        dp // 2, 2, 1, ctx * each
    )
    extra = jnp.pad(extra, ((0, 0), (0, 0), (0, 7), (0, 0)))
    grad_qkv = weight_grad(normed, by_ctx.reshape(count, ctx * each), extra)
    grad_qkv = sum_of_ctx(grad_qkv.reshape(grad_qkv.shape[0], ctx, each).transpose(1, 0, 2))
    rows = width // dp
    gain_out = grad_qkv[rows, :small_size]
    grad_qkv = grad_qkv[:rows]
    q_cols, k_cols = heads * head_dim // ctx, head_dim // ctx
    outs, start = [], 0
    for size in sizes:
        outs.append(gain_out[start : start + size])
        start += size
    return (
        output,
        input_grad,
        grad_qkv[:, :q_cols],
        grad_qkv[:, q_cols : q_cols + k_cols],
        grad_qkv[:, q_cols + k_cols :],
        grad_out,
        grad_gate,
        grad_up,
        grad_down,
        *outs,
    )


def sum_of_ctx(blocks):
    size = lax.axis_size("ctx")
    mine = lax.axis_index("ctx")
    total = pick(blocks, mine).astype(jnp.float32)
    for k in range(1, size):
        got = shift(pick(blocks, (mine + k) % size).astype(jnp.bfloat16), k)
        total = total + got.astype(jnp.float32)
    return total


mega = 2**20


def place(name):
    return {"vmem": pl.BlockSpec(memory_space=pltpu.VMEM), "smem": pl.BlockSpec(memory_space=pltpu.SMEM), "any": pl.BlockSpec(memory_space=pl.ANY)}[name]


def kernel_call(body, outs, args, where=None, scratch=(), out_where=None):
    where, out_where = where or {}, out_where or {}
    return pl.pallas_call(
        body,
        out_shape=[jax.ShapeDtypeStruct(s, t) for s, t in outs],
        in_specs=[place(where.get(i, "vmem")) for i in range(len(args))],
        out_specs=[place(out_where.get(i, "vmem")) for i in range(len(outs))],
        scratch_shapes=list(scratch),
        compiler_params=pltpu.CompilerParams(vmem_limit_bytes=121 * mega // 2),
        cost_estimate=pl.CostEstimate(flops=0, bytes_accessed=0, transcendentals=0),
    )(*args)


def norm_back(value, weight, grad):
    scale = lax.rsqrt(jnp.mean(value * value, axis=-1, keepdims=True) + epsilon)
    normed = value * scale
    weighted = grad * (1.0 + weight)
    value_grad = scale * (weighted - normed * jnp.mean(weighted * normed, axis=-1, keepdims=True))
    return value_grad, jnp.sum(grad * normed, axis=0, keepdims=True)


def spread(index, tails, lane, size, ctx):
    dp = len(tails)
    shards = jnp.concatenate([t[:, lane : lane + 128] for t, _ in tails], axis=0)
    tail = shards.shape[0] // dp
    whole = dp * ctx * size
    column = lax.broadcasted_iota(jnp.int32, (128, whole), 1)
    line = lax.broadcasted_iota(jnp.int32, (128, whole), 0)
    spots = jnp.where(column % size == line, 1.0, 0.0).astype(jnp.bfloat16)
    values = dot(shards, spots, 1, 0)
    column = lax.broadcasted_iota(jnp.int32, (tail, whole), 1) // size
    line = lax.broadcasted_iota(jnp.int32, (tail, whole), 0)
    total = jnp.zeros((tail, whole), jnp.float32)
    for k, (_, mask) in enumerate(tails):
        owner = jnp.where(line < ctx, (index ^ mask) * ctx + line, -1)
        total = total + jnp.where(column == owner, values[k * tail : (k + 1) * tail], 0.0)
    return jnp.sum(total, axis=0, keepdims=True)


def pack(w_query, w_key, w_value, w_out, gains):
    rows = w_query.shape[0]
    parts = [w_query, w_key, w_value, w_out]
    ends = [int(e) for e in np.cumsum([0] + [p.shape[1] for p in parts])]
    tall = -(-max(rows + 1, w_out.shape[0]) // 8) * 8

    def body(*rest):
        shards, lines = rest[: len(parts)], rest[len(parts) : len(parts) + len(gains)]
        out, wide = rest[-2], rest[-1]
        wide[...] = jnp.zeros(wide.shape, jnp.float32)
        for i, shard in enumerate(shards):
            wide[: shard.shape[0], ends[i] : ends[i + 1]] = shard[...].astype(jnp.float32)
        for i, line in enumerate(lines):
            wide[rows : rows + 1, i * 128 : i * 128 + line.shape[1]] = line[...].astype(
                jnp.float32
            )
        out[...] = wide[...].astype(jnp.bfloat16)

    return kernel_call(
        body,
        [((tall, ends[-1]), jnp.bfloat16)],
        [*parts, *[g.reshape(1, -1) for g in gains]],
        scratch=[pltpu.VMEM((tall, ends[-1]), jnp.float32)],
    )[0]


def tables(where, lengths, count, stretch, ctx, head_dim):
    seqs = lengths.shape[1]
    each, half = count // seqs, head_dim // 2
    span = 2 * ctx * stretch
    freqs = rope_base ** (-2.0 * np.arange(half, dtype=np.float64) / head_dim)
    freqs = jnp.asarray(freqs[None].astype(np.float32))

    def positions(index, owner):
        block, step = index // stretch % 2, index % stretch
        return jnp.where(block == 0, owner, 2 * ctx - 1 - owner) * stretch + step

    def body(where_ref, lengths_ref, freqs_ref, cos_out, sin_out, valid_out, allowed_out):
        mine = where_ref[4]
        rows = lax.broadcasted_iota(jnp.int32, (each, 1), 0)
        local = positions(rows, mine)
        angles = local.astype(jnp.float32) * freqs_ref[...]
        cos, sin = jnp.cos(angles), jnp.sin(angles)
        cols = lax.broadcasted_iota(jnp.int32, (1, span), 1)
        owner = (mine - cols // each + ctx) % ctx
        keys = positions(cols % each, owner)
        for s in range(seqs):
            part = slice(s * each, (s + 1) * each)
            for low, high in ((0, half), (half, head_dim)):
                cos_out[part, low:high] = cos
                sin_out[part, low:high] = sin
            length = lengths_ref[0, s]
            valid_out[part, :] = jnp.where(local < length, 1.0, 0.0)
            allowed_out[s] = jnp.where((keys <= local) & (keys < length), 1.0, 0.0)

    return kernel_call(
        body,
        [
            ((count, head_dim), jnp.float32),
            ((count, head_dim), jnp.float32),
            ((count, 1), jnp.float32),
            ((seqs, each, span), jnp.float32),
        ],
        [where, lengths, freqs],
        {0: "smem", 1: "smem"},
    )


def plane_near(value):
    return [value, swap(value, 1), swap(value, 2)]


def cut(near):
    row = near[0].ndim - 2
    first = halves_of(near[0].shape[row])[0]
    low = lax.slice_in_dim(near[1], 0, first, axis=row)
    high = lax.slice_in_dim(near[2], first, None, axis=row)
    return [low, high]


def diagonal(halves):
    return [swap(halves[0], 2), swap(halves[1], 1)]


def plane_whole(near):
    pieces = near + diagonal(cut(near))
    return pieces + [swap(p, 0) for p in pieces]


def late_gains(where, pieces, lanes, sizes, ctx, behind):
    tall = pieces[0].shape[0]

    def body(where_ref, behind_ref, *rest):
        parts, outs = rest[: len(pieces)], rest[len(pieces) :]
        tails = tails_of(parts, tall)
        for out, lane, size in zip(outs, lanes, sizes):
            out[...] = spread(where_ref[0], tails, lane, size, ctx)

    return kernel_call(
        body,
        [((1, len(tails_of([np.zeros((tall, 1))] * len(pieces), tall)) * ctx * size), jnp.float32) for size in sizes],
        [where, behind, *pieces],
        {0: "smem", 1: "any"},
    )


def project(where, tokens, pieces, sizes, cosine, sine, heads, ctx):
    count, width = tokens.shape
    tall = pieces[0].shape[0]
    head_dim = cosine.shape[1]
    wide = (heads + 2) * head_dim
    total = len(pieces)

    def body(where_ref, x_ref, cos_ref, sin_ref, *rest):
        parts = rest[:total]
        normed_ref, query_out, both_out, raw_out, in_ref, query_ref, key_ref = rest[total : total + 7]
        weight, ends, sems, end_sems = rest[total + 7 :]
        copies = load_columns(where_ref[0], parts, tall, tall - 16, 0, weight, sems)
        tails = [
            (ref, mask, rows) for ref, mask, at, rows in pieces_of(parts, tall) if at + rows == tall
        ]
        end_copies = [
            pltpu.make_async_copy(
                ref.at[pl.ds(rows - 16, 16), pl.ds(0, ends.shape[2])], ends.at[i], end_sems.at[i]
            )
            for i, (ref, _, rows) in enumerate(tails)
        ]
        for copy in end_copies:
            copy.start()
        for copy in end_copies:
            copy.wait()
        tails = [(ends[i], mask) for i, (_, mask, _) in enumerate(tails)]
        for i, ref in enumerate((in_ref, query_ref, key_ref)):
            ref[...] = spread(where_ref[0], tails, i * 128, sizes[i], ctx)
        normed = rms_norm(x_ref[...].astype(jnp.float32), in_ref[...]).astype(jnp.bfloat16)
        normed_ref[...] = normed
        cos, sin = cos_ref[...], sin_ref[...]
        for copy in copies:
            copy.wait()
        for h in range(heads + 1):
            cols = slice(h * head_dim, (h + 1) * head_dim)
            raw = dot(normed, weight[:, cols], 1, 0)
            raw_out[:, cols] = raw
            gain = query_ref[...] if h < heads else key_ref[...]
            turned = rotate(rms_norm(raw, gain), cos, sin).astype(jnp.bfloat16)
            if h < heads:
                query_out[:, cols] = turned
            else:
                both_out[:, :head_dim] = turned
        both_out[:, head_dim:] = dot(normed, weight[:, (heads + 1) * head_dim :], 1, 0).astype(
            jnp.bfloat16
        )

    return kernel_call(
        body,
        [
            ((count, width), jnp.bfloat16),
            ((count, heads * head_dim), jnp.bfloat16),
            ((count, 2 * head_dim), jnp.bfloat16),
            ((count, (heads + 1) * head_dim), jnp.float32),
            ((1, width), jnp.float32),
            ((1, head_dim), jnp.float32),
            ((1, head_dim), jnp.float32),
        ],
        [where, tokens, cosine, sine, *pieces],
        {0: "smem", **{4 + i: "any" for i in range(total)}},
        [
            pltpu.VMEM((width, wide), jnp.bfloat16),
            pltpu.VMEM((8, 16, 384), jnp.bfloat16),
            pltpu.SemaphoreType.DMA((total,)),
            pltpu.SemaphoreType.DMA((8,)),
        ],
    )


def attend(
    where, tokens, query, both, allowed, valid, norm_attn, norm_pre, pieces, out_rows, heads
):
    count, width = tokens.shape
    seqs, each, span = allowed.shape
    head_dim = query.shape[1] // heads
    inv_root = head_dim ** (-0.5)
    near, total = len(both), len(pieces)
    tall, wide = pieces[0].shape

    def body(where_ref, x_ref, query_ref, allowed_ref, valid_ref, attn_ref, pre_ref, *rest):
        got, parts = rest[:near], rest[near : near + total]
        probs_out, mixed_out, raw_out, after_out, two_out, weight, sems = rest[near + total :]
        copies = load_columns(where_ref[0], parts, tall, out_rows, wide - width, weight, sems)
        for s in range(seqs):
            rows = slice(s * each, (s + 1) * each)
            queries = jnp.concatenate(
                [query_ref[rows, h * head_dim : (h + 1) * head_dim] for h in range(heads)], axis=0
            )
            keys = jnp.concatenate([g[rows, :head_dim] for g in got], axis=0)
            values = jnp.concatenate([g[rows, head_dim:] for g in got], axis=0)
            scores = dot(queries, keys, 1, 1) * inv_root
            keep = jnp.concatenate([allowed_ref[s]] * heads, axis=0)
            scores = jnp.where(keep > 0.0, scores, -1e30)
            expo = jnp.exp(scores - jnp.max(scores, axis=-1, keepdims=True))
            probs = expo / jnp.sum(expo, axis=-1, keepdims=True)
            probs_out[s] = probs
            mixed = dot(probs.astype(jnp.bfloat16), values, 1, 0).astype(jnp.bfloat16)
            for h in range(heads):
                mixed_out[rows, h * head_dim : (h + 1) * head_dim] = mixed[
                    h * each : (h + 1) * each
                ]
        for copy in copies:
            copy.wait()
        raw = dot(mixed_out[...], weight[...], 1, 0)
        raw_out[...] = raw
        after = x_ref[...].astype(jnp.float32) + valid_ref[...] * rms_norm(raw, attn_ref[...])
        after_out[...] = after
        two_out[...] = rms_norm(after, pre_ref[...]).astype(jnp.bfloat16)

    return kernel_call(
        body,
        [
            ((seqs, heads * each, span), jnp.float32),
            ((count, heads * head_dim), jnp.bfloat16),
            ((count, width), jnp.float32),
            ((count, width), jnp.float32),
            ((count, width), jnp.bfloat16),
        ],
        [where, tokens, query, allowed, valid, norm_attn, norm_pre, *both, *pieces],
        {0: "smem", **{7 + near + i: "any" for i in range(total)}},
        [
            pltpu.VMEM((heads * head_dim, width), jnp.bfloat16),
            pltpu.SemaphoreType.DMA((total,)),
        ],
    )


def column_steps(size, step):
    return [(s, min(size, s + step)) for s in range(0, size, step)]


def halves_of(rows):
    first = -(-rows // 32) * 16
    return first, rows - first


def pieces_of(refs, chunk):
    parts, far = refs[: len(refs) // 2], refs[len(refs) // 2 :]
    first, second = halves_of(chunk)
    shapes = [(0, 0, chunk), (2, 0, chunk), (4, 0, chunk), (6, 0, first), (6, first, second)]
    return [(ref, mask, at, rows) for ref, (mask, at, rows) in zip(parts, shapes)] + [
        (ref, mask ^ 1, at, rows) for ref, (mask, at, rows) in zip(far, shapes)
    ]


def load_weights(index, pair, last, chunk, target, sems):
    def copies(m):
        result = []
        for i, (ref, mask, at, rows) in enumerate(pieces_of(last if m == 2 else pair, chunk)):
            start = pl.multiple_of((index ^ mask) * chunk + at, 16)
            result.append(
                pltpu.make_async_copy(
                    ref if m == 2 else ref.at[m], target.at[m, pl.ds(start, rows)], sems.at[m, i]
                )
            )
        return result

    return [copies(m) for m in range(target.shape[0])]


def load_columns(index, refs, tall, rows, first, target, sems):
    copies = []
    for i, (ref, mask, at, size) in enumerate(pieces_of(refs, tall)):
        size = min(size, rows - at)
        if size > 0:
            start = pl.multiple_of((index ^ mask) * rows + at, 16)
            copies.append(
                pltpu.make_async_copy(
                    ref.at[pl.ds(0, size), pl.ds(first, target.shape[1])],
                    target.at[pl.ds(start, size)],
                    sems.at[i],
                )
            )
    for copy in copies:
        copy.start()
    return copies


def tails_of(refs, tall):
    return [
        (ref[rows - 16 : rows], mask) for ref, mask, at, rows in pieces_of(refs, tall) if at + rows == tall
    ]


def feed_forward(where, pieces, weights, with_own):
    count, width = pieces[0].shape
    (pair, last), kinds = weights, 3
    _, chunk, inner = pair[0].shape
    lanes = -(-inner // 128) * 128
    near, spots = len(pieces), len(pair)
    total = near * count
    slope = (2.0 / np.pi) ** 0.5

    def body(where_ref, *rest):
        pair_refs, last_refs, rest = rest[:spots], rest[spots : 2 * spots], rest[2 * spots :]
        parts, outs, sums = rest[:near], rest[near : near + 3], rest[near + 3 : near + 3 + near]
        weight, group, act, slopes, gates, sems, out_sems = rest[near + 3 + near :]
        copies = load_weights(where_ref[0], pair_refs, last_refs, chunk, weight, sems)
        for kind in copies:
            for copy in kind:
                copy.start()
        for k in range(near):
            group[k * count : (k + 1) * count, :] = parts[k][...]
        stores = [
            pltpu.make_async_copy(source, out, out_sems.at[i])
            for i, (source, out) in enumerate(zip((group, act, slopes), outs))
        ]
        stores[0].start()
        for copy in copies[0]:
            copy.wait()
        for low, high in column_steps(inner, 256):
            gates[:, low:high] = dot(group[...], weight[0, :, low:high], 1, 0)
        for copy in copies[1]:
            copy.wait()
        for low, high in column_steps(inner, 256):
            gate = gates[:, low:high]
            upper = dot(group[...], weight[1, :, low:high], 1, 0)
            square = 0.044715 * slope * gate * gate
            half = 0.5 + 0.5 * jnp.tanh(gate * (slope + square))
            gelu = gate * half
            steep = half * (1.0 + 2.0 * (gate - gelu) * (slope + 3.0 * square))
            act[:, low:high] = (gelu * upper).astype(jnp.bfloat16)
            slopes[0, :, low:high] = (steep * upper).astype(jnp.bfloat16)
            slopes[1, :, low:high] = gelu.astype(jnp.bfloat16)
        if lanes > inner:
            act[:, inner:] = jnp.zeros((total, lanes - inner), jnp.bfloat16)
        for store in stores[1:]:
            store.start()
        for copy in copies[2]:
            copy.wait()
        for low, high in column_steps(width, 256):
            part = dot(act[:, :inner], weight[2, low:high, :], 1, 1)
            for k in range(near):
                sums[k][:, low:high] = part[k * count : (k + 1) * count].astype(sums[k].dtype)
        for store in stores:
            store.wait()

    return kernel_call(
        body,
        [
            ((total, width), jnp.bfloat16),
            ((total, lanes), jnp.bfloat16),
            ((2, total, inner), jnp.bfloat16),
        ]
        + [((count, width), jnp.float32 if with_own and k == 0 else jnp.bfloat16) for k in range(near)],
        [where, *pair, *last, *pieces],
        {0: "smem", **{1 + i: "any" for i in range(2 * spots)}},
        [
            pltpu.VMEM((kinds, width, inner), jnp.bfloat16),
            pltpu.VMEM((total, width), jnp.bfloat16),
            pltpu.VMEM((total, lanes), jnp.bfloat16),
            pltpu.VMEM((2, total, inner), jnp.bfloat16),
            pltpu.VMEM((total, inner), jnp.float32),
            pltpu.SemaphoreType.DMA((kinds, spots)),
            pltpu.SemaphoreType.DMA((3,)),
        ],
        {i: "any" for i in range(3)},
    )


def finish(parts, after, cotangent, valid, norm_post):
    count, width = after.shape
    near = len(parts)

    def body(after_ref, cot_ref, valid_ref, post_ref, *rest):
        got = rest[:near]
        output_out, grad_out, gain_out = rest[near:]
        raw = got[0][...]
        for g in got[1:]:
            raw = raw + g[...].astype(jnp.float32)
        ok = valid_ref[...]
        output_out[...] = (after_ref[...] + ok * rms_norm(raw, post_ref[...])).astype(jnp.bfloat16)
        grad, gain = norm_back(raw, post_ref[...], ok * cot_ref[...].astype(jnp.float32))
        grad_out[...] = grad.astype(jnp.bfloat16)
        gain_out[...] = gain

    return kernel_call(
        body,
        [
            ((count, width), jnp.bfloat16),
            ((count, width), jnp.bfloat16),
            ((1, width), jnp.float32),
        ],
        [after, cotangent, valid, norm_post, *parts],
    )


def feed_back(where, pieces, weights, slopes, with_own):
    count, width = pieces[0].shape
    (pair, last), kinds = weights, 3
    _, chunk, inner = pair[0].shape
    lanes = -(-inner // 128) * 128
    near, spots = len(pieces), len(pair)
    total = near * count

    def body(where_ref, slopes_ref, *rest):
        pair_refs, last_refs, rest = rest[:spots], rest[spots : 2 * spots], rest[2 * spots :]
        parts = rest[:near]
        group_out, both_out = rest[near : near + 2]
        sums = rest[near + 2 : near + 2 + near]
        weight, sems = rest[near + 2 + near :]
        copies = load_weights(where_ref[0], pair_refs, last_refs, chunk, weight, sems)
        for kind in (copies[2], copies[0], copies[1]):
            for copy in kind:
                copy.start()
        for k in range(near):
            group_out[k * count : (k + 1) * count, :] = parts[k][...]
        for copy in copies[2]:
            copy.wait()
        for low, high in column_steps(inner, 256):
            grad = dot(group_out[...], weight[2, :, low:high], 1, 0)
            for i in range(2):
                slope = slopes_ref[i, :, low:high].astype(jnp.float32)
                both_out[i, :, low:high] = (grad * slope).astype(jnp.bfloat16)
        if lanes > inner:
            both_out[:, :, inner:] = jnp.zeros((2, total, lanes - inner), jnp.bfloat16)
        for kind in copies[:2]:
            for copy in kind:
                copy.wait()
        for low, high in column_steps(width, 256):
            part = dot(both_out[0, :, :inner], weight[0, low:high, :], 1, 1)
            part = part + dot(both_out[1, :, :inner], weight[1, low:high, :], 1, 1)
            for k in range(near):
                sums[k][:, low:high] = part[k * count : (k + 1) * count].astype(sums[k].dtype)

    return kernel_call(
        body,
        [((total, width), jnp.bfloat16)]
        + [((2, total, lanes), jnp.bfloat16)]
        + [((count, width), jnp.float32 if with_own and k == 0 else jnp.bfloat16) for k in range(near)],
        [where, slopes, *pair, *last, *pieces],
        {0: "smem", **{2 + i: "any" for i in range(2 * spots)}},
        [
            pltpu.VMEM((kinds, width, inner), jnp.bfloat16),
            pltpu.SemaphoreType.DMA((kinds, spots)),
        ],
    )


def wide_grads(where, lefts, rights):
    width = lefts[0].shape[1]
    total = sum(left.shape[0] for left in lefts)
    lanes = rights[0][0][0].shape[-1]
    kinds = len(rights)
    chunk = width // 8
    first, second = halves_of(chunk)
    arrays = []
    for array in [r for right in rights for r, _ in right]:
        if all(array is not other for other in arrays):
            arrays.append(array)
    spots = [[[array is other for other in arrays].index(True) for array, _ in right] for right in rights]
    most = max(len(right) for right in rights)

    def body(where_ref, *rest):
        left_refs, right_refs = rest[: len(lefts)], rest[len(lefts) : len(lefts) + len(arrays)]
        outs = rest[len(lefts) + len(arrays) : len(lefts) + len(arrays) + 4]
        turned, left, values, sems = rest[len(lefts) + len(arrays) + 4 :]
        copies = []
        for m, right in enumerate(rights):
            at, row = [], 0
            for i, (array, index) in enumerate(right):
                ref = right_refs[spots[m][i]]
                size = array.shape[-2]
                at.append(
                    pltpu.make_async_copy(
                        ref if index is None else ref.at[index],
                        values.at[m, pl.ds(row, size)],
                        sems.at[m, i],
                    )
                )
                row += size
            copies.append(at)
        for part in copies:
            for copy in part:
                copy.start()
        core, x, y = where_ref[1], where_ref[2], where_ref[3]
        order = []
        for flip in (1, 0):
            order.append([(j * 2 + jnp.bitwise_xor(x, flip), 0, first) for j in range(2)])
        for flip in (1, 0):
            order.append([(jnp.bitwise_xor(y, flip) * 2 + j, first, second) for j in range(2)])
        row = 0
        for ref in left_refs:
            turned[:, row : row + ref.shape[0]] = ref[...].T
            row += ref.shape[0]
        at = 0
        for block in order:
            for plane, offset, size in block:
                start = pl.multiple_of((plane * 2 + core) * chunk + offset, 16)
                left[at : at + size, :] = turned[pl.ds(start, size), :]
                at += size
        for m in range(kinds):
            for copy in copies[m]:
                copy.wait()
            for low, high in column_steps(lanes, 256):
                part = dot(left[...], values[m, :, low:high], 1, 0).astype(jnp.bfloat16)
                at = 0
                for out, block in zip(outs, order):
                    size = 2 * block[0][2]
                    out[m, :, low:high] = part[at : at + size]
                    at += size

    return kernel_call(
        body,
        [
            ((kinds, 2 * first, lanes), jnp.bfloat16),
            ((kinds, 2 * first, lanes), jnp.bfloat16),
            ((kinds, 2 * second, lanes), jnp.bfloat16),
            ((kinds, 2 * second, lanes), jnp.bfloat16),
        ],
        [where, *lefts, *arrays],
        {0: "smem", **{1 + len(lefts) + i: "any" for i in range(len(arrays))}},
        [
            pltpu.VMEM((width, total), jnp.bfloat16),
            pltpu.VMEM((width // 2, total), jnp.bfloat16),
            pltpu.VMEM((kinds, total, lanes), jnp.bfloat16),
            pltpu.SemaphoreType.DMA((kinds, most)),
        ],
    )


def wide_middle(where, wides, gots):
    sizes = [wide[0].shape[0] for wide in wides]
    kinds = sum(sizes)
    first, second = wides[0][1].shape[1] // 2, wides[0][3].shape[1] // 2
    lanes = wides[0][1].shape[2]
    args = [a for wide, got in zip(wides, gots) for a in (wide[1], got[0], wide[3], got[1])]

    def body(where_ref, *rest):
        refs, outs = rest[: len(args)], rest[len(args) :]
        x, y = where_ref[2], where_ref[3]
        at = 0
        for i, size in enumerate(sizes):
            kept_a, got_a, kept_b, got_b = refs[4 * i : 4 * i + 4]
            for m in range(size):
                for kept, got, place, rows, pair in (
                    (kept_a, got_a, y, first, outs[:2]),
                    (kept_b, got_b, x, second, outs[2:]),
                ):
                    for flip, out in ((1, pair[0]), (0, pair[1])):
                        spot = pl.ds(
                            pl.multiple_of(jnp.bitwise_xor(place, flip) * rows, 16), rows
                        )
                        total = kept[m, spot, :].astype(jnp.float32) + got[m, spot, :].astype(
                            jnp.float32
                        )
                        out[at] = total.astype(jnp.bfloat16)
                at += 1

    return kernel_call(
        body,
        [((kinds, first, lanes), jnp.bfloat16)] * 2 + [((kinds, second, lanes), jnp.bfloat16)] * 2,
        [where, *args],
        {0: "smem"},
    )


def wide_last(wide, got, inner):
    (_, kept_a, _, kept_b), (got_a, got_b) = wide, got
    kinds, first, _ = kept_a.shape
    second = kept_b.shape[1]

    def body(kept_a_ref, got_a_ref, kept_b_ref, got_b_ref, *outs):
        for m in range(kinds):
            total = kept_a_ref[m].astype(jnp.float32) + got_a_ref[m].astype(jnp.float32)
            outs[m][:first, :] = total[:, :inner]
            total = kept_b_ref[m].astype(jnp.float32) + got_b_ref[m].astype(jnp.float32)
            outs[m][first:, :] = total[:, :inner]

    return kernel_call(
        body,
        [((first + second, inner), jnp.float32)] * kinds,
        [kept_a, got_a, kept_b, got_b],
    )


def attend_back(
    where,
    parts,
    after,
    cotangent,
    valid,
    attn_raw,
    norm_pre,
    norm_attn,
    norm_query,
    probs,
    query,
    raw,
    both,
    pieces,
    out_rows,
    cosine,
    sine,
    heads,
):
    count, width = after.shape
    seqs, _, span = probs.shape
    each = count // seqs
    head_dim = norm_query.shape[1]
    inv_root = head_dim ** (-0.5)
    near, spots = len(both), len(pieces)
    tall, wide = pieces[0].shape

    def body(
        where_ref,
        after_ref,
        cot_ref,
        valid_ref,
        attn_ref,
        pre_ref,
        norm_ref,
        query_gain_ref,
        probs_ref,
        query_ref,
        raw_ref,
        cos_ref,
        sin_ref,
        *rest,
    ):
        shards, rest = rest[:spots], rest[spots:]
        sums = rest[:near]
        got = rest[near : 2 * near]
        rest = rest[2 * near :]
        dx_out, attn_grad_out, raw_grad_out, pre_out, attn_gain_out, query_gain_out = rest[:6]
        both_outs = rest[6 : 6 + near]
        mixed_grad, query_grad, weight, sems = rest[6 + near :]
        copies = load_columns(where_ref[0], shards, tall, out_rows, wide - width, weight, sems)
        grad = sums[0][...]
        for s in sums[1:]:
            grad = grad + s[...].astype(jnp.float32)
        through, gain = norm_back(after_ref[...], pre_ref[...], grad)
        pre_out[...] = gain
        dx = cot_ref[...].astype(jnp.float32) + through
        dx_out[...] = dx
        attn_grad, gain = norm_back(attn_ref[...], norm_ref[...], valid_ref[...] * dx)
        attn_gain_out[...] = gain
        attn_grad = attn_grad.astype(jnp.bfloat16)
        attn_grad_out[...] = attn_grad
        for copy in copies:
            copy.wait()
        mixed_grad[...] = dot(attn_grad, weight[...], 1, 1).astype(jnp.bfloat16)
        for s in range(seqs):
            rows = slice(s * each, (s + 1) * each)
            queries = jnp.concatenate(
                [query_ref[rows, h * head_dim : (h + 1) * head_dim] for h in range(heads)], axis=0
            )
            grads = jnp.concatenate(
                [mixed_grad[rows, h * head_dim : (h + 1) * head_dim] for h in range(heads)], axis=0
            )
            keys = jnp.concatenate([g[rows, :head_dim] for g in got], axis=0)
            values = jnp.concatenate([g[rows, head_dim:] for g in got], axis=0)
            probs = probs_ref[s]
            prob_grad = dot(grads, values, 1, 1)
            row = jnp.sum(probs * prob_grad, axis=-1, keepdims=True)
            score_grad = (probs * (prob_grad - row)).astype(jnp.bfloat16)
            back = dot(score_grad, keys, 1, 0) * inv_root
            for h in range(heads):
                query_grad[rows, h * head_dim : (h + 1) * head_dim] = back[
                    h * each : (h + 1) * each
                ]
            keys_grad = dot(score_grad, queries, 0, 0) * inv_root
            values_grad = dot(probs.astype(jnp.bfloat16), grads, 0, 0)
            for k in range(near):
                part = slice(k * each, (k + 1) * each)
                both_outs[k][rows, :head_dim] = keys_grad[part].astype(both_outs[k].dtype)
                both_outs[k][rows, head_dim:] = values_grad[part].astype(both_outs[k].dtype)
        cos, sin = cos_ref[...], sin_ref[...]
        gain_sum = jnp.zeros((1, head_dim), jnp.float32)
        for h in range(heads):
            cols = slice(h * head_dim, (h + 1) * head_dim)
            turned = rotate_back(query_grad[:, cols], cos, sin)
            value_grad, gain = norm_back(raw_ref[:, cols], query_gain_ref[...], turned)
            raw_grad_out[:, cols] = value_grad.astype(jnp.bfloat16)
            gain_sum = gain_sum + gain
        query_gain_out[...] = gain_sum

    return kernel_call(
        body,
        [
            ((count, width), jnp.float32),
            ((count, width), jnp.bfloat16),
            ((count, heads * head_dim), jnp.bfloat16),
            ((1, width), jnp.float32),
            ((1, width), jnp.float32),
            ((1, head_dim), jnp.float32),
            ((count, 2 * head_dim), jnp.float32),
        ]
        + [((count, 2 * head_dim), jnp.bfloat16)] * (near - 1),
        [
            where,
            after,
            cotangent,
            valid,
            attn_raw,
            norm_pre,
            norm_attn,
            norm_query,
            probs,
            query,
            raw,
            cosine,
            sine,
            *pieces,
            *parts,
            *both,
        ],
        {0: "smem", **{13 + i: "any" for i in range(spots)}},
        [
            pltpu.VMEM((count, heads * head_dim), jnp.bfloat16),
            pltpu.VMEM((count, heads * head_dim), jnp.float32),
            pltpu.VMEM((heads * head_dim, width), jnp.bfloat16),
            pltpu.SemaphoreType.DMA((spots,)),
        ],
    )


def project_back(
    where,
    parts,
    raw,
    query_grad,
    tokens,
    dx,
    norm_in,
    norm_key,
    cosine,
    sine,
    pieces,
    heads,
    ctx,
    gains,
):
    count, width = tokens.shape
    tall_piece = pieces[0].shape[0]
    head_dim = norm_key.shape[1]
    wide = (heads + 2) * head_dim
    near, spots, total = len(parts), len(pieces), 8
    each = wide // ctx
    count_gains = len(gains)
    tall = count + 16

    def body(
        where_ref, raw_ref, query_ref, x_ref, dx_ref, in_ref, key_ref, cos_ref, sin_ref, *rest
    ):
        sums = rest[:near]
        shards = rest[near : near + spots]
        others = rest[near + spots : near + spots + count_gains]
        input_out = rest[near + spots + count_gains]
        outs = rest[near + spots + count_gains + 1 : near + spots + count_gains + 1 + ctx]
        weight, grads_out, gains_out, sems = rest[near + spots + count_gains + 1 + ctx :]
        copies = load_columns(
            where_ref[0], shards, tall_piece, tall_piece - 16, 0, weight, sems
        )
        grad = sums[0][...]
        for s in sums[1:]:
            grad = grad + s[...].astype(jnp.float32)
        turned = rotate_back(grad[:, :head_dim], cos_ref[...], sin_ref[...])
        key_grad, key_gain = norm_back(raw_ref[:, heads * head_dim :], key_ref[...], turned)
        grads_out[:, : heads * head_dim] = query_ref[...]
        grads_out[:, heads * head_dim : (heads + 1) * head_dim] = key_grad.astype(jnp.bfloat16)
        grads_out[:, (heads + 1) * head_dim :] = grad[:, head_dim:].astype(jnp.bfloat16)
        for copy in copies:
            copy.wait()
        back = dot(grads_out[...], weight[...], 1, 1)
        through, in_gain = norm_back(x_ref[...].astype(jnp.float32), in_ref[...], back)
        input_out[...] = (dx_ref[...] + through).astype(jnp.bfloat16)
        gains_out[...] = jnp.zeros((16, wide), jnp.float32)
        lane = 0
        for gain in (in_gain, others[0][...], key_gain, *[o[...] for o in others[1:]]):
            size = gain.shape[1] // (total * ctx)
            for d in range(total):
                for c in range(ctx):
                    at = c * each + lane
                    gains_out[d : d + 1, at : at + size] = gain[
                        :, (d * ctx + c) * size : (d * ctx + c + 1) * size
                    ]
            lane += size
        spans = [(0, heads * head_dim), (heads * head_dim, head_dim), ((heads + 1) * head_dim, head_dim)]
        mine = where_ref[4]
        for c in range(ctx):

            @pl.when(mine == c)
            def _(c=c):
                for k in range(ctx):
                    j, at = (c + k) % ctx, 0
                    for first, size in spans:
                        step = size // ctx
                        outs[k][:count, at : at + step] = grads_out[
                            :, first + j * step : first + (j + 1) * step
                        ]
                        at += step
                    outs[k][count:, :] = gains_out[:, j * each : (j + 1) * each].astype(
                        jnp.bfloat16
                    )

    return kernel_call(
        body,
        [((count, width), jnp.bfloat16)] + [((tall, each), jnp.bfloat16)] * ctx,
        [
            where,
            raw,
            query_grad,
            tokens,
            dx,
            norm_in,
            norm_key,
            cosine,
            sine,
            *parts,
            *pieces,
            *gains,
        ],
        {0: "smem", **{9 + near + i: "any" for i in range(spots)}},
        [
            pltpu.VMEM((width, wide), jnp.bfloat16),
            pltpu.VMEM((count, wide), jnp.bfloat16),
            pltpu.VMEM((16, wide), jnp.float32),
            pltpu.SemaphoreType.DMA((spots,)),
        ],
    )


def narrow_grads(where, lefts, rights, with_gains):
    count, width = lefts[0].shape
    wide = rights[0].shape[1]
    chunk, near = width // 8, len(lefts)
    total = near * count
    tall = chunk + 16 if with_gains else chunk

    def body(where_ref, *rest):
        left_refs, right_refs, outs = rest[:near], rest[near : 2 * near], rest[2 * near : -3]
        turned, lines, values = rest[-3:]
        for i in range(near):
            turned[:, i * count : (i + 1) * count] = left_refs[i][...].T
            values[i * count : (i + 1) * count, :] = right_refs[i][:count, :]
        plane, core = where_ref[0] // 2, where_ref[1]
        for m in range(4):
            start = pl.multiple_of((jnp.bitwise_xor(plane, m) * 2 + core) * chunk, 16)
            lines[m * chunk : (m + 1) * chunk, :] = turned[pl.ds(start, chunk), :]
        for low, high in column_steps(wide, 256):
            part = dot(lines[...], values[:, low:high], 1, 0)
            for m in range(4):
                outs[m][:chunk, low:high] = part[m * chunk : (m + 1) * chunk].astype(outs[m].dtype)
        if with_gains:
            whole = right_refs[0][count:, :].astype(jnp.float32)
            for r in right_refs[1:]:
                whole = whole + r[count:, :].astype(jnp.float32)
            index = lax.broadcasted_iota(jnp.int32, whole.shape, 0)
            for m in range(4):
                row = jnp.bitwise_xor(plane, m) * 2 + core
                row = jnp.sum(jnp.where(index == row, whole, 0.0), axis=0, keepdims=True)
                outs[m][chunk:, :] = jnp.where(index == 0, row, 0.0).astype(outs[m].dtype)

    return kernel_call(
        body,
        [((tall, wide), jnp.float32)] + [((tall, wide), jnp.bfloat16)] * 3,
        [where, *lefts, *rights],
        {0: "smem"},
        [
            pltpu.VMEM((width, total), jnp.bfloat16),
            pltpu.VMEM((width // 2, total), jnp.bfloat16),
            pltpu.VMEM((total, wide), jnp.bfloat16),
        ],
    )


def narrow_middle(where, parts, sizes, ctx):
    chunk, wide = parts[0].shape
    each = wide // ctx

    def body(where_ref, *rest):
        got = rest[: len(parts)]
        outs = rest[len(parts) :]
        mine = where_ref[4]
        total = got[0][...]
        for g in got[1:]:
            total = total + g[...].astype(jnp.float32)
        for c in range(ctx):

            @pl.when(mine == c)
            def _(c=c):
                for k in range(ctx):
                    j = (c + k) % ctx
                    start, at = 0, 0
                    for size in sizes:
                        piece = size // ctx
                        outs[k][:, at : at + piece] = total[
                            :, start + j * piece : start + (j + 1) * piece
                        ].astype(outs[k].dtype)
                        start += size
                        at += piece

    return kernel_call(
        body,
        [((chunk, each), jnp.float32)] + [((chunk, each), jnp.bfloat16)] * (ctx - 1),
        [where, *parts],
        {0: "smem"},
    )


def narrow_last(blocks, out_blocks, sizes, cols):
    rows = out_blocks[0].shape[0]
    near = len(blocks)
    q, k, v = cols

    def body(*rest):
        outs = rest[2 * near :]
        total = rest[0][...]
        for r in rest[1:near]:
            total = total + r[...].astype(jnp.float32)
        outs[0][...] = total[:rows, :q]
        turned = total[:rows, q:].T
        outs[1][...] = turned[:k]
        outs[2][...] = turned[k:]
        out = rest[near][...]
        for r in rest[near + 1 : 2 * near]:
            out = out + r[...].astype(jnp.float32)
        outs[3][...] = out
        start = 0
        for ref, size in zip(outs[4:], sizes):
            ref[...] = total[rows : rows + 1, start : start + size]
            start += size

    return kernel_call(
        body,
        [
            ((rows, q), jnp.float32),
            ((k, rows), jnp.float32),
            ((v, rows), jnp.float32),
            ((rows, out_blocks[0].shape[1]), jnp.float32),
        ]
        + [((1, size), jnp.float32) for size in sizes],
        [*blocks, *out_blocks],
    )


def split_pair(where, gate, up, ctx):
    rows, whole = gate.shape
    inner = whole // ctx

    def body(where_ref, gate_ref, up_ref, *outs):
        mine = where_ref[4]
        for c in range(ctx):

            @pl.when(mine == c)
            def _(c=c):
                for k in range(ctx):
                    j = (c + k) % ctx
                    outs[k][0] = gate_ref[:, j * inner : (j + 1) * inner]
                    outs[k][1] = up_ref[:, j * inner : (j + 1) * inner]

    return kernel_call(
        body, [((2, rows, inner), jnp.bfloat16)] * ctx, [where, gate, up], {0: "smem"}
    )


def join_pair(where, pieces):
    ctx = len(pieces)
    _, rows, inner = pieces[0].shape

    def body(where_ref, *rest):
        got, out, wide = rest[:ctx], rest[ctx], rest[ctx + 1]
        mine = where_ref[4]
        for c in range(ctx):

            @pl.when(mine == c)
            def _(c=c):
                for m in range(2):
                    for a in range(ctx):
                        wide[a * rows : (a + 1) * rows, :] = got[(c - a) % ctx][m].astype(
                            jnp.float32
                        )
                    out[m] = wide[...].astype(jnp.bfloat16)

    return kernel_call(
        body,
        [((2, ctx * rows, inner), jnp.bfloat16)],
        [where, *pieces],
        {0: "smem"},
        [pltpu.VMEM((ctx * rows, inner), jnp.float32)],
    )[0]


def share_down(where, down):
    width, part = down.shape
    chunk = width // 8

    def body(where_ref, down_ref, *outs):
        plane, core = where_ref[0] // 2, where_ref[1]
        for flip, out in enumerate(outs):
            for m in range(4):
                group = jnp.bitwise_xor(plane, m) * 2 + jnp.bitwise_xor(core, flip)
                out[m] = down_ref[pl.ds(pl.multiple_of(group * chunk, 16), chunk), :]

    return kernel_call(
        body, [((4, chunk, part), jnp.bfloat16)] * 2, [where, down], {0: "smem"}
    )


def split_down(where, pieces, rows, ctx):
    groups = 2 * len(pieces)
    _, chunk, part = pieces[0].shape
    per, steps = groups // ctx, chunk // rows

    def body(where_ref, *rest):
        got, outs, (wide, down_ref) = rest[:4], rest[4 : 4 + ctx], rest[4 + ctx :]
        mine = where_ref[4]
        plane, core = where_ref[0] // 2, where_ref[1]
        for m in range(4):
            for flip in range(2):
                group = jnp.bitwise_xor(plane, m) * 2 + jnp.bitwise_xor(core, flip)
                down_ref[pl.ds(group, 1)] = got[m][flip][None]
        for c in range(ctx):

            @pl.when(mine == c)
            def _(c=c):
                for k in range(ctx):
                    j = (c + k) % ctx
                    for b in range(groups):
                        first = b % steps * rows
                        wide[:, b * part : (b + 1) * part] = down_ref[
                            j * per + b // steps, first : first + rows, :
                        ].astype(jnp.float32)
                    outs[k][...] = wide[...].astype(jnp.bfloat16)

    return kernel_call(
        body,
        [((rows, groups * part), jnp.bfloat16)] * ctx,
        [where, *pieces],
        {0: "smem"},
        [
            pltpu.VMEM((rows, groups * part), jnp.float32),
            pltpu.VMEM((groups, chunk, part), jnp.bfloat16),
        ],
    )


def join_down(where, pieces, part):
    ctx = len(pieces)
    rows, inner = pieces[0].shape
    chunk, groups = ctx * rows, inner // part

    def body(where_ref, *rest):
        got, out, wide = rest[:ctx], rest[ctx], rest[ctx + 1]
        mine = where_ref[4]
        for c in range(ctx):

            @pl.when(mine == c)
            def _(c=c):
                for a in range(ctx):
                    piece = got[(c - a) % ctx][...].astype(jnp.float32)
                    for b in range(groups):
                        first = b % ctx * rows
                        at = (b // ctx * ctx + a) * part
                        wide[first : first + rows, at : at + part] = piece[
                            :, b * part : (b + 1) * part
                        ]
                out[...] = wide[...].astype(jnp.bfloat16)

    return kernel_call(
        body,
        [((chunk, inner), jnp.bfloat16)],
        [where, *pieces],
        {0: "smem"},
        [pltpu.VMEM((chunk, inner), jnp.float32)],
    )[0]


def join_rows(where, pieces, rows, split, out_rows):
    ctx = len(pieces)
    _, wide = pieces[0].shape
    tall = ctx * rows + 16

    def body(where_ref, *rest):
        got, out, lines = rest[:ctx], rest[ctx], rest[ctx + 1]
        mine = where_ref[4]
        lines[ctx * rows :, :] = jnp.zeros((16, wide), jnp.float32)
        lines[ctx * out_rows :, split:] = jnp.zeros((tall - ctx * out_rows, wide - split), jnp.float32)
        for c in range(ctx):

            @pl.when(mine == c)
            def _(c=c):
                for a in range(ctx):
                    piece = got[(c - a) % ctx]
                    lines[a * rows : (a + 1) * rows, :split] = piece[:rows, :split].astype(
                        jnp.float32
                    )
                    lines[a * out_rows : (a + 1) * out_rows, split:] = piece[
                        :out_rows, split:
                    ].astype(jnp.float32)
                    at = ctx * rows + a
                    lines[at : at + 1, :split] = piece[rows : rows + 1, :split].astype(jnp.float32)
                out[...] = lines[...].astype(jnp.bfloat16)

    return kernel_call(
        body,
        [((tall, wide), jnp.bfloat16)],
        [where, *pieces],
        {0: "smem"},
        [pltpu.VMEM((tall, wide), jnp.float32)],
    )[0]


def plane_send(parts):
    size = lax.axis_size("dp")
    return [parts[0]] + [
        lax.ppermute(parts[m], "dp", [(i, i ^ (2 * m)) for i in range(size)])
        for m in range(1, len(parts))
    ]


def ctx_send(parts, sign):
    return [parts[0]] + [shift(parts[k], sign * k) for k in range(1, len(parts))]


def stage(*values):
    return lax.optimization_barrier(values)


def gate(value, *conditions):
    return lax.optimization_barrier((value, conditions))[0]


def fused(
    tokens,
    cotangent,
    lengths,
    w_query,
    w_key,
    w_value,
    w_out,
    w_gate,
    w_up,
    w_down,
    gain_in,
    gain_query,
    gain_key,
    gain_attn,
    gain_pre,
    gain_post,
):
    count, width = tokens.shape
    seq_count = lengths.shape[1]
    stretch = count // (2 * seq_count)
    dp = lax.axis_size("dp")
    ctx = lax.axis_size("ctx")
    mine = lax.axis_index("ctx")
    group = lax.axis_index("dp")
    head_dim = w_key.shape[1]
    heads = w_query.shape[1] // head_dim
    where = jnp.stack([group, group % 2, group // 2 % 2, group // 4, mine]).astype(jnp.int32)

    gains = [gain_in, gain_query, gain_key, gain_attn, gain_pre, gain_post]
    sizes = [g.shape[0] for g in gains]
    chunk, out_rows = width // dp, heads * head_dim // dp
    order = [0, 1, 3, 2]
    packed = pack(w_query, w_key, w_value, w_out, gains)
    split = packed.shape[1] - width
    kept, sent = share_down(where, gate(w_down, packed).T)
    packed = ctx_gather(packed)
    got = swap(sent, 0)
    downs = plane_send([jnp.stack([kept[m], got[m]]) for m in range(4)])
    aux = tables(where, lengths, count, stretch, ctx, head_dim)
    packed, downs, aux = stage(packed, downs, aux)
    cosine, sine, valid, allowed = aux

    blocks = list(split_pair(where, w_gate, w_up, ctx))
    packed = gate(packed, blocks[0])
    blocks = ctx_send(blocks, 1)
    near = plane_near(join_rows(where, packed, w_query.shape[0], split, w_out.shape[0]))
    shared = plane_whole(near)
    pair = join_pair(where, blocks)
    shared, pair, downs = stage(shared, pair, downs)

    normed, query, both, raw, norm_in, norm_query, norm_key = project(
        where, tokens, shared, sizes[:3], cosine, sine, heads, ctx
    )
    pair, normed, query, both, downs = stage(pair, normed, query, both, downs)

    pair = plane_near(pair)
    downs = list(split_down(where, downs, w_gate.shape[0], ctx))
    norm_attn, norm_pre, norm_post = late_gains(
        where, shared, [384, 512, 640], sizes[3:], ctx, both
    )
    both = ctx_gather(both)
    downs = ctx_send(gate(downs, both), 1)
    probs, mixed, attn_raw, residual, normed_two = attend(
        where,
        tokens,
        query,
        both,
        allowed,
        valid,
        norm_attn,
        norm_pre,
        shared,
        out_rows,
        heads,
    )
    pair, pair_cut, downs, normed_two, mixed = stage(pair, cut(pair), downs, normed_two, mixed)

    last = plane_near(join_down(where, downs, w_down.shape[0]))
    two_pieces = [normed_two] + [shift(normed_two, k) for k in order[1:-1]]
    pair_far = [swap(pair[0], 0)]
    two_pieces, pair, pair_far, last, last_cut, normed = stage(
        two_pieces, pair, pair_far, last, cut(last), normed
    )

    two_pieces.append(shift(two_pieces[0], order[-1]))
    pair = pair + diagonal(pair_cut)
    pair_far = pair_far + [swap(p, 0) for p in pair[1:3]]
    two_pieces, pair, pair_far, last, last_cut, normed = stage(
        two_pieces, pair, pair_far, last, last_cut, normed
    )

    last = last + diagonal(last_cut)
    pair_far = pair_far + [swap(p, 0) for p in pair[3:]]
    pair, last = pair + pair_far, last + [swap(p, 0) for p in last]
    two_pieces, pair, last, normed = stage(two_pieces, pair, last, normed)

    weights = (pair, last)
    normed_group = [normed, shift(normed, 1), None, shift(normed, 3)]
    group_two, act, slopes, *sums = feed_forward(where, two_pieces[:-1], weights, True)
    group_two, act, slopes, sums, near_group = stage(
        group_two, act, slopes, sums, [normed_group[1], normed_group[3]]
    )
    normed_group[1], normed_group[3] = near_group

    sums = [sums[0]] + [shift(sums[i], -order[i]) for i in range(1, ctx - 1)]
    two_last, act_last, slopes_last, sum_last = feed_forward(
        where, two_pieces[-1:], weights, False
    )
    sums, two_last, act_last, slopes_last, sum_last, group_two, act, mixed = stage(
        sums, two_last, act_last, slopes_last, sum_last, group_two, act, mixed
    )

    sums.append(shift(sum_last, -order[-1]))
    group_two, act = [group_two, two_last], [act, act_last]
    group_two_far, act_far = [swap(g, 0) for g in group_two], [swap(a, 0) for a in act]
    mixed_far = swap(mixed, 0)
    sums, group_two_far, act_far, mixed_far = stage(sums, group_two_far, act_far, mixed_far)

    output, ffn_grad, gain_post_grad = finish(sums, residual, cotangent, valid, norm_post)
    ffn_early = [ffn_grad] + [shift(ffn_grad, k) for k in order[1:-1]]
    ffn_early, ffn_grad = stage(ffn_early, ffn_grad)

    ffn_last = shift(ffn_grad, order[-1])
    group_ffn, grads, *sums = feed_back(where, ffn_early, weights, slopes, True)
    ffn_last, group_ffn, grads, sums = stage(ffn_last, group_ffn, grads, sums)

    ffn_parts = [group_ffn, ffn_last]
    ffn_far = [swap(f, 0) for f in ffn_parts]
    grads_far = swap(grads, 0)
    _, grads_last, sum_last = feed_back(
        where, [ffn_last], weights, slopes_last, False
    )
    sums[1], sums[2] = shift(sums[1], -order[1]), shift(sums[2], -order[2])
    down_wide = wide_grads(
        where, gate(ffn_parts, grads_last) + ffn_far, [[(a, None) for a in act + act_far]]
    )
    grads_last, sum_last, grads, grads_far, sums, down_wide = stage(
        grads_last, sum_last, grads, grads_far, sums, down_wide
    )

    sums.append(shift(sum_last, -order[-1]))
    down_got = [swap(down_wide[0], 1), swap(down_wide[2], 2)]
    all_grads = [grads, grads_last, grads_far, swap(grads_last, 0)]
    pair_wide = wide_grads(
        where, group_two + group_two_far, [[(g, m) for g in all_grads] for m in range(2)]
    )
    sums, down_wide, down_got, pair_wide = stage(sums, down_wide, down_got, pair_wide)

    pair_got = [swap(pair_wide[0], 1), swap(pair_wide[2], 2)]
    dx, attn_grad, query_grad, gain_pre_grad, gain_attn_grad, gain_query_grad, *parts = attend_back(
        where,
        sums,
        residual,
        cotangent,
        valid,
        attn_raw,
        norm_pre,
        norm_attn,
        norm_query,
        probs,
        query,
        raw,
        both,
        shared,
        out_rows,
        cosine,
        sine,
        heads,
    )
    parts = ctx_send(parts, -1)
    out_blocks = narrow_grads(
        where, [attn_grad, swap(attn_grad, 0)], [mixed, mixed_far], False
    )
    parts, pair_got, out_blocks, query_grad, dx, normed = stage(
        parts, pair_got, out_blocks, query_grad, dx, normed
    )

    input_grad, *blocks = project_back(
        where,
        parts,
        raw,
        query_grad,
        tokens,
        dx,
        norm_in,
        norm_key,
        cosine,
        sine,
        shared,
        heads,
        ctx,
        [gain_query_grad, gain_attn_grad, gain_pre_grad, gain_post_grad],
    )
    normed_group[2] = shift(normed, 2)
    out_blocks = plane_send(out_blocks)
    wide = wide_middle(where, [pair_wide, down_wide], [pair_got, down_got])
    blocks, out_blocks, wide, normed_group = stage(list(blocks), out_blocks, wide, normed_group)

    blocks = ctx_send(blocks, 1)
    wide_got = [swap(wide[0], 2), swap(wide[2], 1)]
    normed_far = [swap(n, 0) for n in normed_group]
    blocks = narrow_grads(
        where, normed_group + normed_far, blocks + [swap(b, 0) for b in blocks], True
    )
    out_blocks = narrow_middle(where, out_blocks, [mixed.shape[1]], ctx)
    wide_got, out_blocks, blocks = stage(wide_got, out_blocks, blocks)

    blocks, out_blocks = plane_send(blocks), ctx_send(out_blocks, 1)
    grad_gate, grad_up, grad_down = wide_last(wide, wide_got, w_gate.shape[1] // ctx)
    blocks, out_blocks, grad_gate = stage(blocks, out_blocks, grad_gate)

    q_cols, k_cols = heads * head_dim // ctx, head_dim // ctx
    grad_query, grad_key, grad_value, grad_out, *gain_outs = narrow_last(
        blocks, out_blocks, sizes, (q_cols, k_cols, k_cols)
    )
    return (
        output,
        input_grad,
        grad_query,
        grad_key.T,
        grad_value.T,
        grad_out.T,
        grad_gate,
        grad_up,
        grad_down.T,
        *[g.reshape(-1) for g in gain_outs],
    )


def on_device(tokens, cotangent, lengths, *params):
    dp, ctx = lax.axis_size("dp"), lax.axis_size("ctx")
    each = tokens.shape[0] // lengths.shape[1]
    fits = dp == 8 and dp % ctx == 0 and tokens.shape[1] // dp % 16 == 0 and each % 16 == 0
    run = fused if fits else plain
    return run(tokens, cotangent, lengths, *params)


def solution(mesh):
    in_specs = (
        P(("dp", "ctx"), None),
        P(("dp", "ctx"), None),
        P("dp", None),
        P(("dp", "ctx"), None),
        P(("dp", "ctx"), None),
        P(("dp", "ctx"), None),
        P(("dp", "ctx"), None),
        P(("dp", "ctx"), None),
        P(("dp", "ctx"), None),
        P(("dp", "ctx"), None),
        P(("dp", "ctx")),
        P(("dp", "ctx")),
        P(("dp", "ctx")),
        P(("dp", "ctx")),
        P(("dp", "ctx")),
        P(("dp", "ctx")),
    )
    out_specs = (
        P(("dp", "ctx"), None),
        P(("dp", "ctx"), None),
        P("dp", "ctx"),
        P("dp", "ctx"),
        P("dp", "ctx"),
        P("ctx", "dp"),
        P("dp", "ctx"),
        P("dp", "ctx"),
        P("ctx", "dp"),
        P(("dp", "ctx")),
        P(("dp", "ctx")),
        P(("dp", "ctx")),
        P(("dp", "ctx")),
        P(("dp", "ctx")),
        P(("dp", "ctx")),
    )
    return jax.shard_map(
        on_device, mesh=mesh, in_specs=in_specs, out_specs=out_specs, check_vma=False
    )
```

```python
import jax
import jax.numpy as jnp
import numpy as np
from jax import lax
from jax.experimental import pallas as pl
from jax.experimental.pallas import tpu as pltpu
from jax.sharding import PartitionSpec as P

epsilon = 1e-06
rope_base = 1000000.0


def rms_norm(value, weight):
    scale = lax.rsqrt(jnp.mean(value * value, axis=-1, keepdims=True) + epsilon)
    return value * scale * (1.0 + weight)


def rms_back(value, weight, grad):
    scale = lax.rsqrt(jnp.mean(value * value, axis=-1, keepdims=True) + epsilon)
    normed = value * scale
    weighted = grad * (1.0 + weight)
    value_grad = scale * (weighted - normed * jnp.mean(weighted * normed, axis=-1, keepdims=True))
    weight_grad = jnp.sum(grad * normed, axis=tuple(range(value.ndim - 1)))
    return (value_grad, weight_grad)


def rope_tables(positions, width):
    half = width // 2
    freqs = jnp.power(rope_base, -2.0 * jnp.arange(half, dtype=jnp.float32) / width)
    angles = positions[:, None] * freqs[None, :]
    cosine = jnp.concatenate([jnp.cos(angles), jnp.cos(angles)], axis=-1)
    sine = jnp.concatenate([jnp.sin(angles), jnp.sin(angles)], axis=-1)
    return (cosine, sine)


def rotate(value, cosine, sine):
    half = value.shape[-1] // 2
    turned = jnp.concatenate([-value[..., half:], value[..., :half]], axis=-1)
    return value * cosine + turned * sine


def rotate_back(grad, cosine, sine):
    half = grad.shape[-1] // 2
    scaled = grad * sine
    return grad * cosine + jnp.concatenate([scaled[..., half:], -scaled[..., :half]], axis=-1)


def geglu(gate, upper):
    return jax.nn.gelu(gate, approximate=True) * upper


def dot(left, right, left_dim, right_dim):
    return lax.dot_general(
        left, right, (((left_dim,), (right_dim,)), ((), ())), preferred_element_type=jnp.float32
    )


def swap(value, bit):
    size = lax.axis_size("dp")
    return lax.ppermute(value, "dp", [(i, i ^ (1 << bit)) for i in range(size)])


def shift(value, step):
    size = lax.axis_size("ctx")
    return lax.ppermute(value, "ctx", [(i, (i + step) % size) for i in range(size)])


def pick(value, index, axis=0):
    return lax.dynamic_index_in_dim(value, index, axis, keepdims=False)


def plane_bits():
    return list(range(1, lax.axis_size("dp").bit_length() - 1))


def ctx_gather(value):
    return [value] + [shift(value, k) for k in range(1, lax.axis_size("ctx"))]


def ctx_ordered(pieces):
    size = lax.axis_size("ctx")
    stacked = jnp.stack(pieces)
    mine = lax.axis_index("ctx")
    return jnp.stack([pick(stacked, (mine - a + size) % size) for a in range(size)])


def ctx_reduce(pieces):
    total = pieces[0].astype(jnp.float32)
    for k in range(1, len(pieces)):
        total = total + shift(pieces[k].astype(jnp.bfloat16), -k).astype(jnp.float32)
    return total


def ctx_exchange(blocks):
    size = lax.axis_size("ctx")
    mine = lax.axis_index("ctx")
    return [pick(blocks, mine)] + [
        shift(pick(blocks, (mine + k) % size), k) for k in range(1, size)
    ]


def row_parts(rows, count):
    unit = 8 if rows % 8 == 0 else 1
    edges = [unit * (rows // unit * p // count) for p in range(count + 1)]
    return [(edges[p], edges[p + 1]) for p in range(count)]


def dp_gather(value):
    bits = plane_bits()
    plane = lax.axis_index("dp") // 2
    core = lax.axis_index("dp") % 2
    count = 1 << len(bits)
    parts = []
    for p, (low, high) in enumerate(row_parts(value.shape[0], len(bits))):
        current = value[None, low:high]
        masks = [0]
        for bit in bits[p:] + bits[:p]:
            current = jnp.concatenate([current, swap(current, bit)])
            masks = masks + [m ^ (1 << (bit - 1)) for m in masks]
        other = swap(current, 0)
        place = jnp.asarray([masks.index(m) for m in range(count)], jnp.int32)
        rows_of = []
        for a in range(count):
            at = pick(place, plane ^ a)
            first, second = pick(current, at), pick(other, at)
            rows_of.append(
                jnp.stack([lax.select(core == 0, first, second), lax.select(core == 0, second, first)])
            )
        parts.append(jnp.stack(rows_of))
    whole = jnp.concatenate(parts, axis=2)
    return whole.reshape((2 * count,) + value.shape)


def dp_reduce(kept, sent):
    bits = plane_bits()
    plane = lax.axis_index("dp") // 2
    total = (kept + swap(sent.astype(jnp.bfloat16), 0).astype(jnp.float32)).astype(jnp.bfloat16)
    parts = []
    for p, (low, high) in enumerate(row_parts(total.shape[1], len(bits))):
        current = total[:, low:high]
        current = current.reshape((2,) * len(bits) + current.shape[1:])
        left = sorted(bits, reverse=True)
        for bit in bits[p:] + bits[:p]:
            axis = left.index(bit)
            mine = (plane >> (bit - 1)) & 1
            got = swap(pick(current, 1 - mine, axis), bit)
            current = pick(current, mine, axis).astype(jnp.float32) + got.astype(jnp.float32)
            left.remove(bit)
            if left:
                current = current.astype(jnp.bfloat16)
        parts.append(current)
    return jnp.concatenate(parts, axis=0)


def columns_of(value, core):
    dp = lax.axis_size("dp")
    wide = value.reshape(value.shape[0], dp // 2, 2, value.shape[1] // dp)
    return pick(wide, core, 2).reshape(value.shape[0], -1)


def weight_grad(left, right, extra=None):
    core = lax.axis_index("dp") % 2
    dp = lax.axis_size("dp")
    blocks = []
    for side in (core, 1 - core):
        block = dot(columns_of(left, side), right, 0, 0)
        block = block.reshape(dp // 2, left.shape[1] // dp, right.shape[1])
        if extra is not None:
            block = jnp.concatenate([block, pick(extra, side, 1)], axis=1)
        blocks.append(block)
    return dp_reduce(blocks[0], blocks[1])


def plain(
    tokens,
    cotangent,
    lengths,
    w_query,
    w_key,
    w_value,
    w_out,
    w_gate,
    w_up,
    w_down,
    gain_in,
    gain_query,
    gain_key,
    gain_attn,
    gain_pre,
    gain_post,
):
    count, width = tokens.shape
    seq_count = lengths.shape[1]
    stretch = count // (2 * seq_count)
    dp = lax.axis_size("dp")
    ctx = lax.axis_size("ctx")
    mine = lax.axis_index("ctx")
    head_dim = w_key.shape[1]
    heads = w_query.shape[1] // head_dim
    inner = w_gate.shape[1] // ctx
    span = 2 * ctx * stretch
    offsets = jnp.arange(stretch, dtype=jnp.int32)

    def positions_of(index):
        return jnp.concatenate(
            [index * stretch + offsets, (2 * ctx - 1 - index) * stretch + offsets]
        )

    local_pos = positions_of(mine)
    valid = (local_pos[None, :] < lengths[0][:, None]).astype(jnp.float32).reshape(count, 1)
    cosine, sine = rope_tables(jnp.tile(local_pos, seq_count).astype(jnp.float32), head_dim)
    key_pos = jnp.concatenate([positions_of((mine - k + ctx) % ctx) for k in range(ctx)])
    query_pos = jnp.repeat(local_pos, heads)
    allowed = (key_pos[None, None, :] <= query_pos[None, :, None]) & (
        key_pos[None, None, :] < lengths[0][:, None, None]
    )
    inv_root = head_dim ** (-0.5)

    gains = [gain_in, gain_query, gain_key, gain_attn, gain_pre, gain_post]
    sizes = [g.shape[0] for g in gains]
    small = jnp.concatenate(gains)
    qkv_shard = jnp.concatenate([w_query, w_key, w_value], axis=1)
    in_rows, in_cols = qkv_shard.shape
    out_rows = w_out.shape[0]
    top = max(in_rows, out_rows)
    packed_rows = -(-(top + 1) // 8) * 8
    packed = jnp.concatenate(
        [
            jnp.pad(qkv_shard, ((0, top - in_rows), (0, 0))),
            jnp.pad(w_out, ((0, top - out_rows), (0, 0))),
        ],
        axis=1,
    )
    last = jnp.pad(small[None], ((0, packed_rows - top - 1), (0, packed.shape[1] - small.shape[0])))
    packed = jnp.concatenate([packed, last], axis=0)
    near = ctx_ordered(ctx_gather(packed)).reshape(ctx * packed_rows, -1)
    everything = dp_gather(near).reshape(dp * ctx, packed_rows, -1)
    full_qkv = everything[:, :in_rows, :in_cols].reshape(width, in_cols)
    full_out = everything[:, :out_rows, in_cols:].reshape(heads * head_dim, width)
    smalls = everything[:, top, : small.shape[0]]
    norms, start = [], 0
    for size in sizes:
        norms.append(smalls[:, start : start + size].reshape(-1).astype(jnp.float32))
        start += size
    norm_in, norm_query, norm_key, norm_attn, norm_pre, norm_post = norms

    def column_blocks(weight):
        return weight.reshape(weight.shape[0], ctx, inner).transpose(1, 0, 2)

    gate_up = jnp.stack([column_blocks(w_gate), column_blocks(w_up)], axis=1)
    gate_up = ctx_ordered(ctx_exchange(gate_up)).transpose(1, 0, 2, 3)
    gate_up = gate_up.reshape(2, width // dp, inner)
    per = dp // ctx
    down = w_down.T.reshape(dp, width // dp, w_down.shape[0])
    down = lax.all_to_all(down, "dp", split_axis=0, concat_axis=0, tiled=True)
    down = down.reshape(ctx, per, width // dp, w_down.shape[0])
    down = ctx_ordered(ctx_exchange(down))
    down = down.transpose(2, 1, 0, 3).reshape(width // dp, inner)
    full_gate = dp_gather(gate_up[0]).reshape(width, inner)
    full_up = dp_gather(gate_up[1]).reshape(width, inner)
    full_down = dp_gather(down).reshape(width, inner)

    hidden = tokens.astype(jnp.float32)
    normed = rms_norm(hidden, norm_in).astype(jnp.bfloat16)
    qkv_raw = dot(normed, full_qkv, 1, 0)
    query_raw = qkv_raw[:, : heads * head_dim]
    key_raw = qkv_raw[:, heads * head_dim : (heads + 1) * head_dim]
    value_raw = qkv_raw[:, (heads + 1) * head_dim :]
    query_heads = query_raw.reshape(count, heads, head_dim)
    query_bf = rotate(
        rms_norm(query_heads, norm_query), cosine[:, None, :], sine[:, None, :]
    ).astype(jnp.bfloat16)
    query_bf = query_bf.reshape(seq_count, 2 * stretch * heads, head_dim)
    key_bf = rotate(rms_norm(key_raw, norm_key), cosine, sine).astype(jnp.bfloat16)
    both = jnp.concatenate([key_bf, value_raw.astype(jnp.bfloat16)], axis=1)
    both = jnp.stack(
        [p.reshape(seq_count, 2 * stretch, 2 * head_dim) for p in ctx_gather(both)], axis=1
    ).reshape(seq_count, span, 2 * head_dim)
    keys, values = both[..., :head_dim], both[..., head_dim:]
    scores = (
        jnp.einsum("sqd,skd->sqk", query_bf, keys, preferred_element_type=jnp.float32) * inv_root
    )
    masked = jnp.where(allowed, scores, -1e30)
    peak = jnp.max(masked, axis=-1, keepdims=True)
    expo = jnp.exp(masked - peak)
    total = jnp.sum(expo, axis=-1, keepdims=True)
    probs = expo / total
    probs_bf = probs.astype(jnp.bfloat16)
    mixed = jnp.einsum("sqk,skd->sqd", probs_bf, values, preferred_element_type=jnp.float32)
    mixed_bf = mixed.astype(jnp.bfloat16).reshape(count, heads * head_dim)
    attn_raw = dot(mixed_bf, full_out, 1, 0)
    after_attn = hidden + valid * rms_norm(attn_raw, norm_attn)
    normed_two = rms_norm(after_attn, norm_pre).astype(jnp.bfloat16)

    group_two = jnp.concatenate(ctx_gather(normed_two))
    gate = dot(group_two, full_gate, 1, 0)
    upper = dot(group_two, full_up, 1, 0)
    inner_bf = geglu(gate, upper).astype(jnp.bfloat16)
    ffn_part = dot(inner_bf, full_down, 1, 1)
    ffn_raw = ctx_reduce(list(ffn_part.reshape(ctx, count, width)))
    output = (after_attn + valid * rms_norm(ffn_raw, norm_post)).astype(jnp.bfloat16)

    grad_top = cotangent.astype(jnp.float32)
    ffn_grad, grad_gain_post = rms_back(ffn_raw, norm_post, valid * grad_top)
    group_ffn = jnp.concatenate(ctx_gather(ffn_grad.astype(jnp.bfloat16)))
    inner_grad = dot(group_ffn, full_down, 1, 0)
    _, geglu_pull = jax.vjp(geglu, gate, upper)
    gate_grad, upper_grad = geglu_pull(inner_grad)
    gate_grad_bf = gate_grad.astype(jnp.bfloat16)
    upper_grad_bf = upper_grad.astype(jnp.bfloat16)
    two_part = dot(gate_grad_bf, full_gate, 1, 1) + dot(upper_grad_bf, full_up, 1, 1)
    normed_two_grad = ctx_reduce(list(two_part.reshape(ctx, count, width)))
    grad_down = weight_grad(group_ffn, inner_bf).T
    grad_gate = weight_grad(group_two, gate_grad_bf)
    grad_up = weight_grad(group_two, upper_grad_bf)

    through_pre, grad_gain_pre = rms_back(after_attn, norm_pre, normed_two_grad)
    after_grad = grad_top + through_pre
    attn_grad, grad_gain_attn = rms_back(attn_raw, norm_attn, valid * after_grad)
    attn_grad_bf = attn_grad.astype(jnp.bfloat16)
    grad_out = weight_grad(attn_grad_bf, mixed_bf)
    grad_out = sum_of_ctx(grad_out.reshape(grad_out.shape[0], ctx, -1).transpose(1, 0, 2)).T
    mixed_grad_bf = dot(attn_grad_bf, full_out, 1, 1).astype(jnp.bfloat16)
    mixed_grad_bf = mixed_grad_bf.reshape(seq_count, 2 * stretch * heads, head_dim)
    prob_grad = jnp.einsum(
        "sqd,skd->sqk", mixed_grad_bf, values, preferred_element_type=jnp.float32
    )
    row_dot = jnp.sum(probs * prob_grad, axis=-1, keepdims=True)
    score_grad_bf = (probs * (prob_grad - row_dot)).astype(jnp.bfloat16)
    query_grad = (
        jnp.einsum("sqk,skd->sqd", score_grad_bf, keys, preferred_element_type=jnp.float32)
        * inv_root
    )
    keys_grad = (
        jnp.einsum("sqk,sqd->skd", score_grad_bf, query_bf, preferred_element_type=jnp.float32)
        * inv_root
    )
    values_grad = jnp.einsum(
        "sqk,sqd->skd", probs_bf, mixed_grad_bf, preferred_element_type=jnp.float32
    )
    both_grad = jnp.concatenate([keys_grad, values_grad], axis=-1)
    both_grad = both_grad.reshape(seq_count, ctx, 2 * stretch, 2 * head_dim).transpose(1, 0, 2, 3)
    own_grad = ctx_reduce(list(both_grad.reshape(ctx, count, 2 * head_dim)))
    own_keys_grad, own_values_grad = own_grad[:, :head_dim], own_grad[:, head_dim:]
    query_grad = rotate_back(
        query_grad.reshape(count, heads, head_dim), cosine[:, None, :], sine[:, None, :]
    )
    query_raw_grad, grad_gain_query = rms_back(query_heads, norm_query, query_grad)
    query_raw_bf = query_raw_grad.reshape(count, heads * head_dim).astype(jnp.bfloat16)
    key_raw_grad, grad_gain_key = rms_back(
        key_raw, norm_key, rotate_back(own_keys_grad, cosine, sine)
    )
    key_raw_bf = key_raw_grad.astype(jnp.bfloat16)
    value_raw_bf = own_values_grad.astype(jnp.bfloat16)
    raw_bf = jnp.concatenate([query_raw_bf, key_raw_bf, value_raw_bf], axis=1)
    normed_grad = dot(raw_bf, full_qkv, 1, 1)
    through_in, grad_gain_in = rms_back(hidden, norm_in, normed_grad)
    input_grad = (after_grad + through_in).astype(jnp.bfloat16)

    by_ctx = jnp.concatenate(
        [r.reshape(count, ctx, -1) for r in (query_raw_bf, key_raw_bf, value_raw_bf)], axis=2
    )
    each = by_ctx.shape[2]
    gain_grads = jnp.concatenate(
        [
            g.reshape(dp * ctx, -1)
            for g in (
                grad_gain_in,
                grad_gain_query,
                grad_gain_key,
                grad_gain_attn,
                grad_gain_pre,
                grad_gain_post,
            )
        ],
        axis=1,
    )
    small_size = gain_grads.shape[1]
    extra = jnp.pad(gain_grads, ((0, 0), (0, each - small_size))).reshape(
        dp // 2, 2, 1, ctx * each
    )
    extra = jnp.pad(extra, ((0, 0), (0, 0), (0, 7), (0, 0)))
    grad_qkv = weight_grad(normed, by_ctx.reshape(count, ctx * each), extra)
    grad_qkv = sum_of_ctx(grad_qkv.reshape(grad_qkv.shape[0], ctx, each).transpose(1, 0, 2))
    rows = width // dp
    gain_out = grad_qkv[rows, :small_size]
    grad_qkv = grad_qkv[:rows]
    q_cols, k_cols = heads * head_dim // ctx, head_dim // ctx
    outs, start = [], 0
    for size in sizes:
        outs.append(gain_out[start : start + size])
        start += size
    return (
        output,
        input_grad,
        grad_qkv[:, :q_cols],
        grad_qkv[:, q_cols : q_cols + k_cols],
        grad_qkv[:, q_cols + k_cols :],
        grad_out,
        grad_gate,
        grad_up,
        grad_down,
        *outs,
    )


def sum_of_ctx(blocks):
    size = lax.axis_size("ctx")
    mine = lax.axis_index("ctx")
    total = pick(blocks, mine).astype(jnp.float32)
    for k in range(1, size):
        got = shift(pick(blocks, (mine + k) % size).astype(jnp.bfloat16), k)
        total = total + got.astype(jnp.float32)
    return total


mega = 2**20
whole_vmem = 121 * mega // 2


def place(name):
    return {"vmem": pl.BlockSpec(memory_space=pltpu.VMEM), "smem": pl.BlockSpec(memory_space=pltpu.SMEM), "any": pl.BlockSpec(memory_space=pl.ANY)}[name]


def kernel_call(body, outs, args, where=None, scratch=(), out_where=None, grant=40 * mega):
    where, out_where = where or {}, out_where or {}
    return pl.pallas_call(
        body,
        out_shape=[jax.ShapeDtypeStruct(s, t) for s, t in outs],
        in_specs=[place(where.get(i, "vmem")) for i in range(len(args))],
        out_specs=[place(out_where.get(i, "vmem")) for i in range(len(outs))],
        scratch_shapes=list(scratch),
        compiler_params=pltpu.CompilerParams(vmem_limit_bytes=grant),
        cost_estimate=pl.CostEstimate(flops=0, bytes_accessed=0, transcendentals=0),
    )(*args)


def norm_back(value, weight, grad):
    scale = lax.rsqrt(jnp.mean(value * value, axis=-1, keepdims=True) + epsilon)
    normed = value * scale
    weighted = grad * (1.0 + weight)
    value_grad = scale * (weighted - normed * jnp.mean(weighted * normed, axis=-1, keepdims=True))
    return value_grad, jnp.sum(grad * normed, axis=0, keepdims=True)


def spread(index, tails, lane, size, ctx):
    dp = len(tails)
    shards = jnp.concatenate([t[:, lane : lane + 128] for t, _ in tails], axis=0)
    tail = shards.shape[0] // dp
    whole = dp * ctx * size
    column = lax.broadcasted_iota(jnp.int32, (128, whole), 1)
    line = lax.broadcasted_iota(jnp.int32, (128, whole), 0)
    spots = jnp.where(column % size == line, 1.0, 0.0).astype(jnp.bfloat16)
    values = dot(shards, spots, 1, 0)
    column = lax.broadcasted_iota(jnp.int32, (tail, whole), 1) // size
    line = lax.broadcasted_iota(jnp.int32, (tail, whole), 0)
    total = jnp.zeros((tail, whole), jnp.float32)
    for k, (_, mask) in enumerate(tails):
        owner = jnp.where(line < ctx, (index ^ mask) * ctx + line, -1)
        total = total + jnp.where(column == owner, values[k * tail : (k + 1) * tail], 0.0)
    return jnp.sum(total, axis=0, keepdims=True)


def pack(where, w_query, w_key, w_value, w_out, w_down, gains):
    part, width = w_down.shape
    chunk = width // 8
    rows = w_query.shape[0]
    parts = [w_query, w_key, w_value, w_out]
    ends = [int(e) for e in np.cumsum([0] + [p.shape[1] for p in parts])]
    tall = -(-max(rows + 1, w_out.shape[0]) // 8) * 8

    def body(where_ref, down_ref, *rest):
        shards, lines = rest[: len(parts)], rest[len(parts) : len(parts) + len(gains)]
        out, *downs, wide, turned = rest[len(parts) + len(gains) :]
        turned[...] = down_ref[...].T
        plane, core = where_ref[0] // 2, where_ref[1]
        for flip, ref in enumerate(downs):
            for m in range(4):
                group = jnp.bitwise_xor(plane, m) * 2 + jnp.bitwise_xor(core, flip)
                ref[m] = turned[pl.ds(pl.multiple_of(group * chunk, 16), chunk), :]
        wide[...] = jnp.zeros(wide.shape, jnp.float32)
        for i, shard in enumerate(shards):
            wide[: shard.shape[0], ends[i] : ends[i + 1]] = shard[...].astype(jnp.float32)
        for i, line in enumerate(lines):
            wide[rows : rows + 1, i * 128 : i * 128 + line.shape[1]] = line[...].astype(
                jnp.float32
            )
        out[...] = wide[...].astype(jnp.bfloat16)

    return kernel_call(
        body,
        [((tall, ends[-1]), jnp.bfloat16)] + [((4, chunk, part), jnp.bfloat16)] * 2,
        [where, w_down, *parts, *[g.reshape(1, -1) for g in gains]],
        {0: "smem"},
        [pltpu.VMEM((tall, ends[-1]), jnp.float32), pltpu.VMEM((width, part), jnp.bfloat16)],
        grant=whole_vmem,
    )


def tables(where, lengths, count, stretch, ctx, head_dim):
    seqs = lengths.shape[1]
    each, half = count // seqs, head_dim // 2
    span = 2 * ctx * stretch
    freqs = rope_base ** (-2.0 * np.arange(half, dtype=np.float64) / head_dim)
    freqs = jnp.asarray(freqs[None].astype(np.float32))

    def positions(index, owner):
        block, step = index // stretch % 2, index % stretch
        return jnp.where(block == 0, owner, 2 * ctx - 1 - owner) * stretch + step

    def body(where_ref, lengths_ref, freqs_ref, cos_out, sin_out, valid_out, allowed_out):
        mine = where_ref[4]
        rows = lax.broadcasted_iota(jnp.int32, (each, 1), 0)
        local = positions(rows, mine)
        angles = local.astype(jnp.float32) * freqs_ref[...]
        cos, sin = jnp.cos(angles), jnp.sin(angles)
        cols = lax.broadcasted_iota(jnp.int32, (1, span), 1)
        owner = (mine - cols // each + ctx) % ctx
        keys = positions(cols % each, owner)
        for s in range(seqs):
            part = slice(s * each, (s + 1) * each)
            for low, high in ((0, half), (half, head_dim)):
                cos_out[part, low:high] = cos
                sin_out[part, low:high] = sin
            length = lengths_ref[0, s]
            valid_out[part, :] = jnp.where(local < length, 1.0, 0.0)
            allowed_out[s] = jnp.where((keys <= local) & (keys < length), 1.0, 0.0)

    return kernel_call(
        body,
        [
            ((count, head_dim), jnp.float32),
            ((count, head_dim), jnp.float32),
            ((count, 1), jnp.float32),
            ((seqs, each, span), jnp.float32),
        ],
        [where, lengths, freqs],
        {0: "smem", 1: "smem"},
    )


def plane_near(value):
    return [value, swap(value, 1), swap(value, 2)]


def cut(near):
    row = near[0].ndim - 2
    first = halves_of(near[0].shape[row])[0]
    low = lax.slice_in_dim(near[1], 0, first, axis=row)
    high = lax.slice_in_dim(near[2], first, None, axis=row)
    return [low, high]


def diagonal(halves):
    return [swap(halves[0], 2), swap(halves[1], 1)]


def plane_whole(near):
    pieces = near + diagonal(cut(near))
    return pieces + [swap(p, 0) for p in pieces]


def late_gains(where, pieces, lanes, sizes, ctx, behind):
    tall = pieces[0].shape[0]

    def body(where_ref, behind_ref, *rest):
        parts, outs = rest[: len(pieces)], rest[len(pieces) :]
        tails = tails_of(parts, tall)
        for out, lane, size in zip(outs, lanes, sizes):
            out[...] = spread(where_ref[0], tails, lane, size, ctx)

    return kernel_call(
        body,
        [((1, len(tails_of([np.zeros((tall, 1))] * len(pieces), tall)) * ctx * size), jnp.float32) for size in sizes],
        [where, behind, *pieces],
        {0: "smem", 1: "any"},
    )


def project(where, tokens, pieces, sizes, cosine, sine, heads, ctx):
    count, width = tokens.shape
    tall = pieces[0].shape[0]
    head_dim = cosine.shape[1]
    wide = (heads + 2) * head_dim
    total = len(pieces)

    def body(where_ref, x_ref, cos_ref, sin_ref, *rest):
        parts = rest[:total]
        normed_ref, query_out, both_out, raw_out, in_ref, query_ref, key_ref = rest[total : total + 7]
        weight, ends, sems, end_sems = rest[total + 7 :]
        copies = load_columns(where_ref[0], parts, tall, tall - 16, 0, weight, sems)
        tails = [
            (ref, mask, rows) for ref, mask, at, rows in pieces_of(parts, tall) if at + rows == tall
        ]
        end_copies = [
            pltpu.make_async_copy(
                ref.at[pl.ds(rows - 16, 16), pl.ds(0, ends.shape[2])], ends.at[i], end_sems.at[i]
            )
            for i, (ref, _, rows) in enumerate(tails)
        ]
        for copy in end_copies:
            copy.start()
        for copy in end_copies:
            copy.wait()
        tails = [(ends[i], mask) for i, (_, mask, _) in enumerate(tails)]
        for i, ref in enumerate((in_ref, query_ref, key_ref)):
            ref[...] = spread(where_ref[0], tails, i * 128, sizes[i], ctx)
        normed = rms_norm(x_ref[...].astype(jnp.float32), in_ref[...]).astype(jnp.bfloat16)
        normed_ref[...] = normed
        cos, sin = cos_ref[...], sin_ref[...]
        for copy in copies:
            copy.wait()
        for h in range(heads + 1):
            cols = slice(h * head_dim, (h + 1) * head_dim)
            raw = dot(normed, weight[:, cols], 1, 0)
            raw_out[:, cols] = raw
            gain = query_ref[...] if h < heads else key_ref[...]
            turned = rotate(rms_norm(raw, gain), cos, sin).astype(jnp.bfloat16)
            if h < heads:
                query_out[:, cols] = turned
            else:
                both_out[:, :head_dim] = turned
        both_out[:, head_dim:] = dot(normed, weight[:, (heads + 1) * head_dim :], 1, 0).astype(
            jnp.bfloat16
        )

    return kernel_call(
        body,
        [
            ((count, width), jnp.bfloat16),
            ((count, heads * head_dim), jnp.bfloat16),
            ((count, 2 * head_dim), jnp.bfloat16),
            ((count, (heads + 1) * head_dim), jnp.float32),
            ((1, width), jnp.float32),
            ((1, head_dim), jnp.float32),
            ((1, head_dim), jnp.float32),
        ],
        [where, tokens, cosine, sine, *pieces],
        {0: "smem", **{4 + i: "any" for i in range(total)}},
        [
            pltpu.VMEM((width, wide), jnp.bfloat16),
            pltpu.VMEM((8, 16, 384), jnp.bfloat16),
            pltpu.SemaphoreType.DMA((total,)),
            pltpu.SemaphoreType.DMA((8,)),
        ],
    )


def attend(
    where, tokens, query, both, allowed, valid, norm_attn, norm_pre, pieces, out_rows, heads
):
    count, width = tokens.shape
    seqs, each, span = allowed.shape
    head_dim = query.shape[1] // heads
    inv_root = head_dim ** (-0.5)
    near, total = len(both), len(pieces)
    tall, wide = pieces[0].shape

    def body(where_ref, x_ref, query_ref, allowed_ref, valid_ref, attn_ref, pre_ref, *rest):
        got, parts = rest[:near], rest[near : near + total]
        probs_out, mixed_out, raw_out, after_out, two_out, weight, sems = rest[near + total :]
        copies = load_columns(where_ref[0], parts, tall, out_rows, wide - width, weight, sems)
        for s in range(seqs):
            rows = slice(s * each, (s + 1) * each)
            queries = jnp.concatenate(
                [query_ref[rows, h * head_dim : (h + 1) * head_dim] for h in range(heads)], axis=0
            )
            keys = jnp.concatenate([g[rows, :head_dim] for g in got], axis=0)
            values = jnp.concatenate([g[rows, head_dim:] for g in got], axis=0)
            scores = dot(queries, keys, 1, 1) * inv_root
            keep = jnp.concatenate([allowed_ref[s]] * heads, axis=0)
            scores = jnp.where(keep > 0.0, scores, -1e30)
            expo = jnp.exp(scores - jnp.max(scores, axis=-1, keepdims=True))
            probs = expo / jnp.sum(expo, axis=-1, keepdims=True)
            probs_out[s] = probs
            mixed = dot(probs.astype(jnp.bfloat16), values, 1, 0).astype(jnp.bfloat16)
            for h in range(heads):
                mixed_out[rows, h * head_dim : (h + 1) * head_dim] = mixed[
                    h * each : (h + 1) * each
                ]
        for copy in copies:
            copy.wait()
        raw = dot(mixed_out[...], weight[...], 1, 0)
        raw_out[...] = raw
        after = x_ref[...].astype(jnp.float32) + valid_ref[...] * rms_norm(raw, attn_ref[...])
        after_out[...] = after
        two_out[...] = rms_norm(after, pre_ref[...]).astype(jnp.bfloat16)

    return kernel_call(
        body,
        [
            ((seqs, heads * each, span), jnp.float32),
            ((count, heads * head_dim), jnp.bfloat16),
            ((count, width), jnp.float32),
            ((count, width), jnp.float32),
            ((count, width), jnp.bfloat16),
        ],
        [where, tokens, query, allowed, valid, norm_attn, norm_pre, *both, *pieces],
        {0: "smem", **{7 + near + i: "any" for i in range(total)}},
        [
            pltpu.VMEM((heads * head_dim, width), jnp.bfloat16),
            pltpu.SemaphoreType.DMA((total,)),
        ],
    )


def column_steps(size, step):
    return [(s, min(size, s + step)) for s in range(0, size, step)]


def halves_of(rows):
    first = -(-rows // 32) * 16
    return first, rows - first


def pieces_of(refs, chunk):
    parts, far = refs[: len(refs) // 2], refs[len(refs) // 2 :]
    first, second = halves_of(chunk)
    shapes = [(0, 0, chunk), (2, 0, chunk), (4, 0, chunk), (6, 0, first), (6, first, second)]
    return [(ref, mask, at, rows) for ref, (mask, at, rows) in zip(parts, shapes)] + [
        (ref, mask ^ 1, at, rows) for ref, (mask, at, rows) in zip(far, shapes)
    ]


def load_weights(index, pair, last, chunk, target, sems):
    def copies(m):
        result = []
        for i, (ref, mask, at, rows) in enumerate(pieces_of(last if m == 2 else pair, chunk)):
            start = pl.multiple_of((index ^ mask) * chunk + at, 16)
            result.append(
                pltpu.make_async_copy(
                    ref if m == 2 else ref.at[m], target.at[m, pl.ds(start, rows)], sems.at[m, i]
                )
            )
        return result

    return [copies(m) for m in range(target.shape[0])]


def load_columns(index, refs, tall, rows, first, target, sems):
    copies = []
    for i, (ref, mask, at, size) in enumerate(pieces_of(refs, tall)):
        size = min(size, rows - at)
        if size > 0:
            start = pl.multiple_of((index ^ mask) * rows + at, 16)
            copies.append(
                pltpu.make_async_copy(
                    ref.at[pl.ds(0, size), pl.ds(first, target.shape[1])],
                    target.at[pl.ds(start, size)],
                    sems.at[i],
                )
            )
    for copy in copies:
        copy.start()
    return copies


def tails_of(refs, tall):
    return [
        (ref[rows - 16 : rows], mask) for ref, mask, at, rows in pieces_of(refs, tall) if at + rows == tall
    ]


def feed_forward(where, pieces, weights, with_own):
    count, width = pieces[0].shape
    (pair, last), kinds = weights, 3
    _, chunk, inner = pair[0].shape
    lanes = -(-inner // 128) * 128
    near, spots = len(pieces), len(pair)
    total = near * count
    slope = (2.0 / np.pi) ** 0.5

    def body(where_ref, *rest):
        pair_refs, last_refs, rest = rest[:spots], rest[spots : 2 * spots], rest[2 * spots :]
        parts, outs, sums = rest[:near], rest[near : near + 3], rest[near + 3 : near + 3 + near]
        weight, group, act, slopes, gates, sems, out_sems = rest[near + 3 + near :]
        copies = load_weights(where_ref[0], pair_refs, last_refs, chunk, weight, sems)
        for kind in copies:
            for copy in kind:
                copy.start()
        for k in range(near):
            group[k * count : (k + 1) * count, :] = parts[k][...]
        stores = [
            pltpu.make_async_copy(source, out, out_sems.at[i])
            for i, (source, out) in enumerate(zip((group, act, slopes), outs))
        ]
        stores[0].start()
        for copy in copies[0]:
            copy.wait()
        for low, high in column_steps(inner, 256):
            gates[:, low:high] = dot(group[...], weight[0, :, low:high], 1, 0)
        for copy in copies[1]:
            copy.wait()
        for low, high in column_steps(inner, 256):
            gate = gates[:, low:high]
            upper = dot(group[...], weight[1, :, low:high], 1, 0)
            square = 0.044715 * slope * gate * gate
            half = 0.5 + 0.5 * jnp.tanh(gate * (slope + square))
            gelu = gate * half
            steep = half * (1.0 + 2.0 * (gate - gelu) * (slope + 3.0 * square))
            act[:, low:high] = (gelu * upper).astype(jnp.bfloat16)
            slopes[0, :, low:high] = (steep * upper).astype(jnp.bfloat16)
            slopes[1, :, low:high] = gelu.astype(jnp.bfloat16)
        if lanes > inner:
            act[:, inner:] = jnp.zeros((total, lanes - inner), jnp.bfloat16)
        for store in stores[1:]:
            store.start()
        for copy in copies[2]:
            copy.wait()
        for low, high in column_steps(width, 256):
            part = dot(act[:, :inner], weight[2, low:high, :], 1, 1)
            for k in range(near):
                sums[k][:, low:high] = part[k * count : (k + 1) * count].astype(sums[k].dtype)
        for store in stores:
            store.wait()

    return kernel_call(
        body,
        [
            ((total, width), jnp.bfloat16),
            ((total, lanes), jnp.bfloat16),
            ((2, total, inner), jnp.bfloat16),
        ]
        + [((count, width), jnp.float32 if with_own and k == 0 else jnp.bfloat16) for k in range(near)],
        [where, *pair, *last, *pieces],
        {0: "smem", **{1 + i: "any" for i in range(2 * spots)}},
        [
            pltpu.VMEM((kinds, width, inner), jnp.bfloat16),
            pltpu.VMEM((total, width), jnp.bfloat16),
            pltpu.VMEM((total, lanes), jnp.bfloat16),
            pltpu.VMEM((2, total, inner), jnp.bfloat16),
            pltpu.VMEM((total, inner), jnp.float32),
            pltpu.SemaphoreType.DMA((kinds, spots)),
            pltpu.SemaphoreType.DMA((3,)),
        ],
        {i: "any" for i in range(3)},
        grant=whole_vmem,
    )


def finish(parts, after, cotangent, valid, norm_post):
    count, width = after.shape
    near = len(parts)

    def body(after_ref, cot_ref, valid_ref, post_ref, *rest):
        got = rest[:near]
        output_out, grad_out, gain_out = rest[near:]
        raw = got[0][...]
        for g in got[1:]:
            raw = raw + g[...].astype(jnp.float32)
        ok = valid_ref[...]
        output_out[...] = (after_ref[...] + ok * rms_norm(raw, post_ref[...])).astype(jnp.bfloat16)
        grad, gain = norm_back(raw, post_ref[...], ok * cot_ref[...].astype(jnp.float32))
        grad_out[...] = grad.astype(jnp.bfloat16)
        gain_out[...] = gain

    return kernel_call(
        body,
        [
            ((count, width), jnp.bfloat16),
            ((count, width), jnp.bfloat16),
            ((1, width), jnp.float32),
        ],
        [after, cotangent, valid, norm_post, *parts],
        grant=whole_vmem,
    )


def feed_back(where, pieces, weights, slopes, with_own):
    count, width = pieces[0].shape
    (pair, last), kinds = weights, 3
    _, chunk, inner = pair[0].shape
    lanes = -(-inner // 128) * 128
    near, spots = len(pieces), len(pair)
    total = near * count

    def body(where_ref, slopes_ref, *rest):
        pair_refs, last_refs, rest = rest[:spots], rest[spots : 2 * spots], rest[2 * spots :]
        parts = rest[:near]
        group_out, both_out = rest[near : near + 2]
        sums = rest[near + 2 : near + 2 + near]
        weight, sems = rest[near + 2 + near :]
        copies = load_weights(where_ref[0], pair_refs, last_refs, chunk, weight, sems)
        for kind in (copies[2], copies[0], copies[1]):
            for copy in kind:
                copy.start()
        for k in range(near):
            group_out[k * count : (k + 1) * count, :] = parts[k][...]
        for copy in copies[2]:
            copy.wait()
        for low, high in column_steps(inner, 256):
            grad = dot(group_out[...], weight[2, :, low:high], 1, 0)
            for i in range(2):
                slope = slopes_ref[i, :, low:high].astype(jnp.float32)
                both_out[i, :, low:high] = (grad * slope).astype(jnp.bfloat16)
        if lanes > inner:
            both_out[:, :, inner:] = jnp.zeros((2, total, lanes - inner), jnp.bfloat16)
        for kind in copies[:2]:
            for copy in kind:
                copy.wait()
        for low, high in column_steps(width, 256):
            part = dot(both_out[0, :, :inner], weight[0, low:high, :], 1, 1)
            part = part + dot(both_out[1, :, :inner], weight[1, low:high, :], 1, 1)
            for k in range(near):
                sums[k][:, low:high] = part[k * count : (k + 1) * count].astype(sums[k].dtype)

    return kernel_call(
        body,
        [((total, width), jnp.bfloat16)]
        + [((2, total, lanes), jnp.bfloat16)]
        + [((count, width), jnp.float32 if with_own and k == 0 else jnp.bfloat16) for k in range(near)],
        [where, slopes, *pair, *last, *pieces],
        {0: "smem", **{2 + i: "any" for i in range(2 * spots)}},
        [
            pltpu.VMEM((kinds, width, inner), jnp.bfloat16),
            pltpu.SemaphoreType.DMA((kinds, spots)),
        ],
        grant=whole_vmem,
    )


def wide_grads(where, lefts, rights):
    width = lefts[0].shape[1]
    total = sum(left.shape[0] for left in lefts)
    lanes = rights[0][0][0].shape[-1]
    kinds = len(rights)
    chunk = width // 8
    first, second = halves_of(chunk)
    arrays = []
    for array in [r for right in rights for r, _ in right]:
        if all(array is not other for other in arrays):
            arrays.append(array)
    spots = [[[array is other for other in arrays].index(True) for array, _ in right] for right in rights]
    most = max(len(right) for right in rights)

    def body(where_ref, *rest):
        left_refs, right_refs = rest[: len(lefts)], rest[len(lefts) : len(lefts) + len(arrays)]
        outs = rest[len(lefts) + len(arrays) : len(lefts) + len(arrays) + 4]
        turned, left, values, sems = rest[len(lefts) + len(arrays) + 4 :]
        copies = []
        for m, right in enumerate(rights):
            at, row = [], 0
            for i, (array, index) in enumerate(right):
                ref = right_refs[spots[m][i]]
                size = array.shape[-2]
                at.append(
                    pltpu.make_async_copy(
                        ref if index is None else ref.at[index],
                        values.at[m, pl.ds(row, size)],
                        sems.at[m, i],
                    )
                )
                row += size
            copies.append(at)
        for part in copies:
            for copy in part:
                copy.start()
        core, x, y = where_ref[1], where_ref[2], where_ref[3]
        order = []
        for flip in (1, 0):
            order.append([(j * 2 + jnp.bitwise_xor(x, flip), 0, first) for j in range(2)])
        for flip in (1, 0):
            order.append([(jnp.bitwise_xor(y, flip) * 2 + j, first, second) for j in range(2)])
        row = 0
        for ref in left_refs:
            turned[:, row : row + ref.shape[0]] = ref[...].T
            row += ref.shape[0]
        at = 0
        for block in order:
            for plane, offset, size in block:
                start = pl.multiple_of((plane * 2 + core) * chunk + offset, 16)
                left[at : at + size, :] = turned[pl.ds(start, size), :]
                at += size
        for m in range(kinds):
            for copy in copies[m]:
                copy.wait()
            for low, high in column_steps(lanes, 256):
                part = dot(left[...], values[m, :, low:high], 1, 0).astype(jnp.bfloat16)
                at = 0
                for out, block in zip(outs, order):
                    size = 2 * block[0][2]
                    out[m, :, low:high] = part[at : at + size]
                    at += size

    return kernel_call(
        body,
        [
            ((kinds, 2 * first, lanes), jnp.bfloat16),
            ((kinds, 2 * first, lanes), jnp.bfloat16),
            ((kinds, 2 * second, lanes), jnp.bfloat16),
            ((kinds, 2 * second, lanes), jnp.bfloat16),
        ],
        [where, *lefts, *arrays],
        {0: "smem", **{1 + len(lefts) + i: "any" for i in range(len(arrays))}},
        [
            pltpu.VMEM((width, total), jnp.bfloat16),
            pltpu.VMEM((width // 2, total), jnp.bfloat16),
            pltpu.VMEM((kinds, total, lanes), jnp.bfloat16),
            pltpu.SemaphoreType.DMA((kinds, most)),
        ],
        grant=whole_vmem,
    )


def wide_middle(where, wides, gots):
    sizes = [wide[0].shape[0] for wide in wides]
    kinds = sum(sizes)
    first, second = wides[0][1].shape[1] // 2, wides[0][3].shape[1] // 2
    lanes = wides[0][1].shape[2]
    args = [a for wide, got in zip(wides, gots) for a in (wide[1], got[0], wide[3], got[1])]

    def body(where_ref, *rest):
        refs, outs = rest[: len(args)], rest[len(args) :]
        x, y = where_ref[2], where_ref[3]
        at = 0
        for i, size in enumerate(sizes):
            kept_a, got_a, kept_b, got_b = refs[4 * i : 4 * i + 4]
            for m in range(size):
                for kept, got, place, rows, pair in (
                    (kept_a, got_a, y, first, outs[:2]),
                    (kept_b, got_b, x, second, outs[2:]),
                ):
                    for flip, out in ((1, pair[0]), (0, pair[1])):
                        spot = pl.ds(
                            pl.multiple_of(jnp.bitwise_xor(place, flip) * rows, 16), rows
                        )
                        total = kept[m, spot, :].astype(jnp.float32) + got[m, spot, :].astype(
                            jnp.float32
                        )
                        out[at] = total.astype(jnp.bfloat16)
                at += 1

    return kernel_call(
        body,
        [((kinds, first, lanes), jnp.bfloat16)] * 2 + [((kinds, second, lanes), jnp.bfloat16)] * 2,
        [where, *args],
        {0: "smem"},
    )


def wide_last(wide, got, inner):
    (_, kept_a, _, kept_b), (got_a, got_b) = wide, got
    kinds, first, _ = kept_a.shape
    second = kept_b.shape[1]

    def body(kept_a_ref, got_a_ref, kept_b_ref, got_b_ref, *outs):
        for m in range(kinds):
            total = kept_a_ref[m].astype(jnp.float32) + got_a_ref[m].astype(jnp.float32)
            outs[m][:first, :] = total[:, :inner]
            total = kept_b_ref[m].astype(jnp.float32) + got_b_ref[m].astype(jnp.float32)
            outs[m][first:, :] = total[:, :inner]

    return kernel_call(
        body,
        [((first + second, inner), jnp.float32)] * kinds,
        [kept_a, got_a, kept_b, got_b],
    )


def attend_back(
    where,
    parts,
    after,
    cotangent,
    valid,
    attn_raw,
    norm_pre,
    norm_attn,
    norm_query,
    probs,
    query,
    raw,
    both,
    pieces,
    out_rows,
    cosine,
    sine,
    heads,
):
    count, width = after.shape
    seqs, _, span = probs.shape
    each = count // seqs
    head_dim = norm_query.shape[1]
    inv_root = head_dim ** (-0.5)
    near, spots = len(both), len(pieces)
    tall, wide = pieces[0].shape

    def body(
        where_ref,
        after_ref,
        cot_ref,
        valid_ref,
        attn_ref,
        pre_ref,
        norm_ref,
        query_gain_ref,
        probs_ref,
        query_ref,
        raw_ref,
        cos_ref,
        sin_ref,
        *rest,
    ):
        shards, rest = rest[:spots], rest[spots:]
        sums = rest[:near]
        got = rest[near : 2 * near]
        rest = rest[2 * near :]
        dx_out, attn_grad_out, raw_grad_out, pre_out, attn_gain_out, query_gain_out = rest[:6]
        both_outs = rest[6 : 6 + near]
        mixed_grad, query_grad, weight, sems = rest[6 + near :]
        copies = load_columns(where_ref[0], shards, tall, out_rows, wide - width, weight, sems)
        grad = sums[0][...]
        for s in sums[1:]:
            grad = grad + s[...].astype(jnp.float32)
        through, gain = norm_back(after_ref[...], pre_ref[...], grad)
        pre_out[...] = gain
        dx = cot_ref[...].astype(jnp.float32) + through
        dx_out[...] = dx
        attn_grad, gain = norm_back(attn_ref[...], norm_ref[...], valid_ref[...] * dx)
        attn_gain_out[...] = gain
        attn_grad = attn_grad.astype(jnp.bfloat16)
        attn_grad_out[...] = attn_grad
        for copy in copies:
            copy.wait()
        mixed_grad[...] = dot(attn_grad, weight[...], 1, 1).astype(jnp.bfloat16)
        for s in range(seqs):
            rows = slice(s * each, (s + 1) * each)
            queries = jnp.concatenate(
                [query_ref[rows, h * head_dim : (h + 1) * head_dim] for h in range(heads)], axis=0
            )
            grads = jnp.concatenate(
                [mixed_grad[rows, h * head_dim : (h + 1) * head_dim] for h in range(heads)], axis=0
            )
            keys = jnp.concatenate([g[rows, :head_dim] for g in got], axis=0)
            values = jnp.concatenate([g[rows, head_dim:] for g in got], axis=0)
            probs = probs_ref[s]
            prob_grad = dot(grads, values, 1, 1)
            row = jnp.sum(probs * prob_grad, axis=-1, keepdims=True)
            score_grad = (probs * (prob_grad - row)).astype(jnp.bfloat16)
            back = dot(score_grad, keys, 1, 0) * inv_root
            for h in range(heads):
                query_grad[rows, h * head_dim : (h + 1) * head_dim] = back[
                    h * each : (h + 1) * each
                ]
            keys_grad = dot(score_grad, queries, 0, 0) * inv_root
            values_grad = dot(probs.astype(jnp.bfloat16), grads, 0, 0)
            for k in range(near):
                part = slice(k * each, (k + 1) * each)
                both_outs[k][rows, :head_dim] = keys_grad[part].astype(both_outs[k].dtype)
                both_outs[k][rows, head_dim:] = values_grad[part].astype(both_outs[k].dtype)
        cos, sin = cos_ref[...], sin_ref[...]
        gain_sum = jnp.zeros((1, head_dim), jnp.float32)
        for h in range(heads):
            cols = slice(h * head_dim, (h + 1) * head_dim)
            turned = rotate_back(query_grad[:, cols], cos, sin)
            value_grad, gain = norm_back(raw_ref[:, cols], query_gain_ref[...], turned)
            raw_grad_out[:, cols] = value_grad.astype(jnp.bfloat16)
            gain_sum = gain_sum + gain
        query_gain_out[...] = gain_sum

    return kernel_call(
        body,
        [
            ((count, width), jnp.float32),
            ((count, width), jnp.bfloat16),
            ((count, heads * head_dim), jnp.bfloat16),
            ((1, width), jnp.float32),
            ((1, width), jnp.float32),
            ((1, head_dim), jnp.float32),
            ((count, 2 * head_dim), jnp.float32),
        ]
        + [((count, 2 * head_dim), jnp.bfloat16)] * (near - 1),
        [
            where,
            after,
            cotangent,
            valid,
            attn_raw,
            norm_pre,
            norm_attn,
            norm_query,
            probs,
            query,
            raw,
            cosine,
            sine,
            *pieces,
            *parts,
            *both,
        ],
        {0: "smem", **{13 + i: "any" for i in range(spots)}},
        [
            pltpu.VMEM((count, heads * head_dim), jnp.bfloat16),
            pltpu.VMEM((count, heads * head_dim), jnp.float32),
            pltpu.VMEM((heads * head_dim, width), jnp.bfloat16),
            pltpu.SemaphoreType.DMA((spots,)),
        ],
        grant=whole_vmem,
    )


def project_back(
    where,
    parts,
    raw,
    query_grad,
    tokens,
    dx,
    norm_in,
    norm_key,
    cosine,
    sine,
    pieces,
    heads,
    ctx,
    gains,
):
    count, width = tokens.shape
    tall_piece = pieces[0].shape[0]
    head_dim = norm_key.shape[1]
    wide = (heads + 2) * head_dim
    near, spots, total = len(parts), len(pieces), 8
    each = wide // ctx
    count_gains = len(gains)
    tall = count + 16

    def body(
        where_ref, raw_ref, query_ref, x_ref, dx_ref, in_ref, key_ref, cos_ref, sin_ref, *rest
    ):
        sums = rest[:near]
        shards = rest[near : near + spots]
        others = rest[near + spots : near + spots + count_gains]
        input_out = rest[near + spots + count_gains]
        outs = rest[near + spots + count_gains + 1 : near + spots + count_gains + 1 + ctx]
        weight, grads_out, gains_out, sems = rest[near + spots + count_gains + 1 + ctx :]
        copies = load_columns(
            where_ref[0], shards, tall_piece, tall_piece - 16, 0, weight, sems
        )
        grad = sums[0][...]
        for s in sums[1:]:
            grad = grad + s[...].astype(jnp.float32)
        turned = rotate_back(grad[:, :head_dim], cos_ref[...], sin_ref[...])
        key_grad, key_gain = norm_back(raw_ref[:, heads * head_dim :], key_ref[...], turned)
        grads_out[:, : heads * head_dim] = query_ref[...]
        grads_out[:, heads * head_dim : (heads + 1) * head_dim] = key_grad.astype(jnp.bfloat16)
        grads_out[:, (heads + 1) * head_dim :] = grad[:, head_dim:].astype(jnp.bfloat16)
        for copy in copies:
            copy.wait()
        back = dot(grads_out[...], weight[...], 1, 1)
        through, in_gain = norm_back(x_ref[...].astype(jnp.float32), in_ref[...], back)
        input_out[...] = (dx_ref[...] + through).astype(jnp.bfloat16)
        gains_out[...] = jnp.zeros((16, wide), jnp.float32)
        lane = 0
        for gain in (in_gain, others[0][...], key_gain, *[o[...] for o in others[1:]]):
            size = gain.shape[1] // (total * ctx)
            for d in range(total):
                for c in range(ctx):
                    at = c * each + lane
                    gains_out[d : d + 1, at : at + size] = gain[
                        :, (d * ctx + c) * size : (d * ctx + c + 1) * size
                    ]
            lane += size
        spans = [(0, heads * head_dim), (heads * head_dim, head_dim), ((heads + 1) * head_dim, head_dim)]
        mine = where_ref[4]
        for c in range(ctx):

            @pl.when(mine == c)
            def _(c=c):
                for k in range(ctx):
                    j, at = (c + k) % ctx, 0
                    for first, size in spans:
                        step = size // ctx
                        outs[k][:count, at : at + step] = grads_out[
                            :, first + j * step : first + (j + 1) * step
                        ]
                        at += step
                    outs[k][count:, :] = gains_out[:, j * each : (j + 1) * each].astype(
                        jnp.bfloat16
                    )

    return kernel_call(
        body,
        [((count, width), jnp.bfloat16)] + [((tall, each), jnp.bfloat16)] * ctx,
        [
            where,
            raw,
            query_grad,
            tokens,
            dx,
            norm_in,
            norm_key,
            cosine,
            sine,
            *parts,
            *pieces,
            *gains,
        ],
        {0: "smem", **{9 + near + i: "any" for i in range(spots)}},
        [
            pltpu.VMEM((width, wide), jnp.bfloat16),
            pltpu.VMEM((count, wide), jnp.bfloat16),
            pltpu.VMEM((16, wide), jnp.float32),
            pltpu.SemaphoreType.DMA((spots,)),
        ],
    )


def narrow_grads(where, lefts, rights, with_gains):
    count, width = lefts[0].shape
    wide = rights[0].shape[1]
    chunk, near = width // 8, len(lefts)
    total = near * count
    tall = chunk + 16 if with_gains else chunk

    def body(where_ref, *rest):
        left_refs, right_refs, outs = rest[:near], rest[near : 2 * near], rest[2 * near : -3]
        turned, lines, values = rest[-3:]
        for i in range(near):
            turned[:, i * count : (i + 1) * count] = left_refs[i][...].T
            values[i * count : (i + 1) * count, :] = right_refs[i][:count, :]
        plane, core = where_ref[0] // 2, where_ref[1]
        for m in range(4):
            start = pl.multiple_of((jnp.bitwise_xor(plane, m) * 2 + core) * chunk, 16)
            lines[m * chunk : (m + 1) * chunk, :] = turned[pl.ds(start, chunk), :]
        for low, high in column_steps(wide, 256):
            part = dot(lines[...], values[:, low:high], 1, 0)
            for m in range(4):
                outs[m][:chunk, low:high] = part[m * chunk : (m + 1) * chunk].astype(outs[m].dtype)
        if with_gains:
            whole = right_refs[0][count:, :].astype(jnp.float32)
            for r in right_refs[1:]:
                whole = whole + r[count:, :].astype(jnp.float32)
            index = lax.broadcasted_iota(jnp.int32, whole.shape, 0)
            for m in range(4):
                row = jnp.bitwise_xor(plane, m) * 2 + core
                row = jnp.sum(jnp.where(index == row, whole, 0.0), axis=0, keepdims=True)
                outs[m][chunk:, :] = jnp.where(index == 0, row, 0.0).astype(outs[m].dtype)

    return kernel_call(
        body,
        [((tall, wide), jnp.float32)] + [((tall, wide), jnp.bfloat16)] * 3,
        [where, *lefts, *rights],
        {0: "smem"},
        [
            pltpu.VMEM((width, total), jnp.bfloat16),
            pltpu.VMEM((width // 2, total), jnp.bfloat16),
            pltpu.VMEM((total, wide), jnp.bfloat16),
        ],
    )


def narrow_middle(where, parts, sizes, ctx):
    chunk, wide = parts[0].shape
    each = wide // ctx

    def body(where_ref, *rest):
        got = rest[: len(parts)]
        outs = rest[len(parts) :]
        mine = where_ref[4]
        total = got[0][...]
        for g in got[1:]:
            total = total + g[...].astype(jnp.float32)
        for c in range(ctx):

            @pl.when(mine == c)
            def _(c=c):
                for k in range(ctx):
                    j = (c + k) % ctx
                    start, at = 0, 0
                    for size in sizes:
                        piece = size // ctx
                        outs[k][:, at : at + piece] = total[
                            :, start + j * piece : start + (j + 1) * piece
                        ].astype(outs[k].dtype)
                        start += size
                        at += piece

    return kernel_call(
        body,
        [((chunk, each), jnp.float32)] + [((chunk, each), jnp.bfloat16)] * (ctx - 1),
        [where, *parts],
        {0: "smem"},
    )


def narrow_last(blocks, out_blocks, sizes, cols):
    rows = out_blocks[0].shape[0]
    near = len(blocks)
    q, k, v = cols

    def body(*rest):
        outs = rest[2 * near :]
        total = rest[0][...]
        for r in rest[1:near]:
            total = total + r[...].astype(jnp.float32)
        outs[0][...] = total[:rows, :q]
        turned = total[:rows, q:].T
        outs[1][...] = turned[:k]
        outs[2][...] = turned[k:]
        out = rest[near][...]
        for r in rest[near + 1 : 2 * near]:
            out = out + r[...].astype(jnp.float32)
        outs[3][...] = out
        start = 0
        for ref, size in zip(outs[4:], sizes):
            ref[...] = total[rows : rows + 1, start : start + size]
            start += size

    return kernel_call(
        body,
        [
            ((rows, q), jnp.float32),
            ((k, rows), jnp.float32),
            ((v, rows), jnp.float32),
            ((rows, out_blocks[0].shape[1]), jnp.float32),
        ]
        + [((1, size), jnp.float32) for size in sizes],
        [*blocks, *out_blocks],
    )


def split_pair(where, gate, up, ctx):
    rows, whole = gate.shape
    inner = whole // ctx

    def body(where_ref, gate_ref, up_ref, *outs):
        mine = where_ref[4]
        for c in range(ctx):

            @pl.when(mine == c)
            def _(c=c):
                for k in range(ctx):
                    j = (c + k) % ctx
                    outs[k][0] = gate_ref[:, j * inner : (j + 1) * inner]
                    outs[k][1] = up_ref[:, j * inner : (j + 1) * inner]

    return kernel_call(
        body, [((2, rows, inner), jnp.bfloat16)] * ctx, [where, gate, up], {0: "smem"}, grant=whole_vmem
    )


def join_pair(where, pieces):
    ctx = len(pieces)
    _, rows, inner = pieces[0].shape

    def body(where_ref, *rest):
        got, out, wide = rest[:ctx], rest[ctx], rest[ctx + 1]
        mine = where_ref[4]
        for c in range(ctx):

            @pl.when(mine == c)
            def _(c=c):
                for m in range(2):
                    for a in range(ctx):
                        wide[a * rows : (a + 1) * rows, :] = got[(c - a) % ctx][m].astype(
                            jnp.float32
                        )
                    out[m] = wide[...].astype(jnp.bfloat16)

    return kernel_call(
        body,
        [((2, ctx * rows, inner), jnp.bfloat16)],
        [where, *pieces],
        {0: "smem"},
        [pltpu.VMEM((ctx * rows, inner), jnp.float32)],
    )[0]


def split_down(where, pieces, rows, ctx):
    groups = 2 * len(pieces)
    _, chunk, part = pieces[0].shape
    per, steps = groups // ctx, chunk // rows

    def body(where_ref, *rest):
        got, outs, (wide, down_ref) = rest[:4], rest[4 : 4 + ctx], rest[4 + ctx :]
        mine = where_ref[4]
        plane, core = where_ref[0] // 2, where_ref[1]
        for m in range(4):
            for flip in range(2):
                group = jnp.bitwise_xor(plane, m) * 2 + jnp.bitwise_xor(core, flip)
                down_ref[pl.ds(group, 1)] = got[m][flip][None]
        for c in range(ctx):

            @pl.when(mine == c)
            def _(c=c):
                for k in range(ctx):
                    j = (c + k) % ctx
                    for b in range(groups):
                        first = b % steps * rows
                        wide[:, b * part : (b + 1) * part] = down_ref[
                            j * per + b // steps, first : first + rows, :
                        ].astype(jnp.float32)
                    outs[k][...] = wide[...].astype(jnp.bfloat16)

    return kernel_call(
        body,
        [((rows, groups * part), jnp.bfloat16)] * ctx,
        [where, *pieces],
        {0: "smem"},
        [
            pltpu.VMEM((rows, groups * part), jnp.float32),
            pltpu.VMEM((groups, chunk, part), jnp.bfloat16),
        ],
    )


def join_down(where, pieces, part):
    ctx = len(pieces)
    rows, inner = pieces[0].shape
    chunk, groups = ctx * rows, inner // part

    def body(where_ref, *rest):
        got, out, wide = rest[:ctx], rest[ctx], rest[ctx + 1]
        mine = where_ref[4]
        for c in range(ctx):

            @pl.when(mine == c)
            def _(c=c):
                for a in range(ctx):
                    piece = got[(c - a) % ctx][...].astype(jnp.float32)
                    for b in range(groups):
                        first = b % ctx * rows
                        at = (b // ctx * ctx + a) * part
                        wide[first : first + rows, at : at + part] = piece[
                            :, b * part : (b + 1) * part
                        ]
                out[...] = wide[...].astype(jnp.bfloat16)

    return kernel_call(
        body,
        [((chunk, inner), jnp.bfloat16)],
        [where, *pieces],
        {0: "smem"},
        [pltpu.VMEM((chunk, inner), jnp.float32)],
    )[0]


def join_rows(where, pieces, rows, split, out_rows):
    ctx = len(pieces)
    _, wide = pieces[0].shape
    tall = ctx * rows + 16

    def body(where_ref, *rest):
        got, out, lines = rest[:ctx], rest[ctx], rest[ctx + 1]
        mine = where_ref[4]
        lines[ctx * rows :, :] = jnp.zeros((16, wide), jnp.float32)
        lines[ctx * out_rows :, split:] = jnp.zeros((tall - ctx * out_rows, wide - split), jnp.float32)
        for c in range(ctx):

            @pl.when(mine == c)
            def _(c=c):
                for a in range(ctx):
                    piece = got[(c - a) % ctx]
                    lines[a * rows : (a + 1) * rows, :split] = piece[:rows, :split].astype(
                        jnp.float32
                    )
                    lines[a * out_rows : (a + 1) * out_rows, split:] = piece[
                        :out_rows, split:
                    ].astype(jnp.float32)
                    at = ctx * rows + a
                    lines[at : at + 1, :split] = piece[rows : rows + 1, :split].astype(jnp.float32)
                out[...] = lines[...].astype(jnp.bfloat16)

    return kernel_call(
        body,
        [((tall, wide), jnp.bfloat16)],
        [where, *pieces],
        {0: "smem"},
        [pltpu.VMEM((tall, wide), jnp.float32)],
    )[0]


def plane_send(parts):
    size = lax.axis_size("dp")
    return [parts[0]] + [
        lax.ppermute(parts[m], "dp", [(i, i ^ (2 * m)) for i in range(size)])
        for m in range(1, len(parts))
    ]


def ctx_send(parts, sign):
    return [parts[0]] + [shift(parts[k], sign * k) for k in range(1, len(parts))]


def stage(*values):
    return lax.optimization_barrier(values)


def gate(value, *conditions):
    return lax.optimization_barrier((value, conditions))[0]


def fused(
    tokens,
    cotangent,
    lengths,
    w_query,
    w_key,
    w_value,
    w_out,
    w_gate,
    w_up,
    w_down,
    gain_in,
    gain_query,
    gain_key,
    gain_attn,
    gain_pre,
    gain_post,
):
    count, width = tokens.shape
    seq_count = lengths.shape[1]
    stretch = count // (2 * seq_count)
    dp = lax.axis_size("dp")
    ctx = lax.axis_size("ctx")
    mine = lax.axis_index("ctx")
    group = lax.axis_index("dp")
    head_dim = w_key.shape[1]
    heads = w_query.shape[1] // head_dim
    where = jnp.stack([group, group % 2, group // 2 % 2, group // 4, mine]).astype(jnp.int32)

    gains = [gain_in, gain_query, gain_key, gain_attn, gain_pre, gain_post]
    sizes = [g.shape[0] for g in gains]
    chunk, out_rows = width // dp, heads * head_dim // dp
    order = [0, 1, 3, 2]
    packed, kept, sent = pack(where, w_query, w_key, w_value, w_out, w_down, gains)
    split = packed.shape[1] - width
    packed = ctx_gather(packed)
    got = swap(sent, 0)
    aux = tables(where, lengths, count, stretch, ctx, head_dim)
    blocks = split_pair(where, w_gate, w_up, ctx)
    kept = gate(kept, aux, blocks)
    downs = plane_send([jnp.stack([kept[m], got[m]]) for m in range(4)])
    packed, downs, aux, blocks = stage(packed, downs, aux, list(blocks))
    cosine, sine, valid, allowed = aux

    blocks = ctx_send(blocks, 1)
    near = plane_near(join_rows(where, packed, w_query.shape[0], split, w_out.shape[0]))
    shared = plane_whole(near)
    pair = join_pair(where, blocks)
    shared, pair, downs = stage(shared, pair, downs)

    normed, query, both, raw, norm_in, norm_query, norm_key = project(
        where, tokens, shared, sizes[:3], cosine, sine, heads, ctx
    )
    pair, normed, query, both, downs = stage(pair, normed, query, both, downs)

    pair = plane_near(pair)
    downs = list(split_down(where, downs, w_gate.shape[0], ctx))
    norm_attn, norm_pre, norm_post = late_gains(
        where, shared, [384, 512, 640], sizes[3:], ctx, both
    )
    both = ctx_gather(both)
    downs = ctx_send(gate(downs, both), 1)
    probs, mixed, attn_raw, residual, normed_two = attend(
        where,
        tokens,
        query,
        both,
        allowed,
        valid,
        norm_attn,
        norm_pre,
        shared,
        out_rows,
        heads,
    )
    pair, pair_cut, downs, normed_two, mixed = stage(pair, cut(pair), downs, normed_two, mixed)

    last = plane_near(join_down(where, downs, w_down.shape[0]))
    two_pieces = [normed_two] + [shift(normed_two, k) for k in order[1:-1]]
    pair_far = [swap(pair[0], 0)]
    two_pieces, pair, pair_far, last, last_cut, normed = stage(
        two_pieces, pair, pair_far, last, cut(last), normed
    )

    two_pieces.append(shift(two_pieces[0], order[-1]))
    pair = pair + diagonal(pair_cut)
    pair_far = pair_far + [swap(p, 0) for p in pair[1:3]]
    two_pieces, pair, pair_far, last, last_cut, normed = stage(
        two_pieces, pair, pair_far, last, last_cut, normed
    )

    last = last + diagonal(last_cut)
    pair_far = pair_far + [swap(p, 0) for p in pair[3:]]
    pair, last = pair + pair_far, last + [swap(p, 0) for p in last]
    two_pieces, pair, last, normed = stage(two_pieces, pair, last, normed)

    weights = (pair, last)
    normed_group = [normed, shift(normed, 1), None, shift(normed, 3)]
    group_two, act, slopes, *sums = feed_forward(where, two_pieces[:-1], weights, True)
    group_two, act, slopes, sums, near_group = stage(
        group_two, act, slopes, sums, [normed_group[1], normed_group[3]]
    )
    normed_group[1], normed_group[3] = near_group

    sums = [sums[0]] + [shift(sums[i], -order[i]) for i in range(1, ctx - 1)]
    two_last, act_last, slopes_last, sum_last = feed_forward(
        where, two_pieces[-1:], weights, False
    )
    sums, two_last, act_last, slopes_last, sum_last, group_two, act, mixed = stage(
        sums, two_last, act_last, slopes_last, sum_last, group_two, act, mixed
    )

    sums.append(shift(sum_last, -order[-1]))
    group_two, act = [group_two, two_last], [act, act_last]
    group_two_far, act_far = [swap(g, 0) for g in group_two], [swap(a, 0) for a in act]
    mixed_far = swap(mixed, 0)
    sums, group_two_far, act_far, mixed_far = stage(sums, group_two_far, act_far, mixed_far)

    output, ffn_grad, gain_post_grad = finish(sums, residual, cotangent, valid, norm_post)
    ffn_early = [ffn_grad] + [shift(ffn_grad, k) for k in order[1:-1]]
    ffn_early, ffn_grad = stage(ffn_early, ffn_grad)

    ffn_last = shift(ffn_grad, order[-1])
    group_ffn, grads, *sums = feed_back(where, ffn_early, weights, slopes, True)
    ffn_last, group_ffn, grads, sums = stage(ffn_last, group_ffn, grads, sums)

    ffn_parts = [group_ffn, ffn_last]
    ffn_far = [swap(f, 0) for f in ffn_parts]
    grads_far = swap(grads, 0)
    _, grads_last, sum_last = feed_back(
        where, [ffn_last], weights, slopes_last, False
    )
    sums[1], sums[2] = shift(sums[1], -order[1]), shift(sums[2], -order[2])
    down_wide = wide_grads(
        where, gate(ffn_parts, grads_last) + ffn_far, [[(a, None) for a in act + act_far]]
    )
    grads_last, sum_last, grads, grads_far, sums, down_wide = stage(
        grads_last, sum_last, grads, grads_far, sums, down_wide
    )

    sums.append(shift(sum_last, -order[-1]))
    down_got = [swap(down_wide[0], 1), swap(down_wide[2], 2)]
    all_grads = [grads, grads_last, grads_far, swap(grads_last, 0)]
    pair_wide = wide_grads(
        where, group_two + group_two_far, [[(g, m) for g in all_grads] for m in range(2)]
    )
    sums, down_wide, down_got, pair_wide = stage(sums, down_wide, down_got, pair_wide)

    pair_got = [swap(pair_wide[0], 1), swap(pair_wide[2], 2)]
    dx, attn_grad, query_grad, gain_pre_grad, gain_attn_grad, gain_query_grad, *parts = attend_back(
        where,
        sums,
        residual,
        cotangent,
        valid,
        attn_raw,
        norm_pre,
        norm_attn,
        norm_query,
        probs,
        query,
        raw,
        both,
        shared,
        out_rows,
        cosine,
        sine,
        heads,
    )
    parts = ctx_send(parts, -1)
    out_blocks = narrow_grads(
        where, [attn_grad, swap(attn_grad, 0)], [mixed, mixed_far], False
    )
    parts, pair_got, out_blocks, query_grad, dx, normed = stage(
        parts, pair_got, out_blocks, query_grad, dx, normed
    )

    input_grad, *blocks = project_back(
        where,
        parts,
        raw,
        query_grad,
        tokens,
        dx,
        norm_in,
        norm_key,
        cosine,
        sine,
        shared,
        heads,
        ctx,
        [gain_query_grad, gain_attn_grad, gain_pre_grad, gain_post_grad],
    )
    normed_group[2] = shift(normed, 2)
    out_blocks = plane_send(out_blocks)
    wide = wide_middle(where, [pair_wide, down_wide], [pair_got, down_got])
    blocks, out_blocks, wide, normed_group = stage(list(blocks), out_blocks, wide, normed_group)

    blocks = ctx_send(blocks, 1)
    wide_got = [swap(wide[0], 2), swap(wide[2], 1)]
    normed_far = [swap(n, 0) for n in normed_group]
    blocks = narrow_grads(
        where, normed_group + normed_far, blocks + [swap(b, 0) for b in blocks], True
    )
    out_blocks = narrow_middle(where, out_blocks, [mixed.shape[1]], ctx)
    wide_got, out_blocks, blocks = stage(wide_got, out_blocks, blocks)

    blocks, out_blocks = plane_send(blocks), ctx_send(out_blocks, 1)
    grad_gate, grad_up, grad_down = wide_last(wide, wide_got, w_gate.shape[1] // ctx)
    blocks, out_blocks, grad_gate = stage(blocks, out_blocks, grad_gate)

    q_cols, k_cols = heads * head_dim // ctx, head_dim // ctx
    grad_query, grad_key, grad_value, grad_out, *gain_outs = narrow_last(
        blocks, out_blocks, sizes, (q_cols, k_cols, k_cols)
    )
    return (
        output,
        input_grad,
        grad_query,
        grad_key.T,
        grad_value.T,
        grad_out.T,
        grad_gate,
        grad_up,
        grad_down.T,
        *[g.reshape(-1) for g in gain_outs],
    )


def on_device(tokens, cotangent, lengths, *params):
    dp, ctx = lax.axis_size("dp"), lax.axis_size("ctx")
    each = tokens.shape[0] // lengths.shape[1]
    fits = dp == 8 and dp % ctx == 0 and tokens.shape[1] // dp % 16 == 0 and each % 16 == 0
    run = fused if fits else plain
    return run(tokens, cotangent, lengths, *params)


def solution(mesh):
    in_specs = (
        P(("dp", "ctx"), None),
        P(("dp", "ctx"), None),
        P("dp", None),
        P(("dp", "ctx"), None),
        P(("dp", "ctx"), None),
        P(("dp", "ctx"), None),
        P(("dp", "ctx"), None),
        P(("dp", "ctx"), None),
        P(("dp", "ctx"), None),
        P(("dp", "ctx"), None),
        P(("dp", "ctx")),
        P(("dp", "ctx")),
        P(("dp", "ctx")),
        P(("dp", "ctx")),
        P(("dp", "ctx")),
        P(("dp", "ctx")),
    )
    out_specs = (
        P(("dp", "ctx"), None),
        P(("dp", "ctx"), None),
        P("dp", "ctx"),
        P("dp", "ctx"),
        P("dp", "ctx"),
        P("ctx", "dp"),
        P("dp", "ctx"),
        P("dp", "ctx"),
        P("ctx", "dp"),
        P(("dp", "ctx")),
        P(("dp", "ctx")),
        P(("dp", "ctx")),
        P(("dp", "ctx")),
        P(("dp", "ctx")),
        P(("dp", "ctx")),
    )
    return jax.shard_map(
        on_device, mesh=mesh, in_specs=in_specs, out_specs=out_specs, check_vma=False
    )
```

```python
import jax
import jax.numpy as jnp
import numpy as np
from jax import lax
from jax.experimental import pallas as pl
from jax.experimental.pallas import tpu as pltpu
from jax.sharding import PartitionSpec as P

epsilon = 1e-06
rope_base = 1000000.0


def rms_norm(value, weight):
    scale = lax.rsqrt(jnp.mean(value * value, axis=-1, keepdims=True) + epsilon)
    return value * scale * (1.0 + weight)


def rms_back(value, weight, grad):
    scale = lax.rsqrt(jnp.mean(value * value, axis=-1, keepdims=True) + epsilon)
    normed = value * scale
    weighted = grad * (1.0 + weight)
    value_grad = scale * (weighted - normed * jnp.mean(weighted * normed, axis=-1, keepdims=True))
    weight_grad = jnp.sum(grad * normed, axis=tuple(range(value.ndim - 1)))
    return (value_grad, weight_grad)


def rope_tables(positions, width):
    half = width // 2
    freqs = jnp.power(rope_base, -2.0 * jnp.arange(half, dtype=jnp.float32) / width)
    angles = positions[:, None] * freqs[None, :]
    cosine = jnp.concatenate([jnp.cos(angles), jnp.cos(angles)], axis=-1)
    sine = jnp.concatenate([jnp.sin(angles), jnp.sin(angles)], axis=-1)
    return (cosine, sine)


def rotate(value, cosine, sine):
    half = value.shape[-1] // 2
    turned = jnp.concatenate([-value[..., half:], value[..., :half]], axis=-1)
    return value * cosine + turned * sine


def rotate_back(grad, cosine, sine):
    half = grad.shape[-1] // 2
    scaled = grad * sine
    return grad * cosine + jnp.concatenate([scaled[..., half:], -scaled[..., :half]], axis=-1)


def geglu(gate, upper):
    return jax.nn.gelu(gate, approximate=True) * upper


def dot(left, right, left_dim, right_dim):
    return lax.dot_general(
        left, right, (((left_dim,), (right_dim,)), ((), ())), preferred_element_type=jnp.float32
    )


def swap(value, bit):
    size = lax.axis_size("dp")
    return lax.ppermute(value, "dp", [(i, i ^ (1 << bit)) for i in range(size)])


def shift(value, step):
    size = lax.axis_size("ctx")
    return lax.ppermute(value, "ctx", [(i, (i + step) % size) for i in range(size)])


def pick(value, index, axis=0):
    return lax.dynamic_index_in_dim(value, index, axis, keepdims=False)


def plane_bits():
    return list(range(1, lax.axis_size("dp").bit_length() - 1))


def ctx_gather(value):
    return [value] + [shift(value, k) for k in range(1, lax.axis_size("ctx"))]


def ctx_ordered(pieces):
    size = lax.axis_size("ctx")
    stacked = jnp.stack(pieces)
    mine = lax.axis_index("ctx")
    return jnp.stack([pick(stacked, (mine - a + size) % size) for a in range(size)])


def ctx_reduce(pieces):
    total = pieces[0].astype(jnp.float32)
    for k in range(1, len(pieces)):
        total = total + shift(pieces[k].astype(jnp.bfloat16), -k).astype(jnp.float32)
    return total


def ctx_exchange(blocks):
    size = lax.axis_size("ctx")
    mine = lax.axis_index("ctx")
    return [pick(blocks, mine)] + [
        shift(pick(blocks, (mine + k) % size), k) for k in range(1, size)
    ]


def row_parts(rows, count):
    unit = 8 if rows % 8 == 0 else 1
    edges = [unit * (rows // unit * p // count) for p in range(count + 1)]
    return [(edges[p], edges[p + 1]) for p in range(count)]


def dp_gather(value):
    bits = plane_bits()
    plane = lax.axis_index("dp") // 2
    core = lax.axis_index("dp") % 2
    count = 1 << len(bits)
    parts = []
    for p, (low, high) in enumerate(row_parts(value.shape[0], len(bits))):
        current = value[None, low:high]
        masks = [0]
        for bit in bits[p:] + bits[:p]:
            current = jnp.concatenate([current, swap(current, bit)])
            masks = masks + [m ^ (1 << (bit - 1)) for m in masks]
        other = swap(current, 0)
        place = jnp.asarray([masks.index(m) for m in range(count)], jnp.int32)
        rows_of = []
        for a in range(count):
            at = pick(place, plane ^ a)
            first, second = pick(current, at), pick(other, at)
            rows_of.append(
                jnp.stack([lax.select(core == 0, first, second), lax.select(core == 0, second, first)])
            )
        parts.append(jnp.stack(rows_of))
    whole = jnp.concatenate(parts, axis=2)
    return whole.reshape((2 * count,) + value.shape)


def dp_reduce(kept, sent):
    bits = plane_bits()
    plane = lax.axis_index("dp") // 2
    total = (kept + swap(sent.astype(jnp.bfloat16), 0).astype(jnp.float32)).astype(jnp.bfloat16)
    parts = []
    for p, (low, high) in enumerate(row_parts(total.shape[1], len(bits))):
        current = total[:, low:high]
        current = current.reshape((2,) * len(bits) + current.shape[1:])
        left = sorted(bits, reverse=True)
        for bit in bits[p:] + bits[:p]:
            axis = left.index(bit)
            mine = (plane >> (bit - 1)) & 1
            got = swap(pick(current, 1 - mine, axis), bit)
            current = pick(current, mine, axis).astype(jnp.float32) + got.astype(jnp.float32)
            left.remove(bit)
            if left:
                current = current.astype(jnp.bfloat16)
        parts.append(current)
    return jnp.concatenate(parts, axis=0)


def columns_of(value, core):
    dp = lax.axis_size("dp")
    wide = value.reshape(value.shape[0], dp // 2, 2, value.shape[1] // dp)
    return pick(wide, core, 2).reshape(value.shape[0], -1)


def weight_grad(left, right, extra=None):
    core = lax.axis_index("dp") % 2
    dp = lax.axis_size("dp")
    blocks = []
    for side in (core, 1 - core):
        block = dot(columns_of(left, side), right, 0, 0)
        block = block.reshape(dp // 2, left.shape[1] // dp, right.shape[1])
        if extra is not None:
            block = jnp.concatenate([block, pick(extra, side, 1)], axis=1)
        blocks.append(block)
    return dp_reduce(blocks[0], blocks[1])


def plain(
    tokens,
    cotangent,
    lengths,
    w_query,
    w_key,
    w_value,
    w_out,
    w_gate,
    w_up,
    w_down,
    gain_in,
    gain_query,
    gain_key,
    gain_attn,
    gain_pre,
    gain_post,
):
    count, width = tokens.shape
    seq_count = lengths.shape[1]
    stretch = count // (2 * seq_count)
    dp = lax.axis_size("dp")
    ctx = lax.axis_size("ctx")
    mine = lax.axis_index("ctx")
    head_dim = w_key.shape[1]
    heads = w_query.shape[1] // head_dim
    inner = w_gate.shape[1] // ctx
    span = 2 * ctx * stretch
    offsets = jnp.arange(stretch, dtype=jnp.int32)

    def positions_of(index):
        return jnp.concatenate(
            [index * stretch + offsets, (2 * ctx - 1 - index) * stretch + offsets]
        )

    local_pos = positions_of(mine)
    valid = (local_pos[None, :] < lengths[0][:, None]).astype(jnp.float32).reshape(count, 1)
    cosine, sine = rope_tables(jnp.tile(local_pos, seq_count).astype(jnp.float32), head_dim)
    key_pos = jnp.concatenate([positions_of((mine - k + ctx) % ctx) for k in range(ctx)])
    query_pos = jnp.repeat(local_pos, heads)
    allowed = (key_pos[None, None, :] <= query_pos[None, :, None]) & (
        key_pos[None, None, :] < lengths[0][:, None, None]
    )
    inv_root = head_dim ** (-0.5)

    gains = [gain_in, gain_query, gain_key, gain_attn, gain_pre, gain_post]
    sizes = [g.shape[0] for g in gains]
    small = jnp.concatenate(gains)
    qkv_shard = jnp.concatenate([w_query, w_key, w_value], axis=1)
    in_rows, in_cols = qkv_shard.shape
    out_rows = w_out.shape[0]
    top = max(in_rows, out_rows)
    packed_rows = -(-(top + 1) // 8) * 8
    packed = jnp.concatenate(
        [
            jnp.pad(qkv_shard, ((0, top - in_rows), (0, 0))),
            jnp.pad(w_out, ((0, top - out_rows), (0, 0))),
        ],
        axis=1,
    )
    last = jnp.pad(small[None], ((0, packed_rows - top - 1), (0, packed.shape[1] - small.shape[0])))
    packed = jnp.concatenate([packed, last], axis=0)
    near = ctx_ordered(ctx_gather(packed)).reshape(ctx * packed_rows, -1)
    everything = dp_gather(near).reshape(dp * ctx, packed_rows, -1)
    full_qkv = everything[:, :in_rows, :in_cols].reshape(width, in_cols)
    full_out = everything[:, :out_rows, in_cols:].reshape(heads * head_dim, width)
    smalls = everything[:, top, : small.shape[0]]
    norms, start = [], 0
    for size in sizes:
        norms.append(smalls[:, start : start + size].reshape(-1).astype(jnp.float32))
        start += size
    norm_in, norm_query, norm_key, norm_attn, norm_pre, norm_post = norms

    def column_blocks(weight):
        return weight.reshape(weight.shape[0], ctx, inner).transpose(1, 0, 2)

    gate_up = jnp.stack([column_blocks(w_gate), column_blocks(w_up)], axis=1)
    gate_up = ctx_ordered(ctx_exchange(gate_up)).transpose(1, 0, 2, 3)
    gate_up = gate_up.reshape(2, width // dp, inner)
    per = dp // ctx
    down = w_down.T.reshape(dp, width // dp, w_down.shape[0])
    down = lax.all_to_all(down, "dp", split_axis=0, concat_axis=0, tiled=True)
    down = down.reshape(ctx, per, width // dp, w_down.shape[0])
    down = ctx_ordered(ctx_exchange(down))
    down = down.transpose(2, 1, 0, 3).reshape(width // dp, inner)
    full_gate = dp_gather(gate_up[0]).reshape(width, inner)
    full_up = dp_gather(gate_up[1]).reshape(width, inner)
    full_down = dp_gather(down).reshape(width, inner)

    hidden = tokens.astype(jnp.float32)
    normed = rms_norm(hidden, norm_in).astype(jnp.bfloat16)
    qkv_raw = dot(normed, full_qkv, 1, 0)
    query_raw = qkv_raw[:, : heads * head_dim]
    key_raw = qkv_raw[:, heads * head_dim : (heads + 1) * head_dim]
    value_raw = qkv_raw[:, (heads + 1) * head_dim :]
    query_heads = query_raw.reshape(count, heads, head_dim)
    query_bf = rotate(
        rms_norm(query_heads, norm_query), cosine[:, None, :], sine[:, None, :]
    ).astype(jnp.bfloat16)
    query_bf = query_bf.reshape(seq_count, 2 * stretch * heads, head_dim)
    key_bf = rotate(rms_norm(key_raw, norm_key), cosine, sine).astype(jnp.bfloat16)
    both = jnp.concatenate([key_bf, value_raw.astype(jnp.bfloat16)], axis=1)
    both = jnp.stack(
        [p.reshape(seq_count, 2 * stretch, 2 * head_dim) for p in ctx_gather(both)], axis=1
    ).reshape(seq_count, span, 2 * head_dim)
    keys, values = both[..., :head_dim], both[..., head_dim:]
    scores = (
        jnp.einsum("sqd,skd->sqk", query_bf, keys, preferred_element_type=jnp.float32) * inv_root
    )
    masked = jnp.where(allowed, scores, -1e30)
    peak = jnp.max(masked, axis=-1, keepdims=True)
    expo = jnp.exp(masked - peak)
    total = jnp.sum(expo, axis=-1, keepdims=True)
    probs = expo / total
    probs_bf = probs.astype(jnp.bfloat16)
    mixed = jnp.einsum("sqk,skd->sqd", probs_bf, values, preferred_element_type=jnp.float32)
    mixed_bf = mixed.astype(jnp.bfloat16).reshape(count, heads * head_dim)
    attn_raw = dot(mixed_bf, full_out, 1, 0)
    after_attn = hidden + valid * rms_norm(attn_raw, norm_attn)
    normed_two = rms_norm(after_attn, norm_pre).astype(jnp.bfloat16)

    group_two = jnp.concatenate(ctx_gather(normed_two))
    gate = dot(group_two, full_gate, 1, 0)
    upper = dot(group_two, full_up, 1, 0)
    inner_bf = geglu(gate, upper).astype(jnp.bfloat16)
    ffn_part = dot(inner_bf, full_down, 1, 1)
    ffn_raw = ctx_reduce(list(ffn_part.reshape(ctx, count, width)))
    output = (after_attn + valid * rms_norm(ffn_raw, norm_post)).astype(jnp.bfloat16)

    grad_top = cotangent.astype(jnp.float32)
    ffn_grad, grad_gain_post = rms_back(ffn_raw, norm_post, valid * grad_top)
    group_ffn = jnp.concatenate(ctx_gather(ffn_grad.astype(jnp.bfloat16)))
    inner_grad = dot(group_ffn, full_down, 1, 0)
    _, geglu_pull = jax.vjp(geglu, gate, upper)
    gate_grad, upper_grad = geglu_pull(inner_grad)
    gate_grad_bf = gate_grad.astype(jnp.bfloat16)
    upper_grad_bf = upper_grad.astype(jnp.bfloat16)
    two_part = dot(gate_grad_bf, full_gate, 1, 1) + dot(upper_grad_bf, full_up, 1, 1)
    normed_two_grad = ctx_reduce(list(two_part.reshape(ctx, count, width)))
    grad_down = weight_grad(group_ffn, inner_bf).T
    grad_gate = weight_grad(group_two, gate_grad_bf)
    grad_up = weight_grad(group_two, upper_grad_bf)

    through_pre, grad_gain_pre = rms_back(after_attn, norm_pre, normed_two_grad)
    after_grad = grad_top + through_pre
    attn_grad, grad_gain_attn = rms_back(attn_raw, norm_attn, valid * after_grad)
    attn_grad_bf = attn_grad.astype(jnp.bfloat16)
    grad_out = weight_grad(attn_grad_bf, mixed_bf)
    grad_out = sum_of_ctx(grad_out.reshape(grad_out.shape[0], ctx, -1).transpose(1, 0, 2)).T
    mixed_grad_bf = dot(attn_grad_bf, full_out, 1, 1).astype(jnp.bfloat16)
    mixed_grad_bf = mixed_grad_bf.reshape(seq_count, 2 * stretch * heads, head_dim)
    prob_grad = jnp.einsum(
        "sqd,skd->sqk", mixed_grad_bf, values, preferred_element_type=jnp.float32
    )
    row_dot = jnp.sum(probs * prob_grad, axis=-1, keepdims=True)
    score_grad_bf = (probs * (prob_grad - row_dot)).astype(jnp.bfloat16)
    query_grad = (
        jnp.einsum("sqk,skd->sqd", score_grad_bf, keys, preferred_element_type=jnp.float32)
        * inv_root
    )
    keys_grad = (
        jnp.einsum("sqk,sqd->skd", score_grad_bf, query_bf, preferred_element_type=jnp.float32)
        * inv_root
    )
    values_grad = jnp.einsum(
        "sqk,sqd->skd", probs_bf, mixed_grad_bf, preferred_element_type=jnp.float32
    )
    both_grad = jnp.concatenate([keys_grad, values_grad], axis=-1)
    both_grad = both_grad.reshape(seq_count, ctx, 2 * stretch, 2 * head_dim).transpose(1, 0, 2, 3)
    own_grad = ctx_reduce(list(both_grad.reshape(ctx, count, 2 * head_dim)))
    own_keys_grad, own_values_grad = own_grad[:, :head_dim], own_grad[:, head_dim:]
    query_grad = rotate_back(
        query_grad.reshape(count, heads, head_dim), cosine[:, None, :], sine[:, None, :]
    )
    query_raw_grad, grad_gain_query = rms_back(query_heads, norm_query, query_grad)
    query_raw_bf = query_raw_grad.reshape(count, heads * head_dim).astype(jnp.bfloat16)
    key_raw_grad, grad_gain_key = rms_back(
        key_raw, norm_key, rotate_back(own_keys_grad, cosine, sine)
    )
    key_raw_bf = key_raw_grad.astype(jnp.bfloat16)
    value_raw_bf = own_values_grad.astype(jnp.bfloat16)
    raw_bf = jnp.concatenate([query_raw_bf, key_raw_bf, value_raw_bf], axis=1)
    normed_grad = dot(raw_bf, full_qkv, 1, 1)
    through_in, grad_gain_in = rms_back(hidden, norm_in, normed_grad)
    input_grad = (after_grad + through_in).astype(jnp.bfloat16)

    by_ctx = jnp.concatenate(
        [r.reshape(count, ctx, -1) for r in (query_raw_bf, key_raw_bf, value_raw_bf)], axis=2
    )
    each = by_ctx.shape[2]
    gain_grads = jnp.concatenate(
        [
            g.reshape(dp * ctx, -1)
            for g in (
                grad_gain_in,
                grad_gain_query,
                grad_gain_key,
                grad_gain_attn,
                grad_gain_pre,
                grad_gain_post,
            )
        ],
        axis=1,
    )
    small_size = gain_grads.shape[1]
    extra = jnp.pad(gain_grads, ((0, 0), (0, each - small_size))).reshape(
        dp // 2, 2, 1, ctx * each
    )
    extra = jnp.pad(extra, ((0, 0), (0, 0), (0, 7), (0, 0)))
    grad_qkv = weight_grad(normed, by_ctx.reshape(count, ctx * each), extra)
    grad_qkv = sum_of_ctx(grad_qkv.reshape(grad_qkv.shape[0], ctx, each).transpose(1, 0, 2))
    rows = width // dp
    gain_out = grad_qkv[rows, :small_size]
    grad_qkv = grad_qkv[:rows]
    q_cols, k_cols = heads * head_dim // ctx, head_dim // ctx
    outs, start = [], 0
    for size in sizes:
        outs.append(gain_out[start : start + size])
        start += size
    return (
        output,
        input_grad,
        grad_qkv[:, :q_cols],
        grad_qkv[:, q_cols : q_cols + k_cols],
        grad_qkv[:, q_cols + k_cols :],
        grad_out,
        grad_gate,
        grad_up,
        grad_down,
        *outs,
    )


def sum_of_ctx(blocks):
    size = lax.axis_size("ctx")
    mine = lax.axis_index("ctx")
    total = pick(blocks, mine).astype(jnp.float32)
    for k in range(1, size):
        got = shift(pick(blocks, (mine + k) % size).astype(jnp.bfloat16), k)
        total = total + got.astype(jnp.float32)
    return total


mega = 2**20
whole_vmem = 121 * mega // 2


def place(name):
    return {"vmem": pl.BlockSpec(memory_space=pltpu.VMEM), "smem": pl.BlockSpec(memory_space=pltpu.SMEM), "any": pl.BlockSpec(memory_space=pl.ANY)}[name]


def kernel_call(body, outs, args, where=None, scratch=(), out_where=None, grant=40 * mega):
    where, out_where = where or {}, out_where or {}
    return pl.pallas_call(
        body,
        out_shape=[jax.ShapeDtypeStruct(s, t) for s, t in outs],
        in_specs=[place(where.get(i, "vmem")) for i in range(len(args))],
        out_specs=[place(out_where.get(i, "vmem")) for i in range(len(outs))],
        scratch_shapes=list(scratch),
        compiler_params=pltpu.CompilerParams(vmem_limit_bytes=grant),
        cost_estimate=pl.CostEstimate(flops=0, bytes_accessed=0, transcendentals=0),
    )(*args)


def norm_back(value, weight, grad):
    scale = lax.rsqrt(jnp.mean(value * value, axis=-1, keepdims=True) + epsilon)
    normed = value * scale
    weighted = grad * (1.0 + weight)
    value_grad = scale * (weighted - normed * jnp.mean(weighted * normed, axis=-1, keepdims=True))
    return value_grad, jnp.sum(grad * normed, axis=0, keepdims=True)


def spread(index, tails, lane, size, ctx):
    dp = len(tails)
    shards = jnp.concatenate([t[:, lane : lane + 128] for t, _ in tails], axis=0)
    tail = shards.shape[0] // dp
    whole = dp * ctx * size
    column = lax.broadcasted_iota(jnp.int32, (128, whole), 1)
    line = lax.broadcasted_iota(jnp.int32, (128, whole), 0)
    spots = jnp.where(column % size == line, 1.0, 0.0).astype(jnp.bfloat16)
    values = dot(shards, spots, 1, 0)
    column = lax.broadcasted_iota(jnp.int32, (tail, whole), 1) // size
    line = lax.broadcasted_iota(jnp.int32, (tail, whole), 0)
    total = jnp.zeros((tail, whole), jnp.float32)
    for k, (_, mask) in enumerate(tails):
        owner = jnp.where(line < ctx, (index ^ mask) * ctx + line, -1)
        total = total + jnp.where(column == owner, values[k * tail : (k + 1) * tail], 0.0)
    return jnp.sum(total, axis=0, keepdims=True)


def pack(where, w_query, w_key, w_value, w_out, w_down, gains):
    part, width = w_down.shape
    chunk = width // 8
    rows = w_query.shape[0]
    parts = [w_query, w_key, w_value, w_out]
    ends = [int(e) for e in np.cumsum([0] + [p.shape[1] for p in parts])]
    tall = -(-max(rows + 1, w_out.shape[0]) // 8) * 8

    def body(where_ref, down_ref, *rest):
        shards, lines = rest[: len(parts)], rest[len(parts) : len(parts) + len(gains)]
        out, *downs, wide, turned = rest[len(parts) + len(gains) :]
        turned[...] = down_ref[...].T
        plane, core = where_ref[0] // 2, where_ref[1]
        for flip, ref in enumerate(downs):
            for m in range(4):
                group = jnp.bitwise_xor(plane, m) * 2 + jnp.bitwise_xor(core, flip)
                ref[m] = turned[pl.ds(pl.multiple_of(group * chunk, 16), chunk), :]
        wide[...] = jnp.zeros(wide.shape, jnp.float32)
        for i, shard in enumerate(shards):
            wide[: shard.shape[0], ends[i] : ends[i + 1]] = shard[...].astype(jnp.float32)
        for i, line in enumerate(lines):
            wide[rows : rows + 1, i * 128 : i * 128 + line.shape[1]] = line[...].astype(
                jnp.float32
            )
        out[...] = wide[...].astype(jnp.bfloat16)

    return kernel_call(
        body,
        [((tall, ends[-1]), jnp.bfloat16)] + [((4, chunk, part), jnp.bfloat16)] * 2,
        [where, w_down, *parts, *[g.reshape(1, -1) for g in gains]],
        {0: "smem"},
        [pltpu.VMEM((tall, ends[-1]), jnp.float32), pltpu.VMEM((width, part), jnp.bfloat16)],
        grant=whole_vmem,
    )


def tables(where, lengths, count, stretch, ctx, head_dim):
    seqs = lengths.shape[1]
    each, half = count // seqs, head_dim // 2
    span = 2 * ctx * stretch
    freqs = rope_base ** (-2.0 * np.arange(half, dtype=np.float64) / head_dim)
    freqs = jnp.asarray(freqs[None].astype(np.float32))

    def positions(index, owner):
        block, step = index // stretch % 2, index % stretch
        return jnp.where(block == 0, owner, 2 * ctx - 1 - owner) * stretch + step

    def body(where_ref, lengths_ref, freqs_ref, cos_out, sin_out, valid_out, allowed_out):
        mine = where_ref[4]
        rows = lax.broadcasted_iota(jnp.int32, (each, 1), 0)
        local = positions(rows, mine)
        angles = local.astype(jnp.float32) * freqs_ref[...]
        cos, sin = jnp.cos(angles), jnp.sin(angles)
        cols = lax.broadcasted_iota(jnp.int32, (1, span), 1)
        owner = (mine - cols // each + ctx) % ctx
        keys = positions(cols % each, owner)
        for s in range(seqs):
            part = slice(s * each, (s + 1) * each)
            for low, high in ((0, half), (half, head_dim)):
                cos_out[part, low:high] = cos
                sin_out[part, low:high] = sin
            length = lengths_ref[0, s]
            valid_out[part, :] = jnp.where(local < length, 1.0, 0.0)
            allowed_out[s] = jnp.where((keys <= local) & (keys < length), 1.0, 0.0)

    return kernel_call(
        body,
        [
            ((count, head_dim), jnp.float32),
            ((count, head_dim), jnp.float32),
            ((count, 1), jnp.float32),
            ((seqs, each, span), jnp.float32),
        ],
        [where, lengths, freqs],
        {0: "smem", 1: "smem"},
    )


def plane_near(value):
    return [value, swap(value, 1), swap(value, 2)]


def cut(near):
    row = near[0].ndim - 2
    first = halves_of(near[0].shape[row])[0]
    low = lax.slice_in_dim(near[1], 0, first, axis=row)
    high = lax.slice_in_dim(near[2], first, None, axis=row)
    return [low, high]


def diagonal(halves):
    return [swap(halves[0], 2), swap(halves[1], 1)]


def plane_whole(near):
    pieces = near + diagonal(cut(near))
    return pieces + [swap(p, 0) for p in pieces]


def late_gains(where, pieces, lanes, sizes, ctx, behind):
    tall = pieces[0].shape[0]

    def body(where_ref, behind_ref, *rest):
        parts, outs = rest[: len(pieces)], rest[len(pieces) :]
        tails = tails_of(parts, tall)
        for out, lane, size in zip(outs, lanes, sizes):
            out[...] = spread(where_ref[0], tails, lane, size, ctx)

    return kernel_call(
        body,
        [((1, len(tails_of([np.zeros((tall, 1))] * len(pieces), tall)) * ctx * size), jnp.float32) for size in sizes],
        [where, behind, *pieces],
        {0: "smem", 1: "any"},
    )


def project(where, tokens, pieces, sizes, cosine, sine, heads, ctx):
    count, width = tokens.shape
    tall = pieces[0].shape[0]
    head_dim = cosine.shape[1]
    wide = (heads + 2) * head_dim
    total = len(pieces)

    def body(where_ref, x_ref, cos_ref, sin_ref, *rest):
        parts = rest[:total]
        normed_ref, query_out, both_out, raw_out, in_ref, query_ref, key_ref = rest[total : total + 7]
        weight, ends, sems, end_sems = rest[total + 7 :]
        copies = load_columns(where_ref[0], parts, tall, tall - 16, 0, weight, sems)
        tails = [
            (ref, mask, rows) for ref, mask, at, rows in pieces_of(parts, tall) if at + rows == tall
        ]
        end_copies = [
            pltpu.make_async_copy(
                ref.at[pl.ds(rows - 16, 16), pl.ds(0, ends.shape[2])], ends.at[i], end_sems.at[i]
            )
            for i, (ref, _, rows) in enumerate(tails)
        ]
        for copy in end_copies:
            copy.start()
        for copy in end_copies:
            copy.wait()
        tails = [(ends[i], mask) for i, (_, mask, _) in enumerate(tails)]
        for i, ref in enumerate((in_ref, query_ref, key_ref)):
            ref[...] = spread(where_ref[0], tails, i * 128, sizes[i], ctx)
        normed = rms_norm(x_ref[...].astype(jnp.float32), in_ref[...]).astype(jnp.bfloat16)
        normed_ref[...] = normed
        cos, sin = cos_ref[...], sin_ref[...]
        for copy in copies:
            copy.wait()
        for h in range(heads + 1):
            cols = slice(h * head_dim, (h + 1) * head_dim)
            raw = dot(normed, weight[:, cols], 1, 0)
            raw_out[:, cols] = raw
            gain = query_ref[...] if h < heads else key_ref[...]
            turned = rotate(rms_norm(raw, gain), cos, sin).astype(jnp.bfloat16)
            if h < heads:
                query_out[:, cols] = turned
            else:
                both_out[:, :head_dim] = turned
        both_out[:, head_dim:] = dot(normed, weight[:, (heads + 1) * head_dim :], 1, 0).astype(
            jnp.bfloat16
        )

    return kernel_call(
        body,
        [
            ((count, width), jnp.bfloat16),
            ((count, heads * head_dim), jnp.bfloat16),
            ((count, 2 * head_dim), jnp.bfloat16),
            ((count, (heads + 1) * head_dim), jnp.float32),
            ((1, width), jnp.float32),
            ((1, head_dim), jnp.float32),
            ((1, head_dim), jnp.float32),
        ],
        [where, tokens, cosine, sine, *pieces],
        {0: "smem", **{4 + i: "any" for i in range(total)}},
        [
            pltpu.VMEM((width, wide), jnp.bfloat16),
            pltpu.VMEM((8, 16, 384), jnp.bfloat16),
            pltpu.SemaphoreType.DMA((total,)),
            pltpu.SemaphoreType.DMA((8,)),
        ],
    )


def attend(
    where, tokens, query, both, allowed, valid, norm_attn, norm_pre, pieces, out_rows, heads
):
    count, width = tokens.shape
    seqs, each, span = allowed.shape
    head_dim = query.shape[1] // heads
    inv_root = head_dim ** (-0.5)
    near, total = len(both), len(pieces)
    tall, wide = pieces[0].shape

    def body(where_ref, x_ref, query_ref, allowed_ref, valid_ref, attn_ref, pre_ref, *rest):
        got, parts = rest[:near], rest[near : near + total]
        probs_out, mixed_out, raw_out, after_out, two_out, weight, sems = rest[near + total :]
        copies = load_columns(where_ref[0], parts, tall, out_rows, wide - width, weight, sems)
        for s in range(seqs):
            rows = slice(s * each, (s + 1) * each)
            queries = jnp.concatenate(
                [query_ref[rows, h * head_dim : (h + 1) * head_dim] for h in range(heads)], axis=0
            )
            keys = jnp.concatenate([g[rows, :head_dim] for g in got], axis=0)
            values = jnp.concatenate([g[rows, head_dim:] for g in got], axis=0)
            scores = dot(queries, keys, 1, 1) * inv_root
            keep = jnp.concatenate([allowed_ref[s]] * heads, axis=0)
            scores = jnp.where(keep > 0.0, scores, -1e30)
            expo = jnp.exp(scores - jnp.max(scores, axis=-1, keepdims=True))
            probs = expo / jnp.sum(expo, axis=-1, keepdims=True)
            probs_out[s] = probs
            mixed = dot(probs.astype(jnp.bfloat16), values, 1, 0).astype(jnp.bfloat16)
            for h in range(heads):
                mixed_out[rows, h * head_dim : (h + 1) * head_dim] = mixed[
                    h * each : (h + 1) * each
                ]
        for copy in copies:
            copy.wait()
        raw = dot(mixed_out[...], weight[...], 1, 0)
        raw_out[...] = raw
        after = x_ref[...].astype(jnp.float32) + valid_ref[...] * rms_norm(raw, attn_ref[...])
        after_out[...] = after
        two_out[...] = rms_norm(after, pre_ref[...]).astype(jnp.bfloat16)

    return kernel_call(
        body,
        [
            ((seqs, heads * each, span), jnp.float32),
            ((count, heads * head_dim), jnp.bfloat16),
            ((count, width), jnp.float32),
            ((count, width), jnp.float32),
            ((count, width), jnp.bfloat16),
        ],
        [where, tokens, query, allowed, valid, norm_attn, norm_pre, *both, *pieces],
        {0: "smem", **{7 + near + i: "any" for i in range(total)}},
        [
            pltpu.VMEM((heads * head_dim, width), jnp.bfloat16),
            pltpu.SemaphoreType.DMA((total,)),
        ],
    )


def column_steps(size, step):
    return [(s, min(size, s + step)) for s in range(0, size, step)]


def halves_of(rows):
    first = -(-rows // 32) * 16
    return first, rows - first


def pieces_of(refs, chunk):
    parts, far = refs[: len(refs) // 2], refs[len(refs) // 2 :]
    first, second = halves_of(chunk)
    shapes = [(0, 0, chunk), (2, 0, chunk), (4, 0, chunk), (6, 0, first), (6, first, second)]
    return [(ref, mask, at, rows) for ref, (mask, at, rows) in zip(parts, shapes)] + [
        (ref, mask ^ 1, at, rows) for ref, (mask, at, rows) in zip(far, shapes)
    ]


def load_weights(index, pair, last, chunk, target, sems):
    def copies(m):
        result = []
        for i, (ref, mask, at, rows) in enumerate(pieces_of(last if m == 2 else pair, chunk)):
            start = pl.multiple_of((index ^ mask) * chunk + at, 16)
            result.append(
                pltpu.make_async_copy(
                    ref if m == 2 else ref.at[m], target.at[m, pl.ds(start, rows)], sems.at[m, i]
                )
            )
        return result

    return [copies(m) for m in range(target.shape[0])]


def load_columns(index, refs, tall, rows, first, target, sems):
    copies = []
    for i, (ref, mask, at, size) in enumerate(pieces_of(refs, tall)):
        size = min(size, rows - at)
        if size > 0:
            start = pl.multiple_of((index ^ mask) * rows + at, 16)
            copies.append(
                pltpu.make_async_copy(
                    ref.at[pl.ds(0, size), pl.ds(first, target.shape[1])],
                    target.at[pl.ds(start, size)],
                    sems.at[i],
                )
            )
    for copy in copies:
        copy.start()
    return copies


def tails_of(refs, tall):
    return [
        (ref[rows - 16 : rows], mask) for ref, mask, at, rows in pieces_of(refs, tall) if at + rows == tall
    ]


def feed_forward(where, pieces, weights, with_own):
    count, width = pieces[0].shape
    (pair, last), kinds = weights, 3
    _, chunk, inner = pair[0].shape
    lanes = -(-inner // 128) * 128
    near, spots = len(pieces), len(pair)
    total = near * count
    slope = (2.0 / np.pi) ** 0.5

    def body(where_ref, *rest):
        pair_refs, last_refs, rest = rest[:spots], rest[spots : 2 * spots], rest[2 * spots :]
        parts, outs, sums = rest[:near], rest[near : near + 3], rest[near + 3 : near + 3 + near]
        weight, group, act, slopes, gates, sems, out_sems = rest[near + 3 + near :]
        copies = load_weights(where_ref[0], pair_refs, last_refs, chunk, weight, sems)
        for kind in copies:
            for copy in kind:
                copy.start()
        for k in range(near):
            group[k * count : (k + 1) * count, :] = parts[k][...]
        stores = [
            pltpu.make_async_copy(source, out, out_sems.at[i])
            for i, (source, out) in enumerate(zip((group, act, slopes), outs))
        ]
        stores[0].start()
        for copy in copies[0]:
            copy.wait()
        for low, high in column_steps(inner, 256):
            gates[:, low:high] = dot(group[...], weight[0, :, low:high], 1, 0)
        for copy in copies[1]:
            copy.wait()
        for low, high in column_steps(inner, 256):
            gate = gates[:, low:high]
            upper = dot(group[...], weight[1, :, low:high], 1, 0)
            square = 0.044715 * slope * gate * gate
            half = 0.5 + 0.5 * jnp.tanh(gate * (slope + square))
            gelu = gate * half
            steep = half * (1.0 + 2.0 * (gate - gelu) * (slope + 3.0 * square))
            act[:, low:high] = (gelu * upper).astype(jnp.bfloat16)
            slopes[0, :, low:high] = (steep * upper).astype(jnp.bfloat16)
            slopes[1, :, low:high] = gelu.astype(jnp.bfloat16)
        if lanes > inner:
            act[:, inner:] = jnp.zeros((total, lanes - inner), jnp.bfloat16)
        for store in stores[1:]:
            store.start()
        for copy in copies[2]:
            copy.wait()
        for low, high in column_steps(width, 256):
            part = dot(act[:, :inner], weight[2, low:high, :], 1, 1)
            for k in range(near):
                sums[k][:, low:high] = part[k * count : (k + 1) * count].astype(sums[k].dtype)
        for store in stores:
            store.wait()

    return kernel_call(
        body,
        [
            ((total, width), jnp.bfloat16),
            ((total, lanes), jnp.bfloat16),
            ((2, total, inner), jnp.bfloat16),
        ]
        + [((count, width), jnp.float32 if with_own and k == 0 else jnp.bfloat16) for k in range(near)],
        [where, *pair, *last, *pieces],
        {0: "smem", **{1 + i: "any" for i in range(2 * spots)}},
        [
            pltpu.VMEM((kinds, width, inner), jnp.bfloat16),
            pltpu.VMEM((total, width), jnp.bfloat16),
            pltpu.VMEM((total, lanes), jnp.bfloat16),
            pltpu.VMEM((2, total, inner), jnp.bfloat16),
            pltpu.VMEM((total, inner), jnp.float32),
            pltpu.SemaphoreType.DMA((kinds, spots)),
            pltpu.SemaphoreType.DMA((3,)),
        ],
        {i: "any" for i in range(3)},
        grant=whole_vmem,
    )


def finish(parts, after, cotangent, valid, norm_post):
    count, width = after.shape
    near = len(parts)

    def body(after_ref, cot_ref, valid_ref, post_ref, *rest):
        got = rest[:near]
        output_out, grad_out, gain_out = rest[near:]
        raw = got[0][...]
        for g in got[1:]:
            raw = raw + g[...].astype(jnp.float32)
        ok = valid_ref[...]
        output_out[...] = (after_ref[...] + ok * rms_norm(raw, post_ref[...])).astype(jnp.bfloat16)
        grad, gain = norm_back(raw, post_ref[...], ok * cot_ref[...].astype(jnp.float32))
        grad_out[...] = grad.astype(jnp.bfloat16)
        gain_out[...] = gain

    return kernel_call(
        body,
        [
            ((count, width), jnp.bfloat16),
            ((count, width), jnp.bfloat16),
            ((1, width), jnp.float32),
        ],
        [after, cotangent, valid, norm_post, *parts],
        grant=whole_vmem,
    )


def feed_back(where, pieces, weights, slopes, with_own):
    count, width = pieces[0].shape
    (pair, last), kinds = weights, 3
    _, chunk, inner = pair[0].shape
    lanes = -(-inner // 128) * 128
    near, spots = len(pieces), len(pair)
    total = near * count

    def body(where_ref, slopes_ref, *rest):
        pair_refs, last_refs, rest = rest[:spots], rest[spots : 2 * spots], rest[2 * spots :]
        parts = rest[:near]
        group_out, both_out = rest[near : near + 2]
        sums = rest[near + 2 : near + 2 + near]
        weight, sems = rest[near + 2 + near :]
        copies = load_weights(where_ref[0], pair_refs, last_refs, chunk, weight, sems)
        for kind in (copies[2], copies[0], copies[1]):
            for copy in kind:
                copy.start()
        for k in range(near):
            group_out[k * count : (k + 1) * count, :] = parts[k][...]
        for copy in copies[2]:
            copy.wait()
        for low, high in column_steps(inner, 256):
            grad = dot(group_out[...], weight[2, :, low:high], 1, 0)
            for i in range(2):
                slope = slopes_ref[i, :, low:high].astype(jnp.float32)
                both_out[i, :, low:high] = (grad * slope).astype(jnp.bfloat16)
        if lanes > inner:
            both_out[:, :, inner:] = jnp.zeros((2, total, lanes - inner), jnp.bfloat16)
        for kind in copies[:2]:
            for copy in kind:
                copy.wait()
        for low, high in column_steps(width, 256):
            part = dot(both_out[0, :, :inner], weight[0, low:high, :], 1, 1)
            part = part + dot(both_out[1, :, :inner], weight[1, low:high, :], 1, 1)
            for k in range(near):
                sums[k][:, low:high] = part[k * count : (k + 1) * count].astype(sums[k].dtype)

    return kernel_call(
        body,
        [((total, width), jnp.bfloat16)]
        + [((2, total, lanes), jnp.bfloat16)]
        + [((count, width), jnp.float32 if with_own and k == 0 else jnp.bfloat16) for k in range(near)],
        [where, slopes, *pair, *last, *pieces],
        {0: "smem", **{2 + i: "any" for i in range(2 * spots)}},
        [
            pltpu.VMEM((kinds, width, inner), jnp.bfloat16),
            pltpu.SemaphoreType.DMA((kinds, spots)),
        ],
        grant=whole_vmem,
    )


def wide_grads(where, lefts, rights):
    width = lefts[0].shape[1]
    total = sum(left.shape[0] for left in lefts)
    lanes = rights[0][0][0].shape[-1]
    kinds = len(rights)
    chunk = width // 8
    first, second = halves_of(chunk)
    arrays = []
    for array in [r for right in rights for r, _ in right]:
        if all(array is not other for other in arrays):
            arrays.append(array)
    spots = [[[array is other for other in arrays].index(True) for array, _ in right] for right in rights]
    most = max(len(right) for right in rights)

    def body(where_ref, *rest):
        left_refs, right_refs = rest[: len(lefts)], rest[len(lefts) : len(lefts) + len(arrays)]
        outs = rest[len(lefts) + len(arrays) : len(lefts) + len(arrays) + 4]
        turned, left, values, sems = rest[len(lefts) + len(arrays) + 4 :]
        copies = []
        for m, right in enumerate(rights):
            at, row = [], 0
            for i, (array, index) in enumerate(right):
                ref = right_refs[spots[m][i]]
                size = array.shape[-2]
                at.append(
                    pltpu.make_async_copy(
                        ref if index is None else ref.at[index],
                        values.at[m, pl.ds(row, size)],
                        sems.at[m, i],
                    )
                )
                row += size
            copies.append(at)
        for part in copies:
            for copy in part:
                copy.start()
        core, x, y = where_ref[1], where_ref[2], where_ref[3]
        order = []
        for flip in (1, 0):
            order.append([(j * 2 + jnp.bitwise_xor(x, flip), 0, first) for j in range(2)])
        for flip in (1, 0):
            order.append([(jnp.bitwise_xor(y, flip) * 2 + j, first, second) for j in range(2)])
        row = 0
        for ref in left_refs:
            turned[:, row : row + ref.shape[0]] = ref[...].T
            row += ref.shape[0]
        at = 0
        for block in order:
            for plane, offset, size in block:
                start = pl.multiple_of((plane * 2 + core) * chunk + offset, 16)
                left[at : at + size, :] = turned[pl.ds(start, size), :]
                at += size
        for m in range(kinds):
            for copy in copies[m]:
                copy.wait()
            for low, high in column_steps(lanes, 256):
                part = dot(left[...], values[m, :, low:high], 1, 0).astype(jnp.bfloat16)
                at = 0
                for out, block in zip(outs, order):
                    size = 2 * block[0][2]
                    out[m, :, low:high] = part[at : at + size]
                    at += size

    return kernel_call(
        body,
        [
            ((kinds, 2 * first, lanes), jnp.bfloat16),
            ((kinds, 2 * first, lanes), jnp.bfloat16),
            ((kinds, 2 * second, lanes), jnp.bfloat16),
            ((kinds, 2 * second, lanes), jnp.bfloat16),
        ],
        [where, *lefts, *arrays],
        {0: "smem", **{1 + len(lefts) + i: "any" for i in range(len(arrays))}},
        [
            pltpu.VMEM((width, total), jnp.bfloat16),
            pltpu.VMEM((width // 2, total), jnp.bfloat16),
            pltpu.VMEM((kinds, total, lanes), jnp.bfloat16),
            pltpu.SemaphoreType.DMA((kinds, most)),
        ],
        grant=whole_vmem,
    )


def wide_middle(where, wides, gots):
    sizes = [wide[0].shape[0] for wide in wides]
    kinds = sum(sizes)
    first, second = wides[0][1].shape[1] // 2, wides[0][3].shape[1] // 2
    lanes = wides[0][1].shape[2]
    args = [a for wide, got in zip(wides, gots) for a in (wide[1], got[0], wide[3], got[1])]

    def body(where_ref, *rest):
        refs, outs = rest[: len(args)], rest[len(args) :]
        x, y = where_ref[2], where_ref[3]
        at = 0
        for i, size in enumerate(sizes):
            kept_a, got_a, kept_b, got_b = refs[4 * i : 4 * i + 4]
            for m in range(size):
                for kept, got, place, rows, pair in (
                    (kept_a, got_a, y, first, outs[:2]),
                    (kept_b, got_b, x, second, outs[2:]),
                ):
                    for flip, out in ((1, pair[0]), (0, pair[1])):
                        spot = pl.ds(
                            pl.multiple_of(jnp.bitwise_xor(place, flip) * rows, 16), rows
                        )
                        total = kept[m, spot, :].astype(jnp.float32) + got[m, spot, :].astype(
                            jnp.float32
                        )
                        out[at] = total.astype(jnp.bfloat16)
                at += 1

    return kernel_call(
        body,
        [((kinds, first, lanes), jnp.bfloat16)] * 2 + [((kinds, second, lanes), jnp.bfloat16)] * 2,
        [where, *args],
        {0: "smem"},
        grant=whole_vmem,
    )


def wide_last(wide, got, inner):
    (_, kept_a, _, kept_b), (got_a, got_b) = wide, got
    kinds, first, _ = kept_a.shape
    second = kept_b.shape[1]

    def body(kept_a_ref, got_a_ref, kept_b_ref, got_b_ref, *outs):
        for m in range(kinds):
            total = kept_a_ref[m].astype(jnp.float32) + got_a_ref[m].astype(jnp.float32)
            outs[m][:first, :] = total[:, :inner]
            total = kept_b_ref[m].astype(jnp.float32) + got_b_ref[m].astype(jnp.float32)
            outs[m][first:, :] = total[:, :inner]

    return kernel_call(
        body,
        [((first + second, inner), jnp.float32)] * kinds,
        [kept_a, got_a, kept_b, got_b],
    )


def attend_back(
    where,
    parts,
    after,
    cotangent,
    valid,
    attn_raw,
    norm_pre,
    norm_attn,
    norm_query,
    probs,
    query,
    raw,
    both,
    pieces,
    out_rows,
    cosine,
    sine,
    heads,
):
    count, width = after.shape
    seqs, _, span = probs.shape
    each = count // seqs
    head_dim = norm_query.shape[1]
    inv_root = head_dim ** (-0.5)
    near, spots = len(both), len(pieces)
    tall, wide = pieces[0].shape

    def body(
        where_ref,
        after_ref,
        cot_ref,
        valid_ref,
        attn_ref,
        pre_ref,
        norm_ref,
        query_gain_ref,
        probs_ref,
        query_ref,
        raw_ref,
        cos_ref,
        sin_ref,
        *rest,
    ):
        shards, rest = rest[:spots], rest[spots:]
        sums = rest[:near]
        got = rest[near : 2 * near]
        rest = rest[2 * near :]
        dx_out, attn_grad_out, raw_grad_out, pre_out, attn_gain_out, query_gain_out = rest[:6]
        both_outs = rest[6 : 6 + near]
        mixed_grad, query_grad, weight, sems = rest[6 + near :]
        copies = load_columns(where_ref[0], shards, tall, out_rows, wide - width, weight, sems)
        grad = sums[0][...]
        for s in sums[1:]:
            grad = grad + s[...].astype(jnp.float32)
        through, gain = norm_back(after_ref[...], pre_ref[...], grad)
        pre_out[...] = gain
        dx = cot_ref[...].astype(jnp.float32) + through
        dx_out[...] = dx
        attn_grad, gain = norm_back(attn_ref[...], norm_ref[...], valid_ref[...] * dx)
        attn_gain_out[...] = gain
        attn_grad = attn_grad.astype(jnp.bfloat16)
        attn_grad_out[...] = attn_grad
        for copy in copies:
            copy.wait()
        mixed_grad[...] = dot(attn_grad, weight[...], 1, 1).astype(jnp.bfloat16)
        for s in range(seqs):
            rows = slice(s * each, (s + 1) * each)
            queries = jnp.concatenate(
                [query_ref[rows, h * head_dim : (h + 1) * head_dim] for h in range(heads)], axis=0
            )
            grads = jnp.concatenate(
                [mixed_grad[rows, h * head_dim : (h + 1) * head_dim] for h in range(heads)], axis=0
            )
            keys = jnp.concatenate([g[rows, :head_dim] for g in got], axis=0)
            values = jnp.concatenate([g[rows, head_dim:] for g in got], axis=0)
            probs = probs_ref[s]
            prob_grad = dot(grads, values, 1, 1)
            row = jnp.sum(probs * prob_grad, axis=-1, keepdims=True)
            score_grad = (probs * (prob_grad - row)).astype(jnp.bfloat16)
            back = dot(score_grad, keys, 1, 0) * inv_root
            for h in range(heads):
                query_grad[rows, h * head_dim : (h + 1) * head_dim] = back[
                    h * each : (h + 1) * each
                ]
            keys_grad = dot(score_grad, queries, 0, 0) * inv_root
            values_grad = dot(probs.astype(jnp.bfloat16), grads, 0, 0)
            for k in range(near):
                part = slice(k * each, (k + 1) * each)
                both_outs[k][rows, :head_dim] = keys_grad[part].astype(both_outs[k].dtype)
                both_outs[k][rows, head_dim:] = values_grad[part].astype(both_outs[k].dtype)
        cos, sin = cos_ref[...], sin_ref[...]
        gain_sum = jnp.zeros((1, head_dim), jnp.float32)
        for h in range(heads):
            cols = slice(h * head_dim, (h + 1) * head_dim)
            turned = rotate_back(query_grad[:, cols], cos, sin)
            value_grad, gain = norm_back(raw_ref[:, cols], query_gain_ref[...], turned)
            raw_grad_out[:, cols] = value_grad.astype(jnp.bfloat16)
            gain_sum = gain_sum + gain
        query_gain_out[...] = gain_sum

    return kernel_call(
        body,
        [
            ((count, width), jnp.float32),
            ((count, width), jnp.bfloat16),
            ((count, heads * head_dim), jnp.bfloat16),
            ((1, width), jnp.float32),
            ((1, width), jnp.float32),
            ((1, head_dim), jnp.float32),
            ((count, 2 * head_dim), jnp.float32),
        ]
        + [((count, 2 * head_dim), jnp.bfloat16)] * (near - 1),
        [
            where,
            after,
            cotangent,
            valid,
            attn_raw,
            norm_pre,
            norm_attn,
            norm_query,
            probs,
            query,
            raw,
            cosine,
            sine,
            *pieces,
            *parts,
            *both,
        ],
        {0: "smem", **{13 + i: "any" for i in range(spots)}},
        [
            pltpu.VMEM((count, heads * head_dim), jnp.bfloat16),
            pltpu.VMEM((count, heads * head_dim), jnp.float32),
            pltpu.VMEM((heads * head_dim, width), jnp.bfloat16),
            pltpu.SemaphoreType.DMA((spots,)),
        ],
        grant=whole_vmem,
    )


def project_back(
    where,
    parts,
    raw,
    query_grad,
    tokens,
    dx,
    norm_in,
    norm_key,
    cosine,
    sine,
    pieces,
    heads,
    ctx,
    gains,
):
    count, width = tokens.shape
    tall_piece = pieces[0].shape[0]
    head_dim = norm_key.shape[1]
    wide = (heads + 2) * head_dim
    near, spots, total = len(parts), len(pieces), 8
    each = wide // ctx
    count_gains = len(gains)
    tall = count + 16

    def body(
        where_ref, raw_ref, query_ref, x_ref, dx_ref, in_ref, key_ref, cos_ref, sin_ref, *rest
    ):
        sums = rest[:near]
        shards = rest[near : near + spots]
        others = rest[near + spots : near + spots + count_gains]
        input_out = rest[near + spots + count_gains]
        outs = rest[near + spots + count_gains + 1 : near + spots + count_gains + 1 + ctx]
        weight, grads_out, gains_out, sems = rest[near + spots + count_gains + 1 + ctx :]
        copies = load_columns(
            where_ref[0], shards, tall_piece, tall_piece - 16, 0, weight, sems
        )
        grad = sums[0][...]
        for s in sums[1:]:
            grad = grad + s[...].astype(jnp.float32)
        turned = rotate_back(grad[:, :head_dim], cos_ref[...], sin_ref[...])
        key_grad, key_gain = norm_back(raw_ref[:, heads * head_dim :], key_ref[...], turned)
        grads_out[:, : heads * head_dim] = query_ref[...]
        grads_out[:, heads * head_dim : (heads + 1) * head_dim] = key_grad.astype(jnp.bfloat16)
        grads_out[:, (heads + 1) * head_dim :] = grad[:, head_dim:].astype(jnp.bfloat16)
        for copy in copies:
            copy.wait()
        back = dot(grads_out[...], weight[...], 1, 1)
        through, in_gain = norm_back(x_ref[...].astype(jnp.float32), in_ref[...], back)
        input_out[...] = (dx_ref[...] + through).astype(jnp.bfloat16)
        gains_out[...] = jnp.zeros((16, wide), jnp.float32)
        lane = 0
        for gain in (in_gain, others[0][...], key_gain, *[o[...] for o in others[1:]]):
            size = gain.shape[1] // (total * ctx)
            for d in range(total):
                for c in range(ctx):
                    at = c * each + lane
                    gains_out[d : d + 1, at : at + size] = gain[
                        :, (d * ctx + c) * size : (d * ctx + c + 1) * size
                    ]
            lane += size
        spans = [(0, heads * head_dim), (heads * head_dim, head_dim), ((heads + 1) * head_dim, head_dim)]
        mine = where_ref[4]
        for c in range(ctx):

            @pl.when(mine == c)
            def _(c=c):
                for k in range(ctx):
                    j, at = (c + k) % ctx, 0
                    for first, size in spans:
                        step = size // ctx
                        outs[k][:count, at : at + step] = grads_out[
                            :, first + j * step : first + (j + 1) * step
                        ]
                        at += step
                    outs[k][count:, :] = gains_out[:, j * each : (j + 1) * each].astype(
                        jnp.bfloat16
                    )

    return kernel_call(
        body,
        [((count, width), jnp.bfloat16)] + [((tall, each), jnp.bfloat16)] * ctx,
        [
            where,
            raw,
            query_grad,
            tokens,
            dx,
            norm_in,
            norm_key,
            cosine,
            sine,
            *parts,
            *pieces,
            *gains,
        ],
        {0: "smem", **{9 + near + i: "any" for i in range(spots)}},
        [
            pltpu.VMEM((width, wide), jnp.bfloat16),
            pltpu.VMEM((count, wide), jnp.bfloat16),
            pltpu.VMEM((16, wide), jnp.float32),
            pltpu.SemaphoreType.DMA((spots,)),
        ],
        grant=whole_vmem,
    )


def narrow_grads(where, lefts, rights, with_gains):
    count, width = lefts[0].shape
    wide = rights[0].shape[1]
    chunk, near = width // 8, len(lefts)
    total = near * count
    tall = chunk + 16 if with_gains else chunk

    def body(where_ref, *rest):
        left_refs, right_refs, outs = rest[:near], rest[near : 2 * near], rest[2 * near : -3]
        turned, lines, values = rest[-3:]
        for i in range(near):
            turned[:, i * count : (i + 1) * count] = left_refs[i][...].T
            values[i * count : (i + 1) * count, :] = right_refs[i][:count, :]
        plane, core = where_ref[0] // 2, where_ref[1]
        for m in range(4):
            start = pl.multiple_of((jnp.bitwise_xor(plane, m) * 2 + core) * chunk, 16)
            lines[m * chunk : (m + 1) * chunk, :] = turned[pl.ds(start, chunk), :]
        for low, high in column_steps(wide, 256):
            part = dot(lines[...], values[:, low:high], 1, 0)
            for m in range(4):
                outs[m][:chunk, low:high] = part[m * chunk : (m + 1) * chunk].astype(outs[m].dtype)
        if with_gains:
            whole = right_refs[0][count:, :].astype(jnp.float32)
            for r in right_refs[1:]:
                whole = whole + r[count:, :].astype(jnp.float32)
            index = lax.broadcasted_iota(jnp.int32, whole.shape, 0)
            for m in range(4):
                row = jnp.bitwise_xor(plane, m) * 2 + core
                row = jnp.sum(jnp.where(index == row, whole, 0.0), axis=0, keepdims=True)
                outs[m][chunk:, :] = jnp.where(index == 0, row, 0.0).astype(outs[m].dtype)

    return kernel_call(
        body,
        [((tall, wide), jnp.float32)] + [((tall, wide), jnp.bfloat16)] * 3,
        [where, *lefts, *rights],
        {0: "smem"},
        [
            pltpu.VMEM((width, total), jnp.bfloat16),
            pltpu.VMEM((width // 2, total), jnp.bfloat16),
            pltpu.VMEM((total, wide), jnp.bfloat16),
        ],
    )


def narrow_middle(where, parts, sizes, ctx):
    chunk, wide = parts[0].shape
    each = wide // ctx

    def body(where_ref, *rest):
        got = rest[: len(parts)]
        outs = rest[len(parts) :]
        mine = where_ref[4]
        total = got[0][...]
        for g in got[1:]:
            total = total + g[...].astype(jnp.float32)
        for c in range(ctx):

            @pl.when(mine == c)
            def _(c=c):
                for k in range(ctx):
                    j = (c + k) % ctx
                    start, at = 0, 0
                    for size in sizes:
                        piece = size // ctx
                        outs[k][:, at : at + piece] = total[
                            :, start + j * piece : start + (j + 1) * piece
                        ].astype(outs[k].dtype)
                        start += size
                        at += piece

    return kernel_call(
        body,
        [((chunk, each), jnp.float32)] + [((chunk, each), jnp.bfloat16)] * (ctx - 1),
        [where, *parts],
        {0: "smem"},
    )


def narrow_last(blocks, out_blocks, sizes, cols):
    rows = out_blocks[0].shape[0]
    near = len(blocks)
    q, k, v = cols

    def body(*rest):
        outs = rest[2 * near :]
        total = rest[0][...]
        for r in rest[1:near]:
            total = total + r[...].astype(jnp.float32)
        outs[0][...] = total[:rows, :q]
        turned = total[:rows, q:].T
        outs[1][...] = turned[:k]
        outs[2][...] = turned[k:]
        out = rest[near][...]
        for r in rest[near + 1 : 2 * near]:
            out = out + r[...].astype(jnp.float32)
        outs[3][...] = out
        start = 0
        for ref, size in zip(outs[4:], sizes):
            ref[...] = total[rows : rows + 1, start : start + size]
            start += size

    return kernel_call(
        body,
        [
            ((rows, q), jnp.float32),
            ((k, rows), jnp.float32),
            ((v, rows), jnp.float32),
            ((rows, out_blocks[0].shape[1]), jnp.float32),
        ]
        + [((1, size), jnp.float32) for size in sizes],
        [*blocks, *out_blocks],
    )


def split_pair(where, gate, up, ctx):
    rows, whole = gate.shape
    inner = whole // ctx

    def body(where_ref, gate_ref, up_ref, *outs):
        mine = where_ref[4]
        for c in range(ctx):

            @pl.when(mine == c)
            def _(c=c):
                for k in range(ctx):
                    j = (c + k) % ctx
                    outs[k][0] = gate_ref[:, j * inner : (j + 1) * inner]
                    outs[k][1] = up_ref[:, j * inner : (j + 1) * inner]

    return kernel_call(
        body, [((2, rows, inner), jnp.bfloat16)] * ctx, [where, gate, up], {0: "smem"}, grant=whole_vmem
    )


def join_pair(where, pieces):
    ctx = len(pieces)
    _, rows, inner = pieces[0].shape

    def body(where_ref, *rest):
        got, out, wide = rest[:ctx], rest[ctx], rest[ctx + 1]
        mine = where_ref[4]
        for c in range(ctx):

            @pl.when(mine == c)
            def _(c=c):
                for m in range(2):
                    for a in range(ctx):
                        wide[a * rows : (a + 1) * rows, :] = got[(c - a) % ctx][m].astype(
                            jnp.float32
                        )
                    out[m] = wide[...].astype(jnp.bfloat16)

    return kernel_call(
        body,
        [((2, ctx * rows, inner), jnp.bfloat16)],
        [where, *pieces],
        {0: "smem"},
        [pltpu.VMEM((ctx * rows, inner), jnp.float32)],
    )[0]


def split_down(where, pieces, rows, ctx):
    groups = 2 * len(pieces)
    _, chunk, part = pieces[0].shape
    per, steps = groups // ctx, chunk // rows

    def body(where_ref, *rest):
        got, outs, (wide, down_ref) = rest[:4], rest[4 : 4 + ctx], rest[4 + ctx :]
        mine = where_ref[4]
        plane, core = where_ref[0] // 2, where_ref[1]
        for m in range(4):
            for flip in range(2):
                group = jnp.bitwise_xor(plane, m) * 2 + jnp.bitwise_xor(core, flip)
                down_ref[pl.ds(group, 1)] = got[m][flip][None]
        for c in range(ctx):

            @pl.when(mine == c)
            def _(c=c):
                for k in range(ctx):
                    j = (c + k) % ctx
                    for b in range(groups):
                        first = b % steps * rows
                        wide[:, b * part : (b + 1) * part] = down_ref[
                            j * per + b // steps, first : first + rows, :
                        ].astype(jnp.float32)
                    outs[k][...] = wide[...].astype(jnp.bfloat16)

    return kernel_call(
        body,
        [((rows, groups * part), jnp.bfloat16)] * ctx,
        [where, *pieces],
        {0: "smem"},
        [
            pltpu.VMEM((rows, groups * part), jnp.float32),
            pltpu.VMEM((groups, chunk, part), jnp.bfloat16),
        ],
    )


def join_down(where, pieces, part):
    ctx = len(pieces)
    rows, inner = pieces[0].shape
    chunk, groups = ctx * rows, inner // part

    def body(where_ref, *rest):
        got, out, wide = rest[:ctx], rest[ctx], rest[ctx + 1]
        mine = where_ref[4]
        for c in range(ctx):

            @pl.when(mine == c)
            def _(c=c):
                for a in range(ctx):
                    piece = got[(c - a) % ctx][...].astype(jnp.float32)
                    for b in range(groups):
                        first = b % ctx * rows
                        at = (b // ctx * ctx + a) * part
                        wide[first : first + rows, at : at + part] = piece[
                            :, b * part : (b + 1) * part
                        ]
                out[...] = wide[...].astype(jnp.bfloat16)

    return kernel_call(
        body,
        [((chunk, inner), jnp.bfloat16)],
        [where, *pieces],
        {0: "smem"},
        [pltpu.VMEM((chunk, inner), jnp.float32)],
    )[0]


def join_rows(where, pieces, rows, split, out_rows):
    ctx = len(pieces)
    _, wide = pieces[0].shape
    tall = ctx * rows + 16

    def body(where_ref, *rest):
        got, out, lines = rest[:ctx], rest[ctx], rest[ctx + 1]
        mine = where_ref[4]
        lines[ctx * rows :, :] = jnp.zeros((16, wide), jnp.float32)
        lines[ctx * out_rows :, split:] = jnp.zeros((tall - ctx * out_rows, wide - split), jnp.float32)
        for c in range(ctx):

            @pl.when(mine == c)
            def _(c=c):
                for a in range(ctx):
                    piece = got[(c - a) % ctx]
                    lines[a * rows : (a + 1) * rows, :split] = piece[:rows, :split].astype(
                        jnp.float32
                    )
                    lines[a * out_rows : (a + 1) * out_rows, split:] = piece[
                        :out_rows, split:
                    ].astype(jnp.float32)
                    at = ctx * rows + a
                    lines[at : at + 1, :split] = piece[rows : rows + 1, :split].astype(jnp.float32)
                out[...] = lines[...].astype(jnp.bfloat16)

    return kernel_call(
        body,
        [((tall, wide), jnp.bfloat16)],
        [where, *pieces],
        {0: "smem"},
        [pltpu.VMEM((tall, wide), jnp.float32)],
    )[0]


def plane_send(parts):
    size = lax.axis_size("dp")
    return [parts[0]] + [
        lax.ppermute(parts[m], "dp", [(i, i ^ (2 * m)) for i in range(size)])
        for m in range(1, len(parts))
    ]


def ctx_send(parts, sign):
    return [parts[0]] + [shift(parts[k], sign * k) for k in range(1, len(parts))]


def stage(*values):
    return lax.optimization_barrier(values)


def gate(value, *conditions):
    return lax.optimization_barrier((value, conditions))[0]


def fused(
    tokens,
    cotangent,
    lengths,
    w_query,
    w_key,
    w_value,
    w_out,
    w_gate,
    w_up,
    w_down,
    gain_in,
    gain_query,
    gain_key,
    gain_attn,
    gain_pre,
    gain_post,
):
    count, width = tokens.shape
    seq_count = lengths.shape[1]
    stretch = count // (2 * seq_count)
    dp = lax.axis_size("dp")
    ctx = lax.axis_size("ctx")
    mine = lax.axis_index("ctx")
    group = lax.axis_index("dp")
    head_dim = w_key.shape[1]
    heads = w_query.shape[1] // head_dim
    where = jnp.stack([group, group % 2, group // 2 % 2, group // 4, mine]).astype(jnp.int32)

    gains = [gain_in, gain_query, gain_key, gain_attn, gain_pre, gain_post]
    sizes = [g.shape[0] for g in gains]
    chunk, out_rows = width // dp, heads * head_dim // dp
    order = [0, 1, 3, 2]
    packed, kept, sent = pack(where, w_query, w_key, w_value, w_out, w_down, gains)
    split = packed.shape[1] - width
    packed = ctx_gather(packed)
    got = swap(sent, 0)
    aux = tables(where, lengths, count, stretch, ctx, head_dim)
    blocks = split_pair(where, w_gate, w_up, ctx)
    kept = gate(kept, aux, blocks)
    downs = plane_send([jnp.stack([kept[m], got[m]]) for m in range(4)])
    packed, downs, aux, blocks = stage(packed, downs, aux, list(blocks))
    cosine, sine, valid, allowed = aux

    blocks = ctx_send(blocks, 1)
    near = plane_near(join_rows(where, packed, w_query.shape[0], split, w_out.shape[0]))
    shared = plane_whole(near)
    pair = join_pair(where, blocks)
    shared, pair, downs = stage(shared, pair, downs)

    normed, query, both, raw, norm_in, norm_query, norm_key = project(
        where, tokens, shared, sizes[:3], cosine, sine, heads, ctx
    )
    pair, normed, query, both, downs = stage(pair, normed, query, both, downs)

    pair = plane_near(pair)
    downs = list(split_down(where, downs, w_gate.shape[0], ctx))
    norm_attn, norm_pre, norm_post = late_gains(
        where, shared, [384, 512, 640], sizes[3:], ctx, both
    )
    both = ctx_gather(both)
    downs = ctx_send(gate(downs, both), 1)
    probs, mixed, attn_raw, residual, normed_two = attend(
        where,
        tokens,
        query,
        both,
        allowed,
        valid,
        norm_attn,
        norm_pre,
        shared,
        out_rows,
        heads,
    )
    pair, pair_cut, downs, normed_two, mixed = stage(pair, cut(pair), downs, normed_two, mixed)

    last = plane_near(join_down(where, downs, w_down.shape[0]))
    two_pieces = [normed_two] + [shift(normed_two, k) for k in order[1:-1]]
    pair_far = [swap(pair[0], 0)]
    two_pieces, pair, pair_far, last, last_cut, normed = stage(
        two_pieces, pair, pair_far, last, cut(last), normed
    )

    two_pieces.append(shift(two_pieces[0], order[-1]))
    pair = pair + diagonal(pair_cut)
    pair_far = pair_far + [swap(p, 0) for p in pair[1:3]]
    two_pieces, pair, pair_far, last, last_cut, normed = stage(
        two_pieces, pair, pair_far, last, last_cut, normed
    )

    last = last + diagonal(last_cut)
    pair_far = pair_far + [swap(p, 0) for p in pair[3:]]
    pair, last = pair + pair_far, last + [swap(p, 0) for p in last]
    two_pieces, pair, last, normed = stage(two_pieces, pair, last, normed)

    weights = (pair, last)
    normed_group = [normed, shift(normed, 1), None, shift(normed, 3)]
    group_two, act, slopes, *sums = feed_forward(where, two_pieces[:-1], weights, True)
    group_two, act, slopes, sums, near_group = stage(
        group_two, act, slopes, sums, [normed_group[1], normed_group[3]]
    )
    normed_group[1], normed_group[3] = near_group

    sums = [sums[0]] + [shift(sums[i], -order[i]) for i in range(1, ctx - 1)]
    two_last, act_last, slopes_last, sum_last = feed_forward(
        where, two_pieces[-1:], weights, False
    )
    sums, two_last, act_last, slopes_last, sum_last, group_two, act, mixed = stage(
        sums, two_last, act_last, slopes_last, sum_last, group_two, act, mixed
    )

    sums.append(shift(sum_last, -order[-1]))
    group_two, act = [group_two, two_last], [act, act_last]
    group_two_far, act_far = [swap(g, 0) for g in group_two], [swap(a, 0) for a in act]
    mixed_far = swap(mixed, 0)
    sums, group_two_far, act_far, mixed_far = stage(sums, group_two_far, act_far, mixed_far)

    output, ffn_grad, gain_post_grad = finish(sums, residual, cotangent, valid, norm_post)
    ffn_early = [ffn_grad] + [shift(ffn_grad, k) for k in order[1:-1]]
    ffn_early, ffn_grad = stage(ffn_early, ffn_grad)

    ffn_last = shift(ffn_grad, order[-1])
    group_ffn, grads, *sums = feed_back(where, ffn_early, weights, slopes, True)
    ffn_last, group_ffn, grads, sums = stage(ffn_last, group_ffn, grads, sums)

    ffn_parts = [group_ffn, ffn_last]
    ffn_far = [swap(f, 0) for f in ffn_parts]
    grads_far = swap(grads, 0)
    _, grads_last, sum_last = feed_back(
        where, [ffn_last], weights, slopes_last, False
    )
    sums[1], sums[2] = shift(sums[1], -order[1]), shift(sums[2], -order[2])
    down_wide = wide_grads(
        where, gate(ffn_parts, grads_last) + ffn_far, [[(a, None) for a in act + act_far]]
    )
    grads_last, sum_last, grads, grads_far, sums, down_wide = stage(
        grads_last, sum_last, grads, grads_far, sums, down_wide
    )

    sums.append(shift(sum_last, -order[-1]))
    down_got = [swap(down_wide[0], 1), swap(down_wide[2], 2)]
    all_grads = [grads, grads_last, grads_far, swap(grads_last, 0)]
    pair_wide = wide_grads(
        where, group_two + group_two_far, [[(g, m) for g in all_grads] for m in range(2)]
    )
    sums, down_wide, down_got, pair_wide = stage(sums, down_wide, down_got, pair_wide)

    pair_got = [swap(pair_wide[0], 1), swap(pair_wide[2], 2)]
    dx, attn_grad, query_grad, gain_pre_grad, gain_attn_grad, gain_query_grad, *parts = attend_back(
        where,
        sums,
        residual,
        cotangent,
        valid,
        attn_raw,
        norm_pre,
        norm_attn,
        norm_query,
        probs,
        query,
        raw,
        both,
        shared,
        out_rows,
        cosine,
        sine,
        heads,
    )
    parts = ctx_send(parts, -1)
    out_blocks = narrow_grads(
        where, [attn_grad, swap(attn_grad, 0)], [mixed, mixed_far], False
    )
    parts, pair_got, out_blocks, query_grad, dx, normed = stage(
        parts, pair_got, out_blocks, query_grad, dx, normed
    )

    input_grad, *blocks = project_back(
        where,
        parts,
        raw,
        query_grad,
        tokens,
        dx,
        norm_in,
        norm_key,
        cosine,
        sine,
        shared,
        heads,
        ctx,
        [gain_query_grad, gain_attn_grad, gain_pre_grad, gain_post_grad],
    )
    normed_group[2] = shift(normed, 2)
    out_blocks = plane_send(out_blocks)
    wide = wide_middle(where, [pair_wide, down_wide], [pair_got, down_got])
    blocks, out_blocks, wide, normed_group = stage(list(blocks), out_blocks, wide, normed_group)

    blocks = ctx_send(blocks, 1)
    wide_got = [swap(wide[0], 2), swap(wide[2], 1)]
    normed_far = [swap(n, 0) for n in normed_group]
    blocks = narrow_grads(
        where, normed_group + normed_far, blocks + [swap(b, 0) for b in blocks], True
    )
    out_blocks = narrow_middle(where, out_blocks, [mixed.shape[1]], ctx)
    wide_got, out_blocks, blocks = stage(wide_got, out_blocks, blocks)

    blocks, out_blocks = plane_send(blocks), ctx_send(out_blocks, 1)
    grad_gate, grad_up, grad_down = wide_last(wide, wide_got, w_gate.shape[1] // ctx)
    blocks, out_blocks, grad_gate = stage(blocks, out_blocks, grad_gate)

    q_cols, k_cols = heads * head_dim // ctx, head_dim // ctx
    grad_query, grad_key, grad_value, grad_out, *gain_outs = narrow_last(
        blocks, out_blocks, sizes, (q_cols, k_cols, k_cols)
    )
    return (
        output,
        input_grad,
        grad_query,
        grad_key.T,
        grad_value.T,
        grad_out.T,
        grad_gate,
        grad_up,
        grad_down.T,
        *[g.reshape(-1) for g in gain_outs],
    )


def on_device(tokens, cotangent, lengths, *params):
    dp, ctx = lax.axis_size("dp"), lax.axis_size("ctx")
    each = tokens.shape[0] // lengths.shape[1]
    fits = dp == 8 and dp % ctx == 0 and tokens.shape[1] // dp % 16 == 0 and each % 16 == 0
    run = fused if fits else plain
    return run(tokens, cotangent, lengths, *params)


def solution(mesh):
    in_specs = (
        P(("dp", "ctx"), None),
        P(("dp", "ctx"), None),
        P("dp", None),
        P(("dp", "ctx"), None),
        P(("dp", "ctx"), None),
        P(("dp", "ctx"), None),
        P(("dp", "ctx"), None),
        P(("dp", "ctx"), None),
        P(("dp", "ctx"), None),
        P(("dp", "ctx"), None),
        P(("dp", "ctx")),
        P(("dp", "ctx")),
        P(("dp", "ctx")),
        P(("dp", "ctx")),
        P(("dp", "ctx")),
        P(("dp", "ctx")),
    )
    out_specs = (
        P(("dp", "ctx"), None),
        P(("dp", "ctx"), None),
        P("dp", "ctx"),
        P("dp", "ctx"),
        P("dp", "ctx"),
        P("ctx", "dp"),
        P("dp", "ctx"),
        P("dp", "ctx"),
        P("ctx", "dp"),
        P(("dp", "ctx")),
        P(("dp", "ctx")),
        P(("dp", "ctx")),
        P(("dp", "ctx")),
        P(("dp", "ctx")),
        P(("dp", "ctx")),
    )
    return jax.shard_map(
        on_device, mesh=mesh, in_specs=in_specs, out_specs=out_specs, check_vma=False
    )
```

```python
import jax
import jax.numpy as jnp
import numpy as np
from jax import lax
from jax.experimental import pallas as pl
from jax.experimental.pallas import tpu as pltpu
from jax.sharding import PartitionSpec as P

epsilon = 1e-06
rope_base = 1000000.0


def rms_norm(value, weight):
    scale = lax.rsqrt(jnp.mean(value * value, axis=-1, keepdims=True) + epsilon)
    return value * scale * (1.0 + weight)


def rms_back(value, weight, grad):
    scale = lax.rsqrt(jnp.mean(value * value, axis=-1, keepdims=True) + epsilon)
    normed = value * scale
    weighted = grad * (1.0 + weight)
    value_grad = scale * (weighted - normed * jnp.mean(weighted * normed, axis=-1, keepdims=True))
    weight_grad = jnp.sum(grad * normed, axis=tuple(range(value.ndim - 1)))
    return (value_grad, weight_grad)


def rope_tables(positions, width):
    half = width // 2
    freqs = jnp.power(rope_base, -2.0 * jnp.arange(half, dtype=jnp.float32) / width)
    angles = positions[:, None] * freqs[None, :]
    cosine = jnp.concatenate([jnp.cos(angles), jnp.cos(angles)], axis=-1)
    sine = jnp.concatenate([jnp.sin(angles), jnp.sin(angles)], axis=-1)
    return (cosine, sine)


def rotate(value, cosine, sine):
    half = value.shape[-1] // 2
    turned = jnp.concatenate([-value[..., half:], value[..., :half]], axis=-1)
    return value * cosine + turned * sine


def rotate_back(grad, cosine, sine):
    half = grad.shape[-1] // 2
    scaled = grad * sine
    return grad * cosine + jnp.concatenate([scaled[..., half:], -scaled[..., :half]], axis=-1)


def geglu(gate, upper):
    return jax.nn.gelu(gate, approximate=True) * upper


def dot(left, right, left_dim, right_dim):
    return lax.dot_general(
        left, right, (((left_dim,), (right_dim,)), ((), ())), preferred_element_type=jnp.float32
    )


def swap(value, bit):
    size = lax.axis_size("dp")
    return lax.ppermute(value, "dp", [(i, i ^ (1 << bit)) for i in range(size)])


def shift(value, step):
    size = lax.axis_size("ctx")
    return lax.ppermute(value, "ctx", [(i, (i + step) % size) for i in range(size)])


def pick(value, index, axis=0):
    return lax.dynamic_index_in_dim(value, index, axis, keepdims=False)


def plane_bits():
    return list(range(1, lax.axis_size("dp").bit_length() - 1))


def ctx_gather(value):
    return [value] + [shift(value, k) for k in range(1, lax.axis_size("ctx"))]


def ctx_ordered(pieces):
    size = lax.axis_size("ctx")
    stacked = jnp.stack(pieces)
    mine = lax.axis_index("ctx")
    return jnp.stack([pick(stacked, (mine - a + size) % size) for a in range(size)])


def ctx_reduce(pieces):
    total = pieces[0].astype(jnp.float32)
    for k in range(1, len(pieces)):
        total = total + shift(pieces[k].astype(jnp.bfloat16), -k).astype(jnp.float32)
    return total


def ctx_exchange(blocks):
    size = lax.axis_size("ctx")
    mine = lax.axis_index("ctx")
    return [pick(blocks, mine)] + [
        shift(pick(blocks, (mine + k) % size), k) for k in range(1, size)
    ]


def row_parts(rows, count):
    unit = 8 if rows % 8 == 0 else 1
    edges = [unit * (rows // unit * p // count) for p in range(count + 1)]
    return [(edges[p], edges[p + 1]) for p in range(count)]


def dp_gather(value):
    bits = plane_bits()
    plane = lax.axis_index("dp") // 2
    core = lax.axis_index("dp") % 2
    count = 1 << len(bits)
    parts = []
    for p, (low, high) in enumerate(row_parts(value.shape[0], len(bits))):
        current = value[None, low:high]
        masks = [0]
        for bit in bits[p:] + bits[:p]:
            current = jnp.concatenate([current, swap(current, bit)])
            masks = masks + [m ^ (1 << (bit - 1)) for m in masks]
        other = swap(current, 0)
        place = jnp.asarray([masks.index(m) for m in range(count)], jnp.int32)
        rows_of = []
        for a in range(count):
            at = pick(place, plane ^ a)
            first, second = pick(current, at), pick(other, at)
            rows_of.append(
                jnp.stack([lax.select(core == 0, first, second), lax.select(core == 0, second, first)])
            )
        parts.append(jnp.stack(rows_of))
    whole = jnp.concatenate(parts, axis=2)
    return whole.reshape((2 * count,) + value.shape)


def dp_reduce(kept, sent):
    bits = plane_bits()
    plane = lax.axis_index("dp") // 2
    total = (kept + swap(sent.astype(jnp.bfloat16), 0).astype(jnp.float32)).astype(jnp.bfloat16)
    parts = []
    for p, (low, high) in enumerate(row_parts(total.shape[1], len(bits))):
        current = total[:, low:high]
        current = current.reshape((2,) * len(bits) + current.shape[1:])
        left = sorted(bits, reverse=True)
        for bit in bits[p:] + bits[:p]:
            axis = left.index(bit)
            mine = (plane >> (bit - 1)) & 1
            got = swap(pick(current, 1 - mine, axis), bit)
            current = pick(current, mine, axis).astype(jnp.float32) + got.astype(jnp.float32)
            left.remove(bit)
            if left:
                current = current.astype(jnp.bfloat16)
        parts.append(current)
    return jnp.concatenate(parts, axis=0)


def columns_of(value, core):
    dp = lax.axis_size("dp")
    wide = value.reshape(value.shape[0], dp // 2, 2, value.shape[1] // dp)
    return pick(wide, core, 2).reshape(value.shape[0], -1)


def weight_grad(left, right, extra=None):
    core = lax.axis_index("dp") % 2
    dp = lax.axis_size("dp")
    blocks = []
    for side in (core, 1 - core):
        block = dot(columns_of(left, side), right, 0, 0)
        block = block.reshape(dp // 2, left.shape[1] // dp, right.shape[1])
        if extra is not None:
            block = jnp.concatenate([block, pick(extra, side, 1)], axis=1)
        blocks.append(block)
    return dp_reduce(blocks[0], blocks[1])


def plain(
    tokens,
    cotangent,
    lengths,
    w_query,
    w_key,
    w_value,
    w_out,
    w_gate,
    w_up,
    w_down,
    gain_in,
    gain_query,
    gain_key,
    gain_attn,
    gain_pre,
    gain_post,
):
    count, width = tokens.shape
    seq_count = lengths.shape[1]
    stretch = count // (2 * seq_count)
    dp = lax.axis_size("dp")
    ctx = lax.axis_size("ctx")
    mine = lax.axis_index("ctx")
    head_dim = w_key.shape[1]
    heads = w_query.shape[1] // head_dim
    inner = w_gate.shape[1] // ctx
    span = 2 * ctx * stretch
    offsets = jnp.arange(stretch, dtype=jnp.int32)

    def positions_of(index):
        return jnp.concatenate(
            [index * stretch + offsets, (2 * ctx - 1 - index) * stretch + offsets]
        )

    local_pos = positions_of(mine)
    valid = (local_pos[None, :] < lengths[0][:, None]).astype(jnp.float32).reshape(count, 1)
    cosine, sine = rope_tables(jnp.tile(local_pos, seq_count).astype(jnp.float32), head_dim)
    key_pos = jnp.concatenate([positions_of((mine - k + ctx) % ctx) for k in range(ctx)])
    query_pos = jnp.repeat(local_pos, heads)
    allowed = (key_pos[None, None, :] <= query_pos[None, :, None]) & (
        key_pos[None, None, :] < lengths[0][:, None, None]
    )
    inv_root = head_dim ** (-0.5)

    gains = [gain_in, gain_query, gain_key, gain_attn, gain_pre, gain_post]
    sizes = [g.shape[0] for g in gains]
    small = jnp.concatenate(gains)
    qkv_shard = jnp.concatenate([w_query, w_key, w_value], axis=1)
    in_rows, in_cols = qkv_shard.shape
    out_rows = w_out.shape[0]
    top = max(in_rows, out_rows)
    packed_rows = -(-(top + 1) // 8) * 8
    packed = jnp.concatenate(
        [
            jnp.pad(qkv_shard, ((0, top - in_rows), (0, 0))),
            jnp.pad(w_out, ((0, top - out_rows), (0, 0))),
        ],
        axis=1,
    )
    last = jnp.pad(small[None], ((0, packed_rows - top - 1), (0, packed.shape[1] - small.shape[0])))
    packed = jnp.concatenate([packed, last], axis=0)
    near = ctx_ordered(ctx_gather(packed)).reshape(ctx * packed_rows, -1)
    everything = dp_gather(near).reshape(dp * ctx, packed_rows, -1)
    full_qkv = everything[:, :in_rows, :in_cols].reshape(width, in_cols)
    full_out = everything[:, :out_rows, in_cols:].reshape(heads * head_dim, width)
    smalls = everything[:, top, : small.shape[0]]
    norms, start = [], 0
    for size in sizes:
        norms.append(smalls[:, start : start + size].reshape(-1).astype(jnp.float32))
        start += size
    norm_in, norm_query, norm_key, norm_attn, norm_pre, norm_post = norms

    def column_blocks(weight):
        return weight.reshape(weight.shape[0], ctx, inner).transpose(1, 0, 2)

    gate_up = jnp.stack([column_blocks(w_gate), column_blocks(w_up)], axis=1)
    gate_up = ctx_ordered(ctx_exchange(gate_up)).transpose(1, 0, 2, 3)
    gate_up = gate_up.reshape(2, width // dp, inner)
    per = dp // ctx
    down = w_down.T.reshape(dp, width // dp, w_down.shape[0])
    down = lax.all_to_all(down, "dp", split_axis=0, concat_axis=0, tiled=True)
    down = down.reshape(ctx, per, width // dp, w_down.shape[0])
    down = ctx_ordered(ctx_exchange(down))
    down = down.transpose(2, 1, 0, 3).reshape(width // dp, inner)
    full_gate = dp_gather(gate_up[0]).reshape(width, inner)
    full_up = dp_gather(gate_up[1]).reshape(width, inner)
    full_down = dp_gather(down).reshape(width, inner)

    hidden = tokens.astype(jnp.float32)
    normed = rms_norm(hidden, norm_in).astype(jnp.bfloat16)
    qkv_raw = dot(normed, full_qkv, 1, 0)
    query_raw = qkv_raw[:, : heads * head_dim]
    key_raw = qkv_raw[:, heads * head_dim : (heads + 1) * head_dim]
    value_raw = qkv_raw[:, (heads + 1) * head_dim :]
    query_heads = query_raw.reshape(count, heads, head_dim)
    query_bf = rotate(
        rms_norm(query_heads, norm_query), cosine[:, None, :], sine[:, None, :]
    ).astype(jnp.bfloat16)
    query_bf = query_bf.reshape(seq_count, 2 * stretch * heads, head_dim)
    key_bf = rotate(rms_norm(key_raw, norm_key), cosine, sine).astype(jnp.bfloat16)
    both = jnp.concatenate([key_bf, value_raw.astype(jnp.bfloat16)], axis=1)
    both = jnp.stack(
        [p.reshape(seq_count, 2 * stretch, 2 * head_dim) for p in ctx_gather(both)], axis=1
    ).reshape(seq_count, span, 2 * head_dim)
    keys, values = both[..., :head_dim], both[..., head_dim:]
    scores = (
        jnp.einsum("sqd,skd->sqk", query_bf, keys, preferred_element_type=jnp.float32) * inv_root
    )
    masked = jnp.where(allowed, scores, -1e30)
    peak = jnp.max(masked, axis=-1, keepdims=True)
    expo = jnp.exp(masked - peak)
    total = jnp.sum(expo, axis=-1, keepdims=True)
    probs = expo / total
    probs_bf = probs.astype(jnp.bfloat16)
    mixed = jnp.einsum("sqk,skd->sqd", probs_bf, values, preferred_element_type=jnp.float32)
    mixed_bf = mixed.astype(jnp.bfloat16).reshape(count, heads * head_dim)
    attn_raw = dot(mixed_bf, full_out, 1, 0)
    after_attn = hidden + valid * rms_norm(attn_raw, norm_attn)
    normed_two = rms_norm(after_attn, norm_pre).astype(jnp.bfloat16)

    group_two = jnp.concatenate(ctx_gather(normed_two))
    gate = dot(group_two, full_gate, 1, 0)
    upper = dot(group_two, full_up, 1, 0)
    inner_bf = geglu(gate, upper).astype(jnp.bfloat16)
    ffn_part = dot(inner_bf, full_down, 1, 1)
    ffn_raw = ctx_reduce(list(ffn_part.reshape(ctx, count, width)))
    output = (after_attn + valid * rms_norm(ffn_raw, norm_post)).astype(jnp.bfloat16)

    grad_top = cotangent.astype(jnp.float32)
    ffn_grad, grad_gain_post = rms_back(ffn_raw, norm_post, valid * grad_top)
    group_ffn = jnp.concatenate(ctx_gather(ffn_grad.astype(jnp.bfloat16)))
    inner_grad = dot(group_ffn, full_down, 1, 0)
    _, geglu_pull = jax.vjp(geglu, gate, upper)
    gate_grad, upper_grad = geglu_pull(inner_grad)
    gate_grad_bf = gate_grad.astype(jnp.bfloat16)
    upper_grad_bf = upper_grad.astype(jnp.bfloat16)
    two_part = dot(gate_grad_bf, full_gate, 1, 1) + dot(upper_grad_bf, full_up, 1, 1)
    normed_two_grad = ctx_reduce(list(two_part.reshape(ctx, count, width)))
    grad_down = weight_grad(group_ffn, inner_bf).T
    grad_gate = weight_grad(group_two, gate_grad_bf)
    grad_up = weight_grad(group_two, upper_grad_bf)

    through_pre, grad_gain_pre = rms_back(after_attn, norm_pre, normed_two_grad)
    after_grad = grad_top + through_pre
    attn_grad, grad_gain_attn = rms_back(attn_raw, norm_attn, valid * after_grad)
    attn_grad_bf = attn_grad.astype(jnp.bfloat16)
    grad_out = weight_grad(attn_grad_bf, mixed_bf)
    grad_out = sum_of_ctx(grad_out.reshape(grad_out.shape[0], ctx, -1).transpose(1, 0, 2)).T
    mixed_grad_bf = dot(attn_grad_bf, full_out, 1, 1).astype(jnp.bfloat16)
    mixed_grad_bf = mixed_grad_bf.reshape(seq_count, 2 * stretch * heads, head_dim)
    prob_grad = jnp.einsum(
        "sqd,skd->sqk", mixed_grad_bf, values, preferred_element_type=jnp.float32
    )
    row_dot = jnp.sum(probs * prob_grad, axis=-1, keepdims=True)
    score_grad_bf = (probs * (prob_grad - row_dot)).astype(jnp.bfloat16)
    query_grad = (
        jnp.einsum("sqk,skd->sqd", score_grad_bf, keys, preferred_element_type=jnp.float32)
        * inv_root
    )
    keys_grad = (
        jnp.einsum("sqk,sqd->skd", score_grad_bf, query_bf, preferred_element_type=jnp.float32)
        * inv_root
    )
    values_grad = jnp.einsum(
        "sqk,sqd->skd", probs_bf, mixed_grad_bf, preferred_element_type=jnp.float32
    )
    both_grad = jnp.concatenate([keys_grad, values_grad], axis=-1)
    both_grad = both_grad.reshape(seq_count, ctx, 2 * stretch, 2 * head_dim).transpose(1, 0, 2, 3)
    own_grad = ctx_reduce(list(both_grad.reshape(ctx, count, 2 * head_dim)))
    own_keys_grad, own_values_grad = own_grad[:, :head_dim], own_grad[:, head_dim:]
    query_grad = rotate_back(
        query_grad.reshape(count, heads, head_dim), cosine[:, None, :], sine[:, None, :]
    )
    query_raw_grad, grad_gain_query = rms_back(query_heads, norm_query, query_grad)
    query_raw_bf = query_raw_grad.reshape(count, heads * head_dim).astype(jnp.bfloat16)
    key_raw_grad, grad_gain_key = rms_back(
        key_raw, norm_key, rotate_back(own_keys_grad, cosine, sine)
    )
    key_raw_bf = key_raw_grad.astype(jnp.bfloat16)
    value_raw_bf = own_values_grad.astype(jnp.bfloat16)
    raw_bf = jnp.concatenate([query_raw_bf, key_raw_bf, value_raw_bf], axis=1)
    normed_grad = dot(raw_bf, full_qkv, 1, 1)
    through_in, grad_gain_in = rms_back(hidden, norm_in, normed_grad)
    input_grad = (after_grad + through_in).astype(jnp.bfloat16)

    by_ctx = jnp.concatenate(
        [r.reshape(count, ctx, -1) for r in (query_raw_bf, key_raw_bf, value_raw_bf)], axis=2
    )
    each = by_ctx.shape[2]
    gain_grads = jnp.concatenate(
        [
            g.reshape(dp * ctx, -1)
            for g in (
                grad_gain_in,
                grad_gain_query,
                grad_gain_key,
                grad_gain_attn,
                grad_gain_pre,
                grad_gain_post,
            )
        ],
        axis=1,
    )
    small_size = gain_grads.shape[1]
    extra = jnp.pad(gain_grads, ((0, 0), (0, each - small_size))).reshape(
        dp // 2, 2, 1, ctx * each
    )
    extra = jnp.pad(extra, ((0, 0), (0, 0), (0, 7), (0, 0)))
    grad_qkv = weight_grad(normed, by_ctx.reshape(count, ctx * each), extra)
    grad_qkv = sum_of_ctx(grad_qkv.reshape(grad_qkv.shape[0], ctx, each).transpose(1, 0, 2))
    rows = width // dp
    gain_out = grad_qkv[rows, :small_size]
    grad_qkv = grad_qkv[:rows]
    q_cols, k_cols = heads * head_dim // ctx, head_dim // ctx
    outs, start = [], 0
    for size in sizes:
        outs.append(gain_out[start : start + size])
        start += size
    return (
        output,
        input_grad,
        grad_qkv[:, :q_cols],
        grad_qkv[:, q_cols : q_cols + k_cols],
        grad_qkv[:, q_cols + k_cols :],
        grad_out,
        grad_gate,
        grad_up,
        grad_down,
        *outs,
    )


def sum_of_ctx(blocks):
    size = lax.axis_size("ctx")
    mine = lax.axis_index("ctx")
    total = pick(blocks, mine).astype(jnp.float32)
    for k in range(1, size):
        got = shift(pick(blocks, (mine + k) % size).astype(jnp.bfloat16), k)
        total = total + got.astype(jnp.float32)
    return total


mega = 2**20
whole_vmem = 121 * mega // 2


def place(name):
    return {"vmem": pl.BlockSpec(memory_space=pltpu.VMEM), "smem": pl.BlockSpec(memory_space=pltpu.SMEM), "any": pl.BlockSpec(memory_space=pl.ANY)}[name]


def kernel_call(body, outs, args, where=None, scratch=(), out_where=None, grant=40 * mega):
    where, out_where = where or {}, out_where or {}
    return pl.pallas_call(
        body,
        out_shape=[jax.ShapeDtypeStruct(s, t) for s, t in outs],
        in_specs=[place(where.get(i, "vmem")) for i in range(len(args))],
        out_specs=[place(out_where.get(i, "vmem")) for i in range(len(outs))],
        scratch_shapes=list(scratch),
        compiler_params=pltpu.CompilerParams(vmem_limit_bytes=grant),
        cost_estimate=pl.CostEstimate(flops=0, bytes_accessed=0, transcendentals=0),
    )(*args)


def norm_back(value, weight, grad):
    scale = lax.rsqrt(jnp.mean(value * value, axis=-1, keepdims=True) + epsilon)
    normed = value * scale
    weighted = grad * (1.0 + weight)
    value_grad = scale * (weighted - normed * jnp.mean(weighted * normed, axis=-1, keepdims=True))
    return value_grad, jnp.sum(grad * normed, axis=0, keepdims=True)


def spread(index, tails, lane, size, ctx):
    dp = len(tails)
    shards = jnp.concatenate([t[:, lane : lane + 128] for t, _ in tails], axis=0)
    tail = shards.shape[0] // dp
    whole = dp * ctx * size
    column = lax.broadcasted_iota(jnp.int32, (128, whole), 1)
    line = lax.broadcasted_iota(jnp.int32, (128, whole), 0)
    spots = jnp.where(column % size == line, 1.0, 0.0).astype(jnp.bfloat16)
    values = dot(shards, spots, 1, 0)
    column = lax.broadcasted_iota(jnp.int32, (tail, whole), 1) // size
    line = lax.broadcasted_iota(jnp.int32, (tail, whole), 0)
    total = jnp.zeros((tail, whole), jnp.float32)
    for k, (_, mask) in enumerate(tails):
        owner = jnp.where(line < ctx, (index ^ mask) * ctx + line, -1)
        total = total + jnp.where(column == owner, values[k * tail : (k + 1) * tail], 0.0)
    return jnp.sum(total, axis=0, keepdims=True)


def pack(w_query, w_key, w_value, w_out, w_down, gains):
    part, width = w_down.shape
    chunk = width // 8
    rows = w_query.shape[0]
    parts = [w_query, w_key, w_value, w_out]
    ends = [int(e) for e in np.cumsum([0] + [p.shape[1] for p in parts])]
    tall = -(-max(rows + 1, w_out.shape[0]) // 8) * 8

    def body(down_ref, *rest):
        shards, lines = rest[: len(parts)], rest[len(parts) : len(parts) + len(gains)]
        out, *downs, wide, turned = rest[len(parts) + len(gains) :]
        turned[...] = down_ref[...].T
        group = lax.axis_index("dp")
        plane, core = group // 2, group % 2
        for flip, ref in enumerate(downs):
            for m in range(4):
                group = jnp.bitwise_xor(plane, m) * 2 + jnp.bitwise_xor(core, flip)
                ref[m] = turned[pl.ds(pl.multiple_of(group * chunk, 16), chunk), :]
        wide[...] = jnp.zeros(wide.shape, jnp.float32)
        for i, shard in enumerate(shards):
            wide[: shard.shape[0], ends[i] : ends[i + 1]] = shard[...].astype(jnp.float32)
        for i, line in enumerate(lines):
            wide[rows : rows + 1, i * 128 : i * 128 + line.shape[1]] = line[...].astype(
                jnp.float32
            )
        out[...] = wide[...].astype(jnp.bfloat16)

    return kernel_call(
        body,
        [((tall, ends[-1]), jnp.bfloat16)] + [((4, chunk, part), jnp.bfloat16)] * 2,
        [w_down, *parts, *[g.reshape(1, -1) for g in gains]],
        None,
        [pltpu.VMEM((tall, ends[-1]), jnp.float32), pltpu.VMEM((width, part), jnp.bfloat16)],
        grant=whole_vmem,
    )


def tables(where, lengths, count, stretch, ctx, head_dim):
    seqs = lengths.shape[1]
    each, half = count // seqs, head_dim // 2
    span = 2 * ctx * stretch
    freqs = rope_base ** (-2.0 * np.arange(half, dtype=np.float64) / head_dim)
    freqs = jnp.asarray(freqs[None].astype(np.float32))

    def positions(index, owner):
        block, step = index // stretch % 2, index % stretch
        return jnp.where(block == 0, owner, 2 * ctx - 1 - owner) * stretch + step

    def body(where_ref, lengths_ref, freqs_ref, cos_out, sin_out, valid_out, allowed_out):
        mine = where_ref[4]
        rows = lax.broadcasted_iota(jnp.int32, (each, 1), 0)
        local = positions(rows, mine)
        angles = local.astype(jnp.float32) * freqs_ref[...]
        cos, sin = jnp.cos(angles), jnp.sin(angles)
        cols = lax.broadcasted_iota(jnp.int32, (1, span), 1)
        owner = (mine - cols // each + ctx) % ctx
        keys = positions(cols % each, owner)
        for s in range(seqs):
            part = slice(s * each, (s + 1) * each)
            for low, high in ((0, half), (half, head_dim)):
                cos_out[part, low:high] = cos
                sin_out[part, low:high] = sin
            length = lengths_ref[0, s]
            valid_out[part, :] = jnp.where(local < length, 1.0, 0.0)
            allowed_out[s] = jnp.where((keys <= local) & (keys < length), 1.0, 0.0)

    return kernel_call(
        body,
        [
            ((count, head_dim), jnp.float32),
            ((count, head_dim), jnp.float32),
            ((count, 1), jnp.float32),
            ((seqs, each, span), jnp.float32),
        ],
        [where, lengths, freqs],
        {0: "smem", 1: "smem"},
    )


def plane_near(value):
    return [value, swap(value, 1), swap(value, 2)]


def cut(near):
    row = near[0].ndim - 2
    first = halves_of(near[0].shape[row])[0]
    low = lax.slice_in_dim(near[1], 0, first, axis=row)
    high = lax.slice_in_dim(near[2], first, None, axis=row)
    return [low, high]


def diagonal(halves):
    return [swap(halves[0], 2), swap(halves[1], 1)]


def plane_whole(near):
    pieces = near + diagonal(cut(near))
    return pieces + [swap(p, 0) for p in pieces]


def late_gains(where, pieces, lanes, sizes, ctx, behind):
    tall = pieces[0].shape[0]

    def body(where_ref, behind_ref, *rest):
        parts, outs = rest[: len(pieces)], rest[len(pieces) :]
        tails = tails_of(parts, tall)
        for out, lane, size in zip(outs, lanes, sizes):
            out[...] = spread(where_ref[0], tails, lane, size, ctx)

    return kernel_call(
        body,
        [((1, len(tails_of([np.zeros((tall, 1))] * len(pieces), tall)) * ctx * size), jnp.float32) for size in sizes],
        [where, behind, *pieces],
        {0: "smem", 1: "any"},
    )


def project(where, tokens, pieces, sizes, cosine, sine, heads, ctx):
    count, width = tokens.shape
    tall = pieces[0].shape[0]
    head_dim = cosine.shape[1]
    wide = (heads + 2) * head_dim
    total = len(pieces)

    def body(where_ref, x_ref, cos_ref, sin_ref, *rest):
        parts = rest[:total]
        normed_ref, query_out, both_out, raw_out, in_ref, query_ref, key_ref = rest[total : total + 7]
        weight, ends, sems, end_sems = rest[total + 7 :]
        copies = load_columns(where_ref[0], parts, tall, tall - 16, 0, weight, sems)
        tails = [
            (ref, mask, rows) for ref, mask, at, rows in pieces_of(parts, tall) if at + rows == tall
        ]
        end_copies = [
            pltpu.make_async_copy(
                ref.at[pl.ds(rows - 16, 16), pl.ds(0, ends.shape[2])], ends.at[i], end_sems.at[i]
            )
            for i, (ref, _, rows) in enumerate(tails)
        ]
        for copy in end_copies:
            copy.start()
        for copy in end_copies:
            copy.wait()
        tails = [(ends[i], mask) for i, (_, mask, _) in enumerate(tails)]
        for i, ref in enumerate((in_ref, query_ref, key_ref)):
            ref[...] = spread(where_ref[0], tails, i * 128, sizes[i], ctx)
        normed = rms_norm(x_ref[...].astype(jnp.float32), in_ref[...]).astype(jnp.bfloat16)
        normed_ref[...] = normed
        cos, sin = cos_ref[...], sin_ref[...]
        for copy in copies:
            copy.wait()
        for h in range(heads + 1):
            cols = slice(h * head_dim, (h + 1) * head_dim)
            raw = dot(normed, weight[:, cols], 1, 0)
            raw_out[:, cols] = raw
            gain = query_ref[...] if h < heads else key_ref[...]
            turned = rotate(rms_norm(raw, gain), cos, sin).astype(jnp.bfloat16)
            if h < heads:
                query_out[:, cols] = turned
            else:
                both_out[:, :head_dim] = turned
        both_out[:, head_dim:] = dot(normed, weight[:, (heads + 1) * head_dim :], 1, 0).astype(
            jnp.bfloat16
        )

    return kernel_call(
        body,
        [
            ((count, width), jnp.bfloat16),
            ((count, heads * head_dim), jnp.bfloat16),
            ((count, 2 * head_dim), jnp.bfloat16),
            ((count, (heads + 1) * head_dim), jnp.float32),
            ((1, width), jnp.float32),
            ((1, head_dim), jnp.float32),
            ((1, head_dim), jnp.float32),
        ],
        [where, tokens, cosine, sine, *pieces],
        {0: "smem", **{4 + i: "any" for i in range(total)}},
        [
            pltpu.VMEM((width, wide), jnp.bfloat16),
            pltpu.VMEM((8, 16, 384), jnp.bfloat16),
            pltpu.SemaphoreType.DMA((total,)),
            pltpu.SemaphoreType.DMA((8,)),
        ],
    )


def attend(
    where, tokens, query, both, allowed, valid, norm_attn, norm_pre, pieces, out_rows, heads
):
    count, width = tokens.shape
    seqs, each, span = allowed.shape
    head_dim = query.shape[1] // heads
    inv_root = head_dim ** (-0.5)
    near, total = len(both), len(pieces)
    tall, wide = pieces[0].shape

    def body(where_ref, x_ref, query_ref, allowed_ref, valid_ref, attn_ref, pre_ref, *rest):
        got, parts = rest[:near], rest[near : near + total]
        probs_out, mixed_out, raw_out, after_out, two_out, weight, sems = rest[near + total :]
        copies = load_columns(where_ref[0], parts, tall, out_rows, wide - width, weight, sems)
        for s in range(seqs):
            rows = slice(s * each, (s + 1) * each)
            queries = jnp.concatenate(
                [query_ref[rows, h * head_dim : (h + 1) * head_dim] for h in range(heads)], axis=0
            )
            keys = jnp.concatenate([g[rows, :head_dim] for g in got], axis=0)
            values = jnp.concatenate([g[rows, head_dim:] for g in got], axis=0)
            scores = dot(queries, keys, 1, 1) * inv_root
            keep = jnp.concatenate([allowed_ref[s]] * heads, axis=0)
            scores = jnp.where(keep > 0.0, scores, -1e30)
            expo = jnp.exp(scores - jnp.max(scores, axis=-1, keepdims=True))
            probs = expo / jnp.sum(expo, axis=-1, keepdims=True)
            probs_out[s] = probs
            mixed = dot(probs.astype(jnp.bfloat16), values, 1, 0).astype(jnp.bfloat16)
            for h in range(heads):
                mixed_out[rows, h * head_dim : (h + 1) * head_dim] = mixed[
                    h * each : (h + 1) * each
                ]
        for copy in copies:
            copy.wait()
        raw = dot(mixed_out[...], weight[...], 1, 0)
        raw_out[...] = raw
        after = x_ref[...].astype(jnp.float32) + valid_ref[...] * rms_norm(raw, attn_ref[...])
        after_out[...] = after
        two_out[...] = rms_norm(after, pre_ref[...]).astype(jnp.bfloat16)

    return kernel_call(
        body,
        [
            ((seqs, heads * each, span), jnp.float32),
            ((count, heads * head_dim), jnp.bfloat16),
            ((count, width), jnp.float32),
            ((count, width), jnp.float32),
            ((count, width), jnp.bfloat16),
        ],
        [where, tokens, query, allowed, valid, norm_attn, norm_pre, *both, *pieces],
        {0: "smem", **{7 + near + i: "any" for i in range(total)}},
        [
            pltpu.VMEM((heads * head_dim, width), jnp.bfloat16),
            pltpu.SemaphoreType.DMA((total,)),
        ],
    )


def column_steps(size, step):
    return [(s, min(size, s + step)) for s in range(0, size, step)]


def halves_of(rows):
    first = -(-rows // 32) * 16
    return first, rows - first


def pieces_of(refs, chunk):
    parts, far = refs[: len(refs) // 2], refs[len(refs) // 2 :]
    first, second = halves_of(chunk)
    shapes = [(0, 0, chunk), (2, 0, chunk), (4, 0, chunk), (6, 0, first), (6, first, second)]
    return [(ref, mask, at, rows) for ref, (mask, at, rows) in zip(parts, shapes)] + [
        (ref, mask ^ 1, at, rows) for ref, (mask, at, rows) in zip(far, shapes)
    ]


def load_weights(index, pair, last, chunk, target, sems):
    def copies(m):
        result = []
        for i, (ref, mask, at, rows) in enumerate(pieces_of(last if m == 2 else pair, chunk)):
            start = pl.multiple_of((index ^ mask) * chunk + at, 16)
            result.append(
                pltpu.make_async_copy(
                    ref if m == 2 else ref.at[m], target.at[m, pl.ds(start, rows)], sems.at[m, i]
                )
            )
        return result

    return [copies(m) for m in range(target.shape[0])]


def load_columns(index, refs, tall, rows, first, target, sems):
    copies = []
    for i, (ref, mask, at, size) in enumerate(pieces_of(refs, tall)):
        size = min(size, rows - at)
        if size > 0:
            start = pl.multiple_of((index ^ mask) * rows + at, 16)
            copies.append(
                pltpu.make_async_copy(
                    ref.at[pl.ds(0, size), pl.ds(first, target.shape[1])],
                    target.at[pl.ds(start, size)],
                    sems.at[i],
                )
            )
    for copy in copies:
        copy.start()
    return copies


def tails_of(refs, tall):
    return [
        (ref[rows - 16 : rows], mask) for ref, mask, at, rows in pieces_of(refs, tall) if at + rows == tall
    ]


def feed_forward(where, pieces, weights, with_own):
    count, width = pieces[0].shape
    (pair, last), kinds = weights, 3
    _, chunk, inner = pair[0].shape
    lanes = -(-inner // 128) * 128
    near, spots = len(pieces), len(pair)
    total = near * count
    slope = (2.0 / np.pi) ** 0.5

    def body(where_ref, *rest):
        pair_refs, last_refs, rest = rest[:spots], rest[spots : 2 * spots], rest[2 * spots :]
        parts, outs, sums = rest[:near], rest[near : near + 3], rest[near + 3 : near + 3 + near]
        weight, group, act, slopes, gates, sems, out_sems = rest[near + 3 + near :]
        copies = load_weights(where_ref[0], pair_refs, last_refs, chunk, weight, sems)
        for kind in copies:
            for copy in kind:
                copy.start()
        for k in range(near):
            group[k * count : (k + 1) * count, :] = parts[k][...]
        stores = [
            pltpu.make_async_copy(source, out, out_sems.at[i])
            for i, (source, out) in enumerate(zip((group, act, slopes), outs))
        ]
        stores[0].start()
        for copy in copies[0]:
            copy.wait()
        for low, high in column_steps(inner, 256):
            gates[:, low:high] = dot(group[...], weight[0, :, low:high], 1, 0)
        for copy in copies[1]:
            copy.wait()
        for low, high in column_steps(inner, 256):
            gate = gates[:, low:high]
            upper = dot(group[...], weight[1, :, low:high], 1, 0)
            square = 0.044715 * slope * gate * gate
            half = 0.5 + 0.5 * jnp.tanh(gate * (slope + square))
            gelu = gate * half
            steep = half * (1.0 + 2.0 * (gate - gelu) * (slope + 3.0 * square))
            act[:, low:high] = (gelu * upper).astype(jnp.bfloat16)
            slopes[0, :, low:high] = (steep * upper).astype(jnp.bfloat16)
            slopes[1, :, low:high] = gelu.astype(jnp.bfloat16)
        if lanes > inner:
            act[:, inner:] = jnp.zeros((total, lanes - inner), jnp.bfloat16)
        for store in stores[1:]:
            store.start()
        for copy in copies[2]:
            copy.wait()
        for low, high in column_steps(width, 256):
            part = dot(act[:, :inner], weight[2, low:high, :], 1, 1)
            for k in range(near):
                sums[k][:, low:high] = part[k * count : (k + 1) * count].astype(sums[k].dtype)
        for store in stores:
            store.wait()

    return kernel_call(
        body,
        [
            ((total, width), jnp.bfloat16),
            ((total, lanes), jnp.bfloat16),
            ((2, total, inner), jnp.bfloat16),
        ]
        + [((count, width), jnp.float32 if with_own and k == 0 else jnp.bfloat16) for k in range(near)],
        [where, *pair, *last, *pieces],
        {0: "smem", **{1 + i: "any" for i in range(2 * spots)}},
        [
            pltpu.VMEM((kinds, width, inner), jnp.bfloat16),
            pltpu.VMEM((total, width), jnp.bfloat16),
            pltpu.VMEM((total, lanes), jnp.bfloat16),
            pltpu.VMEM((2, total, inner), jnp.bfloat16),
            pltpu.VMEM((total, inner), jnp.float32),
            pltpu.SemaphoreType.DMA((kinds, spots)),
            pltpu.SemaphoreType.DMA((3,)),
        ],
        {i: "any" for i in range(3)},
        grant=whole_vmem,
    )


def finish(parts, after, cotangent, valid, norm_post):
    count, width = after.shape
    near = len(parts)

    def body(after_ref, cot_ref, valid_ref, post_ref, *rest):
        got = rest[:near]
        output_out, grad_out, gain_out = rest[near:]
        raw = got[0][...]
        for g in got[1:]:
            raw = raw + g[...].astype(jnp.float32)
        ok = valid_ref[...]
        output_out[...] = (after_ref[...] + ok * rms_norm(raw, post_ref[...])).astype(jnp.bfloat16)
        grad, gain = norm_back(raw, post_ref[...], ok * cot_ref[...].astype(jnp.float32))
        grad_out[...] = grad.astype(jnp.bfloat16)
        gain_out[...] = gain

    return kernel_call(
        body,
        [
            ((count, width), jnp.bfloat16),
            ((count, width), jnp.bfloat16),
            ((1, width), jnp.float32),
        ],
        [after, cotangent, valid, norm_post, *parts],
        grant=whole_vmem,
    )


def feed_back(where, pieces, weights, slopes, with_own):
    count, width = pieces[0].shape
    (pair, last), kinds = weights, 3
    _, chunk, inner = pair[0].shape
    lanes = -(-inner // 128) * 128
    near, spots = len(pieces), len(pair)
    total = near * count

    def body(where_ref, slopes_ref, *rest):
        pair_refs, last_refs, rest = rest[:spots], rest[spots : 2 * spots], rest[2 * spots :]
        parts = rest[:near]
        group_out, both_out = rest[near : near + 2]
        sums = rest[near + 2 : near + 2 + near]
        weight, sems = rest[near + 2 + near :]
        copies = load_weights(where_ref[0], pair_refs, last_refs, chunk, weight, sems)
        for kind in (copies[2], copies[0], copies[1]):
            for copy in kind:
                copy.start()
        for k in range(near):
            group_out[k * count : (k + 1) * count, :] = parts[k][...]
        for copy in copies[2]:
            copy.wait()
        for low, high in column_steps(inner, 256):
            grad = dot(group_out[...], weight[2, :, low:high], 1, 0)
            for i in range(2):
                slope = slopes_ref[i, :, low:high].astype(jnp.float32)
                both_out[i, :, low:high] = (grad * slope).astype(jnp.bfloat16)
        if lanes > inner:
            both_out[:, :, inner:] = jnp.zeros((2, total, lanes - inner), jnp.bfloat16)
        for kind in copies[:2]:
            for copy in kind:
                copy.wait()
        for low, high in column_steps(width, 256):
            part = dot(both_out[0, :, :inner], weight[0, low:high, :], 1, 1)
            part = part + dot(both_out[1, :, :inner], weight[1, low:high, :], 1, 1)
            for k in range(near):
                sums[k][:, low:high] = part[k * count : (k + 1) * count].astype(sums[k].dtype)

    return kernel_call(
        body,
        [((total, width), jnp.bfloat16)]
        + [((2, total, lanes), jnp.bfloat16)]
        + [((count, width), jnp.float32 if with_own and k == 0 else jnp.bfloat16) for k in range(near)],
        [where, slopes, *pair, *last, *pieces],
        {0: "smem", **{2 + i: "any" for i in range(2 * spots)}},
        [
            pltpu.VMEM((kinds, width, inner), jnp.bfloat16),
            pltpu.SemaphoreType.DMA((kinds, spots)),
        ],
        grant=whole_vmem,
    )


def wide_grads(where, lefts, rights):
    width = lefts[0].shape[1]
    total = sum(left.shape[0] for left in lefts)
    lanes = rights[0][0][0].shape[-1]
    kinds = len(rights)
    chunk = width // 8
    first, second = halves_of(chunk)
    arrays = []
    for array in [r for right in rights for r, _ in right]:
        if all(array is not other for other in arrays):
            arrays.append(array)
    spots = [[[array is other for other in arrays].index(True) for array, _ in right] for right in rights]
    most = max(len(right) for right in rights)

    def body(where_ref, *rest):
        left_refs, right_refs = rest[: len(lefts)], rest[len(lefts) : len(lefts) + len(arrays)]
        outs = rest[len(lefts) + len(arrays) : len(lefts) + len(arrays) + 4]
        turned, left, values, sems = rest[len(lefts) + len(arrays) + 4 :]
        copies = []
        for m, right in enumerate(rights):
            at, row = [], 0
            for i, (array, index) in enumerate(right):
                ref = right_refs[spots[m][i]]
                size = array.shape[-2]
                at.append(
                    pltpu.make_async_copy(
                        ref if index is None else ref.at[index],
                        values.at[m, pl.ds(row, size)],
                        sems.at[m, i],
                    )
                )
                row += size
            copies.append(at)
        for part in copies:
            for copy in part:
                copy.start()
        core, x, y = where_ref[1], where_ref[2], where_ref[3]
        order = []
        for flip in (1, 0):
            order.append([(j * 2 + jnp.bitwise_xor(x, flip), 0, first) for j in range(2)])
        for flip in (1, 0):
            order.append([(jnp.bitwise_xor(y, flip) * 2 + j, first, second) for j in range(2)])
        row = 0
        for ref in left_refs:
            turned[:, row : row + ref.shape[0]] = ref[...].T
            row += ref.shape[0]
        at = 0
        for block in order:
            for plane, offset, size in block:
                start = pl.multiple_of((plane * 2 + core) * chunk + offset, 16)
                left[at : at + size, :] = turned[pl.ds(start, size), :]
                at += size
        for m in range(kinds):
            for copy in copies[m]:
                copy.wait()
            for low, high in column_steps(lanes, 256):
                part = dot(left[...], values[m, :, low:high], 1, 0).astype(jnp.bfloat16)
                at = 0
                for out, block in zip(outs, order):
                    size = 2 * block[0][2]
                    out[m, :, low:high] = part[at : at + size]
                    at += size

    return kernel_call(
        body,
        [
            ((kinds, 2 * first, lanes), jnp.bfloat16),
            ((kinds, 2 * first, lanes), jnp.bfloat16),
            ((kinds, 2 * second, lanes), jnp.bfloat16),
            ((kinds, 2 * second, lanes), jnp.bfloat16),
        ],
        [where, *lefts, *arrays],
        {0: "smem", **{1 + len(lefts) + i: "any" for i in range(len(arrays))}},
        [
            pltpu.VMEM((width, total), jnp.bfloat16),
            pltpu.VMEM((width // 2, total), jnp.bfloat16),
            pltpu.VMEM((kinds, total, lanes), jnp.bfloat16),
            pltpu.SemaphoreType.DMA((kinds, most)),
        ],
        grant=whole_vmem,
    )


def wide_middle(where, wides, gots):
    sizes = [wide[0].shape[0] for wide in wides]
    kinds = sum(sizes)
    first, second = wides[0][1].shape[1] // 2, wides[0][3].shape[1] // 2
    lanes = wides[0][1].shape[2]
    args = [a for wide, got in zip(wides, gots) for a in (wide[1], got[0], wide[3], got[1])]

    def body(where_ref, *rest):
        refs, outs = rest[: len(args)], rest[len(args) :]
        x, y = where_ref[2], where_ref[3]
        at = 0
        for i, size in enumerate(sizes):
            kept_a, got_a, kept_b, got_b = refs[4 * i : 4 * i + 4]
            for m in range(size):
                for kept, got, place, rows, pair in (
                    (kept_a, got_a, y, first, outs[:2]),
                    (kept_b, got_b, x, second, outs[2:]),
                ):
                    for flip, out in ((1, pair[0]), (0, pair[1])):
                        spot = pl.ds(
                            pl.multiple_of(jnp.bitwise_xor(place, flip) * rows, 16), rows
                        )
                        total = kept[m, spot, :].astype(jnp.float32) + got[m, spot, :].astype(
                            jnp.float32
                        )
                        out[at] = total.astype(jnp.bfloat16)
                at += 1

    return kernel_call(
        body,
        [((kinds, first, lanes), jnp.bfloat16)] * 2 + [((kinds, second, lanes), jnp.bfloat16)] * 2,
        [where, *args],
        {0: "smem"},
        grant=whole_vmem,
    )


def wide_last(wide, got, inner):
    (_, kept_a, _, kept_b), (got_a, got_b) = wide, got
    kinds, first, _ = kept_a.shape
    second = kept_b.shape[1]

    def body(kept_a_ref, got_a_ref, kept_b_ref, got_b_ref, *outs):
        for m in range(kinds):
            total = kept_a_ref[m].astype(jnp.float32) + got_a_ref[m].astype(jnp.float32)
            outs[m][:first, :] = total[:, :inner]
            total = kept_b_ref[m].astype(jnp.float32) + got_b_ref[m].astype(jnp.float32)
            outs[m][first:, :] = total[:, :inner]

    return kernel_call(
        body,
        [((first + second, inner), jnp.float32)] * kinds,
        [kept_a, got_a, kept_b, got_b],
    )


def attend_back(
    where,
    parts,
    after,
    cotangent,
    valid,
    attn_raw,
    norm_pre,
    norm_attn,
    norm_query,
    probs,
    query,
    raw,
    both,
    pieces,
    out_rows,
    cosine,
    sine,
    heads,
):
    count, width = after.shape
    seqs, _, span = probs.shape
    each = count // seqs
    head_dim = norm_query.shape[1]
    inv_root = head_dim ** (-0.5)
    near, spots = len(both), len(pieces)
    tall, wide = pieces[0].shape

    def body(
        where_ref,
        after_ref,
        cot_ref,
        valid_ref,
        attn_ref,
        pre_ref,
        norm_ref,
        query_gain_ref,
        probs_ref,
        query_ref,
        raw_ref,
        cos_ref,
        sin_ref,
        *rest,
    ):
        shards, rest = rest[:spots], rest[spots:]
        sums = rest[:near]
        got = rest[near : 2 * near]
        rest = rest[2 * near :]
        dx_out, attn_grad_out, raw_grad_out, pre_out, attn_gain_out, query_gain_out = rest[:6]
        both_outs = rest[6 : 6 + near]
        mixed_grad, query_grad, weight, sems = rest[6 + near :]
        copies = load_columns(where_ref[0], shards, tall, out_rows, wide - width, weight, sems)
        grad = sums[0][...]
        for s in sums[1:]:
            grad = grad + s[...].astype(jnp.float32)
        through, gain = norm_back(after_ref[...], pre_ref[...], grad)
        pre_out[...] = gain
        dx = cot_ref[...].astype(jnp.float32) + through
        dx_out[...] = dx
        attn_grad, gain = norm_back(attn_ref[...], norm_ref[...], valid_ref[...] * dx)
        attn_gain_out[...] = gain
        attn_grad = attn_grad.astype(jnp.bfloat16)
        attn_grad_out[...] = attn_grad
        for copy in copies:
            copy.wait()
        mixed_grad[...] = dot(attn_grad, weight[...], 1, 1).astype(jnp.bfloat16)
        for s in range(seqs):
            rows = slice(s * each, (s + 1) * each)
            queries = jnp.concatenate(
                [query_ref[rows, h * head_dim : (h + 1) * head_dim] for h in range(heads)], axis=0
            )
            grads = jnp.concatenate(
                [mixed_grad[rows, h * head_dim : (h + 1) * head_dim] for h in range(heads)], axis=0
            )
            keys = jnp.concatenate([g[rows, :head_dim] for g in got], axis=0)
            values = jnp.concatenate([g[rows, head_dim:] for g in got], axis=0)
            probs = probs_ref[s]
            prob_grad = dot(grads, values, 1, 1)
            row = jnp.sum(probs * prob_grad, axis=-1, keepdims=True)
            score_grad = (probs * (prob_grad - row)).astype(jnp.bfloat16)
            back = dot(score_grad, keys, 1, 0) * inv_root
            for h in range(heads):
                query_grad[rows, h * head_dim : (h + 1) * head_dim] = back[
                    h * each : (h + 1) * each
                ]
            keys_grad = dot(score_grad, queries, 0, 0) * inv_root
            values_grad = dot(probs.astype(jnp.bfloat16), grads, 0, 0)
            for k in range(near):
                part = slice(k * each, (k + 1) * each)
                both_outs[k][rows, :head_dim] = keys_grad[part].astype(both_outs[k].dtype)
                both_outs[k][rows, head_dim:] = values_grad[part].astype(both_outs[k].dtype)
        cos, sin = cos_ref[...], sin_ref[...]
        gain_sum = jnp.zeros((1, head_dim), jnp.float32)
        for h in range(heads):
            cols = slice(h * head_dim, (h + 1) * head_dim)
            turned = rotate_back(query_grad[:, cols], cos, sin)
            value_grad, gain = norm_back(raw_ref[:, cols], query_gain_ref[...], turned)
            raw_grad_out[:, cols] = value_grad.astype(jnp.bfloat16)
            gain_sum = gain_sum + gain
        query_gain_out[...] = gain_sum

    return kernel_call(
        body,
        [
            ((count, width), jnp.float32),
            ((count, width), jnp.bfloat16),
            ((count, heads * head_dim), jnp.bfloat16),
            ((1, width), jnp.float32),
            ((1, width), jnp.float32),
            ((1, head_dim), jnp.float32),
            ((count, 2 * head_dim), jnp.float32),
        ]
        + [((count, 2 * head_dim), jnp.bfloat16)] * (near - 1),
        [
            where,
            after,
            cotangent,
            valid,
            attn_raw,
            norm_pre,
            norm_attn,
            norm_query,
            probs,
            query,
            raw,
            cosine,
            sine,
            *pieces,
            *parts,
            *both,
        ],
        {0: "smem", **{13 + i: "any" for i in range(spots)}},
        [
            pltpu.VMEM((count, heads * head_dim), jnp.bfloat16),
            pltpu.VMEM((count, heads * head_dim), jnp.float32),
            pltpu.VMEM((heads * head_dim, width), jnp.bfloat16),
            pltpu.SemaphoreType.DMA((spots,)),
        ],
        grant=whole_vmem,
    )


def project_back(
    where,
    parts,
    raw,
    query_grad,
    tokens,
    dx,
    norm_in,
    norm_key,
    cosine,
    sine,
    pieces,
    heads,
    ctx,
    gains,
):
    count, width = tokens.shape
    tall_piece = pieces[0].shape[0]
    head_dim = norm_key.shape[1]
    wide = (heads + 2) * head_dim
    near, spots, total = len(parts), len(pieces), 8
    each = wide // ctx
    count_gains = len(gains)
    tall = count + 16

    def body(
        where_ref, raw_ref, query_ref, x_ref, dx_ref, in_ref, key_ref, cos_ref, sin_ref, *rest
    ):
        sums = rest[:near]
        shards = rest[near : near + spots]
        others = rest[near + spots : near + spots + count_gains]
        input_out = rest[near + spots + count_gains]
        outs = rest[near + spots + count_gains + 1 : near + spots + count_gains + 1 + ctx]
        weight, grads_out, gains_out, sems = rest[near + spots + count_gains + 1 + ctx :]
        copies = load_columns(
            where_ref[0], shards, tall_piece, tall_piece - 16, 0, weight, sems
        )
        grad = sums[0][...]
        for s in sums[1:]:
            grad = grad + s[...].astype(jnp.float32)
        turned = rotate_back(grad[:, :head_dim], cos_ref[...], sin_ref[...])
        key_grad, key_gain = norm_back(raw_ref[:, heads * head_dim :], key_ref[...], turned)
        grads_out[:, : heads * head_dim] = query_ref[...]
        grads_out[:, heads * head_dim : (heads + 1) * head_dim] = key_grad.astype(jnp.bfloat16)
        grads_out[:, (heads + 1) * head_dim :] = grad[:, head_dim:].astype(jnp.bfloat16)
        for copy in copies:
            copy.wait()
        back = dot(grads_out[...], weight[...], 1, 1)
        through, in_gain = norm_back(x_ref[...].astype(jnp.float32), in_ref[...], back)
        input_out[...] = (dx_ref[...] + through).astype(jnp.bfloat16)
        gains_out[...] = jnp.zeros((16, wide), jnp.float32)
        lane = 0
        for gain in (in_gain, others[0][...], key_gain, *[o[...] for o in others[1:]]):
            size = gain.shape[1] // (total * ctx)
            for d in range(total):
                for c in range(ctx):
                    at = c * each + lane
                    gains_out[d : d + 1, at : at + size] = gain[
                        :, (d * ctx + c) * size : (d * ctx + c + 1) * size
                    ]
            lane += size
        spans = [(0, heads * head_dim), (heads * head_dim, head_dim), ((heads + 1) * head_dim, head_dim)]
        mine = where_ref[4]
        for c in range(ctx):

            @pl.when(mine == c)
            def _(c=c):
                for k in range(ctx):
                    j, at = (c + k) % ctx, 0
                    for first, size in spans:
                        step = size // ctx
                        outs[k][:count, at : at + step] = grads_out[
                            :, first + j * step : first + (j + 1) * step
                        ]
                        at += step
                    outs[k][count:, :] = gains_out[:, j * each : (j + 1) * each].astype(
                        jnp.bfloat16
                    )

    return kernel_call(
        body,
        [((count, width), jnp.bfloat16)] + [((tall, each), jnp.bfloat16)] * ctx,
        [
            where,
            raw,
            query_grad,
            tokens,
            dx,
            norm_in,
            norm_key,
            cosine,
            sine,
            *parts,
            *pieces,
            *gains,
        ],
        {0: "smem", **{9 + near + i: "any" for i in range(spots)}},
        [
            pltpu.VMEM((width, wide), jnp.bfloat16),
            pltpu.VMEM((count, wide), jnp.bfloat16),
            pltpu.VMEM((16, wide), jnp.float32),
            pltpu.SemaphoreType.DMA((spots,)),
        ],
        grant=whole_vmem,
    )


def narrow_grads(where, lefts, rights, with_gains):
    count, width = lefts[0].shape
    wide = rights[0].shape[1]
    chunk, near = width // 8, len(lefts)
    total = near * count
    tall = chunk + 16 if with_gains else chunk

    def body(where_ref, *rest):
        left_refs, right_refs, outs = rest[:near], rest[near : 2 * near], rest[2 * near : -3]
        turned, lines, values = rest[-3:]
        for i in range(near):
            turned[:, i * count : (i + 1) * count] = left_refs[i][...].T
            values[i * count : (i + 1) * count, :] = right_refs[i][:count, :]
        plane, core = where_ref[0] // 2, where_ref[1]
        for m in range(4):
            start = pl.multiple_of((jnp.bitwise_xor(plane, m) * 2 + core) * chunk, 16)
            lines[m * chunk : (m + 1) * chunk, :] = turned[pl.ds(start, chunk), :]
        for low, high in column_steps(wide, 256):
            part = dot(lines[...], values[:, low:high], 1, 0)
            for m in range(4):
                outs[m][:chunk, low:high] = part[m * chunk : (m + 1) * chunk].astype(outs[m].dtype)
        if with_gains:
            whole = right_refs[0][count:, :].astype(jnp.float32)
            for r in right_refs[1:]:
                whole = whole + r[count:, :].astype(jnp.float32)
            index = lax.broadcasted_iota(jnp.int32, whole.shape, 0)
            for m in range(4):
                row = jnp.bitwise_xor(plane, m) * 2 + core
                row = jnp.sum(jnp.where(index == row, whole, 0.0), axis=0, keepdims=True)
                outs[m][chunk:, :] = jnp.where(index == 0, row, 0.0).astype(outs[m].dtype)

    return kernel_call(
        body,
        [((tall, wide), jnp.float32)] + [((tall, wide), jnp.bfloat16)] * 3,
        [where, *lefts, *rights],
        {0: "smem"},
        [
            pltpu.VMEM((width, total), jnp.bfloat16),
            pltpu.VMEM((width // 2, total), jnp.bfloat16),
            pltpu.VMEM((total, wide), jnp.bfloat16),
        ],
    )


def narrow_middle(where, parts, sizes, ctx):
    chunk, wide = parts[0].shape
    each = wide // ctx

    def body(where_ref, *rest):
        got = rest[: len(parts)]
        outs = rest[len(parts) :]
        mine = where_ref[4]
        total = got[0][...]
        for g in got[1:]:
            total = total + g[...].astype(jnp.float32)
        for c in range(ctx):

            @pl.when(mine == c)
            def _(c=c):
                for k in range(ctx):
                    j = (c + k) % ctx
                    start, at = 0, 0
                    for size in sizes:
                        piece = size // ctx
                        outs[k][:, at : at + piece] = total[
                            :, start + j * piece : start + (j + 1) * piece
                        ].astype(outs[k].dtype)
                        start += size
                        at += piece

    return kernel_call(
        body,
        [((chunk, each), jnp.float32)] + [((chunk, each), jnp.bfloat16)] * (ctx - 1),
        [where, *parts],
        {0: "smem"},
    )


def narrow_last(blocks, out_blocks, sizes, cols):
    rows = out_blocks[0].shape[0]
    near = len(blocks)
    q, k, v = cols

    def body(*rest):
        outs = rest[2 * near :]
        total = rest[0][...]
        for r in rest[1:near]:
            total = total + r[...].astype(jnp.float32)
        outs[0][...] = total[:rows, :q]
        turned = total[:rows, q:].T
        outs[1][...] = turned[:k]
        outs[2][...] = turned[k:]
        out = rest[near][...]
        for r in rest[near + 1 : 2 * near]:
            out = out + r[...].astype(jnp.float32)
        outs[3][...] = out
        start = 0
        for ref, size in zip(outs[4:], sizes):
            ref[...] = total[rows : rows + 1, start : start + size]
            start += size

    return kernel_call(
        body,
        [
            ((rows, q), jnp.float32),
            ((k, rows), jnp.float32),
            ((v, rows), jnp.float32),
            ((rows, out_blocks[0].shape[1]), jnp.float32),
        ]
        + [((1, size), jnp.float32) for size in sizes],
        [*blocks, *out_blocks],
    )


def split_pair(where, gate, up, ctx):
    rows, whole = gate.shape
    inner = whole // ctx

    def body(where_ref, gate_ref, up_ref, *outs):
        mine = where_ref[4]
        for c in range(ctx):

            @pl.when(mine == c)
            def _(c=c):
                for k in range(ctx):
                    j = (c + k) % ctx
                    outs[k][0] = gate_ref[:, j * inner : (j + 1) * inner]
                    outs[k][1] = up_ref[:, j * inner : (j + 1) * inner]

    return kernel_call(
        body, [((2, rows, inner), jnp.bfloat16)] * ctx, [where, gate, up], {0: "smem"}, grant=whole_vmem
    )


def join_pair(where, pieces):
    ctx = len(pieces)
    _, rows, inner = pieces[0].shape

    def body(where_ref, *rest):
        got, out, wide = rest[:ctx], rest[ctx], rest[ctx + 1]
        mine = where_ref[4]
        for c in range(ctx):

            @pl.when(mine == c)
            def _(c=c):
                for m in range(2):
                    for a in range(ctx):
                        wide[a * rows : (a + 1) * rows, :] = got[(c - a) % ctx][m].astype(
                            jnp.float32
                        )
                    out[m] = wide[...].astype(jnp.bfloat16)

    return kernel_call(
        body,
        [((2, ctx * rows, inner), jnp.bfloat16)],
        [where, *pieces],
        {0: "smem"},
        [pltpu.VMEM((ctx * rows, inner), jnp.float32)],
    )[0]


def split_down(where, pieces, rows, ctx):
    groups = 2 * len(pieces)
    _, chunk, part = pieces[0].shape
    per, steps = groups // ctx, chunk // rows

    def body(where_ref, *rest):
        got, outs, (wide, down_ref) = rest[:4], rest[4 : 4 + ctx], rest[4 + ctx :]
        mine = where_ref[4]
        plane, core = where_ref[0] // 2, where_ref[1]
        for m in range(4):
            for flip in range(2):
                group = jnp.bitwise_xor(plane, m) * 2 + jnp.bitwise_xor(core, flip)
                down_ref[pl.ds(group, 1)] = got[m][flip][None]
        for c in range(ctx):

            @pl.when(mine == c)
            def _(c=c):
                for k in range(ctx):
                    j = (c + k) % ctx
                    for b in range(groups):
                        first = b % steps * rows
                        wide[:, b * part : (b + 1) * part] = down_ref[
                            j * per + b // steps, first : first + rows, :
                        ].astype(jnp.float32)
                    outs[k][...] = wide[...].astype(jnp.bfloat16)

    return kernel_call(
        body,
        [((rows, groups * part), jnp.bfloat16)] * ctx,
        [where, *pieces],
        {0: "smem"},
        [
            pltpu.VMEM((rows, groups * part), jnp.float32),
            pltpu.VMEM((groups, chunk, part), jnp.bfloat16),
        ],
    )


def join_down(where, pieces, part):
    ctx = len(pieces)
    rows, inner = pieces[0].shape
    chunk, groups = ctx * rows, inner // part

    def body(where_ref, *rest):
        got, out, wide = rest[:ctx], rest[ctx], rest[ctx + 1]
        mine = where_ref[4]
        for c in range(ctx):

            @pl.when(mine == c)
            def _(c=c):
                for a in range(ctx):
                    piece = got[(c - a) % ctx][...].astype(jnp.float32)
                    for b in range(groups):
                        first = b % ctx * rows
                        at = (b // ctx * ctx + a) * part
                        wide[first : first + rows, at : at + part] = piece[
                            :, b * part : (b + 1) * part
                        ]
                out[...] = wide[...].astype(jnp.bfloat16)

    return kernel_call(
        body,
        [((chunk, inner), jnp.bfloat16)],
        [where, *pieces],
        {0: "smem"},
        [pltpu.VMEM((chunk, inner), jnp.float32)],
    )[0]


def join_rows(where, pieces, rows, split, out_rows):
    ctx = len(pieces)
    _, wide = pieces[0].shape
    tall = ctx * rows + 16

    def body(where_ref, *rest):
        got, out, lines = rest[:ctx], rest[ctx], rest[ctx + 1]
        mine = where_ref[4]
        lines[ctx * rows :, :] = jnp.zeros((16, wide), jnp.float32)
        lines[ctx * out_rows :, split:] = jnp.zeros((tall - ctx * out_rows, wide - split), jnp.float32)
        for c in range(ctx):

            @pl.when(mine == c)
            def _(c=c):
                for a in range(ctx):
                    piece = got[(c - a) % ctx]
                    lines[a * rows : (a + 1) * rows, :split] = piece[:rows, :split].astype(
                        jnp.float32
                    )
                    lines[a * out_rows : (a + 1) * out_rows, split:] = piece[
                        :out_rows, split:
                    ].astype(jnp.float32)
                    at = ctx * rows + a
                    lines[at : at + 1, :split] = piece[rows : rows + 1, :split].astype(jnp.float32)
                out[...] = lines[...].astype(jnp.bfloat16)

    return kernel_call(
        body,
        [((tall, wide), jnp.bfloat16)],
        [where, *pieces],
        {0: "smem"},
        [pltpu.VMEM((tall, wide), jnp.float32)],
    )[0]


def plane_send(parts):
    size = lax.axis_size("dp")
    return [parts[0]] + [
        lax.ppermute(parts[m], "dp", [(i, i ^ (2 * m)) for i in range(size)])
        for m in range(1, len(parts))
    ]


def ctx_send(parts, sign):
    return [parts[0]] + [shift(parts[k], sign * k) for k in range(1, len(parts))]


def stage(*values):
    return lax.optimization_barrier(values)


def gate(value, *conditions):
    return lax.optimization_barrier((value, conditions))[0]


def fused(
    tokens,
    cotangent,
    lengths,
    w_query,
    w_key,
    w_value,
    w_out,
    w_gate,
    w_up,
    w_down,
    gain_in,
    gain_query,
    gain_key,
    gain_attn,
    gain_pre,
    gain_post,
):
    count, width = tokens.shape
    seq_count = lengths.shape[1]
    stretch = count // (2 * seq_count)
    dp = lax.axis_size("dp")
    ctx = lax.axis_size("ctx")
    mine = lax.axis_index("ctx")
    group = lax.axis_index("dp")
    head_dim = w_key.shape[1]
    heads = w_query.shape[1] // head_dim
    where = jnp.stack([group, group % 2, group // 2 % 2, group // 4, mine]).astype(jnp.int32)

    gains = [gain_in, gain_query, gain_key, gain_attn, gain_pre, gain_post]
    sizes = [g.shape[0] for g in gains]
    chunk, out_rows = width // dp, heads * head_dim // dp
    order = [0, 1, 3, 2]
    packed, kept, sent = pack(w_query, w_key, w_value, w_out, w_down, gains)
    split = packed.shape[1] - width
    packed = ctx_gather(packed)
    got = swap(sent, 0)
    aux = tables(where, lengths, count, stretch, ctx, head_dim)
    blocks = split_pair(where, w_gate, w_up, ctx)
    kept = gate(kept, aux, blocks)
    downs = plane_send([jnp.stack([kept[m], got[m]]) for m in range(4)])
    packed, downs, aux, blocks = stage(packed, downs, aux, list(blocks))
    cosine, sine, valid, allowed = aux

    blocks = ctx_send(blocks, 1)
    near = plane_near(join_rows(where, packed, w_query.shape[0], split, w_out.shape[0]))
    shared = plane_whole(near)
    pair = join_pair(where, blocks)
    shared, pair, downs = stage(shared, pair, downs)

    normed, query, both, raw, norm_in, norm_query, norm_key = project(
        where, tokens, shared, sizes[:3], cosine, sine, heads, ctx
    )
    pair, normed, query, both, downs = stage(pair, normed, query, both, downs)

    pair = plane_near(pair)
    downs = list(split_down(where, downs, w_gate.shape[0], ctx))
    norm_attn, norm_pre, norm_post = late_gains(
        where, shared, [384, 512, 640], sizes[3:], ctx, both
    )
    both = ctx_gather(both)
    downs = ctx_send(gate(downs, both), 1)
    probs, mixed, attn_raw, residual, normed_two = attend(
        where,
        tokens,
        query,
        both,
        allowed,
        valid,
        norm_attn,
        norm_pre,
        shared,
        out_rows,
        heads,
    )
    pair, pair_cut, downs, normed_two, mixed = stage(pair, cut(pair), downs, normed_two, mixed)

    last = plane_near(join_down(where, downs, w_down.shape[0]))
    two_pieces = [normed_two] + [shift(normed_two, k) for k in order[1:-1]]
    pair_far = [swap(pair[0], 0)]
    two_pieces, pair, pair_far, last, last_cut, normed = stage(
        two_pieces, pair, pair_far, last, cut(last), normed
    )

    two_pieces.append(shift(two_pieces[0], order[-1]))
    pair = pair + diagonal(pair_cut)
    pair_far = pair_far + [swap(p, 0) for p in pair[1:3]]
    two_pieces, pair, pair_far, last, last_cut, normed = stage(
        two_pieces, pair, pair_far, last, last_cut, normed
    )

    last = last + diagonal(last_cut)
    pair_far = pair_far + [swap(p, 0) for p in pair[3:]]
    pair, last = pair + pair_far, last + [swap(p, 0) for p in last]
    two_pieces, pair, last, normed = stage(two_pieces, pair, last, normed)

    weights = (pair, last)
    normed_group = [normed, shift(normed, 1), None, shift(normed, 3)]
    group_two, act, slopes, *sums = feed_forward(where, two_pieces[:-1], weights, True)
    group_two, act, slopes, sums, near_group = stage(
        group_two, act, slopes, sums, [normed_group[1], normed_group[3]]
    )
    normed_group[1], normed_group[3] = near_group

    sums = [sums[0]] + [shift(sums[i], -order[i]) for i in range(1, ctx - 1)]
    two_last, act_last, slopes_last, sum_last = feed_forward(
        where, two_pieces[-1:], weights, False
    )
    sums, two_last, act_last, slopes_last, sum_last, group_two, act, mixed = stage(
        sums, two_last, act_last, slopes_last, sum_last, group_two, act, mixed
    )

    sums.append(shift(sum_last, -order[-1]))
    group_two, act = [group_two, two_last], [act, act_last]
    group_two_far, act_far = [swap(g, 0) for g in group_two], [swap(a, 0) for a in act]
    mixed_far = swap(mixed, 0)
    sums, group_two_far, act_far, mixed_far = stage(sums, group_two_far, act_far, mixed_far)

    output, ffn_grad, gain_post_grad = finish(sums, residual, cotangent, valid, norm_post)
    ffn_early = [ffn_grad] + [shift(ffn_grad, k) for k in order[1:-1]]
    ffn_early, ffn_grad = stage(ffn_early, ffn_grad)

    ffn_last = shift(ffn_grad, order[-1])
    group_ffn, grads, *sums = feed_back(where, ffn_early, weights, slopes, True)
    ffn_last, group_ffn, grads, sums = stage(ffn_last, group_ffn, grads, sums)

    ffn_parts = [group_ffn, ffn_last]
    ffn_far = [swap(f, 0) for f in ffn_parts]
    grads_far = swap(grads, 0)
    _, grads_last, sum_last = feed_back(
        where, [ffn_last], weights, slopes_last, False
    )
    sums[1], sums[2] = shift(sums[1], -order[1]), shift(sums[2], -order[2])
    down_wide = wide_grads(
        where, gate(ffn_parts, grads_last) + ffn_far, [[(a, None) for a in act + act_far]]
    )
    grads_last, sum_last, grads, grads_far, sums, down_wide = stage(
        grads_last, sum_last, grads, grads_far, sums, down_wide
    )

    sums.append(shift(sum_last, -order[-1]))
    down_got = [swap(down_wide[0], 1), swap(down_wide[2], 2)]
    all_grads = [grads, grads_last, grads_far, swap(grads_last, 0)]
    pair_wide = wide_grads(
        where, group_two + group_two_far, [[(g, m) for g in all_grads] for m in range(2)]
    )
    sums, down_wide, down_got, pair_wide = stage(sums, down_wide, down_got, pair_wide)

    pair_got = [swap(pair_wide[0], 1), swap(pair_wide[2], 2)]
    dx, attn_grad, query_grad, gain_pre_grad, gain_attn_grad, gain_query_grad, *parts = attend_back(
        where,
        sums,
        residual,
        cotangent,
        valid,
        attn_raw,
        norm_pre,
        norm_attn,
        norm_query,
        probs,
        query,
        raw,
        both,
        shared,
        out_rows,
        cosine,
        sine,
        heads,
    )
    parts = ctx_send(parts, -1)
    out_blocks = narrow_grads(
        where, [attn_grad, swap(attn_grad, 0)], [mixed, mixed_far], False
    )
    parts, pair_got, out_blocks, query_grad, dx, normed = stage(
        parts, pair_got, out_blocks, query_grad, dx, normed
    )

    input_grad, *blocks = project_back(
        where,
        parts,
        raw,
        query_grad,
        tokens,
        dx,
        norm_in,
        norm_key,
        cosine,
        sine,
        shared,
        heads,
        ctx,
        [gain_query_grad, gain_attn_grad, gain_pre_grad, gain_post_grad],
    )
    normed_group[2] = shift(normed, 2)
    out_blocks = plane_send(out_blocks)
    wide = wide_middle(where, [pair_wide, down_wide], [pair_got, down_got])
    blocks, out_blocks, wide, normed_group = stage(list(blocks), out_blocks, wide, normed_group)

    blocks = ctx_send(blocks, 1)
    wide_got = [swap(wide[0], 2), swap(wide[2], 1)]
    normed_far = [swap(n, 0) for n in normed_group]
    blocks = narrow_grads(
        where, normed_group + normed_far, blocks + [swap(b, 0) for b in blocks], True
    )
    out_blocks = narrow_middle(where, out_blocks, [mixed.shape[1]], ctx)
    wide_got, out_blocks, blocks = stage(wide_got, out_blocks, blocks)

    blocks, out_blocks = plane_send(blocks), ctx_send(out_blocks, 1)
    grad_gate, grad_up, grad_down = wide_last(wide, wide_got, w_gate.shape[1] // ctx)
    blocks, out_blocks, grad_gate = stage(blocks, out_blocks, grad_gate)

    q_cols, k_cols = heads * head_dim // ctx, head_dim // ctx
    grad_query, grad_key, grad_value, grad_out, *gain_outs = narrow_last(
        blocks, out_blocks, sizes, (q_cols, k_cols, k_cols)
    )
    return (
        output,
        input_grad,
        grad_query,
        grad_key.T,
        grad_value.T,
        grad_out.T,
        grad_gate,
        grad_up,
        grad_down.T,
        *[g.reshape(-1) for g in gain_outs],
    )


def on_device(tokens, cotangent, lengths, *params):
    dp, ctx = lax.axis_size("dp"), lax.axis_size("ctx")
    each = tokens.shape[0] // lengths.shape[1]
    fits = dp == 8 and dp % ctx == 0 and tokens.shape[1] // dp % 16 == 0 and each % 16 == 0
    run = fused if fits else plain
    return run(tokens, cotangent, lengths, *params)


def solution(mesh):
    in_specs = (
        P(("dp", "ctx"), None),
        P(("dp", "ctx"), None),
        P("dp", None),
        P(("dp", "ctx"), None),
        P(("dp", "ctx"), None),
        P(("dp", "ctx"), None),
        P(("dp", "ctx"), None),
        P(("dp", "ctx"), None),
        P(("dp", "ctx"), None),
        P(("dp", "ctx"), None),
        P(("dp", "ctx")),
        P(("dp", "ctx")),
        P(("dp", "ctx")),
        P(("dp", "ctx")),
        P(("dp", "ctx")),
        P(("dp", "ctx")),
    )
    out_specs = (
        P(("dp", "ctx"), None),
        P(("dp", "ctx"), None),
        P("dp", "ctx"),
        P("dp", "ctx"),
        P("dp", "ctx"),
        P("ctx", "dp"),
        P("dp", "ctx"),
        P("dp", "ctx"),
        P("ctx", "dp"),
        P(("dp", "ctx")),
        P(("dp", "ctx")),
        P(("dp", "ctx")),
        P(("dp", "ctx")),
        P(("dp", "ctx")),
        P(("dp", "ctx")),
    )
    return jax.shard_map(
        on_device, mesh=mesh, in_specs=in_specs, out_specs=out_specs, check_vma=False
    )
```
